32 devices in a mesh: dp: 8 (over z, y), row: 2 (over core), col: 2 (over x).
Axes of the slice: x: 2, y: 2, z: 4, core: 2. Of those that a mesh axis runs over, the one named last changes fastest.
Arguments:
- tokens: bfloat16 [8192, 1024], P(('dp', 'row'), 'col'), may hold values from -13 to 13
- cotangent: bfloat16 [8192, 1024], P(('dp', 'row'), 'col'), may hold values from -13 to 13
- input_projection_weight: float32 [1024, 3, 1024], P('col', None, 'row'), may hold values from -0.1875 to 0.1875
- conv_weight: float32 [3, 1024], P(None, 'row'), may hold values from -3 to 3
- output_projection_weight: float32 [1024, 1024], P('row', 'col'), may hold values from -0.1875 to 0.1875
- norm_gains: float32 [2, 1024], P(None, 'col'), may hold values from 0.5 to 1.5
- gate_up_weight: float32 [1024, 2, 4608], P('col', None, 'row'), may hold values from -0.21875 to 0.21875
- down_projection_weight: float32 [4608, 1024], P('row', 'col'), may hold values from -0.09375 to 0.09375
- in_first: float32 [1024, 3, 1024], P('col', None, 'row'), may hold values from -512 to 512
- in_second: float32 [1024, 3, 1024], P('col', None, 'row'), may hold values from 5464.064 to 21848.064
- conv_first: float32 [3, 1024], P(None, 'row'), may hold values from -512 to 512
- conv_second: float32 [3, 1024], P(None, 'row'), may hold values from 5464.064 to 21848.064
- out_first: float32 [1024, 1024], P('row', 'col'), may hold values from -512 to 512
- out_second: float32 [1024, 1024], P('row', 'col'), may hold values from 5464.064 to 21848.064
- gain_first: float32 [2, 1024], P(None, 'col'), may hold values from -640 to 640
- gain_second: float32 [2, 1024], P(None, 'col'), may hold values from 8192 to 32768
- gu_first: float32 [1024, 2, 4608], P('col', None, 'row'), may hold values from -160 to 160
- gu_second: float32 [1024, 2, 4608], P('col', None, 'row'), may hold values from 434.176 to 1744.896
- down_first: float32 [4608, 1024], P('row', 'col'), may hold values from -320 to 320
- down_second: float32 [4608, 1024], P('row', 'col'), may hold values from 1966.08 to 7864.32
Outputs:
- output: bfloat16 [8192, 1024], P(('dp', 'row'), 'col')
- token_grad: bfloat16 [8192, 1024], P(('dp', 'row'), 'col')
- in_weight_new: float32 [1024, 3, 1024], P('col', None, 'row')
- in_first_new: float32 [1024, 3, 1024], P('col', None, 'row')
- in_second_new: float32 [1024, 3, 1024], P('col', None, 'row')
- conv_weight_new: float32 [3, 1024], P(None, 'row')
- conv_first_new: float32 [3, 1024], P(None, 'row')
- conv_second_new: float32 [3, 1024], P(None, 'row')
- out_weight_new: float32 [1024, 1024], P('row', 'col')
- out_first_new: float32 [1024, 1024], P('row', 'col')
- out_second_new: float32 [1024, 1024], P('row', 'col')
- gains_new: float32 [2, 1024], P(None, 'col')
- gain_first_new: float32 [2, 1024], P(None, 'col')
- gain_second_new: float32 [2, 1024], P(None, 'col')
- gate_up_new: float32 [1024, 2, 4608], P('col', None, 'row')
- gu_first_new: float32 [1024, 2, 4608], P('col', None, 'row')
- gu_second_new: float32 [1024, 2, 4608], P('col', None, 'row')
- down_weight_new: float32 [4608, 1024], P('row', 'col')
- down_first_new: float32 [4608, 1024], P('row', 'col')
- down_second_new: float32 [4608, 1024], P('row', 'col')
- trust_norms: float32 [7, 2], replicated
The draws below stay inside these ranges and needn't reach their ends.
All inputs are finite; a program needn't handle non-finite values.
Results may differ from the reference program's by a relative error of at most 0.013.
Values may be sent and summed in bfloat16 or wider, within the bound.
No kernel may reach another device: no remote copies, remote signals or barrier semaphores. Data moves between devices by JAX's collectives and lax.ppermute only.
A program may use at most 256 MiB of HBM per device.

```python
import math
import jax
import jax.numpy as jnp
from jax import lax

D = 1024
FF = 4608
STEP = 5
TOKENS = 8192
SEQ = 8192


def ramp_profile(count, top):
    steps = jnp.arange(count, dtype=jnp.float32) / (count - 1)
    level = 1.0 + (top - 1.0) * steps
    return level / jnp.sqrt(jnp.float32((top ** 3 - 1.0) / (3.0 * (top - 1.0))))


def row_scaled(key, top):
    first, second = jax.random.split(key)
    return (first, jnp.exp(jax.random.uniform(second, (TOKENS, 1), jnp.float32, -0.69, 0.69)) * ramp_profile(D, top))


def draw_tokens(key, part):
    key = jax.random.fold_in(key, 3)
    first, scales = row_scaled(key, 3.0)
    values = jnp.clip(jax.random.normal(first, (TOKENS, D), jnp.float32), -4.0, 4.0)
    return (values * scales).astype(jnp.bfloat16)


def draw_cotangent(key, part):
    key = jax.random.fold_in(key, 4)
    first, scales = row_scaled(key, 3.0)
    values = jnp.clip(jax.random.normal(first, (TOKENS, D), jnp.float32), -4.0, 4.0)
    return (values * scales).astype(jnp.bfloat16)


def draw_conv_weight(key, part):
    key = jax.random.fold_in(key, 5)
    values = jnp.clip(jax.random.normal(key, (3, D), jnp.float32), -3.0, 3.0) * ramp_profile(D, 3.0)
    return values / jnp.sqrt(jnp.float32(3.0))


def draw_gate_up_weight(key, part):
    key = jax.random.fold_in(key, 6)
    values = jnp.clip(jax.random.normal(key, (D, 2, FF), jnp.float32), -4.0, 4.0) * ramp_profile(FF, 3.0)
    return values * lax.rsqrt(jnp.float32(D))


def block_scale(key, extent, shards, smallest, high):
    loudness = 1.0
    for axis_at, parts in shards:
        heights = jax.random.uniform(jax.random.fold_in(jax.random.fold_in(key, 6), axis_at), (parts,), jnp.float32, smallest / len(shards), high / len(shards))
        loudness = loudness * jnp.repeat(jnp.exp(heights), extent[axis_at] // parts).reshape((-1,) + (1,) * (len(extent) - 1 - axis_at))
    return loudness


def scatter_about(own_key, dims, deviation, reach, cuts=(), held_as=jnp.bfloat16):
    values = jax.random.normal(own_key, dims, jnp.float32) * deviation
    if len(cuts) > 0:
        values = block_scale(own_key, dims, cuts, -0.22, 0.18) * values
    return jnp.clip(values, min=-reach, max=reach).astype(held_as)


def setup_inputs(seed: int = 0) -> dict:
    streams_of = jax.random.split(jax.random.key(seed), 21)
    return {
        "tokens": draw_tokens(jax.random.fold_in(streams_of[20], 71), 0),
        "cotangent": draw_cotangent(jax.random.fold_in(streams_of[20], 71), 0),
        "input_projection_weight": scatter_about(streams_of[2], (D, 3, D), D ** -0.5, 0.1875, ((0, 2), (2, 2)), jnp.float32),
        "conv_weight": draw_conv_weight(jax.random.fold_in(streams_of[20], 71), 0),
        "output_projection_weight": scatter_about(streams_of[4], (D, D), D ** -0.5, 0.1875, ((0, 2), (1, 2)), jnp.float32),
        "norm_gains": jnp.clip(1.0 + 0.1 * jax.random.normal(streams_of[5], (2, D), jnp.float32), 0.5, 1.5),
        "gate_up_weight": draw_gate_up_weight(jax.random.fold_in(streams_of[20], 71), 0),
        "down_projection_weight": scatter_about(streams_of[7], (FF, D), FF ** -0.5, 0.09375, ((0, 2), (1, 2)), jnp.float32),
        "in_first": scatter_about(streams_of[8], (D, 3, D), (TOKENS ** 0.5), 512.0, ((0, 2), (2, 2)), jnp.float32),
        "in_second": jnp.clip(jnp.exp(math.log(21848.064) - 1.3859195 * jax.random.uniform(streams_of[9], (D, 3, D), jnp.float32) ** block_scale(streams_of[9], (D, 3, D), ((0, 2), (2, 2)), -0.2, 0.2)), 5464.064, 21848.064),
        "conv_first": scatter_about(streams_of[10], (3, D), (TOKENS ** 0.5), 512.0, ((1, 2),), jnp.float32),
        "conv_second": jnp.clip(jnp.exp(math.log(21848.064) - 1.3859195 * jax.random.uniform(streams_of[11], (3, D), jnp.float32) ** block_scale(streams_of[11], (3, D), ((1, 2),), -0.2, 0.2)), 5464.064, 21848.064),
        "out_first": scatter_about(streams_of[12], (D, D), (TOKENS ** 0.5), 512.0, ((0, 2), (1, 2)), jnp.float32),
        "out_second": jnp.clip(jnp.exp(math.log(21848.064) - 1.3859195 * jax.random.uniform(streams_of[13], (D, D), jnp.float32) ** block_scale(streams_of[13], (D, D), ((0, 2), (1, 2)), -0.2, 0.2)), 5464.064, 21848.064),
        "gain_first": scatter_about(streams_of[14], (2, D), ((1.5 * TOKENS) ** 0.5), 640.0, ((1, 2),), jnp.float32),
        "gain_second": jnp.clip(jnp.exp(math.log(32768.0) - 1.3862944 * jax.random.uniform(streams_of[15], (2, D), jnp.float32) ** block_scale(streams_of[15], (2, D), ((1, 2),), -0.2, 0.2)), 8192.0, 32768.0),
        "gu_first": scatter_about(streams_of[16], (D, 2, FF), ((0.08 * TOKENS) ** 0.5), 160.0, ((0, 2), (2, 2)), jnp.float32),
        "gu_second": jnp.clip(jnp.exp(math.log(1744.896) - 1.3910003 * jax.random.uniform(streams_of[17], (D, 2, FF), jnp.float32) ** block_scale(streams_of[17], (D, 2, FF), ((0, 2), (2, 2)), -0.2, 0.2)), 434.176, 1744.896),
        "down_first": scatter_about(streams_of[18], (FF, D), ((0.36 * TOKENS) ** 0.5), 320.0, ((0, 2), (1, 2)), jnp.float32),
        "down_second": jnp.clip(jnp.exp(math.log(7864.32) - 1.3862944 * jax.random.uniform(streams_of[19], (FF, D), jnp.float32) ** block_scale(streams_of[19], (FF, D), ((0, 2), (1, 2)), -0.2, 0.2)), 1966.08, 7864.32),
    }


norm_eps = 1e-05
adam_eps = 1e-06
beta_one = 0.5
beta_two = 0.6
learn_rate = 0.5
decay_rate = 0.01
highest_precision = lax.Precision.HIGHEST

@jax.custom_vjp
def lower_precision(v):
    return lax.optimization_barrier(v.astype(jnp.bfloat16)).astype(jnp.float32)

@jax.custom_vjp
def lower_precision_backward(v):
    return v

def low_keep(v):
    return (lower_precision(v), None)

def low_pass(kept, grad):
    return (grad,)

def back_keep(v):
    return (v, None)

def back_low(kept, grad):
    return (lower_precision(grad),)
lower_precision.defvjp(low_keep, low_pass)
lower_precision_backward.defvjp(back_keep, back_low)

def normalize(values, gain):
    scale = lax.rsqrt(lax.optimization_barrier(jnp.mean(values * values, axis=-1, keepdims=True)) + norm_eps)
    return values * scale * gain

def forward(tokens, input_projection_weight, conv_weight, output_projection_weight, norm_gains, gate_up_weight, down_projection_weight):
    seqs = tokens.reshape(-1, SEQ, D)
    first_normed_hidden = lower_precision(normalize(seqs, norm_gains[0]))
    projected_gates = lower_precision_backward(jnp.einsum('bpo,ovw->bpvw', first_normed_hidden, lower_precision(input_projection_weight), precision=highest_precision))
    mixed = projected_gates[:, :, 0] * projected_gates[:, :, 2]
    padded = jnp.pad(mixed, ((0, 0), (2, 0), (0, 0)))
    conv = conv_weight[0] * padded[:, :-2] + conv_weight[1] * padded[:, 1:-1] + conv_weight[2] * padded[:, 2:]
    hidden_after_mixer = lower_precision(projected_gates[:, :, 1] * conv)
    conv_branch_output = lower_precision_backward(jnp.einsum('ocu,uw->ocw', hidden_after_mixer, lower_precision(output_projection_weight), precision=highest_precision))
    residual_stream = seqs + conv_branch_output
    second_normed_hidden = lower_precision(normalize(residual_stream, norm_gains[1]))
    gated_product = lower_precision_backward(jnp.einsum('bpo,ovw->bpvw', second_normed_hidden, lower_precision(gate_up_weight), precision=highest_precision))
    activation_values = lower_precision(jax.nn.silu(gated_product[:, :, 0]) * gated_product[:, :, 1])
    block_output = residual_stream + jnp.einsum('ocu,uw->ocw', activation_values, lower_precision(down_projection_weight), precision=highest_precision)
    return block_output.reshape(-1, D)

def lamb_moments(weight, grad, first, second, decay):
    first_new = beta_one * first + (1.0 - beta_one) * grad
    second_new = beta_two * second + (1.0 - beta_two) * grad * grad
    direction = first_new / (1.0 - beta_one ** STEP) / (jnp.sqrt(second_new / (1.0 - beta_two ** STEP)) + adam_eps) + decay * weight
    return (first_new, second_new, direction)

def norms_of(weight, direction):
    return jnp.stack([jnp.sqrt(jnp.sum(weight * weight)), jnp.sqrt(jnp.sum(direction * direction))])

def apply_trust(weight, direction, norms):
    return weight - learn_rate * (norms[0] / (norms[1] + adam_eps)) * direction

def reference(tokens, cotangent, input_projection_weight, conv_weight, output_projection_weight, norm_gains, gate_up_weight, down_projection_weight, in_first, in_second, conv_first, conv_second, out_first, out_second, gain_first, gain_second, gu_first, gu_second, down_first, down_second):
    block_output, pullback = jax.vjp(forward, tokens.astype(jnp.float32), input_projection_weight, conv_weight, output_projection_weight, norm_gains, gate_up_weight, down_projection_weight)
    grads = pullback(cotangent.astype(jnp.float32))
    output = block_output.astype(jnp.bfloat16)
    token_grad = grads[0].astype(jnp.bfloat16)
    in_m, in_v, in_u = lamb_moments(input_projection_weight, grads[1], in_first, in_second, decay_rate)
    conv_m, conv_v, conv_u = lamb_moments(conv_weight, grads[2], conv_first, conv_second, 0.0)
    out_m, out_v, out_u = lamb_moments(output_projection_weight, grads[3], out_first, out_second, decay_rate)
    gain_m, gain_v, gain_u = lamb_moments(norm_gains, grads[4], gain_first, gain_second, 0.0)
    gu_m, gu_v, gu_u = lamb_moments(gate_up_weight, grads[5], gu_first, gu_second, decay_rate)
    down_m, down_v, down_u = lamb_moments(down_projection_weight, grads[6], down_first, down_second, decay_rate)
    trust_norms = jnp.stack([norms_of(input_projection_weight, in_u), norms_of(conv_weight, conv_u), norms_of(output_projection_weight, out_u), norms_of(norm_gains[0], gain_u[0]), norms_of(norm_gains[1], gain_u[1]), norms_of(gate_up_weight, gu_u), norms_of(down_projection_weight, down_u)])
    gains_new = jnp.stack([apply_trust(norm_gains[0], gain_u[0], trust_norms[3]), apply_trust(norm_gains[1], gain_u[1], trust_norms[4])])
    return (output, token_grad, apply_trust(input_projection_weight, in_u, trust_norms[0]), in_m, in_v, apply_trust(conv_weight, conv_u, trust_norms[1]), conv_m, conv_v, apply_trust(output_projection_weight, out_u, trust_norms[2]), out_m, out_v, gains_new, gain_m, gain_v, apply_trust(gate_up_weight, gu_u, trust_norms[5]), gu_m, gu_v, apply_trust(down_projection_weight, down_u, trust_norms[6]), down_m, down_v, trust_norms)
```

```python
import jax
import jax.numpy as jnp
from jax import lax
from jax.sharding import PartitionSpec as P

D = 1024
SEQ_LEAST = 4096
STEP = 5


norm_eps = 1e-05
adam_eps = 1e-06
beta_one = 0.5
beta_two = 0.6
learn_rate = 0.5
decay_rate = 0.01
low = jnp.bfloat16
wide = jnp.float32


def from_behind(block, axis, distance):
    devices = range(lax.axis_size(axis))
    route = [(i - distance, i) for i in devices if i - distance in devices]
    return lax.ppermute(block, axis, route)


def swap(values, axis):
    return lax.ppermute(values, axis, [(0, 1), (1, 0)])


def to_home(values):
    return lax.ppermute(values, ("row", "col"), [(1, 0), (2, 3)])


def home_to_sibling(values):
    return lax.ppermute(values, ("row", "col"), [(0, 2), (3, 1)])


def home_to_away(values):
    return lax.ppermute(values, ("row", "col"), [(0, 1), (3, 2)])


def contract(left, right, left_dim, right_dim):
    return lax.dot_general(
        left, right, (((left_dim,), (right_dim,)), ((), ())), preferred_element_type=wide
    )


def mul(left, right):
    return contract(left, right, 1, 0)


def mul_t(left, right):
    return contract(left, right, 1, 1)


def t_mul(left, right):
    return contract(left, right, 0, 0)


def row_total(values):
    mine = [v.astype(low) for v in values]
    theirs = swap(jnp.stack(mine), "row")
    return [m.astype(wide) + theirs[i].astype(wide) for i, m in enumerate(mine)]


def lamb_moments(weight, grad, first, second, decay):
    first_new = beta_one * first + (1.0 - beta_one) * grad
    second_new = beta_two * second + (1.0 - beta_two) * grad * grad
    direction = (
        first_new
        / (1.0 - beta_one**STEP)
        / (jnp.sqrt(second_new / (1.0 - beta_two**STEP)) + adam_eps)
        + decay * weight
    )
    return (first_new, second_new, direction)


def square_pair(weight, direction):
    return jnp.stack([jnp.sum(weight * weight), jnp.sum(direction * direction)])


def apply_trust(weight, direction, norms):
    return weight - learn_rate * (norms[0] / (norms[1] + adam_eps)) * direction


def reduce_grad(mine, other):
    got = swap(other.astype(low), "col")
    total = (mine + got.astype(wide)).astype(low)
    part = lax.psum_scatter(total, "dp", scatter_dimension=0, tiled=True)
    return lax.all_gather(part, "dp", axis=0, tiled=True)


def shards(
    tokens,
    cotangent,
    input_projection_weight,
    conv_weight,
    output_projection_weight,
    norm_gains,
    gate_up_weight,
    down_projection_weight,
    in_first,
    in_second,
    conv_first,
    conv_second,
    out_first,
    out_second,
    gain_first,
    gain_second,
    gu_first,
    gu_second,
    down_first,
    down_second,
):
    feat_cols = tokens.shape[1]
    branch_cols = conv_weight.shape[1]
    hidden_cols = down_projection_weight.shape[0]
    block_rows = tokens.shape[0]
    seq_len = max(SEQ_LEAST, block_rows * lax.axis_size("dp") * lax.axis_size("col"))
    data_pos = lax.axis_index("dp")
    row_pos = lax.axis_index("row")
    col_pos = lax.axis_index("col")
    home = row_pos == col_pos
    block_start = (data_pos * lax.axis_size("col") + col_pos) * block_rows
    keep_before = (block_start % seq_len != 0).astype(wide)
    keep_after = ((block_start + block_rows) % seq_len != 0).astype(wide)

    pair = jnp.stack([tokens, cotangent])
    away = to_home(pair)
    full = jnp.stack([pair, away])
    full = jnp.where(home, full, home_to_sibling(full))
    tok = [full[0, 0].astype(wide), full[1, 0].astype(wide)]
    cot = [full[0, 1], full[1, 1]]
    gains = [norm_gains, swap(norm_gains, "col")]

    in_low = jnp.transpose(input_projection_weight, (1, 0, 2)).astype(low)
    in_all = [in_low, swap(in_low, "col")]
    out_low = output_projection_weight.astype(low)
    out_all = [out_low, swap(out_low, "col")]
    gate_low = gate_up_weight[:, 0, :].astype(low)
    up_low = gate_up_weight[:, 1, :].astype(low)
    gate_all = [gate_low, swap(gate_low, "col")]
    up_all = [up_low, swap(up_low, "col")]
    down_low = down_projection_weight.astype(low)
    down_all = [down_low, swap(down_low, "col")]

    def scale_of(values):
        total = jnp.sum(values[0] * values[0], axis=1) + jnp.sum(values[1] * values[1], axis=1)
        return lax.rsqrt(total / D + norm_eps)

    def norm_back(values, scale, index, grad):
        weighted = [grad[h] * gains[h][index] for h in range(2)]
        inner = jnp.sum(weighted[0] * values[0], axis=1) + jnp.sum(weighted[1] * values[1], axis=1)
        factor = (scale * scale * scale * inner / D)[:, None]
        back = [scale[:, None] * weighted[h] - values[h] * factor for h in range(2)]
        gain_grad = [jnp.sum(grad[h] * values[h] * scale[:, None], axis=0) for h in range(2)]
        return back, gain_grad

    scale_one = scale_of(tok)
    n1 = [(tok[h] * scale_one[:, None] * gains[h][0]).astype(low) for h in range(2)]
    gate_b, gate_c, gate_x = [
        mul(n1[0], in_all[0][g]) + mul(n1[1], in_all[1][g]) for g in range(3)
    ]
    mixed = gate_b * gate_x
    before = from_behind(mixed[-2:], ("dp", "col"), 1) * keep_before
    padded = jnp.concatenate([before, mixed], axis=0)
    conv = (
        conv_weight[0] * padded[:-2] + conv_weight[1] * padded[1:-1] + conv_weight[2] * padded[2:]
    )
    hidden = (gate_c * conv).astype(low)
    branch = row_total([mul(hidden, out_all[h]) for h in range(2)])
    res = [tok[h] + branch[h] for h in range(2)]
    scale_two = scale_of(res)
    n2 = [(res[h] * scale_two[:, None] * gains[h][1]).astype(low) for h in range(2)]
    gate = mul(n2[0], gate_all[0]) + mul(n2[1], gate_all[1])
    upper = mul(n2[0], up_all[0]) + mul(n2[1], up_all[1])
    sigma = jax.nn.sigmoid(gate)
    silu = gate * sigma
    act = (silu * upper).astype(low)
    ffn = row_total([mul(act, down_all[h]) for h in range(2)])
    out_half = [(res[h] + ffn[h]).astype(low) for h in range(2)]

    down_sum = reduce_grad(t_mul(act, cot[0]), t_mul(act, cot[1]))
    g_act = mul_t(cot[0], down_all[0]) + mul_t(cot[1], down_all[1])
    g_gate = (g_act * upper * sigma * (1.0 + gate * (1.0 - sigma))).astype(low)
    g_up = (g_act * silu).astype(low)
    gate_sum = reduce_grad(t_mul(n2[0], g_gate), t_mul(n2[1], g_gate))
    up_sum = reduce_grad(t_mul(n2[0], g_up), t_mul(n2[1], g_up))
    g_n2 = row_total([mul_t(g_gate, gate_all[h]) + mul_t(g_up, up_all[h]) for h in range(2)])
    back_two, gain_two_grad = norm_back(res, scale_two, 1, g_n2)
    g_res = [cot[h].astype(wide) + back_two[h] for h in range(2)]
    g_branch = [g_res[h].astype(low) for h in range(2)]
    out_sum = reduce_grad(t_mul(hidden, g_branch[0]), t_mul(hidden, g_branch[1]))
    g_hidden = mul_t(g_branch[0], out_all[0]) + mul_t(g_branch[1], out_all[1])
    g_conv = g_hidden * gate_c
    after = from_behind(g_conv[:2], ("dp", "col"), -1) * keep_after
    extended = jnp.concatenate([g_conv, after], axis=0)
    g_mixed = (
        conv_weight[2] * extended[:-2]
        + conv_weight[1] * extended[1:-1]
        + conv_weight[0] * extended[2:]
    )
    conv_grad = jnp.stack(
        [jnp.sum(g_conv * padded[offset : offset + block_rows], axis=0) for offset in range(3)]
    )
    g_proj = [
        (g_mixed * gate_x).astype(low),
        (g_hidden * conv).astype(low),
        (g_mixed * gate_b).astype(low),
    ]
    in_part = [jnp.concatenate([t_mul(n1[h], g_proj[g]) for g in range(3)]) for h in range(2)]
    in_sum = reduce_grad(in_part[0], in_part[1])
    g_n1 = row_total([sum(mul_t(g_proj[g], in_all[h][g]) for g in range(3)) for h in range(2)])
    back_one, gain_one_grad = norm_back(tok, scale_one, 0, g_n1)
    tok_half = [(g_res[h] + back_one[h]).astype(low) for h in range(2)]
    ends = [jnp.stack([out_half[h], tok_half[h]]) for h in range(2)]
    ends = jnp.where(home, ends[0], home_to_away(ends[1]))

    gain_part = [jnp.stack([gain_one_grad[h], gain_two_grad[h]]) for h in range(2)]
    gain_part = gain_part[0] + swap(gain_part[1], "col")
    conv_part = conv_grad + swap(conv_grad, "col")
    conv_grad, gains_grad = lax.psum((conv_part, gain_part), "dp")

    in_grad = jnp.transpose(in_sum.reshape(3, feat_cols, branch_cols), (1, 0, 2)).astype(wide)
    gu_grad = jnp.stack([gate_sum, up_sum], axis=1).astype(wide)
    in_m, in_v, in_u = lamb_moments(
        input_projection_weight, in_grad, in_first, in_second, decay_rate
    )
    conv_m, conv_v, conv_u = lamb_moments(conv_weight, conv_grad, conv_first, conv_second, 0.0)
    out_m, out_v, out_u = lamb_moments(
        output_projection_weight, out_sum.astype(wide), out_first, out_second, decay_rate
    )
    gain_m, gain_v, gain_u = lamb_moments(norm_gains, gains_grad, gain_first, gain_second, 0.0)
    gu_m, gu_v, gu_u = lamb_moments(gate_up_weight, gu_grad, gu_first, gu_second, decay_rate)
    down_m, down_v, down_u = lamb_moments(
        down_projection_weight, down_sum.astype(wide), down_first, down_second, decay_rate
    )
    col_first = (col_pos == 0).astype(wide)
    row_first = (row_pos == 0).astype(wide)
    partial_sums = jnp.stack(
        [
            square_pair(input_projection_weight, in_u),
            square_pair(conv_weight, conv_u) * col_first,
            square_pair(output_projection_weight, out_u),
            square_pair(norm_gains[0], gain_u[0]) * row_first,
            square_pair(norm_gains[1], gain_u[1]) * row_first,
            square_pair(gate_up_weight, gu_u),
            square_pair(down_projection_weight, down_u),
        ]
    )
    trust_norms = jnp.sqrt(lax.psum(partial_sums, ("row", "col")))
    gains_new = jnp.stack(
        [
            apply_trust(norm_gains[0], gain_u[0], trust_norms[3]),
            apply_trust(norm_gains[1], gain_u[1], trust_norms[4]),
        ]
    )
    return (
        ends[0],
        ends[1],
        apply_trust(input_projection_weight, in_u, trust_norms[0]),
        in_m,
        in_v,
        apply_trust(conv_weight, conv_u, trust_norms[1]),
        conv_m,
        conv_v,
        apply_trust(output_projection_weight, out_u, trust_norms[2]),
        out_m,
        out_v,
        gains_new,
        gain_m,
        gain_v,
        apply_trust(gate_up_weight, gu_u, trust_norms[5]),
        gu_m,
        gu_v,
        apply_trust(down_projection_weight, down_u, trust_norms[6]),
        down_m,
        down_v,
        trust_norms,
    )


def solution(mesh):
    in_specs = (
        P(("dp", "row"), "col"),
        P(("dp", "row"), "col"),
        P("col", None, "row"),
        P(None, "row"),
        P("row", "col"),
        P(None, "col"),
        P("col", None, "row"),
        P("row", "col"),
        P("col", None, "row"),
        P("col", None, "row"),
        P(None, "row"),
        P(None, "row"),
        P("row", "col"),
        P("row", "col"),
        P(None, "col"),
        P(None, "col"),
        P("col", None, "row"),
        P("col", None, "row"),
        P("row", "col"),
        P("row", "col"),
    )
    out_specs = (
        P(("dp", "row"), "col"),
        P(("dp", "row"), "col"),
        P("col", None, "row"),
        P("col", None, "row"),
        P("col", None, "row"),
        P(None, "row"),
        P(None, "row"),
        P(None, "row"),
        P("row", "col"),
        P("row", "col"),
        P("row", "col"),
        P(None, "col"),
        P(None, "col"),
        P(None, "col"),
        P("col", None, "row"),
        P("col", None, "row"),
        P("col", None, "row"),
        P("row", "col"),
        P("row", "col"),
        P("row", "col"),
        P(),
    )
    return jax.shard_map(shards, mesh=mesh, in_specs=in_specs, out_specs=out_specs, check_vma=False)
```

```python
import jax
import jax.numpy as jnp
from jax import lax
from jax.sharding import PartitionSpec as P

D = 1024
SEQ_LEAST = 4096
STEP = 5


norm_eps = 1e-05
adam_eps = 1e-06
beta_one = 0.5
beta_two = 0.6
learn_rate = 0.5
decay_rate = 0.01
low = jnp.bfloat16
wide = jnp.float32


def from_behind(block, axis, distance):
    devices = range(lax.axis_size(axis))
    route = [(i - distance, i) for i in devices if i - distance in devices]
    return lax.ppermute(block, axis, route)


def swap(values, axis):
    return lax.ppermute(values, axis, [(0, 1), (1, 0)])


def to_home(values):
    return lax.ppermute(values, ("row", "col"), [(1, 0), (2, 3)])


def home_to_sibling(values):
    return lax.ppermute(values, ("row", "col"), [(0, 2), (3, 1)])


def home_to_away(values):
    return lax.ppermute(values, ("row", "col"), [(0, 1), (3, 2)])


def contract(left, right, left_dim, right_dim):
    return lax.dot_general(
        left, right, (((left_dim,), (right_dim,)), ((), ())), preferred_element_type=wide
    )


def mul(left, right):
    return contract(left, right, 1, 0)


def mul_t(left, right):
    return contract(left, right, 1, 1)


def t_mul(left, right):
    return contract(left, right, 0, 0)


def row_total(values):
    mine = [v.astype(low) for v in values]
    theirs = swap(jnp.stack(mine), "row")
    return [m.astype(wide) + theirs[i].astype(wide) for i, m in enumerate(mine)]


def lamb_moments(weight, grad, first, second, decay):
    first_new = beta_one * first + (1.0 - beta_one) * grad
    second_new = beta_two * second + (1.0 - beta_two) * grad * grad
    direction = (
        first_new
        / (1.0 - beta_one**STEP)
        / (jnp.sqrt(second_new / (1.0 - beta_two**STEP)) + adam_eps)
        + decay * weight
    )
    return (first_new, second_new, direction)


def square_pair(weight, direction):
    return jnp.stack([jnp.sum(weight * weight), jnp.sum(direction * direction)])


def apply_trust(weight, direction, norms):
    return weight - learn_rate * (norms[0] / (norms[1] + adam_eps)) * direction


def flip(values, bit):
    size = lax.axis_size("dp")
    return lax.ppermute(values, "dp", [(i, i ^ (1 << bit)) for i in range(size)])


def dp_bit(bit):
    return (lax.axis_index("dp") >> bit) & 1


def rows_of(values, start, rows):
    return lax.dynamic_slice_in_dim(values, start, rows, 0)


def total_of(pieces):
    total = pieces[0].astype(wide)
    for piece in pieces[1:]:
        total = total + piece.astype(wide)
    return total


def reduce_bits(pieces, order):
    rows = pieces[0].shape[0]
    for bit in order:
        rows = rows // 2
        here = dp_bit(bit)
        send = total_of([rows_of(p, (1 - here) * rows, rows) for p in pieces]).astype(low)
        pieces = [rows_of(p, here * rows, rows) for p in pieces]
        pieces.append(flip(send, bit))
    return total_of(pieces).astype(low)


def gather_bits(part, order):
    for bit in reversed(order):
        other = flip(part, bit)
        part = jnp.where(
            dp_bit(bit) == 0,
            jnp.concatenate([part, other]),
            jnp.concatenate([other, part]),
        )
    return part


def all_bits():
    return list(range((lax.axis_size("dp") - 1).bit_length()))


def reduce_grad(mine, other):
    got = swap(other.astype(low), "col")
    order = all_bits()
    return gather_bits(reduce_bits([mine, got], order), order)


def fetch(weight, order):
    count = 1 << len(order)
    rows = weight.shape[0] // count
    index = 0
    for bit in order:
        index = 2 * index + dp_bit(bit)
    return gather_bits(swap(rows_of(weight, index * rows, rows), "col"), order)


def shards(
    tokens,
    cotangent,
    input_projection_weight,
    conv_weight,
    output_projection_weight,
    norm_gains,
    gate_up_weight,
    down_projection_weight,
    in_first,
    in_second,
    conv_first,
    conv_second,
    out_first,
    out_second,
    gain_first,
    gain_second,
    gu_first,
    gu_second,
    down_first,
    down_second,
):
    feat_cols = tokens.shape[1]
    branch_cols = conv_weight.shape[1]
    hidden_cols = down_projection_weight.shape[0]
    block_rows = tokens.shape[0]
    seq_len = max(SEQ_LEAST, block_rows * lax.axis_size("dp") * lax.axis_size("col"))
    data_pos = lax.axis_index("dp")
    row_pos = lax.axis_index("row")
    col_pos = lax.axis_index("col")
    home = row_pos == col_pos
    block_start = (data_pos * lax.axis_size("col") + col_pos) * block_rows
    keep_before = (block_start % seq_len != 0).astype(wide)
    keep_after = ((block_start + block_rows) % seq_len != 0).astype(wide)

    pair = jnp.stack([tokens, cotangent])
    away = to_home(pair)
    full = jnp.stack([pair, away])
    full = jnp.where(home, full, home_to_sibling(full))
    tok = [full[0, 0].astype(wide), full[1, 0].astype(wide)]
    cot = [full[0, 1], full[1, 1]]
    gains = [norm_gains, swap(norm_gains, "col")]

    in_low = jnp.transpose(input_projection_weight, (1, 0, 2)).astype(low)
    in_all = [in_low, swap(in_low, "col")]
    out_low = output_projection_weight.astype(low)
    out_all = [out_low, fetch(out_low, (1, 0))]
    gate_low = gate_up_weight[:, 0, :].astype(low)
    up_low = gate_up_weight[:, 1, :].astype(low)
    gate_all = [gate_low, fetch(gate_low, (1, 0))]
    up_all = [up_low, fetch(up_low, (0, 1))]
    down_low = down_projection_weight.astype(low)
    down_all = [down_low, fetch(down_low, (0, 1))]

    def scale_of(values):
        total = jnp.sum(values[0] * values[0], axis=1) + jnp.sum(values[1] * values[1], axis=1)
        return lax.rsqrt(total / D + norm_eps)

    def norm_back(values, scale, index, grad):
        weighted = [grad[h] * gains[h][index] for h in range(2)]
        inner = jnp.sum(weighted[0] * values[0], axis=1) + jnp.sum(weighted[1] * values[1], axis=1)
        factor = (scale * scale * scale * inner / D)[:, None]
        back = [scale[:, None] * weighted[h] - values[h] * factor for h in range(2)]
        gain_grad = [jnp.sum(grad[h] * values[h] * scale[:, None], axis=0) for h in range(2)]
        return back, gain_grad

    scale_one = scale_of(tok)
    n1 = [(tok[h] * scale_one[:, None] * gains[h][0]).astype(low) for h in range(2)]
    gate_b, gate_c, gate_x = [
        mul(n1[0], in_all[0][g]) + mul(n1[1], in_all[1][g]) for g in range(3)
    ]
    mixed = gate_b * gate_x
    before = from_behind(mixed[-2:], ("dp", "col"), 1) * keep_before
    padded = jnp.concatenate([before, mixed], axis=0)
    conv = (
        conv_weight[0] * padded[:-2] + conv_weight[1] * padded[1:-1] + conv_weight[2] * padded[2:]
    )
    hidden = (gate_c * conv).astype(low)
    branch = row_total([mul(hidden, out_all[h]) for h in range(2)])
    res = [tok[h] + branch[h] for h in range(2)]
    scale_two = scale_of(res)
    n2 = [(res[h] * scale_two[:, None] * gains[h][1]).astype(low) for h in range(2)]
    gate = mul(n2[0], gate_all[0]) + mul(n2[1], gate_all[1])
    upper = mul(n2[0], up_all[0]) + mul(n2[1], up_all[1])
    sigma = jax.nn.sigmoid(gate)
    silu = gate * sigma
    act = (silu * upper).astype(low)
    ffn = row_total([mul(act, down_all[h]) for h in range(2)])
    out_half = [(res[h] + ffn[h]).astype(low) for h in range(2)]

    down_sum = reduce_grad(t_mul(act, cot[0]), t_mul(act, cot[1]))
    g_act = mul_t(cot[0], down_all[0]) + mul_t(cot[1], down_all[1])
    g_gate = (g_act * upper * sigma * (1.0 + gate * (1.0 - sigma))).astype(low)
    g_up = (g_act * silu).astype(low)
    gate_sum = reduce_grad(t_mul(n2[0], g_gate), t_mul(n2[1], g_gate))
    up_sum = reduce_grad(t_mul(n2[0], g_up), t_mul(n2[1], g_up))
    g_n2 = row_total([mul_t(g_gate, gate_all[h]) + mul_t(g_up, up_all[h]) for h in range(2)])
    back_two, gain_two_grad = norm_back(res, scale_two, 1, g_n2)
    g_res = [cot[h].astype(wide) + back_two[h] for h in range(2)]
    g_branch = [g_res[h].astype(low) for h in range(2)]
    out_part = [t_mul(hidden, g_branch[h]) for h in range(2)]
    g_hidden = mul_t(g_branch[0], out_all[0]) + mul_t(g_branch[1], out_all[1])
    g_conv = g_hidden * gate_c
    after = from_behind(g_conv[:2], ("dp", "col"), -1) * keep_after
    extended = jnp.concatenate([g_conv, after], axis=0)
    g_mixed = (
        conv_weight[2] * extended[:-2]
        + conv_weight[1] * extended[1:-1]
        + conv_weight[0] * extended[2:]
    )
    conv_grad = jnp.stack(
        [jnp.sum(g_conv * padded[offset : offset + block_rows], axis=0) for offset in range(3)]
    )
    g_proj = [
        (g_mixed * gate_x).astype(low),
        (g_hidden * conv).astype(low),
        (g_mixed * gate_b).astype(low),
    ]
    in_part = [
        jnp.concatenate([out_part[h]] + [t_mul(n1[h], g_proj[g]) for g in range(3)])
        for h in range(2)
    ]
    in_sum = reduce_grad(in_part[0], in_part[1])
    out_sum, in_sum = in_sum[:branch_cols], in_sum[branch_cols:]
    g_n1 = row_total([sum(mul_t(g_proj[g], in_all[h][g]) for g in range(3)) for h in range(2)])
    back_one, gain_one_grad = norm_back(tok, scale_one, 0, g_n1)
    tok_half = [(g_res[h] + back_one[h]).astype(low) for h in range(2)]
    ends = [jnp.stack([out_half[h], tok_half[h]]) for h in range(2)]
    ends = jnp.where(home, ends[0], home_to_away(ends[1]))

    small = [
        jnp.concatenate([conv_grad, gain_one_grad[h][None], gain_two_grad[h][None]])
        for h in range(2)
    ]
    small = small[0] + swap(small[1], "col")
    for bit in all_bits():
        small = small + flip(small, bit)
    conv_grad, gains_grad = small[:3], small[3:]

    in_grad = jnp.transpose(in_sum.reshape(3, feat_cols, branch_cols), (1, 0, 2)).astype(wide)
    gu_grad = jnp.stack([gate_sum, up_sum], axis=1).astype(wide)
    in_m, in_v, in_u = lamb_moments(
        input_projection_weight, in_grad, in_first, in_second, decay_rate
    )
    conv_m, conv_v, conv_u = lamb_moments(conv_weight, conv_grad, conv_first, conv_second, 0.0)
    out_m, out_v, out_u = lamb_moments(
        output_projection_weight, out_sum.astype(wide), out_first, out_second, decay_rate
    )
    gain_m, gain_v, gain_u = lamb_moments(norm_gains, gains_grad, gain_first, gain_second, 0.0)
    gu_m, gu_v, gu_u = lamb_moments(gate_up_weight, gu_grad, gu_first, gu_second, decay_rate)
    down_m, down_v, down_u = lamb_moments(
        down_projection_weight, down_sum.astype(wide), down_first, down_second, decay_rate
    )
    col_first = (col_pos == 0).astype(wide)
    row_first = (row_pos == 0).astype(wide)
    partial_sums = jnp.stack(
        [
            square_pair(input_projection_weight, in_u),
            square_pair(conv_weight, conv_u) * col_first,
            square_pair(output_projection_weight, out_u),
            square_pair(norm_gains[0], gain_u[0]) * row_first,
            square_pair(norm_gains[1], gain_u[1]) * row_first,
            square_pair(gate_up_weight, gu_u),
            square_pair(down_projection_weight, down_u),
        ]
    )
    trust_norms = jnp.sqrt(lax.psum(partial_sums, ("row", "col")))
    gains_new = jnp.stack(
        [
            apply_trust(norm_gains[0], gain_u[0], trust_norms[3]),
            apply_trust(norm_gains[1], gain_u[1], trust_norms[4]),
        ]
    )
    return (
        ends[0],
        ends[1],
        apply_trust(input_projection_weight, in_u, trust_norms[0]),
        in_m,
        in_v,
        apply_trust(conv_weight, conv_u, trust_norms[1]),
        conv_m,
        conv_v,
        apply_trust(output_projection_weight, out_u, trust_norms[2]),
        out_m,
        out_v,
        gains_new,
        gain_m,
        gain_v,
        apply_trust(gate_up_weight, gu_u, trust_norms[5]),
        gu_m,
        gu_v,
        apply_trust(down_projection_weight, down_u, trust_norms[6]),
        down_m,
        down_v,
        trust_norms,
    )


def solution(mesh):
    in_specs = (
        P(("dp", "row"), "col"),
        P(("dp", "row"), "col"),
        P("col", None, "row"),
        P(None, "row"),
        P("row", "col"),
        P(None, "col"),
        P("col", None, "row"),
        P("row", "col"),
        P("col", None, "row"),
        P("col", None, "row"),
        P(None, "row"),
        P(None, "row"),
        P("row", "col"),
        P("row", "col"),
        P(None, "col"),
        P(None, "col"),
        P("col", None, "row"),
        P("col", None, "row"),
        P("row", "col"),
        P("row", "col"),
    )
    out_specs = (
        P(("dp", "row"), "col"),
        P(("dp", "row"), "col"),
        P("col", None, "row"),
        P("col", None, "row"),
        P("col", None, "row"),
        P(None, "row"),
        P(None, "row"),
        P(None, "row"),
        P("row", "col"),
        P("row", "col"),
        P("row", "col"),
        P(None, "col"),
        P(None, "col"),
        P(None, "col"),
        P("col", None, "row"),
        P("col", None, "row"),
        P("col", None, "row"),
        P("row", "col"),
        P("row", "col"),
        P("row", "col"),
        P(),
    )
    return jax.shard_map(shards, mesh=mesh, in_specs=in_specs, out_specs=out_specs, check_vma=False)
```

```python
import jax
import jax.numpy as jnp
from jax import lax
from jax.experimental import pallas as pl
from jax.experimental.layout import Layout, with_layout_constraint
from jax.experimental.pallas import tpu as pltpu
from jax.sharding import PartitionSpec as P

D = 1024
SEQ_LEAST = 4096
STEP = 5


norm_eps = 1e-05
adam_eps = 1e-06
beta_one = 0.5
beta_two = 0.6
learn_rate = 0.5
decay_rate = 0.01
low = jnp.bfloat16
wide = jnp.float32


def from_behind(block, axis, distance):
    devices = range(lax.axis_size(axis))
    route = [(i - distance, i) for i in devices if i - distance in devices]
    return lax.ppermute(block, axis, route)


def swap(values, axis):
    return lax.ppermute(values, axis, [(0, 1), (1, 0)])


def to_home(values):
    return lax.ppermute(values, ("row", "col"), [(1, 0), (2, 3)])


def home_to_sibling(values):
    return lax.ppermute(values, ("row", "col"), [(0, 2), (3, 1)])


def home_to_away(values):
    return lax.ppermute(values, ("row", "col"), [(0, 1), (3, 2)])


def sibling_to_home(values):
    return lax.ppermute(values, ("row", "col"), [(2, 0), (1, 3)])


def contract(left, right, left_dim, right_dim):
    return lax.dot_general(
        left, right, (((left_dim,), (right_dim,)), ((), ())), preferred_element_type=wide
    )


def mul(left, right):
    return contract(left, right, 1, 0)


def mul_t(left, right):
    return contract(left, right, 1, 1)


def t_mul(left, right):
    return contract(left, right, 0, 0)


def row_total(values):
    mine = [v.astype(low) for v in values]
    theirs = swap(jnp.stack(mine), "row")
    return [m.astype(wide) + theirs[i].astype(wide) for i, m in enumerate(mine)]


def lamb_moments(weight, grad, first, second, decay):
    first_new = beta_one * first + (1.0 - beta_one) * grad
    second_new = beta_two * second + (1.0 - beta_two) * grad * grad
    direction = (
        first_new
        / (1.0 - beta_one**STEP)
        / (jnp.sqrt(second_new / (1.0 - beta_two**STEP)) + adam_eps)
        + decay * weight
    )
    return (first_new, second_new, direction)


def square_pair(weight, direction):
    return jnp.stack([jnp.sum(weight * weight), jnp.sum(direction * direction)])


def lamb_rows(p, g, m, v, m_out, v_out, u_out):
    weight = p[...]
    grad = g[...].astype(wide)
    first_new, second_new, direction = lamb_moments(weight, grad, m[...], v[...], decay_rate)
    m_out[...] = first_new
    v_out[...] = second_new
    u_out[...] = direction
    return weight * weight, direction * direction


def lamb_loop(refs, sums, rows, step):
    lanes = sums.shape[2]

    @pl.when(pl.program_id(0) == 0)
    def _():
        sums[...] = jnp.zeros_like(sums)

    def body(at, total):
        here = pl.ds(pl.multiple_of(at * step, step), step)
        squares = lamb_rows(*[ref.at[here, :] for ref in refs])
        return tuple(
            t + jnp.sum(sq.reshape(step // 8, 8, lanes), axis=0) for t, sq in zip(total, squares)
        )

    zero = jnp.zeros((8, lanes), wide)
    total = lax.fori_loop(0, rows // step, body, (zero, zero))
    sums[0] += total[0]
    sums[1] += total[1]


def lamb_plain(p, g, m, v, m_out, v_out, u_out, sums):
    lamb_loop((p, g, m, v, m_out, v_out, u_out), sums, p.shape[0], 16)


def lamb_pairs(p, gate, up, m, v, m_out, v_out, u_out, sums, mixed):
    rows, cols = gate.shape
    tiles = cols // 128
    for tile in range(tiles):
        for side, ref in enumerate((gate, up)):
            mixed[pl.ds(2 * tile + side, rows, stride=2 * tiles), :] = ref[
                :, tile * 128 : (tile + 1) * 128
            ].astype(wide)
    lamb_loop((p, mixed, m, v, m_out, v_out, u_out), sums, p.shape[0], 64)


def lamb_call(kernel, weight, grads, first, second, block, grad_block, grad_at, scratch):
    rows, cols = weight.shape
    flat = pl.BlockSpec((block, cols), lambda i: (i, 0))
    grad_spec = pl.BlockSpec((grad_block, grads[0].shape[1]), lambda i: (i + grad_at, 0))
    whole = jax.ShapeDtypeStruct((rows, cols), wide)
    m_new, v_new, direction, sums = pl.pallas_call(
        kernel,
        grid=(rows // block,),
        in_specs=[flat] + [grad_spec] * len(grads) + [flat, flat],
        out_specs=[flat, flat, flat, pl.BlockSpec((2, 8, cols), lambda i: (0, 0, 0))],
        out_shape=[whole, whole, whole, jax.ShapeDtypeStruct((2, 8, cols), wide)],
        scratch_shapes=scratch,
        compiler_params=pltpu.CompilerParams(vmem_limit_bytes=40 * 1024 * 1024),
        cost_estimate=pl.CostEstimate(
            flops=20 * rows * cols, bytes_accessed=26 * rows * cols, transcendentals=2 * rows * cols
        ),
    )(weight, *grads, first, second)
    return m_new, v_new, direction, jnp.sum(sums, axis=(1, 2))


def lamb_dense(weight, grad, grad_at, first, second):
    block = 256
    return lamb_call(
        lamb_plain, weight, [grad], first, second, block, block, grad_at // block, []
    )


def to_linear(values):
    rows, sides, cols = values.shape
    split = with_layout_constraint(
        values.reshape(rows, sides, cols // 128, 128), Layout(major_to_minor=(0, 2, 1, 3))
    )
    return split.transpose(0, 2, 1, 3).reshape(rows * sides * cols // 128, 128)


def from_linear(values, rows, sides):
    cols = values.size // (rows * sides)
    split = values.reshape(rows, cols // 128, sides, 128).transpose(0, 2, 1, 3)
    split = with_layout_constraint(split, Layout(major_to_minor=(0, 2, 1, 3)))
    return split.reshape(rows, sides, cols)


def apply_trust(weight, direction, norms):
    return weight - learn_rate * (norms[0] / (norms[1] + adam_eps)) * direction


def flip(values, bit):
    size = lax.axis_size("dp")
    return lax.ppermute(values, "dp", [(i, i ^ (1 << bit)) for i in range(size)])


def dp_bit(bit):
    return (lax.axis_index("dp") >> bit) & 1


def rows_of(values, start, rows):
    return lax.dynamic_slice_in_dim(values, start, rows, 0)


def total_of(pieces):
    total = pieces[0].astype(wide)
    for piece in pieces[1:]:
        total = total + piece.astype(wide)
    return total


def tie(values, *deps):
    return lax.optimization_barrier((values, *deps))[0]


def low_total(pieces):
    return total_of(pieces).astype(low)


def keep_or_join(bit, part, other):
    return jnp.where(
        dp_bit(bit) == 0,
        jnp.concatenate([part, other]),
        jnp.concatenate([other, part]),
    )


def gather_bits(part, order):
    for bit in reversed(order):
        part = keep_or_join(bit, part, flip(part, bit))
    return part


def share_of(weight, order):
    rows = weight.shape[0] // (1 << len(order))
    index = 0
    for bit in order:
        index = 2 * index + dp_bit(bit)
    return rows_of(weight, index * rows, rows)


def chunk_sum(mine, other, order):
    bits = {"y": 0, "l": 1}
    steps = [name if name == "x" else bits[name] for name in order]
    mine = [mine]
    other = [other]
    for step in steps:
        if step == "x":
            got = yield step, low_total(other)
            mine.append(got)
            other = None
            continue
        rows = mine[0].shape[0] // 2
        here = dp_bit(step)
        groups = [mine] if other is None else [mine, other]
        send = [low_total([rows_of(p, (1 - here) * rows, rows) for p in g]) for g in groups]
        got = yield step, jnp.concatenate(send) if len(send) > 1 else send[0]
        mine = [rows_of(p, here * rows, rows) for p in mine] + [got[:rows]]
        if other is not None:
            other = [rows_of(p, here * rows, rows) for p in other] + [got[rows:]]
    part = low_total(mine)
    for step in range((lax.axis_size("dp") - 1).bit_length()):
        if step not in steps:
            got = yield step, part
            part = low_total([part, got])
    for step in reversed(steps):
        if step != "x":
            got = yield step, part
            part = keep_or_join(step, part, got)
    return part


def move(step, send):
    return swap(send, "col") if step == "x" else flip(send, step)


def first_step(chunk):
    step, send = next(chunk)
    return move(step, send)


def run_chunks(chunks, arrivals, sequence, after):
    done = {}
    seen = {name: [] for name in chunks}
    pending = list(sequence)
    while len(done) < len(chunks):
        names = [pending.pop(0)] if pending else [n for n in chunks if n not in done]
        for name in names:
            if name in done:
                continue
            got = arrivals[name]
            seen[name].append(got)
            try:
                step, send = chunks[name].send(got)
            except StopIteration as end:
                done[name] = end.value
                continue
            arrivals[name] = move(step, tie(send, after))
            after = got
    return done, seen


def deinterleave(pairs, gate, up):
    rows, cols = gate.shape
    tiles = cols // 128
    for tile in range(tiles):
        for side, out in enumerate((gate, up)):
            out[:, tile * 128 : (tile + 1) * 128] = pairs[
                pl.ds(2 * tile + side, rows, stride=2 * tiles), :
            ].astype(low)


def split_pairs(linear, rows, cols):
    block = 64
    half = jax.ShapeDtypeStruct((rows, cols), low)
    out_spec = pl.BlockSpec((block, cols), lambda i: (i, 0))
    return pl.pallas_call(
        deinterleave,
        grid=(rows // block,),
        in_specs=[pl.BlockSpec((block * 2 * cols // 128, 128), lambda i: (i, 0))],
        out_specs=[out_spec, out_spec],
        out_shape=[half, half],
        compiler_params=pltpu.CompilerParams(vmem_limit_bytes=24 * 1024 * 1024),
        cost_estimate=pl.CostEstimate(
            flops=rows * cols, bytes_accessed=12 * rows * cols, transcendentals=0
        ),
    )(linear)


def shards(
    tokens,
    cotangent,
    input_projection_weight,
    conv_weight,
    output_projection_weight,
    norm_gains,
    gate_up_weight,
    down_projection_weight,
    in_first,
    in_second,
    conv_first,
    conv_second,
    out_first,
    out_second,
    gain_first,
    gain_second,
    gu_first,
    gu_second,
    down_first,
    down_second,
):
    feat_cols = tokens.shape[1]
    branch_cols = conv_weight.shape[1]
    hidden_cols = down_projection_weight.shape[0]
    block_rows = tokens.shape[0]
    seq_len = max(SEQ_LEAST, block_rows * lax.axis_size("dp") * lax.axis_size("col"))
    data_pos = lax.axis_index("dp")
    row_pos = lax.axis_index("row")
    col_pos = lax.axis_index("col")
    home = row_pos == col_pos
    block_start = (data_pos * lax.axis_size("col") + col_pos) * block_rows
    keep_before = (block_start % seq_len != 0).astype(wide)

    tok_away = to_home(tokens)
    in_low = jnp.transpose(input_projection_weight, (1, 0, 2)).astype(low).reshape(-1, branch_cols)
    io_low = jnp.concatenate([in_low, output_projection_weight.astype(low)])
    io_got = swap(share_of(io_low, (1, 0)), "col")
    gu_weight = to_linear(gate_up_weight)
    gate_low, up_low = split_pairs(gu_weight, feat_cols, hidden_cols)
    down_low = down_projection_weight.astype(low)
    gains = [norm_gains, swap(norm_gains, "col")]

    def both_halves(own, away):
        full = jnp.stack([own, away])
        return jnp.where(home, full, home_to_sibling(full))

    tok_low = both_halves(tokens, tok_away)
    tok = [tok_low[0].astype(wide), tok_low[1].astype(wide)]
    gate_got = swap(tie(share_of(gate_low, (0,)), tok_away), "col")
    cot_away = to_home(tie(cotangent, io_got))
    up_got = swap(tie(share_of(up_low, (1,)), cot_away), "col")
    down_got = swap(tie(down_low, gate_got), "col")
    io_pair = keep_or_join(0, io_got, flip(io_got, 0))
    io_other = keep_or_join(1, io_pair, flip(io_pair, 1))
    gate_all = [gate_low, gather_bits(tie(gate_got, io_pair), (0,))]
    up_all = [up_low, gather_bits(tie(up_got, io_other), (1,))]
    down_all = [down_low, down_got]
    in_all = [io[: 3 * feat_cols].reshape(3, feat_cols, branch_cols) for io in (io_low, io_other)]
    out_all = [io[3 * feat_cols :] for io in (io_low, io_other)]
    cot = both_halves(cotangent, cot_away)

    def scale_of(values):
        total = jnp.sum(values[0] * values[0], axis=1) + jnp.sum(values[1] * values[1], axis=1)
        return lax.rsqrt(total / D + norm_eps)

    def norm_back(values, scale, index, grad):
        weighted = [grad[h] * gains[h][index] for h in range(2)]
        inner = jnp.sum(weighted[0] * values[0], axis=1) + jnp.sum(weighted[1] * values[1], axis=1)
        factor = (scale * scale * scale * inner / D)[:, None]
        back = [scale[:, None] * weighted[h] - values[h] * factor for h in range(2)]
        gain_grad = [jnp.sum(grad[h] * values[h] * scale[:, None], axis=0) for h in range(2)]
        return back, gain_grad

    scale_one = scale_of(tok)
    n1 = [(tok[h] * scale_one[:, None] * gains[h][0]).astype(low) for h in range(2)]
    gate_b, gate_c, gate_x = [
        mul(n1[0], in_all[0][g]) + mul(n1[1], in_all[1][g]) for g in range(3)
    ]
    mixed = gate_b * gate_x
    tail_rows = 16
    halo = jnp.concatenate(
        [gate_b[-2:], gate_x[-2:], n1[0][-2:].astype(wide), n1[1][-2:].astype(wide)]
    )
    halo = from_behind(halo, ("dp", "col"), 1) * keep_before
    before_b, before_x = halo[:2], halo[2:4]
    before = before_b * before_x
    n1_tail = [
        jnp.pad(half.astype(low), ((0, tail_rows - 2), (0, 0))) for half in (halo[6:], halo[4:6])
    ]
    padded = jnp.concatenate([before, mixed], axis=0)
    conv = (
        conv_weight[0] * padded[:-2] + conv_weight[1] * padded[1:-1] + conv_weight[2] * padded[2:]
    )
    hidden = (gate_c * conv).astype(low)
    branch = row_total([mul(hidden, out_all[h]) for h in range(2)])
    res = [tok[h] + branch[h] for h in range(2)]
    scale_two = scale_of(res)
    n2 = [(res[h] * scale_two[:, None] * gains[h][1]).astype(low) for h in range(2)]
    gate = mul(n2[0], gate_all[0]) + mul(n2[1], gate_all[1])
    upper = mul(n2[0], up_all[0]) + mul(n2[1], up_all[1])
    sigma = jax.nn.sigmoid(gate)
    silu = gate * sigma
    act = (silu * upper).astype(low)

    chunks = {"d": chunk_sum(t_mul(act, cot[0]).astype(low), t_mul(act, cot[1]).astype(low), "ylx")}
    arrivals = {"d": first_step(chunks["d"])}
    g_act = mul_t(cot[0], down_all[0]) + mul_t(cot[1], down_all[1])
    g_gate = (g_act * upper * sigma * (1.0 + gate * (1.0 - sigma))).astype(low)
    g_up = (g_act * silu).astype(low)
    for name, grad, order in (("g", g_gate, "lxy"), ("u", g_up, "xly")):
        parts = [t_mul(n2[h], grad).astype(low) for h in range(2)]
        chunks[name] = chunk_sum(parts[0], parts[1], order)
        arrivals[name] = first_step(chunks[name])
    g_n2 = row_total([mul_t(g_gate, gate_all[h]) + mul_t(g_up, up_all[h]) for h in range(2)])
    back_two, gain_two_grad = norm_back(res, scale_two, 1, g_n2)
    g_res = [cot[h].astype(wide) + back_two[h] for h in range(2)]
    g_branch = [g_res[h].astype(low) for h in range(2)]
    out_part = [t_mul(hidden, g_branch[h]).astype(low) for h in range(2)]
    g_hidden = mul_t(g_branch[0], out_all[0]) + mul_t(g_branch[1], out_all[1])
    g_conv = g_hidden * gate_c
    extended = jnp.concatenate([g_conv, jnp.zeros((2, branch_cols), wide)], axis=0)
    g_mixed = (
        conv_weight[2] * extended[:-2]
        + conv_weight[1] * extended[1:-1]
        + conv_weight[0] * extended[2:]
    )
    g_before = jnp.stack(
        [
            conv_weight[0] * g_conv[0],
            conv_weight[1] * g_conv[0] + conv_weight[0] * g_conv[1],
        ]
    )
    conv_grad = jnp.stack(
        [jnp.sum(g_conv * padded[offset : offset + block_rows], axis=0) for offset in range(3)]
    )
    def with_tail(values, tail):
        return jnp.concatenate(
            [values, jnp.pad(tail, ((0, tail_rows - 2), (0, 0)))], axis=0
        ).astype(low)

    g_proj = [
        with_tail(g_mixed * gate_x, g_before * before_x),
        with_tail(g_hidden * conv, jnp.zeros_like(g_before)),
        with_tail(g_mixed * gate_b, g_before * before_b),
    ]
    n1_long = [jnp.concatenate([n1[h], n1_tail[h]]) for h in range(2)]
    in_part = [
        jnp.concatenate([out_part[h]] + [t_mul(n1_long[h], g_proj[g]).astype(low) for g in range(3)])
        for h in range(2)
    ]
    chunks["i"] = chunk_sum(in_part[0], in_part[1], "yxl")
    arrivals["i"] = first_step(chunks["i"])
    sums, seen = run_chunks(chunks, arrivals, "dgudgidguiudiggduidguiui", in_part[1])

    late = seen["i"][1]
    act = tie(act, late)
    g_proj = [tie(part, late) for part in g_proj]
    g_long = row_total([sum(mul_t(g_proj[g], in_all[h][g]) for g in range(3)) for h in range(2)])
    back = jnp.stack([half[block_rows : block_rows + 2] for half in (g_long[1], g_long[0])])
    back = from_behind(back, ("dp", "col"), -1)
    g_n1 = [g_long[h][:block_rows].at[-2:].add(back[h]) for h in range(2)]
    back_one, gain_one_grad = norm_back(tok, scale_one, 0, g_n1)
    tok_half = [(g_res[h] + back_one[h]).astype(low) for h in range(2)]
    token_grad = jnp.where(home, tok_half[0], home_to_away(tok_half[1]))
    ffn = [mul(act, down_all[h]) for h in range(2)]
    ffn_more = sibling_to_home(jnp.stack([part.astype(low) for part in ffn]))
    out_half = [(res[h] + (ffn[h] + ffn_more[h].astype(wide))).astype(low) for h in range(2)]
    output = jnp.where(home, out_half[0], home_to_away(out_half[1]))

    small = jnp.concatenate(
        [conv_grad]
        + [part[None] for h in range(2) for part in (gain_one_grad[h], gain_two_grad[h])]
    )
    small = tie(small, seen["i"][3])
    for bit in range((lax.axis_size("dp") - 1).bit_length()):
        small = small + flip(small, bit)
    small_more = swap(small, "col")
    conv_grad = small[:3] + small_more[:3]
    gains_grad = small[3:5] + small_more[5:]

    conv_m, conv_v, conv_u = lamb_moments(conv_weight, conv_grad, conv_first, conv_second, 0.0)
    gain_m, gain_v, gain_u = lamb_moments(norm_gains, gains_grad, gain_first, gain_second, 0.0)

    def in_flat(values):
        return jnp.transpose(values, (1, 0, 2)).reshape(3 * feat_cols, branch_cols)

    def in_back(values):
        return jnp.transpose(values.reshape(3, feat_cols, branch_cols), (1, 0, 2))

    def gu_back(values):
        return from_linear(values, feat_cols, 2)

    down_m, down_v, down_u, down_norms = lamb_dense(
        down_projection_weight, sums["d"], 0, down_first, down_second
    )
    pairs = 2 * hidden_cols // 128
    gu_rows = 32
    gu_m, gu_v, gu_u, gu_norms = lamb_call(
        lamb_pairs,
        gu_weight,
        [sums["g"], sums["u"]],
        to_linear(gu_first),
        to_linear(gu_second),
        gu_rows * pairs,
        gu_rows,
        0,
        [pltpu.VMEM((gu_rows * pairs, 128), wide)],
    )
    in_weight = in_flat(input_projection_weight)
    in_m, in_v, in_u, in_norms = lamb_dense(
        in_weight, sums["i"], branch_cols, in_flat(in_first), in_flat(in_second)
    )
    out_m, out_v, out_u, out_norms = lamb_dense(
        output_projection_weight, sums["i"], 0, out_first, out_second
    )
    col_first = (col_pos == 0).astype(wide)
    row_first = (row_pos == 0).astype(wide)
    partial_sums = jnp.stack(
        [
            in_norms,
            square_pair(conv_weight, conv_u) * col_first,
            out_norms,
            square_pair(norm_gains[0], gain_u[0]) * row_first,
            square_pair(norm_gains[1], gain_u[1]) * row_first,
            gu_norms,
            down_norms,
        ]
    )
    trust_norms = jnp.sqrt(lax.psum(partial_sums, ("row", "col")))
    gains_new = jnp.stack(
        [
            apply_trust(norm_gains[0], gain_u[0], trust_norms[3]),
            apply_trust(norm_gains[1], gain_u[1], trust_norms[4]),
        ]
    )
    return (
        output,
        token_grad,
        in_back(apply_trust(in_weight, in_u, trust_norms[0])),
        in_back(in_m),
        in_back(in_v),
        apply_trust(conv_weight, conv_u, trust_norms[1]),
        conv_m,
        conv_v,
        apply_trust(output_projection_weight, out_u, trust_norms[2]),
        out_m,
        out_v,
        gains_new,
        gain_m,
        gain_v,
        gu_back(apply_trust(gu_weight, gu_u, trust_norms[5])),
        gu_back(gu_m),
        gu_back(gu_v),
        apply_trust(down_projection_weight, down_u, trust_norms[6]),
        down_m,
        down_v,
        trust_norms,
    )


def solution(mesh):
    in_specs = (
        P(("dp", "row"), "col"),
        P(("dp", "row"), "col"),
        P("col", None, "row"),
        P(None, "row"),
        P("row", "col"),
        P(None, "col"),
        P("col", None, "row"),
        P("row", "col"),
        P("col", None, "row"),
        P("col", None, "row"),
        P(None, "row"),
        P(None, "row"),
        P("row", "col"),
        P("row", "col"),
        P(None, "col"),
        P(None, "col"),
        P("col", None, "row"),
        P("col", None, "row"),
        P("row", "col"),
        P("row", "col"),
    )
    out_specs = (
        P(("dp", "row"), "col"),
        P(("dp", "row"), "col"),
        P("col", None, "row"),
        P("col", None, "row"),
        P("col", None, "row"),
        P(None, "row"),
        P(None, "row"),
        P(None, "row"),
        P("row", "col"),
        P("row", "col"),
        P("row", "col"),
        P(None, "col"),
        P(None, "col"),
        P(None, "col"),
        P("col", None, "row"),
        P("col", None, "row"),
        P("col", None, "row"),
        P("row", "col"),
        P("row", "col"),
        P("row", "col"),
        P(),
    )
    return jax.shard_map(shards, mesh=mesh, in_specs=in_specs, out_specs=out_specs, check_vma=False)
```

```python
import jax
import jax.numpy as jnp
from jax import lax
from jax.experimental import pallas as pl
from jax.experimental.layout import Layout, with_layout_constraint
from jax.experimental.pallas import tpu as pltpu
from jax.sharding import PartitionSpec as P

D = 1024
SEQ_LEAST = 4096
STEP = 5


norm_eps = 1e-05
adam_eps = 1e-06
beta_one = 0.5
beta_two = 0.6
learn_rate = 0.5
decay_rate = 0.01
low = jnp.bfloat16
wide = jnp.float32


def from_behind(block, axis, distance):
    devices = range(lax.axis_size(axis))
    route = [(i - distance, i) for i in devices if i - distance in devices]
    return lax.ppermute(block, axis, route)


def swap(values, axis):
    return lax.ppermute(values, axis, [(0, 1), (1, 0)])


def to_home(values):
    return lax.ppermute(values, ("row", "col"), [(1, 0), (2, 3)])


def home_to_sibling(values):
    return lax.ppermute(values, ("row", "col"), [(0, 2), (3, 1)])


def home_to_away(values):
    return lax.ppermute(values, ("row", "col"), [(0, 1), (3, 2)])


def sibling_to_home(values):
    return lax.ppermute(values, ("row", "col"), [(2, 0), (1, 3)])


def contract(left, right, left_dim, right_dim):
    return lax.dot_general(
        left, right, (((left_dim,), (right_dim,)), ((), ())), preferred_element_type=wide
    )


def mul(left, right):
    return contract(left, right, 1, 0)


def mul_t(left, right):
    return contract(left, right, 1, 1)


def t_mul(left, right):
    return contract(left, right, 0, 0)


def lamb_moments(weight, grad, first, second, decay):
    first_new = beta_one * first + (1.0 - beta_one) * grad
    second_new = beta_two * second + (1.0 - beta_two) * grad * grad
    direction = (
        first_new
        / (1.0 - beta_one**STEP)
        / (jnp.sqrt(second_new / (1.0 - beta_two**STEP)) + adam_eps)
        + decay * weight
    )
    return (first_new, second_new, direction)


def square_pair(weight, direction):
    return jnp.stack([jnp.sum(weight * weight), jnp.sum(direction * direction)])


def lamb_rows(p, g, m, v, m_out, v_out, u_out):
    weight = p[...]
    grad = g[...].astype(wide)
    first_new, second_new, direction = lamb_moments(weight, grad, m[...], v[...], decay_rate)
    m_out[...] = first_new
    v_out[...] = second_new
    u_out[...] = direction
    return weight * weight, direction * direction


def lamb_loop(refs, sums, rows, step):
    lanes = sums.shape[2]

    @pl.when(pl.program_id(0) == 0)
    def _():
        sums[...] = jnp.zeros_like(sums)

    def body(at, total):
        here = pl.ds(pl.multiple_of(at * step, step), step)
        squares = lamb_rows(*[ref.at[here, :] for ref in refs])
        return tuple(
            t + jnp.sum(sq.reshape(step // 8, 8, lanes), axis=0) for t, sq in zip(total, squares)
        )

    zero = jnp.zeros((8, lanes), wide)
    total = lax.fori_loop(0, rows // step, body, (zero, zero))
    sums[0] += total[0]
    sums[1] += total[1]


def lamb_plain(p, g, m, v, m_out, v_out, u_out, sums):
    lamb_loop((p, g, m, v, m_out, v_out, u_out), sums, p.shape[0], 16)


def lamb_pairs(p, gate, up, m, v, m_out, v_out, u_out, sums, mixed):
    rows, cols = gate.shape
    tiles = cols // 128
    for tile in range(tiles):
        for side, ref in enumerate((gate, up)):
            mixed[pl.ds(2 * tile + side, rows, stride=2 * tiles), :] = ref[
                :, tile * 128 : (tile + 1) * 128
            ].astype(wide)
    lamb_loop((p, mixed, m, v, m_out, v_out, u_out), sums, p.shape[0], 64)


def lamb_call(kernel, state, grads, block, start, count, before, scratch):
    rows, cols = state[0].shape
    flat = pl.BlockSpec((block, cols), lambda i: (i + start, 0))
    whole = jax.ShapeDtypeStruct((rows, cols), wide)
    grad_specs = [
        pl.BlockSpec((size, grad.shape[1]), lambda i, at=at: (i + at, 0)) for grad, size, at in grads
    ]
    weight, first, second = state
    args = [weight, *[grad for grad, _, _ in grads], first, second]
    specs = [flat] + grad_specs + [flat, flat]
    aliases = {}
    run = kernel
    if before is not None:
        aliases = {len(args) + k: k for k in range(3)}

        def run(*refs):
            kernel(*refs[: len(args)], *refs[len(args) + 3 :])

    call = pl.pallas_call(
        run,
        grid=(count,),
        in_specs=specs + [pl.BlockSpec(memory_space=pl.ANY)] * len(aliases),
        out_specs=[flat, flat, flat, pl.BlockSpec((2, 8, cols), lambda i: (0, 0, 0))],
        out_shape=[whole, whole, whole, jax.ShapeDtypeStruct((2, 8, cols), wide)],
        scratch_shapes=scratch,
        input_output_aliases=aliases,
        compiler_params=pltpu.CompilerParams(vmem_limit_bytes=40 * 1024 * 1024),
        cost_estimate=pl.CostEstimate(
            flops=20 * count * block * cols,
            bytes_accessed=26 * count * block * cols,
            transcendentals=2 * count * block * cols,
        ),
    )
    m_new, v_new, direction, sums = call(*args, *(before or []))
    return [m_new, v_new, direction], jnp.sum(sums, axis=(1, 2))


def lamb_dense(state, parts, block):
    before, norms = None, 0.0
    for grad, grad_at, at, rows in parts:
        before, sums = lamb_call(
            lamb_plain,
            state,
            [(grad, block, grad_at // block)],
            block,
            at // block,
            rows // block,
            before,
            [],
        )
        norms = norms + sums
    return before, norms


def to_linear(values):
    rows, sides, cols = values.shape
    split = with_layout_constraint(
        values.reshape(rows, sides, cols // 128, 128), Layout(major_to_minor=(0, 2, 1, 3))
    )
    return split.transpose(0, 2, 1, 3).reshape(rows * sides * cols // 128, 128)


def from_linear(values, rows, sides):
    cols = values.size // (rows * sides)
    split = values.reshape(rows, cols // 128, sides, 128).transpose(0, 2, 1, 3)
    split = with_layout_constraint(split, Layout(major_to_minor=(0, 2, 1, 3)))
    return split.reshape(rows, sides, cols)


def apply_trust(weight, direction, norms):
    return weight - learn_rate * (norms[0] / (norms[1] + adam_eps)) * direction


def flip(values, bit):
    size = lax.axis_size("dp")
    return lax.ppermute(values, "dp", [(i, i ^ (1 << bit)) for i in range(size)])


def dp_bit(bit):
    return (lax.axis_index("dp") >> bit) & 1


def rows_of(values, start, rows):
    return lax.dynamic_slice_in_dim(values, start, rows, 0)


def total_of(pieces):
    total = pieces[0].astype(wide)
    for piece in pieces[1:]:
        total = total + piece.astype(wide)
    return total


def tie(values, *deps):
    return lax.optimization_barrier((values, *deps))[0]


def low_total(pieces):
    return total_of(pieces).astype(low)


def keep_or_join(bit, part, other):
    return jnp.where(
        dp_bit(bit) == 0,
        jnp.concatenate([part, other]),
        jnp.concatenate([other, part]),
    )


def share_of(weight, order):
    rows = weight.shape[0] // (1 << len(order))
    index = 0
    for bit in order:
        index = 2 * index + dp_bit(bit)
    return rows_of(weight, index * rows, rows)


def chunk_sum(mine, other, order):
    bits = {"y": 0, "l": 1}
    steps = [name if name == "x" else bits[name] for name in order]
    mine = [mine]
    other = [other]
    for step in steps:
        if step == "x":
            got = yield step, low_total(other)
            mine.append(got)
            other = None
            continue
        rows = mine[0].shape[0] // 2
        here = dp_bit(step)
        groups = [mine] if other is None else [mine, other]
        send = [low_total([rows_of(p, (1 - here) * rows, rows) for p in g]) for g in groups]
        got = yield step, jnp.concatenate(send) if len(send) > 1 else send[0]
        mine = [rows_of(p, here * rows, rows) for p in mine] + [got[:rows]]
        if other is not None:
            other = [rows_of(p, here * rows, rows) for p in other] + [got[rows:]]
    part = low_total(mine)
    for step in range((lax.axis_size("dp") - 1).bit_length()):
        if step not in steps:
            got = yield step, part
            part = low_total([part, got])
    for step in reversed(steps):
        if step != "x":
            got = yield step, part
            part = keep_or_join(step, part, got)
    return part


def move(step, send):
    return swap(send, "col") if step == "x" else flip(send, step)


def first_step(chunk):
    step, send = next(chunk)
    return move(step, send)


def run_chunks(chunks, arrivals, sequence, after):
    done = {}
    seen = {name: [] for name in chunks}
    pending = list(sequence)
    while len(done) < len(chunks):
        names = [pending.pop(0)] if pending else [n for n in chunks if n not in done]
        for name in names:
            if name in done:
                continue
            got = tie(arrivals[name], after)
            seen[name].append(got)
            try:
                step, send = chunks[name].send(got)
            except StopIteration as end:
                done[name] = end.value
                continue
            arrivals[name] = move(step, send)
            after = send
    return done, seen


def deinterleave(pairs, gate, up):
    rows, cols = gate.shape
    tiles = cols // 128
    for tile in range(tiles):
        for side, out in enumerate((gate, up)):
            out[:, tile * 128 : (tile + 1) * 128] = pairs[
                pl.ds(2 * tile + side, rows, stride=2 * tiles), :
            ].astype(low)


def split_pairs(linear, rows, cols):
    block = 64
    half = jax.ShapeDtypeStruct((rows, cols), low)
    out_spec = pl.BlockSpec((block, cols), lambda i: (i, 0))
    return pl.pallas_call(
        deinterleave,
        grid=(rows // block,),
        in_specs=[pl.BlockSpec((block * 2 * cols // 128, 128), lambda i: (i, 0))],
        out_specs=[out_spec, out_spec],
        out_shape=[half, half],
        compiler_params=pltpu.CompilerParams(vmem_limit_bytes=24 * 1024 * 1024),
        cost_estimate=pl.CostEstimate(
            flops=rows * cols, bytes_accessed=12 * rows * cols, transcendentals=0
        ),
    )(linear)


def dot_of(left, right, left_dim, right_dim):
    return lax.dot_general(
        left, right, (((left_dim,), (right_dim,)), ((), ())), preferred_element_type=wide
    )


def local_call(kernel, grid, in_specs, out_specs, out_shape, scratch, args, prefetch=0):
    return pl.pallas_call(
        kernel,
        grid_spec=pltpu.PrefetchScalarGridSpec(
            num_scalar_prefetch=prefetch,
            grid=grid,
            in_specs=in_specs,
            out_specs=out_specs,
            scratch_shapes=scratch,
        ),
        out_shape=out_shape,
        compiler_params=pltpu.CompilerParams(vmem_limit_bytes=48 * 1024 * 1024),
        cost_estimate=pl.CostEstimate(flops=1000000, bytes_accessed=100000, transcendentals=0),
    )(*args)


def whole_spec(shape):
    return pl.BlockSpec(shape, lambda *_: (0,) * len(shape))


def shape_of(dims, kind):
    return jax.ShapeDtypeStruct(dims, kind)


def row_scale(halves):
    total = sum(jnp.sum(half * half, axis=1, keepdims=True) for half in halves)
    return lax.rsqrt(total / D + norm_eps)


def branch_kernel(tok, tail, gains, taps, own, other, n1, gate_b, gate_c, gate_x, conv, hidden, part, ext):
    rows, width = tok.shape[1:]
    tails = tail.shape[1]
    for source, start, count in ((tok, 0, rows), (tail, rows, tails)):
        halves = [source[h].astype(wide) for h in range(2)]
        scale = row_scale(halves)
        for h in range(2):
            n1[h, start : start + count, :] = (halves[h] * scale * gains[h]).astype(low)
    step = (rows + tails) // 3

    def gates(at, carry):
        here = pl.ds(pl.multiple_of(at * step, step), step)
        for g, out in enumerate((gate_b, gate_c, gate_x)):
            w = slice(g * width, (g + 1) * width)
            out[here, :] = dot_of(n1[0, here, :], own[w, :], 1, 0) + dot_of(
                n1[1, here, :], other[w, :], 1, 0
            )
        return carry

    lax.fori_loop(0, 3, gates, 0)
    ext[8 : 8 + rows, :] = gate_b[:rows, :] * gate_x[:rows, :]
    ext[6:8, :] = gate_b[rows : rows + 2, :] * gate_x[rows : rows + 2, :]
    w_out = slice(3 * width, 4 * width)
    quarter = rows // 4
    for at in range(4):
        start = at * quarter
        taken = slice(start, start + quarter)
        value = sum(taps[k] * ext[start + 6 + k : start + 6 + k + quarter, :] for k in range(3))
        conv[taken, :] = value
        low_hidden = (gate_c[taken, :] * value).astype(low)
        hidden[taken, :] = low_hidden
        for h, weight in enumerate((own, other)):
            part[h, taken, :] = dot_of(low_hidden, weight[w_out, :], 1, 0).astype(low)


def branch_forward(tok, tail, gains, taps, own, other):
    _, rows, width = tok.shape
    tails = tail.shape[1]
    gate = shape_of((rows + tails, width), wide)
    outs = [
        shape_of((2, rows + tails, width), low),
        gate,
        gate,
        gate,
        shape_of((rows, width), wide),
        shape_of((rows, width), low),
        shape_of((2, rows, width), low),
    ]
    args = (tok, tail, gains, taps, own, other)
    return local_call(
        branch_kernel,
        (1,),
        [whole_spec(a.shape) for a in args],
        [whole_spec(o.shape) for o in outs],
        outs,
        [pltpu.VMEM((rows + 8, width), wide)],
        args,
    )


def piece_at(bits, which, piece, width):
    place = bits[which] if piece == 0 else 1 - bits[which]
    return pl.ds(pl.multiple_of(place * width, width), width)


def ffn_kernel(bits, tok, mine, theirs, gains, g0, g1, g2, u0, u1, u2, n2, res, gate, up, act):
    width = g1.shape[0]

    @pl.when(pl.program_id(0) == 0)
    def _():
        for h in range(2):
            res[h] = tok[h].astype(wide) + (mine[h].astype(wide) + theirs[h].astype(wide))
        scale = row_scale([res[0], res[1]])
        for h in range(2):
            n2[h] = (res[h] * scale * gains[h]).astype(low)

    for which, (out, w0, w1, w2) in enumerate(((gate, g0, g1, g2), (up, u0, u1, u2))):
        total = dot_of(n2[0], w0[...], 1, 0)
        for piece, w in enumerate((w1, w2)):
            total += dot_of(n2[1, :, piece_at(bits, which, piece, width)], w[...], 1, 0)
        out[...] = total
    value = gate[...]
    act[...] = (value * jax.nn.sigmoid(value) * up[...]).astype(low)


def ffn_forward(bits, tok, mine, theirs, gains, weights):
    _, rows, width = tok.shape
    cols = weights[0].shape[1]
    tile = cols // 3
    full = whole_spec(tok.shape)
    wide_tile = pl.BlockSpec((rows, tile), lambda i, *_: (0, i))
    weight_specs = [pl.BlockSpec((w.shape[0], tile), lambda i, *_: (0, i)) for w in weights]
    return local_call(
        ffn_kernel,
        (3,),
        [full, full, full, whole_spec(gains.shape)] + weight_specs,
        [full, full, wide_tile, wide_tile, wide_tile],
        [
            shape_of(tok.shape, low),
            shape_of(tok.shape, wide),
            shape_of((rows, cols), wide),
            shape_of((rows, cols), wide),
            shape_of((rows, cols), low),
        ],
        [],
        (bits, tok, mine, theirs, gains, *weights),
        prefetch=1,
    )


def ffn_back_kernel(
    bits, cot, d_own, d_other, gate, up, g0, g1, g2, u0, u1, u2, g_gate, g_up, part, total
):
    width = g1.shape[0]

    @pl.when(pl.program_id(0) == 0)
    def _():
        total[...] = jnp.zeros_like(total)

    g_act = dot_of(cot[0], d_own[...], 1, 1) + dot_of(cot[1], d_other[...], 1, 1)
    value = gate[...]
    sigma = jax.nn.sigmoid(value)
    g_gate[...] = (g_act * up[...] * sigma * (1.0 + value * (1.0 - sigma))).astype(low)
    g_up[...] = (g_act * (value * sigma)).astype(low)
    total[0] += dot_of(g_gate[...], g0[...], 1, 1) + dot_of(g_up[...], u0[...], 1, 1)
    for which, (grad, w1, w2) in enumerate(((g_gate, g1, g2), (g_up, u1, u2))):
        for piece, w in enumerate((w1, w2)):
            total[1, :, piece_at(bits, which, piece, width)] += dot_of(grad[...], w[...], 1, 1)

    @pl.when(pl.program_id(0) == pl.num_programs(0) - 1)
    def _():
        part[...] = total[...].astype(low)


def ffn_backward(bits, cot, downs, gate, up, weights):
    rows, cols = gate.shape
    tile = cols // 3
    wide_tile = pl.BlockSpec((rows, tile), lambda i, *_: (0, i))
    weight_specs = [pl.BlockSpec((w.shape[0], tile), lambda i, *_: (0, i)) for w in weights]
    down_spec = pl.BlockSpec((tile, downs[0].shape[1]), lambda i, *_: (i, 0))
    return local_call(
        ffn_back_kernel,
        (3,),
        [whole_spec(cot.shape), down_spec, down_spec, wide_tile, wide_tile] + weight_specs,
        [wide_tile, wide_tile, whole_spec(cot.shape)],
        [shape_of((rows, cols), low), shape_of((rows, cols), low), shape_of(cot.shape, low)],
        [pltpu.VMEM(cot.shape, wide)],
        (bits, cot, *downs, gate, up, *weights),
        prefetch=1,
    )


def pair_grad_kernel(n2, g_gate, g_up, out):
    rows = n2.shape[2]
    for side, grad in enumerate((g_gate, g_up)):
        out[0, 0, side * rows : (side + 1) * rows, :] = dot_of(n2[0], grad[...], 0, 0).astype(low)


def pair_grads(n2, g_gate, g_up, chunks):
    _, rows, width = n2.shape
    cols = g_gate.shape[1]
    part = width // chunks
    return local_call(
        pair_grad_kernel,
        (2, chunks),
        [
            pl.BlockSpec((1, rows, part), lambda h, q: (h, 0, q)),
            whole_spec(g_gate.shape),
            whole_spec(g_up.shape),
        ],
        pl.BlockSpec((1, 1, 2 * part, cols), lambda h, q: (h, q, 0, 0)),
        shape_of((2, chunks, 2 * part, cols), low),
        [],
        (n2, g_gate, g_up),
    )


def branch_back_kernel(
    mine, theirs, res, cot, gains, taps, own, other, gate_b, gate_c, gate_x, conv,
    g_res, g_low, g_proj, gain_grad, tap_grad, ext, ext_grad,
):
    _, rows, width = res.shape
    scale = row_scale([res[0], res[1]])
    grads = [mine[h].astype(wide) + theirs[h].astype(wide) for h in range(2)]
    inner = sum(
        jnp.sum(grads[h] * gains[h] * res[h], axis=1, keepdims=True) for h in range(2)
    )
    factor = scale * scale * scale * inner / D
    for h in range(2):
        gain_grad[h] = jnp.sum(grads[h] * res[h] * scale, axis=0, keepdims=True)
        value = cot[h].astype(wide) + (scale * (grads[h] * gains[h]) - res[h] * factor)
        g_res[h] = value
        g_low[h] = value.astype(low)
    g_hidden = dot_of(g_low[0], own[...], 1, 1) + dot_of(g_low[1], other[...], 1, 1)
    g_proj[1, :rows, :] = (g_hidden * conv[...]).astype(low)
    g_conv = g_hidden * gate_c[:rows, :]
    ext_grad[:rows, :] = g_conv
    ext_grad[rows:, :] = jnp.zeros((8, width), wide)
    ext[8 : 8 + rows, :] = gate_b[:rows, :] * gate_x[:rows, :]
    ext[6:8, :] = gate_b[rows : rows + 2, :] * gate_x[rows : rows + 2, :]
    for k in range(3):
        tap_grad[k : k + 1, :] = jnp.sum(
            g_conv * ext[6 + k : 6 + k + rows, :], axis=0, keepdims=True
        )
    g_mixed = sum(taps[2 - k] * ext_grad[k : k + rows, :] for k in range(3))
    g_proj[0, :rows, :] = (g_mixed * gate_x[:rows, :]).astype(low)
    g_proj[2, :rows, :] = (g_mixed * gate_b[:rows, :]).astype(low)
    tails = g_proj.shape[1] - rows
    row = lax.broadcasted_iota(jnp.int32, (tails, width), 0)
    first, second = ext_grad[0:1, :], ext_grad[1:2, :]
    g_before = jnp.where(
        row == 0,
        taps[0] * first,
        jnp.where(row == 1, taps[1] * first + taps[0] * second, 0.0),
    )
    g_proj[0, rows:, :] = (g_before * gate_x[rows:, :]).astype(low)
    g_proj[1, rows:, :] = jnp.zeros((tails, width), low)
    g_proj[2, rows:, :] = (g_before * gate_b[rows:, :]).astype(low)


def branch_backward(mine, theirs, res, cot, gains, taps, own, other, gates, conv):
    _, rows, width = res.shape
    long = gates[0].shape[0]
    out_weight = pl.BlockSpec((width, width), lambda i, *_: (3, 0))
    outs = [
        shape_of(res.shape, wide),
        shape_of(res.shape, low),
        shape_of((3, long, width), low),
        shape_of((2, 1, width), wide),
        shape_of((3, width), wide),
    ]
    full = whole_spec(res.shape)
    return local_call(
        branch_back_kernel,
        (1,),
        [full, full, full, full, whole_spec(gains.shape), whole_spec(taps.shape)]
        + [out_weight, out_weight]
        + [whole_spec(g.shape) for g in gates]
        + [whole_spec(conv.shape)],
        [whole_spec(o.shape) for o in outs],
        outs,
        [pltpu.VMEM((rows + 8, width), wide), pltpu.VMEM((rows + 8, width), wide)],
        (mine, theirs, res, cot, gains, taps, own, other, *gates, conv),
    )


def branch_grad_kernel(n1, g_proj, hidden, g_low, out):
    kind = pl.program_id(1)

    @pl.when(kind < 3)
    def _():
        out[0, 0] = dot_of(n1[0], g_proj[0], 0, 0).astype(low)

    @pl.when(kind == 3)
    def _():
        out[0, 0] = dot_of(hidden[...], g_low[0], 0, 0).astype(low)


def branch_grads(n1, g_proj, hidden, g_low):
    _, long, width = n1.shape
    rows = hidden.shape[0]
    return local_call(
        branch_grad_kernel,
        (2, 4),
        [
            pl.BlockSpec((1, long, width), lambda h, k: (h, 0, 0)),
            pl.BlockSpec((1, long, width), lambda h, k: (jnp.minimum(k, 2), 0, 0)),
            whole_spec(hidden.shape),
            pl.BlockSpec((1, rows, width), lambda h, k: (h, 0, 0)),
        ],
        pl.BlockSpec((1, 1, width, width), lambda h, k: (h, k, 0, 0)),
        shape_of((2, 4, width, width), low),
        [],
        (n1, g_proj, hidden, g_low),
    )


def shards(
    tokens,
    cotangent,
    input_projection_weight,
    conv_weight,
    output_projection_weight,
    norm_gains,
    gate_up_weight,
    down_projection_weight,
    in_first,
    in_second,
    conv_first,
    conv_second,
    out_first,
    out_second,
    gain_first,
    gain_second,
    gu_first,
    gu_second,
    down_first,
    down_second,
):
    feat_cols = tokens.shape[1]
    branch_cols = conv_weight.shape[1]
    hidden_cols = down_projection_weight.shape[0]
    block_rows = tokens.shape[0]
    seq_len = max(SEQ_LEAST, block_rows * lax.axis_size("dp") * lax.axis_size("col"))
    data_pos = lax.axis_index("dp")
    row_pos = lax.axis_index("row")
    col_pos = lax.axis_index("col")
    home = row_pos == col_pos
    block_start = (data_pos * lax.axis_size("col") + col_pos) * block_rows
    keep_before = block_start % seq_len != 0
    tail_rows = 16

    tok_away = to_home(tokens)
    in_low = jnp.transpose(input_projection_weight, (1, 0, 2)).astype(low).reshape(-1, branch_cols)
    io_low = jnp.concatenate([in_low, output_projection_weight.astype(low)])
    io_got = swap(share_of(io_low, (1, 0)), "col")
    gu_weight = to_linear(gate_up_weight)
    gate_low, up_low = split_pairs(gu_weight, feat_cols, hidden_cols)
    down_low = down_projection_weight.astype(low)
    gains_away = swap(norm_gains, "col")
    gains = [jnp.stack([norm_gains[k : k + 1], gains_away[k : k + 1]]) for k in range(2)]

    def both_halves(own, away):
        full = jnp.stack([own, away])
        return jnp.where(home, full, home_to_sibling(full))

    tok = both_halves(tokens, tok_away)
    tail = from_behind(tok[:, -2:], ("dp", "col"), 1)
    tail = jnp.where(keep_before, tail[::-1], jnp.zeros_like(tail))
    tail = jnp.pad(tail, ((0, 0), (0, tail_rows - 2), (0, 0)))
    gate_got = swap(tie(share_of(gate_low, (0,)), tok_away), "col")
    cot_away = to_home(tie(cotangent, io_got))
    up_got = swap(tie(share_of(up_low, (1,)), cot_away), "col")
    down_got = swap(tie(down_low, gate_got), "col")
    io_pair = keep_or_join(0, io_got, flip(io_got, 0))
    io_other = keep_or_join(1, io_pair, flip(io_pair, 1))
    gate_more = flip(tie(gate_got, io_pair), 0)
    up_more = flip(tie(up_got, io_pair), 1)
    weights = [gate_low, gate_got, gate_more, up_low, up_got, up_more]
    bits = jnp.stack([dp_bit(0), dp_bit(1)]).astype(jnp.int32)
    downs = [down_low, down_got]
    cot = both_halves(cotangent, cot_away)

    n1, gate_b, gate_c, gate_x, conv, hidden, branch = branch_forward(
        tok, tail, gains[0], conv_weight, io_low, io_other
    )
    n2, res, gate, upper, act = ffn_forward(
        bits, tok, branch, swap(branch, "row"), gains[1], weights
    )

    chunks = {}
    arrivals = {}

    def add_chunk(name, mine, other, order):
        chunks[name] = chunk_sum(mine, other, order)
        arrivals[name] = first_step(chunks[name])

    down_part = [t_mul(act, cot[h]).astype(low) for h in range(2)]
    down_half = hidden_cols // 2
    for k, order in enumerate(("ylx", "xyl")):
        rows = slice(k * down_half, (k + 1) * down_half)
        add_chunk("Dd"[k], down_part[0][rows], down_part[1][rows], order)
    g_gate, g_up, part_two = ffn_backward(bits, cot, downs, gate, upper, weights)
    pair_part = pair_grads(n2, g_gate, g_up, 4)
    for k, order in enumerate(("lyx", "yxl", "xly", "yxl")):
        add_chunk("abce"[k], pair_part[0, k], pair_part[1, k], order)
    g_res, g_branch, g_proj, gain_two_grad, conv_grad = branch_backward(
        part_two,
        swap(part_two, "row"),
        res,
        cot,
        gains[1],
        conv_weight,
        io_low,
        io_other,
        (gate_b, gate_c, gate_x),
        conv,
    )
    io_part = branch_grads(n1, g_proj, hidden, g_branch).reshape(2, 2, 2 * feat_cols, branch_cols)
    for k, order in enumerate(("lxy", "yxl")):
        add_chunk("Ii"[k], io_part[0, k], io_part[1, k], order)
    sequence = "DdabDcbDeIdcbeDdIibeaDcidIabeDcidbIcaediIacieIia"
    sums, seen = run_chunks(chunks, arrivals, sequence, io_part)

    late = seen["i"][1]
    act = tie(act, late)
    g_proj = tie(g_proj, late)
    io_half = [half.reshape(4, feat_cols, branch_cols) for half in (io_low, io_other)]
    g_part = jnp.stack(
        [sum(mul_t(g_proj[g], io_half[h][g]) for g in range(3)).astype(low) for h in range(2)]
    )
    g_long = g_part.astype(wide) + swap(g_part, "row").astype(wide)
    back = from_behind(g_long[::-1, block_rows : block_rows + 2], ("dp", "col"), -1)
    g_n1 = g_long[:, :block_rows].at[:, -2:].add(back)
    tok = tok.astype(wide)
    scale = lax.rsqrt(jnp.sum(tok * tok, axis=(0, 2)) / D + norm_eps)[None, :, None]
    weighted = g_n1 * gains[0]
    inner = jnp.sum(weighted * tok, axis=(0, 2))[None, :, None]
    gain_one_grad = jnp.sum(g_n1 * tok * scale, axis=1)
    tok_half = (g_res + (scale * weighted - tok * (scale * scale * scale * inner / D))).astype(low)
    token_grad = jnp.where(home, tok_half[0], home_to_away(tok_half[1]))
    ffn = jnp.stack([mul(act, downs[h]) for h in range(2)])
    out_half = (res + (ffn + sibling_to_home(ffn.astype(low)).astype(wide))).astype(low)
    output = jnp.where(home, out_half[0], home_to_away(out_half[1]))

    small = jnp.concatenate(
        [conv_grad]
        + [part for h in range(2) for part in (gain_one_grad[h : h + 1], gain_two_grad[h])]
    )
    small = tie(small, seen["i"][3])
    for bit in range((lax.axis_size("dp") - 1).bit_length()):
        small = small + flip(small, bit)
    small_more = swap(small, "col")
    conv_grad = small[:3] + small_more[:3]
    gains_grad = small[3:5] + small_more[5:]

    conv_m, conv_v, conv_u = lamb_moments(conv_weight, conv_grad, conv_first, conv_second, 0.0)
    gain_m, gain_v, gain_u = lamb_moments(norm_gains, gains_grad, gain_first, gain_second, 0.0)

    def in_flat(values):
        return jnp.transpose(values, (1, 0, 2)).reshape(3 * feat_cols, branch_cols)

    def in_back(values):
        return jnp.transpose(values.reshape(3, feat_cols, branch_cols), (1, 0, 2))

    def gu_back(values):
        return from_linear(values, feat_cols, 2)

    (down_m, down_v, down_u), down_norms = lamb_dense(
        (down_projection_weight, down_first, down_second),
        [(sums["Dd"[k]], 0, k * down_half, down_half) for k in range(2)],
        384,
    )
    gu_state = (gu_weight, to_linear(gu_first), to_linear(gu_second))
    pairs = 2 * hidden_cols // 128
    gu_rows = 32
    gu_new, gu_norms = None, 0.0
    for k in range(4):
        grad = sums["abce"[k]]
        blocks = grad.shape[0] // 2 // gu_rows
        gu_new, squares = lamb_call(
            lamb_pairs,
            gu_state,
            [(grad, gu_rows, 0), (grad, gu_rows, blocks)],
            gu_rows * pairs,
            k * blocks,
            blocks,
            gu_new,
            [pltpu.VMEM((gu_rows * pairs, 128), wide)],
        )
        gu_norms = gu_norms + squares
    gu_m, gu_v, gu_u = gu_new
    in_weight = in_flat(input_projection_weight)
    (in_m, in_v, in_u), in_norms = lamb_dense(
        (in_weight, in_flat(in_first), in_flat(in_second)),
        [
            (sums["I"], 0, 0, 2 * feat_cols),
            (sums["i"], 0, 2 * feat_cols, feat_cols),
        ],
        256,
    )
    (out_m, out_v, out_u), out_norms = lamb_dense(
        (output_projection_weight, out_first, out_second),
        [(sums["i"], feat_cols, 0, branch_cols)],
        256,
    )
    col_first = (col_pos == 0).astype(wide)
    row_first = (row_pos == 0).astype(wide)
    partial_sums = jnp.stack(
        [
            in_norms,
            square_pair(conv_weight, conv_u) * col_first,
            out_norms,
            square_pair(norm_gains[0], gain_u[0]) * row_first,
            square_pair(norm_gains[1], gain_u[1]) * row_first,
            gu_norms,
            down_norms,
        ]
    )
    trust_norms = jnp.sqrt(lax.psum(partial_sums, ("row", "col")))
    gains_new = jnp.stack(
        [
            apply_trust(norm_gains[0], gain_u[0], trust_norms[3]),
            apply_trust(norm_gains[1], gain_u[1], trust_norms[4]),
        ]
    )
    return (
        output,
        token_grad,
        in_back(apply_trust(in_weight, in_u, trust_norms[0])),
        in_back(in_m),
        in_back(in_v),
        apply_trust(conv_weight, conv_u, trust_norms[1]),
        conv_m,
        conv_v,
        apply_trust(output_projection_weight, out_u, trust_norms[2]),
        out_m,
        out_v,
        gains_new,
        gain_m,
        gain_v,
        gu_back(apply_trust(gu_weight, gu_u, trust_norms[5])),
        gu_back(gu_m),
        gu_back(gu_v),
        apply_trust(down_projection_weight, down_u, trust_norms[6]),
        down_m,
        down_v,
        trust_norms,
    )


def solution(mesh):
    in_specs = (
        P(("dp", "row"), "col"),
        P(("dp", "row"), "col"),
        P("col", None, "row"),
        P(None, "row"),
        P("row", "col"),
        P(None, "col"),
        P("col", None, "row"),
        P("row", "col"),
        P("col", None, "row"),
        P("col", None, "row"),
        P(None, "row"),
        P(None, "row"),
        P("row", "col"),
        P("row", "col"),
        P(None, "col"),
        P(None, "col"),
        P("col", None, "row"),
        P("col", None, "row"),
        P("row", "col"),
        P("row", "col"),
    )
    out_specs = (
        P(("dp", "row"), "col"),
        P(("dp", "row"), "col"),
        P("col", None, "row"),
        P("col", None, "row"),
        P("col", None, "row"),
        P(None, "row"),
        P(None, "row"),
        P(None, "row"),
        P("row", "col"),
        P("row", "col"),
        P("row", "col"),
        P(None, "col"),
        P(None, "col"),
        P(None, "col"),
        P("col", None, "row"),
        P("col", None, "row"),
        P("col", None, "row"),
        P("row", "col"),
        P("row", "col"),
        P("row", "col"),
        P(),
    )
    return jax.shard_map(shards, mesh=mesh, in_specs=in_specs, out_specs=out_specs, check_vma=False)
```

```python
import jax
import jax.numpy as jnp
from jax import lax
from jax.experimental import pallas as pl
from jax.experimental.layout import Layout, with_layout_constraint
from jax.experimental.pallas import tpu as pltpu
from jax.sharding import PartitionSpec as P

D = 1024
SEQ_LEAST = 4096
STEP = 5
FFN_TILES = 6


norm_eps = 1e-05
adam_eps = 1e-06
beta_one = 0.5
beta_two = 0.6
learn_rate = 0.5
decay_rate = 0.01
low = jnp.bfloat16
wide = jnp.float32


def from_behind(block, axis, distance):
    devices = range(lax.axis_size(axis))
    route = [(i - distance, i) for i in devices if i - distance in devices]
    return lax.ppermute(block, axis, route)


def swap(values, axis):
    return lax.ppermute(values, axis, [(0, 1), (1, 0)])


def to_home(values):
    return lax.ppermute(values, ("row", "col"), [(1, 0), (2, 3)])


def home_to_sibling(values):
    return lax.ppermute(values, ("row", "col"), [(0, 2), (3, 1)])


def home_to_away(values):
    return lax.ppermute(values, ("row", "col"), [(0, 1), (3, 2)])


def sibling_to_home(values):
    return lax.ppermute(values, ("row", "col"), [(2, 0), (1, 3)])


def contract(left, right, left_dim, right_dim):
    return lax.dot_general(
        left, right, (((left_dim,), (right_dim,)), ((), ())), preferred_element_type=wide
    )


def mul(left, right):
    return contract(left, right, 1, 0)


def mul_t(left, right):
    return contract(left, right, 1, 1)


def t_mul(left, right):
    return contract(left, right, 0, 0)


def lamb_moments(weight, grad, first, second, decay):
    first_new = beta_one * first + (1.0 - beta_one) * grad
    second_new = beta_two * second + (1.0 - beta_two) * grad * grad
    direction = (
        first_new
        / (1.0 - beta_one**STEP)
        / (jnp.sqrt(second_new / (1.0 - beta_two**STEP)) + adam_eps)
        + decay * weight
    )
    return (first_new, second_new, direction)


def square_pair(weight, direction):
    return jnp.stack([jnp.sum(weight * weight), jnp.sum(direction * direction)])


def lamb_rows(p, g, m, v, m_out, v_out, u_out):
    weight = p[...]
    grad = g[...].astype(wide)
    first_new, second_new, direction = lamb_moments(weight, grad, m[...], v[...], decay_rate)
    m_out[...] = first_new
    v_out[...] = second_new
    u_out[...] = direction
    return weight * weight, direction * direction


def lamb_loop(refs, sums, rows, step):
    lanes = sums.shape[2]

    @pl.when(pl.program_id(0) == 0)
    def _():
        sums[...] = jnp.zeros_like(sums)

    def body(at, total):
        here = pl.ds(pl.multiple_of(at * step, step), step)
        squares = lamb_rows(*[ref.at[here, :] for ref in refs])
        return tuple(
            t + jnp.sum(sq.reshape(step // 8, 8, lanes), axis=0) for t, sq in zip(total, squares)
        )

    zero = jnp.zeros((8, lanes), wide)
    total = lax.fori_loop(0, rows // step, body, (zero, zero))
    sums[0] += total[0]
    sums[1] += total[1]


def lamb_plain(p, g, m, v, m_out, v_out, u_out, sums):
    lamb_loop((p, g, m, v, m_out, v_out, u_out), sums, p.shape[0], 16)


def lamb_pairs(p, gate, up, m, v, m_out, v_out, u_out, sums, mixed):
    rows, cols = gate.shape
    tiles = cols // 128
    for tile in range(tiles):
        for side, ref in enumerate((gate, up)):
            mixed[pl.ds(2 * tile + side, rows, stride=2 * tiles), :] = ref[
                :, tile * 128 : (tile + 1) * 128
            ].astype(wide)
    lamb_loop((p, mixed, m, v, m_out, v_out, u_out), sums, p.shape[0], 64)


def lamb_call(kernel, state, grads, block, start, count, before, scratch):
    rows, cols = state[0].shape
    flat = pl.BlockSpec((block, cols), lambda i: (i + start, 0))
    whole = jax.ShapeDtypeStruct((rows, cols), wide)
    grad_specs = [
        pl.BlockSpec((size, grad.shape[1]), lambda i, at=at: (i + at, 0)) for grad, size, at in grads
    ]
    weight, first, second = state
    args = [weight, *[grad for grad, _, _ in grads], first, second]
    specs = [flat] + grad_specs + [flat, flat]
    aliases = {}
    run = kernel
    if before is not None:
        aliases = {len(args) + k: k for k in range(3)}

        def run(*refs):
            kernel(*refs[: len(args)], *refs[len(args) + 3 :])

    call = pl.pallas_call(
        run,
        grid=(count,),
        in_specs=specs + [pl.BlockSpec(memory_space=pl.ANY)] * len(aliases),
        out_specs=[flat, flat, flat, pl.BlockSpec((2, 8, cols), lambda i: (0, 0, 0))],
        out_shape=[whole, whole, whole, jax.ShapeDtypeStruct((2, 8, cols), wide)],
        scratch_shapes=scratch,
        input_output_aliases=aliases,
        compiler_params=pltpu.CompilerParams(vmem_limit_bytes=40 * 1024 * 1024),
        cost_estimate=pl.CostEstimate(
            flops=20 * count * block * cols,
            bytes_accessed=26 * count * block * cols,
            transcendentals=2 * count * block * cols,
        ),
    )
    m_new, v_new, direction, sums = call(*args, *(before or []))
    return [m_new, v_new, direction], jnp.sum(sums, axis=(1, 2))


def lamb_dense(state, parts, block):
    before, norms = None, 0.0
    for grad, grad_at, at, rows in parts:
        before, sums = lamb_call(
            lamb_plain,
            state,
            [(grad, block, grad_at // block)],
            block,
            at // block,
            rows // block,
            before,
            [],
        )
        norms = norms + sums
    return before, norms


def to_linear(values):
    rows, sides, cols = values.shape
    split = with_layout_constraint(
        values.reshape(rows, sides, cols // 128, 128), Layout(major_to_minor=(0, 2, 1, 3))
    )
    return split.transpose(0, 2, 1, 3).reshape(rows * sides * cols // 128, 128)


def from_linear(values, rows, sides):
    cols = values.size // (rows * sides)
    split = values.reshape(rows, cols // 128, sides, 128).transpose(0, 2, 1, 3)
    split = with_layout_constraint(split, Layout(major_to_minor=(0, 2, 1, 3)))
    return split.reshape(rows, sides, cols)


def apply_trust(weight, direction, norms):
    return weight - learn_rate * (norms[0] / (norms[1] + adam_eps)) * direction


def flip(values, bit):
    size = lax.axis_size("dp")
    return lax.ppermute(values, "dp", [(i, i ^ (1 << bit)) for i in range(size)])


def dp_bit(bit):
    return (lax.axis_index("dp") >> bit) & 1


def rows_of(values, start, rows):
    return lax.dynamic_slice_in_dim(values, start, rows, 0)


def total_of(pieces):
    total = pieces[0].astype(wide)
    for piece in pieces[1:]:
        total = total + piece.astype(wide)
    return total


def tie(values, *deps):
    return lax.optimization_barrier((values, *deps))[0]


def low_total(pieces):
    return total_of(pieces).astype(low)


def keep_or_join(bit, part, other):
    return jnp.where(
        dp_bit(bit) == 0,
        jnp.concatenate([part, other]),
        jnp.concatenate([other, part]),
    )


def share_of(weight, order):
    rows = weight.shape[0] // (1 << len(order))
    index = 0
    for bit in order:
        index = 2 * index + dp_bit(bit)
    return rows_of(weight, index * rows, rows)


def chunk_sum(mine, other, order):
    bits = {"y": 0, "l": 1}
    steps = [name if name == "x" else bits[name] for name in order]
    mine = [mine]
    other = [other]
    for step in steps:
        if step == "x":
            got = yield step, low_total(other)
            mine.append(got)
            other = None
            continue
        rows = mine[0].shape[0] // 2
        here = dp_bit(step)
        groups = [mine] if other is None else [mine, other]
        send = [low_total([rows_of(p, (1 - here) * rows, rows) for p in g]) for g in groups]
        got = yield step, jnp.concatenate(send) if len(send) > 1 else send[0]
        mine = [rows_of(p, here * rows, rows) for p in mine] + [got[:rows]]
        if other is not None:
            other = [rows_of(p, here * rows, rows) for p in other] + [got[rows:]]
    part = low_total(mine)
    for step in range((lax.axis_size("dp") - 1).bit_length()):
        if step not in steps:
            got = yield step, part
            part = low_total([part, got])
    for step in reversed(steps):
        if step != "x":
            got = yield step, part
            part = keep_or_join(step, part, got)
    return part


def move(step, send):
    return swap(send, "col") if step == "x" else flip(send, step)


def first_step(chunk):
    step, send = next(chunk)
    return move(step, send)


def run_chunks(chunks, arrivals, sequence, after):
    done = {}
    seen = {name: [] for name in chunks}
    pending = list(sequence)
    while len(done) < len(chunks):
        names = [pending.pop(0)] if pending else [n for n in chunks if n not in done]
        for name in names:
            if name in done:
                continue
            got = tie(arrivals[name], after)
            seen[name].append(got)
            try:
                step, send = chunks[name].send(got)
            except StopIteration as end:
                done[name] = end.value
                continue
            arrivals[name] = move(step, send)
            after = send
    return done, seen


def deinterleave(pairs, gate, up):
    rows, cols = gate.shape
    tiles = cols // 128
    for tile in range(tiles):
        for side, out in enumerate((gate, up)):
            out[:, tile * 128 : (tile + 1) * 128] = pairs[
                pl.ds(2 * tile + side, rows, stride=2 * tiles), :
            ].astype(low)


def split_pairs(linear, rows, cols):
    block = 64
    half = jax.ShapeDtypeStruct((rows, cols), low)
    out_spec = pl.BlockSpec((block, cols), lambda i: (i, 0))
    return pl.pallas_call(
        deinterleave,
        grid=(rows // block,),
        in_specs=[pl.BlockSpec((block * 2 * cols // 128, 128), lambda i: (i, 0))],
        out_specs=[out_spec, out_spec],
        out_shape=[half, half],
        compiler_params=pltpu.CompilerParams(vmem_limit_bytes=24 * 1024 * 1024),
        cost_estimate=pl.CostEstimate(
            flops=rows * cols, bytes_accessed=12 * rows * cols, transcendentals=0
        ),
    )(linear)


def dot_of(left, right, left_dim, right_dim):
    return lax.dot_general(
        left, right, (((left_dim,), (right_dim,)), ((), ())), preferred_element_type=wide
    )


def local_call(kernel, grid, in_specs, out_specs, out_shape, scratch, args, prefetch=0):
    return pl.pallas_call(
        kernel,
        grid_spec=pltpu.PrefetchScalarGridSpec(
            num_scalar_prefetch=prefetch,
            grid=grid,
            in_specs=in_specs,
            out_specs=out_specs,
            scratch_shapes=scratch,
        ),
        out_shape=out_shape,
        compiler_params=pltpu.CompilerParams(vmem_limit_bytes=48 * 1024 * 1024),
        cost_estimate=pl.CostEstimate(flops=1000000, bytes_accessed=100000, transcendentals=0),
    )(*args)


def whole_spec(shape):
    return pl.BlockSpec(shape, lambda *_: (0,) * len(shape))


def shape_of(dims, kind):
    return jax.ShapeDtypeStruct(dims, kind)


def row_scale(halves):
    total = sum(jnp.sum(half * half, axis=1, keepdims=True) for half in halves)
    return lax.rsqrt(total / D + norm_eps)


def branch_kernel(tok, gains, taps, own, other, n1, gate_b, gate_c, gate_x, conv, hidden, part, ext):
    long, width = tok.shape[1:]
    rows = conv.shape[0]
    step = long // 3

    def gates(at, carry):
        here = pl.ds(pl.multiple_of(at * step, step), step)
        halves = [tok[h, here, :].astype(wide) for h in range(2)]
        scale = row_scale(halves)
        for h in range(2):
            n1[h, here, :] = (halves[h] * scale * gains[h]).astype(low)
        for g, out in enumerate((gate_b, gate_c, gate_x)):
            w = slice(g * width, (g + 1) * width)
            out[here, :] = dot_of(n1[0, here, :], own[w, :], 1, 0) + dot_of(
                n1[1, here, :], other[w, :], 1, 0
            )
        return carry

    lax.fori_loop(0, 3, gates, 0)
    ext[8 : 8 + rows, :] = gate_b[:rows, :] * gate_x[:rows, :]
    ext[6:8, :] = gate_b[rows : rows + 2, :] * gate_x[rows : rows + 2, :]
    w_out = slice(3 * width, 4 * width)
    quarter = rows // 4
    for at in range(4):
        start = at * quarter
        taken = slice(start, start + quarter)
        value = sum(taps[k] * ext[start + 6 + k : start + 6 + k + quarter, :] for k in range(3))
        conv[taken, :] = value
        low_hidden = (gate_c[taken, :] * value).astype(low)
        hidden[taken, :] = low_hidden
        for h, weight in enumerate((own, other)):
            part[h, taken, :] = dot_of(low_hidden, weight[w_out, :], 1, 0).astype(low)


def branch_forward(tok, rows, gains, taps, own, other):
    _, long, width = tok.shape
    gate = shape_of((long, width), wide)
    outs = [
        shape_of((2, long, width), low),
        gate,
        gate,
        gate,
        shape_of((rows, width), wide),
        shape_of((rows, width), low),
        shape_of((2, rows, width), low),
    ]
    args = (tok, gains, taps, own, other)
    return local_call(
        branch_kernel,
        (1,),
        [whole_spec(a.shape) for a in args],
        [whole_spec(o.shape) for o in outs],
        outs,
        [pltpu.VMEM((rows + 8, width), wide)],
        args,
    )


def piece_at(bits, which, piece, width):
    place = bits[which] if piece == 0 else 1 - bits[which]
    return pl.ds(pl.multiple_of(place * width, width), width)


def ffn_kernel(bits, tok, mine, theirs, gains, g0, g1, g2, u0, u1, u2, n2, res, gate, up, act):
    width = g1.shape[0]

    @pl.when(pl.program_id(0) == 0)
    def _():
        for h in range(2):
            res[h] = tok[h, : res.shape[1], :].astype(wide) + (mine[h].astype(wide) + theirs[h].astype(wide))
        scale = row_scale([res[0], res[1]])
        for h in range(2):
            n2[h] = (res[h] * scale * gains[h]).astype(low)

    for which, (out, w0, w1, w2) in enumerate(((gate, g0, g1, g2), (up, u0, u1, u2))):
        total = dot_of(n2[0], w0[...], 1, 0)
        for piece, w in enumerate((w1, w2)):
            total += dot_of(n2[1, :, piece_at(bits, which, piece, width)], w[...], 1, 0)
        out[...] = total
    value = gate[...]
    act[...] = (value * jax.nn.sigmoid(value) * up[...]).astype(low)


def ffn_forward(bits, tok, mine, theirs, gains, weights):
    _, rows, width = mine.shape
    cols = weights[0].shape[1]
    tile = cols // FFN_TILES
    full = whole_spec(mine.shape)
    wide_tile = pl.BlockSpec((rows, tile), lambda i, *_: (0, i))
    weight_specs = [pl.BlockSpec((w.shape[0], tile), lambda i, *_: (0, i)) for w in weights]
    return local_call(
        ffn_kernel,
        (FFN_TILES,),
        [whole_spec(tok.shape), full, full, whole_spec(gains.shape)] + weight_specs,
        [full, full, wide_tile, wide_tile, wide_tile],
        [
            shape_of(mine.shape, low),
            shape_of(mine.shape, wide),
            shape_of((rows, cols), wide),
            shape_of((rows, cols), wide),
            shape_of((rows, cols), low),
        ],
        [],
        (bits, tok, mine, theirs, gains, *weights),
        prefetch=1,
    )


def ffn_back_kernel(
    bits, cot, d_own, d_other, gate, up, g0, g1, g2, u0, u1, u2, g_gate, g_up, part, total
):
    width = g1.shape[0]

    @pl.when(pl.program_id(0) == 0)
    def _():
        total[...] = jnp.zeros_like(total)

    g_act = dot_of(cot[0], d_own[...], 1, 1) + dot_of(cot[1], d_other[...], 1, 1)
    value = gate[...]
    sigma = jax.nn.sigmoid(value)
    g_gate[...] = (g_act * up[...] * sigma * (1.0 + value * (1.0 - sigma))).astype(low)
    g_up[...] = (g_act * (value * sigma)).astype(low)
    total[0] += dot_of(g_gate[...], g0[...], 1, 1) + dot_of(g_up[...], u0[...], 1, 1)
    for which, (grad, w1, w2) in enumerate(((g_gate, g1, g2), (g_up, u1, u2))):
        for piece, w in enumerate((w1, w2)):
            total[1, :, piece_at(bits, which, piece, width)] += dot_of(grad[...], w[...], 1, 1)

    @pl.when(pl.program_id(0) == pl.num_programs(0) - 1)
    def _():
        part[...] = total[...].astype(low)


def ffn_backward(bits, cot, downs, gate, up, weights):
    rows, cols = gate.shape
    tile = cols // FFN_TILES
    wide_tile = pl.BlockSpec((rows, tile), lambda i, *_: (0, i))
    weight_specs = [pl.BlockSpec((w.shape[0], tile), lambda i, *_: (0, i)) for w in weights]
    down_spec = pl.BlockSpec((tile, downs[0].shape[1]), lambda i, *_: (i, 0))
    return local_call(
        ffn_back_kernel,
        (FFN_TILES,),
        [whole_spec(cot.shape), down_spec, down_spec, wide_tile, wide_tile] + weight_specs,
        [wide_tile, wide_tile, whole_spec(cot.shape)],
        [shape_of((rows, cols), low), shape_of((rows, cols), low), shape_of(cot.shape, low)],
        [pltpu.VMEM(cot.shape, wide)],
        (bits, cot, *downs, gate, up, *weights),
        prefetch=1,
    )


def pair_grad_kernel(n2, g_gate, g_up, out):
    rows = n2.shape[2]
    for side, grad in enumerate((g_gate, g_up)):
        out[0, 0, side * rows : (side + 1) * rows, :] = dot_of(n2[0], grad[...], 0, 0).astype(low)


def pair_grads(n2, g_gate, g_up, chunks):
    _, rows, width = n2.shape
    cols = g_gate.shape[1]
    part = width // chunks
    return local_call(
        pair_grad_kernel,
        (2, chunks),
        [
            pl.BlockSpec((1, rows, part), lambda h, q: (h, 0, q)),
            whole_spec(g_gate.shape),
            whole_spec(g_up.shape),
        ],
        pl.BlockSpec((1, 1, 2 * part, cols), lambda h, q: (h, q, 0, 0)),
        shape_of((2, chunks, 2 * part, cols), low),
        [],
        (n2, g_gate, g_up),
    )


def branch_back_kernel(
    mine, theirs, res, cot, gains, taps, own, other, gate_b, gate_c, gate_x, conv,
    g_res, g_low, g_proj, gain_grad, tap_grad, ext, ext_grad,
):
    _, rows, width = res.shape
    scale = row_scale([res[0], res[1]])
    grads = [mine[h].astype(wide) + theirs[h].astype(wide) for h in range(2)]
    inner = sum(
        jnp.sum(grads[h] * gains[h] * res[h], axis=1, keepdims=True) for h in range(2)
    )
    factor = scale * scale * scale * inner / D
    for h in range(2):
        gain_grad[h] = jnp.sum(grads[h] * res[h] * scale, axis=0, keepdims=True)
        value = cot[h].astype(wide) + (scale * (grads[h] * gains[h]) - res[h] * factor)
        g_res[h] = value
        g_low[h] = value.astype(low)
    g_hidden = dot_of(g_low[0], own[...], 1, 1) + dot_of(g_low[1], other[...], 1, 1)
    g_proj[1, :rows, :] = (g_hidden * conv[...]).astype(low)
    g_conv = g_hidden * gate_c[:rows, :]
    ext_grad[:rows, :] = g_conv
    ext_grad[rows:, :] = jnp.zeros((8, width), wide)
    ext[8 : 8 + rows, :] = gate_b[:rows, :] * gate_x[:rows, :]
    ext[6:8, :] = gate_b[rows : rows + 2, :] * gate_x[rows : rows + 2, :]
    for k in range(3):
        tap_grad[k : k + 1, :] = jnp.sum(
            g_conv * ext[6 + k : 6 + k + rows, :], axis=0, keepdims=True
        )
    g_mixed = sum(taps[2 - k] * ext_grad[k : k + rows, :] for k in range(3))
    g_proj[0, :rows, :] = (g_mixed * gate_x[:rows, :]).astype(low)
    g_proj[2, :rows, :] = (g_mixed * gate_b[:rows, :]).astype(low)
    tails = g_proj.shape[1] - rows
    row = lax.broadcasted_iota(jnp.int32, (tails, width), 0)
    first, second = ext_grad[0:1, :], ext_grad[1:2, :]
    g_before = jnp.where(
        row == 0,
        taps[0] * first,
        jnp.where(row == 1, taps[1] * first + taps[0] * second, 0.0),
    )
    g_proj[0, rows:, :] = (g_before * gate_x[rows:, :]).astype(low)
    g_proj[1, rows:, :] = jnp.zeros((tails, width), low)
    g_proj[2, rows:, :] = (g_before * gate_b[rows:, :]).astype(low)


def branch_backward(mine, theirs, res, cot, gains, taps, own, other, gates, conv):
    _, rows, width = res.shape
    long = gates[0].shape[0]
    out_weight = pl.BlockSpec((width, width), lambda i, *_: (3, 0))
    outs = [
        shape_of(res.shape, wide),
        shape_of(res.shape, low),
        shape_of((3, long, width), low),
        shape_of((2, 1, width), wide),
        shape_of((3, width), wide),
    ]
    full = whole_spec(res.shape)
    return local_call(
        branch_back_kernel,
        (1,),
        [full, full, full, full, whole_spec(gains.shape), whole_spec(taps.shape)]
        + [out_weight, out_weight]
        + [whole_spec(g.shape) for g in gates]
        + [whole_spec(conv.shape)],
        [whole_spec(o.shape) for o in outs],
        outs,
        [pltpu.VMEM((rows + 8, width), wide), pltpu.VMEM((rows + 8, width), wide)],
        (mine, theirs, res, cot, gains, taps, own, other, *gates, conv),
    )


def branch_grad_kernel(n1, g_proj, hidden, g_low, out):
    kind = pl.program_id(1)

    @pl.when(kind < 3)
    def _():
        out[0, 0] = dot_of(n1[0], g_proj[0], 0, 0).astype(low)

    @pl.when(kind == 3)
    def _():
        out[0, 0] = dot_of(hidden[...], g_low[0], 0, 0).astype(low)


def branch_grads(n1, g_proj, hidden, g_low):
    _, long, width = n1.shape
    rows = hidden.shape[0]
    return local_call(
        branch_grad_kernel,
        (2, 4),
        [
            pl.BlockSpec((1, long, width), lambda h, k: (h, 0, 0)),
            pl.BlockSpec((1, long, width), lambda h, k: (jnp.minimum(k, 2), 0, 0)),
            whole_spec(hidden.shape),
            pl.BlockSpec((1, rows, width), lambda h, k: (h, 0, 0)),
        ],
        pl.BlockSpec((1, 1, width, width), lambda h, k: (h, k, 0, 0)),
        shape_of((2, 4, width, width), low),
        [],
        (n1, g_proj, hidden, g_low),
    )


def shards(
    tokens,
    cotangent,
    input_projection_weight,
    conv_weight,
    output_projection_weight,
    norm_gains,
    gate_up_weight,
    down_projection_weight,
    in_first,
    in_second,
    conv_first,
    conv_second,
    out_first,
    out_second,
    gain_first,
    gain_second,
    gu_first,
    gu_second,
    down_first,
    down_second,
):
    feat_cols = tokens.shape[1]
    branch_cols = conv_weight.shape[1]
    hidden_cols = down_projection_weight.shape[0]
    block_rows = tokens.shape[0]
    seq_len = max(SEQ_LEAST, block_rows * lax.axis_size("dp") * lax.axis_size("col"))
    data_pos = lax.axis_index("dp")
    row_pos = lax.axis_index("row")
    col_pos = lax.axis_index("col")
    home = row_pos == col_pos
    tail_rows = 16

    row_start = (data_pos * lax.axis_size("row") + row_pos) * block_rows
    tail = from_behind(tokens[-2:], ("dp", "row"), 1)
    tail = jnp.where(row_start % seq_len != 0, tail, jnp.zeros_like(tail))
    tokens = jnp.concatenate([tokens, jnp.pad(tail, ((0, tail_rows - 2), (0, 0)))])
    tok_away = to_home(tokens)
    in_low = jnp.transpose(input_projection_weight, (1, 0, 2)).astype(low).reshape(-1, branch_cols)
    io_low = jnp.concatenate([in_low, output_projection_weight.astype(low)])
    io_got = swap(share_of(io_low, (1, 0)), "col")
    gu_weight = to_linear(gate_up_weight)
    gate_low, up_low = split_pairs(gu_weight, feat_cols, hidden_cols)
    down_low = down_projection_weight.astype(low)
    gains_away = swap(norm_gains, "col")
    gains = [jnp.stack([norm_gains[k : k + 1], gains_away[k : k + 1]]) for k in range(2)]

    def both_halves(own, away):
        full = jnp.stack([own, away])
        return jnp.where(home, full, home_to_sibling(full))

    tok = both_halves(tokens, tok_away)
    gate_got = swap(tie(share_of(gate_low, (1, 0)), tok_away), "col")
    up_got = swap(tie(share_of(up_low, (0, 1)), io_got), "col")
    cot_away = to_home(tie(cotangent, gate_got))
    down_got = swap(tie(down_low, up_got), "col")
    io_pair = keep_or_join(0, io_got, flip(io_got, 0))
    io_other = keep_or_join(1, io_pair, flip(io_pair, 1))
    gate_pair = keep_or_join(0, gate_got, flip(tie(gate_got, io_pair), 0))
    up_pair = keep_or_join(1, up_got, flip(tie(up_got, io_pair), 1))
    gate_more = flip(gate_pair, 1)
    up_more = flip(up_pair, 0)
    weights = [gate_low, gate_pair, gate_more, up_low, up_pair, up_more]
    bits = jnp.stack([dp_bit(1), dp_bit(0)]).astype(jnp.int32)
    downs = [down_low, down_got]
    cot = both_halves(cotangent, cot_away)

    n1, gate_b, gate_c, gate_x, conv, hidden, branch = branch_forward(
        tok, block_rows, gains[0], conv_weight, io_low, io_other
    )
    n2, res, gate, upper, act = ffn_forward(
        bits, tok, branch, swap(branch, "row"), gains[1], weights
    )

    chunks = {}
    arrivals = {}

    def add_chunk(name, mine, other, order):
        chunks[name] = chunk_sum(mine, other, order)
        arrivals[name] = first_step(chunks[name])

    def sum_over_x(mine, other):
        return total_of([mine, swap(other, "col")]).astype(low)

    down_part = [t_mul(act, cot[h]).astype(low) for h in range(2)]
    down_half = hidden_cols // 2
    down_sums = []
    for k in range(2):
        rows = slice(k * down_half, (k + 1) * down_half)
        part = sum_over_x(down_part[0][rows], down_part[1][rows])
        down_sums.append(lax.psum(tie(part, *down_sums), "dp"))
    g_gate, g_up, part_two = ffn_backward(bits, cot, downs, gate, upper, weights)
    pair_part = pair_grads(n2, g_gate, g_up, 4)
    part = sum_over_x(pair_part[0, :2], pair_part[1, :2])
    pair_sums = list(lax.psum(tie(part, *down_sums), "dp"))
    for k, order in ((2, "lyx"), (3, "ylx")):
        add_chunk("ce"[k - 2], pair_part[0, k], pair_part[1, k], order)
    g_res, g_branch, g_proj, gain_two_grad, conv_grad = branch_backward(
        part_two,
        swap(part_two, "row"),
        res,
        cot,
        gains[1],
        conv_weight,
        io_low,
        io_other,
        (gate_b, gate_c, gate_x),
        conv,
    )
    io_part = branch_grads(n1, g_proj, hidden, g_branch).reshape(2, 2, 2 * feat_cols, branch_cols)
    for k, order in enumerate(("xyl", "lyx")):
        add_chunk("Ii"[k], io_part[0, k], io_part[1, k], order)
    sequence = "ceciIceieIcicIeiciIeiIeI"
    sums, seen = run_chunks(chunks, arrivals, sequence, io_part)

    late = seen["i"][2]
    act = tie(act, late)
    g_proj = tie(g_proj, late)
    io_half = [half.reshape(4, feat_cols, branch_cols) for half in (io_low, io_other)]
    g_part = jnp.stack(
        [sum(mul_t(g_proj[g], io_half[h][g]) for g in range(3)).astype(low) for h in range(2)]
    )
    g_long = g_part.astype(wide) + swap(g_part, "row").astype(wide)
    back = from_behind(g_long[::-1, block_rows : block_rows + 2], ("dp", "col"), -1)
    g_n1 = g_long[:, :block_rows].at[:, -2:].add(back)
    tok = tok[:, :block_rows].astype(wide)
    scale = lax.rsqrt(jnp.sum(tok * tok, axis=(0, 2)) / D + norm_eps)[None, :, None]
    weighted = g_n1 * gains[0]
    inner = jnp.sum(weighted * tok, axis=(0, 2))[None, :, None]
    gain_one_grad = jnp.sum(g_n1 * tok * scale, axis=1)
    tok_half = (g_res + (scale * weighted - tok * (scale * scale * scale * inner / D))).astype(low)
    token_grad = jnp.where(home, tok_half[0], home_to_away(tok_half[1]))
    ffn = jnp.stack([mul(act, downs[h]) for h in range(2)])
    out_half = (res + (ffn + sibling_to_home(ffn.astype(low)).astype(wide))).astype(low)
    output = jnp.where(home, out_half[0], home_to_away(out_half[1]))

    small = jnp.concatenate(
        [conv_grad]
        + [part for h in range(2) for part in (gain_one_grad[h : h + 1], gain_two_grad[h])]
    )
    small = tie(small, seen["i"][3])
    for bit in range((lax.axis_size("dp") - 1).bit_length()):
        small = small + flip(small, bit)
    small_more = swap(small, "col")
    conv_grad = small[:3] + small_more[:3]
    gains_grad = small[3:5] + small_more[5:]

    conv_m, conv_v, conv_u = lamb_moments(conv_weight, conv_grad, conv_first, conv_second, 0.0)
    gain_m, gain_v, gain_u = lamb_moments(norm_gains, gains_grad, gain_first, gain_second, 0.0)

    def in_flat(values):
        return jnp.transpose(values, (1, 0, 2)).reshape(3 * feat_cols, branch_cols)

    def in_back(values):
        return jnp.transpose(values.reshape(3, feat_cols, branch_cols), (1, 0, 2))

    def gu_back(values):
        return from_linear(values, feat_cols, 2)

    (down_m, down_v, down_u), down_norms = lamb_dense(
        (down_projection_weight, down_first, down_second),
        [(down_sums[k], 0, k * down_half, down_half) for k in range(2)],
        384,
    )
    gu_state = (gu_weight, to_linear(gu_first), to_linear(gu_second))
    pairs = 2 * hidden_cols // 128
    gu_rows = 32
    gu_new, gu_norms = None, 0.0
    pair_sums += [sums["c"], sums["e"]]
    for k in (2, 3, 0, 1):
        grad = pair_sums[k]
        blocks = grad.shape[0] // 2 // gu_rows
        gu_new, squares = lamb_call(
            lamb_pairs,
            gu_state,
            [(grad, gu_rows, 0), (grad, gu_rows, blocks)],
            gu_rows * pairs,
            k * blocks,
            blocks,
            gu_new,
            [pltpu.VMEM((gu_rows * pairs, 128), wide)],
        )
        gu_norms = gu_norms + squares
    gu_m, gu_v, gu_u = gu_new
    in_weight = in_flat(input_projection_weight)
    (in_m, in_v, in_u), in_norms = lamb_dense(
        (in_weight, in_flat(in_first), in_flat(in_second)),
        [
            (sums["I"], 0, 0, 2 * feat_cols),
            (sums["i"], 0, 2 * feat_cols, feat_cols),
        ],
        256,
    )
    (out_m, out_v, out_u), out_norms = lamb_dense(
        (output_projection_weight, out_first, out_second),
        [(sums["i"], feat_cols, 0, branch_cols)],
        256,
    )
    col_first = (col_pos == 0).astype(wide)
    row_first = (row_pos == 0).astype(wide)
    partial_sums = jnp.stack(
        [
            in_norms,
            square_pair(conv_weight, conv_u) * col_first,
            out_norms,
            square_pair(norm_gains[0], gain_u[0]) * row_first,
            square_pair(norm_gains[1], gain_u[1]) * row_first,
            gu_norms,
            down_norms,
        ]
    )
    trust_norms = jnp.sqrt(lax.psum(partial_sums, ("row", "col")))
    gains_new = jnp.stack(
        [
            apply_trust(norm_gains[0], gain_u[0], trust_norms[3]),
            apply_trust(norm_gains[1], gain_u[1], trust_norms[4]),
        ]
    )
    return (
        output,
        token_grad,
        in_back(apply_trust(in_weight, in_u, trust_norms[0])),
        in_back(in_m),
        in_back(in_v),
        apply_trust(conv_weight, conv_u, trust_norms[1]),
        conv_m,
        conv_v,
        apply_trust(output_projection_weight, out_u, trust_norms[2]),
        out_m,
        out_v,
        gains_new,
        gain_m,
        gain_v,
        gu_back(apply_trust(gu_weight, gu_u, trust_norms[5])),
        gu_back(gu_m),
        gu_back(gu_v),
        apply_trust(down_projection_weight, down_u, trust_norms[6]),
        down_m,
        down_v,
        trust_norms,
    )


def solution(mesh):
    in_specs = (
        P(("dp", "row"), "col"),
        P(("dp", "row"), "col"),
        P("col", None, "row"),
        P(None, "row"),
        P("row", "col"),
        P(None, "col"),
        P("col", None, "row"),
        P("row", "col"),
        P("col", None, "row"),
        P("col", None, "row"),
        P(None, "row"),
        P(None, "row"),
        P("row", "col"),
        P("row", "col"),
        P(None, "col"),
        P(None, "col"),
        P("col", None, "row"),
        P("col", None, "row"),
        P("row", "col"),
        P("row", "col"),
    )
    out_specs = (
        P(("dp", "row"), "col"),
        P(("dp", "row"), "col"),
        P("col", None, "row"),
        P("col", None, "row"),
        P("col", None, "row"),
        P(None, "row"),
        P(None, "row"),
        P(None, "row"),
        P("row", "col"),
        P("row", "col"),
        P("row", "col"),
        P(None, "col"),
        P(None, "col"),
        P(None, "col"),
        P("col", None, "row"),
        P("col", None, "row"),
        P("col", None, "row"),
        P("row", "col"),
        P("row", "col"),
        P("row", "col"),
        P(),
    )
    return jax.shard_map(shards, mesh=mesh, in_specs=in_specs, out_specs=out_specs, check_vma=False)
```

```python
import jax
import jax.numpy as jnp
from jax import lax
from jax.experimental import pallas as pl
from jax.experimental.layout import Layout, with_layout_constraint
from jax.experimental.pallas import tpu as pltpu
from jax.sharding import PartitionSpec as P

D = 1024
SEQ_LEAST = 4096
STEP = 5
VMEM_BYTES = 60 * 1024 * 1024


norm_eps = 1e-05
adam_eps = 1e-06
beta_one = 0.5
beta_two = 0.6
learn_rate = 0.5
decay_rate = 0.01
low = jnp.bfloat16
wide = jnp.float32


def from_behind(block, axis, distance):
    devices = range(lax.axis_size(axis))
    route = [(i - distance, i) for i in devices if i - distance in devices]
    return lax.ppermute(block, axis, route)


def swap(values, axis):
    return lax.ppermute(values, axis, [(0, 1), (1, 0)])


def to_home(values):
    return lax.ppermute(values, ("row", "col"), [(1, 0), (2, 3)])


def home_to_sibling(values):
    return lax.ppermute(values, ("row", "col"), [(0, 2), (3, 1)])


def home_to_away(values):
    return lax.ppermute(values, ("row", "col"), [(0, 1), (3, 2)])


def sibling_to_home(values):
    return lax.ppermute(values, ("row", "col"), [(2, 0), (1, 3)])


def contract(left, right, left_dim, right_dim):
    return lax.dot_general(
        left, right, (((left_dim,), (right_dim,)), ((), ())), preferred_element_type=wide
    )


def mul(left, right):
    return contract(left, right, 1, 0)


def mul_t(left, right):
    return contract(left, right, 1, 1)


def t_mul(left, right):
    return contract(left, right, 0, 0)


def lamb_moments(weight, grad, first, second, decay):
    first_new = beta_one * first + (1.0 - beta_one) * grad
    second_new = beta_two * second + (1.0 - beta_two) * grad * grad
    direction = (
        first_new
        / (1.0 - beta_one**STEP)
        / (jnp.sqrt(second_new / (1.0 - beta_two**STEP)) + adam_eps)
        + decay * weight
    )
    return (first_new, second_new, direction)


def square_pair(weight, direction):
    return jnp.stack([jnp.sum(weight * weight), jnp.sum(direction * direction)])


def lamb_rows(p, g, m, v, m_out, v_out, u_out):
    weight = p[...]
    grad = g[...].astype(wide)
    first_new, second_new, direction = lamb_moments(weight, grad, m[...], v[...], decay_rate)
    m_out[...] = first_new
    v_out[...] = second_new
    u_out[...] = direction
    return weight * weight, direction * direction


def lamb_loop(refs, sums, rows, step):
    lanes = sums.shape[2]

    @pl.when(pl.program_id(0) == 0)
    def _():
        sums[...] = jnp.zeros_like(sums)

    def body(at, total):
        here = pl.ds(pl.multiple_of(at * step, step), step)
        squares = lamb_rows(*[ref.at[here, :] for ref in refs])
        return tuple(
            t + jnp.sum(sq.reshape(step // 8, 8, lanes), axis=0) for t, sq in zip(total, squares)
        )

    zero = jnp.zeros((8, lanes), wide)
    total = lax.fori_loop(0, rows // step, body, (zero, zero))
    sums[0] += total[0]
    sums[1] += total[1]


def lamb_plain(p, g, m, v, m_out, v_out, u_out, sums):
    lamb_loop((p, g, m, v, m_out, v_out, u_out), sums, p.shape[0], 16)


def lamb_pairs(p, gate, up, m, v, m_out, v_out, u_out, sums, mixed):
    rows, cols = gate.shape
    tiles = cols // 128
    for tile in range(tiles):
        for side, ref in enumerate((gate, up)):
            mixed[pl.ds(2 * tile + side, rows, stride=2 * tiles), :] = ref[
                :, tile * 128 : (tile + 1) * 128
            ].astype(wide)
    lamb_loop((p, mixed, m, v, m_out, v_out, u_out), sums, p.shape[0], 64)


def lamb_call(kernel, state, grads, block, start, count, before, scratch):
    rows, cols = state[0].shape
    flat = pl.BlockSpec((block, cols), lambda i: (i + start, 0))
    whole = jax.ShapeDtypeStruct((rows, cols), wide)
    grad_specs = [
        pl.BlockSpec((size, grad.shape[1]), lambda i, at=at: (i + at, 0)) for grad, size, at in grads
    ]
    weight, first, second = state
    args = [weight, *[grad for grad, _, _ in grads], first, second]
    specs = [flat] + grad_specs + [flat, flat]
    aliases = {}
    run = kernel
    if before is not None:
        aliases = {len(args) + k: k for k in range(3)}

        def run(*refs):
            kernel(*refs[: len(args)], *refs[len(args) + 3 :])

    call = pl.pallas_call(
        run,
        grid=(count,),
        in_specs=specs + [pl.BlockSpec(memory_space=pl.ANY)] * len(aliases),
        out_specs=[flat, flat, flat, pl.BlockSpec((2, 8, cols), lambda i: (0, 0, 0))],
        out_shape=[whole, whole, whole, jax.ShapeDtypeStruct((2, 8, cols), wide)],
        scratch_shapes=scratch,
        input_output_aliases=aliases,
        compiler_params=pltpu.CompilerParams(vmem_limit_bytes=VMEM_BYTES),
        cost_estimate=pl.CostEstimate(
            flops=20 * count * block * cols,
            bytes_accessed=26 * count * block * cols,
            transcendentals=2 * count * block * cols,
        ),
    )
    m_new, v_new, direction, sums = call(*args, *(before or []))
    return [m_new, v_new, direction], jnp.sum(sums, axis=(1, 2))


def lamb_dense(state, parts, block):
    before, norms = None, 0.0
    for grad, grad_at, at, rows in parts:
        before, sums = lamb_call(
            lamb_plain,
            state,
            [(grad, block, grad_at // block)],
            block,
            at // block,
            rows // block,
            before,
            [],
        )
        norms = norms + sums
    return before, norms


def to_linear(values):
    rows, sides, cols = values.shape
    split = with_layout_constraint(
        values.reshape(rows, sides, cols // 128, 128), Layout(major_to_minor=(0, 2, 1, 3))
    )
    return split.transpose(0, 2, 1, 3).reshape(rows * sides * cols // 128, 128)


def from_linear(values, rows, sides):
    cols = values.size // (rows * sides)
    split = values.reshape(rows, cols // 128, sides, 128).transpose(0, 2, 1, 3)
    split = with_layout_constraint(split, Layout(major_to_minor=(0, 2, 1, 3)))
    return split.reshape(rows, sides, cols)


def apply_trust(weight, direction, norms):
    return weight - learn_rate * (norms[0] / (norms[1] + adam_eps)) * direction


def flip(values, bit):
    size = lax.axis_size("dp")
    return lax.ppermute(values, "dp", [(i, i ^ (1 << bit)) for i in range(size)])


def dp_bit(bit):
    return (lax.axis_index("dp") >> bit) & 1


def rows_of(values, start, rows):
    return lax.dynamic_slice_in_dim(values, start, rows, 0)


def total_of(pieces):
    total = pieces[0].astype(wide)
    for piece in pieces[1:]:
        total = total + piece.astype(wide)
    return total


def tie(values, *deps):
    return lax.optimization_barrier((values, *deps))[0]


def low_total(pieces):
    return total_of(pieces).astype(low)


def keep_or_join(bit, part, other):
    return jnp.where(
        dp_bit(bit) == 0,
        jnp.concatenate([part, other]),
        jnp.concatenate([other, part]),
    )


def share_of(weight, order):
    rows = weight.shape[0] // (1 << len(order))
    index = 0
    for bit in order:
        index = 2 * index + dp_bit(bit)
    return rows_of(weight, index * rows, rows)


def half_of(piece, place):
    rows = piece.shape[-2] // 2
    return lax.dynamic_slice_in_dim(piece, place * rows, rows, piece.ndim - 2)


def chunk_sum(chunk, order):
    bits = {"y": 0, "l": 1}
    steps = [name if name == "x" else bits[name] for name in order]
    pieces = [chunk]
    for step in steps:
        if step == "x":
            got = yield step, low_total([piece[1] for piece in pieces])
            pieces = [piece[0] for piece in pieces] + [got]
        else:
            here = dp_bit(step)
            got = yield step, low_total([half_of(piece, 1 - here) for piece in pieces])
            pieces = [half_of(piece, here) for piece in pieces] + [got]
    part = low_total(pieces)
    for step in range((lax.axis_size("dp") - 1).bit_length()):
        if step not in steps:
            got = yield step, part
            part = low_total([part, got])
    for step in reversed(steps):
        if step != "x":
            got = yield step, part
            part = keep_or_join(step, part, got)
    return part


def move(step, send):
    return swap(send, "col") if step == "x" else flip(send, step)


def first_step(chunk):
    step, send = next(chunk)
    return move(step, send)


def run_chunks(chunks, arrivals, sequence, after):
    done = {}
    seen = {name: [] for name in chunks}
    pending = list(sequence)
    while len(done) < len(chunks):
        names = [pending.pop(0)] if pending else [n for n in chunks if n not in done]
        for name in names:
            if name in done:
                continue
            got = tie(arrivals[name], after)
            seen[name].append(got)
            try:
                step, send = chunks[name].send(got)
            except StopIteration as end:
                done[name] = end.value
                continue
            arrivals[name] = move(step, send)
            after = send
    return done, seen


def deinterleave(pairs, gate, up):
    rows, cols = gate.shape
    tiles = cols // 128
    for tile in range(tiles):
        for side, out in enumerate((gate, up)):
            out[:, tile * 128 : (tile + 1) * 128] = pairs[
                pl.ds(2 * tile + side, rows, stride=2 * tiles), :
            ].astype(low)


def split_pairs(linear, rows, cols):
    block = 64
    half = jax.ShapeDtypeStruct((rows, cols), low)
    out_spec = pl.BlockSpec((block, cols), lambda i: (i, 0))
    return pl.pallas_call(
        deinterleave,
        grid=(rows // block,),
        in_specs=[pl.BlockSpec((block * 2 * cols // 128, 128), lambda i: (i, 0))],
        out_specs=[out_spec, out_spec],
        out_shape=[half, half],
        compiler_params=pltpu.CompilerParams(vmem_limit_bytes=VMEM_BYTES),
        cost_estimate=pl.CostEstimate(
            flops=rows * cols, bytes_accessed=12 * rows * cols, transcendentals=0
        ),
    )(linear)


def dot_of(left, right, left_dim, right_dim):
    return lax.dot_general(
        left, right, (((left_dim,), (right_dim,)), ((), ())), preferred_element_type=wide
    )


def local_call(kernel, grid, in_specs, out_specs, out_shape, scratch, args, prefetch=0):
    return pl.pallas_call(
        kernel,
        grid_spec=pltpu.PrefetchScalarGridSpec(
            num_scalar_prefetch=prefetch,
            grid=grid,
            in_specs=in_specs,
            out_specs=out_specs,
            scratch_shapes=scratch,
        ),
        out_shape=out_shape,
        compiler_params=pltpu.CompilerParams(vmem_limit_bytes=VMEM_BYTES),
        cost_estimate=pl.CostEstimate(flops=1000000, bytes_accessed=100000, transcendentals=0),
    )(*args)


def whole_spec(shape):
    return pl.BlockSpec(shape, lambda *_: (0,) * len(shape))


def shape_of(dims, kind):
    return jax.ShapeDtypeStruct(dims, kind)


def row_scale(halves):
    total = sum(jnp.sum(half * half, axis=1, keepdims=True) for half in halves)
    return lax.rsqrt(total / D + norm_eps)


def branch_kernel(tok, gains, taps, own, other, n1, gate_b, gate_c, gate_x, conv, hidden, part, ext):
    long, width = n1.shape[1:]
    rows = conv.shape[0]
    step = long // 3

    def gates(at, carry):
        here = pl.ds(pl.multiple_of(at * step, step), step)
        halves = [tok[h, here, :].astype(wide) for h in range(2)]
        scale = row_scale(halves)
        for h in range(2):
            n1[h, here, :] = (halves[h] * scale * gains[h]).astype(low)
        for g, out in enumerate((gate_b, gate_c, gate_x)):
            w = slice(g * width, (g + 1) * width)
            out[here, :] = dot_of(n1[0, here, :], own[w, :], 1, 0) + dot_of(
                n1[1, here, :], other[w, :], 1, 0
            )
        return carry

    lax.fori_loop(0, 3, gates, 0)
    ext[8 : 8 + rows, :] = gate_b[:rows, :] * gate_x[:rows, :]
    ext[6:8, :] = gate_b[rows : rows + 2, :] * gate_x[rows : rows + 2, :]
    w_out = slice(3 * width, 4 * width)
    quarter = rows // 4
    for at in range(4):
        start = at * quarter
        taken = slice(start, start + quarter)
        value = sum(taps[k] * ext[start + 6 + k : start + 6 + k + quarter, :] for k in range(3))
        conv[taken, :] = value
        low_hidden = (gate_c[taken, :] * value).astype(low)
        hidden[taken, :] = low_hidden
        for h, weight in enumerate((own, other)):
            part[h, taken, :] = dot_of(low_hidden, weight[w_out, :], 1, 0).astype(low)


def branch_forward(tok, rows, tails, gains, taps, own, other):
    width = tok.shape[2]
    gate = shape_of((rows + tails, width), wide)
    outs = [
        shape_of((2, rows + tails, width), low),
        gate,
        gate,
        gate,
        shape_of((rows, width), wide),
        shape_of((rows, width), low),
        shape_of((2, rows, width), low),
    ]
    args = (tok, gains, taps, own, other)
    return local_call(
        branch_kernel,
        (1,),
        [whole_spec(a.shape) for a in args],
        [whole_spec(o.shape) for o in outs],
        outs,
        [pltpu.VMEM((rows + 8, width), wide)],
        args,
    )


def piece_at(bits, which, piece, width):
    place = bits[which] if piece == 0 else 1 - bits[which]
    return pl.ds(pl.multiple_of(place * width, width), width)


def ffn_kernel(bits, tok, mine, theirs, gains, g0, g1, g2, u0, u1, u2, n2, res, gate, up, act):
    width = g1.shape[0]

    @pl.when(pl.program_id(0) == 0)
    def _():
        for h in range(2):
            res[h] = tok[h, : res.shape[1], :].astype(wide) + (mine[h].astype(wide) + theirs[h].astype(wide))
        scale = row_scale([res[0], res[1]])
        for h in range(2):
            n2[h] = (res[h] * scale * gains[h]).astype(low)

    for which, (out, w0, w1, w2) in enumerate(((gate, g0, g1, g2), (up, u0, u1, u2))):
        total = dot_of(n2[0], w0[...], 1, 0)
        for piece, w in enumerate((w1, w2)):
            total += dot_of(n2[1, :, piece_at(bits, which, piece, width)], w[...], 1, 0)
        out[...] = total
    value = gate[...]
    act[...] = (value * jax.nn.sigmoid(value) * up[...]).astype(low)


def ffn_forward(bits, tok, mine, theirs, gains, weights):
    _, rows, width = mine.shape
    cols = weights[0].shape[1]
    tile = cols // 3
    full = whole_spec(mine.shape)
    wide_tile = pl.BlockSpec((rows, tile), lambda i, *_: (0, i))
    weight_specs = [pl.BlockSpec((w.shape[0], tile), lambda i, *_: (0, i)) for w in weights]
    return local_call(
        ffn_kernel,
        (3,),
        [whole_spec(tok.shape), full, full, whole_spec(gains.shape)] + weight_specs,
        [full, full, wide_tile, wide_tile, wide_tile],
        [
            shape_of(mine.shape, low),
            shape_of(mine.shape, wide),
            shape_of((rows, cols), wide),
            shape_of((rows, cols), wide),
            shape_of((rows, cols), low),
        ],
        [],
        (bits, tok, mine, theirs, gains, *weights),
        prefetch=1,
    )


def ffn_back_kernel(
    bits, cot, d_own, d_other, gate, up, g0, g1, g2, u0, u1, u2, g_gate, g_up, part, total
):
    width = g1.shape[0]

    @pl.when(pl.program_id(0) == 0)
    def _():
        total[...] = jnp.zeros_like(total)

    start = cot.shape[1] - gate.shape[0]
    g_act = dot_of(cot[0, start:, :], d_own[...], 1, 1) + dot_of(cot[1, start:, :], d_other[...], 1, 1)
    value = gate[...]
    sigma = jax.nn.sigmoid(value)
    g_gate[...] = (g_act * up[...] * sigma * (1.0 + value * (1.0 - sigma))).astype(low)
    g_up[...] = (g_act * (value * sigma)).astype(low)
    total[0] += dot_of(g_gate[...], g0[...], 1, 1) + dot_of(g_up[...], u0[...], 1, 1)
    for which, (grad, w1, w2) in enumerate(((g_gate, g1, g2), (g_up, u1, u2))):
        for piece, w in enumerate((w1, w2)):
            total[1, :, piece_at(bits, which, piece, width)] += dot_of(grad[...], w[...], 1, 1)

    @pl.when(pl.program_id(0) == pl.num_programs(0) - 1)
    def _():
        part[...] = total[...].astype(low)


def ffn_backward(bits, cot, downs, gate, up, weights):
    rows, cols = gate.shape
    tile = cols // 3
    part = (2, rows, cot.shape[2])
    wide_tile = pl.BlockSpec((rows, tile), lambda i, *_: (0, i))
    weight_specs = [pl.BlockSpec((w.shape[0], tile), lambda i, *_: (0, i)) for w in weights]
    down_spec = pl.BlockSpec((tile, downs[0].shape[1]), lambda i, *_: (i, 0))
    return local_call(
        ffn_back_kernel,
        (3,),
        [whole_spec(cot.shape), down_spec, down_spec, wide_tile, wide_tile] + weight_specs,
        [wide_tile, wide_tile, whole_spec(part)],
        [shape_of((rows, cols), low), shape_of((rows, cols), low), shape_of(part, low)],
        [pltpu.VMEM(part, wide)],
        (bits, cot, *downs, gate, up, *weights),
        prefetch=1,
    )


def pair_grad_kernel(n2, g_gate, g_up, out):
    rows = n2.shape[2]
    for side, grad in enumerate((g_gate, g_up)):
        out[0, 0, side * rows : (side + 1) * rows, :] = dot_of(n2[0], grad[...], 0, 0).astype(low)


def pair_grads(n2, g_gate, g_up, chunks):
    _, rows, width = n2.shape
    cols = g_gate.shape[1]
    part = width // chunks
    return local_call(
        pair_grad_kernel,
        (chunks, 2),
        [
            pl.BlockSpec((1, rows, part), lambda q, h: (h, 0, q)),
            whole_spec(g_gate.shape),
            whole_spec(g_up.shape),
        ],
        pl.BlockSpec((1, 1, 2 * part, cols), lambda q, h: (q, h, 0, 0)),
        shape_of((chunks, 2, 2 * part, cols), low),
        [],
        (n2, g_gate, g_up),
    )


def down_grad_kernel(act, cot, out):
    start = cot.shape[1] - act.shape[0]
    out[0, 0] = dot_of(act[...], cot[0, start:, :], 0, 0).astype(low)


def down_grads(act, cot, chunks):
    rows, cols = act.shape
    _, long, width = cot.shape
    part = cols // chunks
    return local_call(
        down_grad_kernel,
        (chunks, 2),
        [
            pl.BlockSpec((rows, part), lambda q, h: (0, q)),
            pl.BlockSpec((1, long, width), lambda q, h: (h, 0, 0)),
        ],
        pl.BlockSpec((1, 1, part, width), lambda q, h: (q, h, 0, 0)),
        shape_of((chunks, 2, part, width), low),
        [],
        (act, cot),
    )


def branch_back_kernel(
    mine, theirs, res, cot, gains, taps, own, other, gate_b, gate_c, gate_x, conv,
    g_res, g_low, g_proj, gain_grad, tap_grad, ext, ext_grad,
):
    _, rows, width = res.shape
    scale = row_scale([res[0], res[1]])
    grads = [mine[h].astype(wide) + theirs[h].astype(wide) for h in range(2)]
    inner = sum(
        jnp.sum(grads[h] * gains[h] * res[h], axis=1, keepdims=True) for h in range(2)
    )
    factor = scale * scale * scale * inner / D
    for h in range(2):
        gain_grad[h] = jnp.sum(grads[h] * res[h] * scale, axis=0, keepdims=True)
        value = cot[h, cot.shape[1] - rows :, :].astype(wide) + (scale * (grads[h] * gains[h]) - res[h] * factor)
        g_res[h] = value
        g_low[h] = value.astype(low)
    g_hidden = dot_of(g_low[0], own[...], 1, 1) + dot_of(g_low[1], other[...], 1, 1)
    g_proj[1, :rows, :] = (g_hidden * conv[...]).astype(low)
    g_conv = g_hidden * gate_c[:rows, :]
    ext_grad[:rows, :] = g_conv
    ext_grad[rows:, :] = jnp.zeros((8, width), wide)
    ext[8 : 8 + rows, :] = gate_b[:rows, :] * gate_x[:rows, :]
    ext[6:8, :] = gate_b[rows : rows + 2, :] * gate_x[rows : rows + 2, :]
    for k in range(3):
        tap_grad[k : k + 1, :] = jnp.sum(
            g_conv * ext[6 + k : 6 + k + rows, :], axis=0, keepdims=True
        )
    g_mixed = sum(taps[2 - k] * ext_grad[k : k + rows, :] for k in range(3))
    g_proj[0, :rows, :] = (g_mixed * gate_x[:rows, :]).astype(low)
    g_proj[2, :rows, :] = (g_mixed * gate_b[:rows, :]).astype(low)
    tails = g_proj.shape[1] - rows
    row = lax.broadcasted_iota(jnp.int32, (tails, width), 0)
    first, second = ext_grad[0:1, :], ext_grad[1:2, :]
    g_before = jnp.where(
        row == 0,
        taps[0] * first,
        jnp.where(row == 1, taps[1] * first + taps[0] * second, 0.0),
    )
    g_proj[0, rows:, :] = (g_before * gate_x[rows:, :]).astype(low)
    g_proj[1, rows:, :] = jnp.zeros((tails, width), low)
    g_proj[2, rows:, :] = (g_before * gate_b[rows:, :]).astype(low)


def branch_backward(mine, theirs, res, cot, gains, taps, own, other, gates, conv):
    _, rows, width = res.shape
    long = gates[0].shape[0]
    out_weight = pl.BlockSpec((width, width), lambda i, *_: (3, 0))
    outs = [
        shape_of(res.shape, wide),
        shape_of(res.shape, low),
        shape_of((3, long, width), low),
        shape_of((2, 1, width), wide),
        shape_of((3, width), wide),
    ]
    full = whole_spec(res.shape)
    return local_call(
        branch_back_kernel,
        (1,),
        [full, full, full, whole_spec(cot.shape), whole_spec(gains.shape), whole_spec(taps.shape)]
        + [out_weight, out_weight]
        + [whole_spec(g.shape) for g in gates]
        + [whole_spec(conv.shape)],
        [whole_spec(o.shape) for o in outs],
        outs,
        [pltpu.VMEM((rows + 8, width), wide), pltpu.VMEM((rows + 8, width), wide)],
        (mine, theirs, res, cot, gains, taps, own, other, *gates, conv),
    )


def branch_grad_kernel(n1, g_proj, hidden, g_low, out):
    kind = pl.program_id(1)

    @pl.when(kind < 3)
    def _():
        out[0, 0, 0] = dot_of(n1[0], g_proj[0], 0, 0).astype(low)

    @pl.when(kind == 3)
    def _():
        out[0, 0, 0] = dot_of(hidden[...], g_low[0], 0, 0).astype(low)


def branch_grads(n1, g_proj, hidden, g_low):
    _, long, width = n1.shape
    rows = hidden.shape[0]
    return local_call(
        branch_grad_kernel,
        (2, 4),
        [
            pl.BlockSpec((1, long, width), lambda h, k: (h, 0, 0)),
            pl.BlockSpec((1, long, width), lambda h, k: (jnp.minimum(k, 2), 0, 0)),
            whole_spec(hidden.shape),
            pl.BlockSpec((1, rows, width), lambda h, k: (h, 0, 0)),
        ],
        pl.BlockSpec((1, 1, 1, width, width), lambda h, k: (k // 2, h, k % 2, 0, 0)),
        shape_of((2, 2, 2, width, width), low),
        [],
        (n1, g_proj, hidden, g_low),
    )


def shards(
    tokens,
    cotangent,
    input_projection_weight,
    conv_weight,
    output_projection_weight,
    norm_gains,
    gate_up_weight,
    down_projection_weight,
    in_first,
    in_second,
    conv_first,
    conv_second,
    out_first,
    out_second,
    gain_first,
    gain_second,
    gu_first,
    gu_second,
    down_first,
    down_second,
):
    feat_cols = tokens.shape[1]
    branch_cols = conv_weight.shape[1]
    hidden_cols = down_projection_weight.shape[0]
    block_rows = tokens.shape[0]
    seq_len = max(SEQ_LEAST, block_rows * lax.axis_size("dp") * lax.axis_size("col"))
    data_pos = lax.axis_index("dp")
    row_pos = lax.axis_index("row")
    col_pos = lax.axis_index("col")
    home = row_pos == col_pos
    tail_rows = 16

    row_start = (data_pos * lax.axis_size("row") + row_pos) * block_rows
    tail = from_behind(tokens[-2:], ("dp", "row"), 1)
    tail = jnp.where(row_start % seq_len != 0, tail, jnp.zeros_like(tail))
    spare = jnp.zeros((tail_rows - 8, feat_cols), low)
    gain_parts = []
    left = norm_gains
    for _ in range(3):
        gain_parts.append(lax.reduce_precision(left, 8, 7))
        left = left - gain_parts[-1]
    gain_parts = jnp.concatenate(gain_parts).astype(low)
    block = jnp.concatenate([tokens, tail, gain_parts, spare, cotangent])
    away = to_home(block)
    in_low = jnp.transpose(input_projection_weight, (1, 0, 2)).astype(low).reshape(-1, branch_cols)
    io_low = jnp.concatenate([in_low, output_projection_weight.astype(low)])
    io_got = swap(share_of(io_low, (1, 0)), "col")
    gu_weight = to_linear(gate_up_weight)
    gate_low, up_low = split_pairs(gu_weight, feat_cols, hidden_cols)
    down_low = down_projection_weight.astype(low)
    both = jnp.stack([block, away])
    both = jnp.where(home, both, home_to_sibling(both))
    gains = both[:, block_rows + 2 : block_rows + 8].astype(wide)
    gains = gains[:, 0:2] + gains[:, 2:4] + gains[:, 4:6]
    gains = [gains[:, k : k + 1] for k in range(2)]
    gate_got = swap(tie(share_of(gate_low, (1, 0)), io_got), "col")
    up_got = swap(tie(share_of(up_low, (0, 1)), away), "col")
    down_got = swap(tie(down_low, gate_got), "col")
    io_pair = keep_or_join(0, io_got, flip(io_got, 0))
    io_other = keep_or_join(1, io_pair, flip(io_pair, 1))
    gate_pair = keep_or_join(0, gate_got, flip(tie(gate_got, io_pair), 0))
    up_pair = keep_or_join(1, up_got, flip(tie(up_got, io_pair), 1))
    gate_more = flip(gate_pair, 1)
    up_more = flip(up_pair, 0)
    weights = [gate_low, gate_pair, gate_more, up_low, up_pair, up_more]
    bits = jnp.stack([dp_bit(1), dp_bit(0)]).astype(jnp.int32)
    downs = [down_low, down_got]

    n1, gate_b, gate_c, gate_x, conv, hidden, branch = branch_forward(
        both, block_rows, tail_rows, gains[0], conv_weight, io_low, io_other
    )
    n2, res, gate, upper, act = ffn_forward(
        bits, both, branch, swap(branch, "row"), gains[1], weights
    )

    chunks = {}
    arrivals = {}

    def add_chunk(name, chunk, order):
        chunks[name] = chunk_sum(chunk, order)
        arrivals[name] = first_step(chunks[name])

    down_half = hidden_cols // 2
    down_part = down_grads(act, both, 2)
    for k, order in enumerate(('lxy', 'yxl')):
        add_chunk("Dd"[k], down_part[k], order)
    g_gate, g_up, part_two = ffn_backward(bits, both, downs, gate, upper, weights)
    pair_part = pair_grads(n2, g_gate, g_up, 4)
    for k, order in enumerate(('xyl', 'lyx', 'ylx', 'lyx')):
        add_chunk("abce"[k], pair_part[k], order)
    g_res, g_branch, g_proj, gain_two_grad, conv_grad = branch_backward(
        part_two,
        swap(part_two, "row"),
        res,
        both,
        gains[1],
        conv_weight,
        io_low,
        io_other,
        (gate_b, gate_c, gate_x),
        conv,
    )
    io_part = branch_grads(n1, g_proj, hidden, g_branch).reshape(2, 2, 2 * feat_cols, branch_cols)
    for k, order in enumerate(('xyl', 'xyl')):
        add_chunk("Ii"[k], io_part[k], order)
    sequence = "DdabcDadebDcIaedDIiaDbIcdiaeDbIacbdieIcdebiIecii"
    sums, seen = run_chunks(chunks, arrivals, sequence, io_part)

    late = seen["i"][0]
    act = tie(act, late)
    g_proj = tie(g_proj, late)
    io_half = [half.reshape(4, feat_cols, branch_cols) for half in (io_low, io_other)]
    g_part = jnp.stack(
        [sum(mul_t(g_proj[g], io_half[h][g]) for g in range(3)).astype(low) for h in range(2)]
    )
    g_long = g_part.astype(wide) + swap(g_part, "row").astype(wide)
    back = from_behind(g_long[::-1, block_rows : block_rows + 2], ("dp", "col"), -1)
    g_n1 = g_long[:, :block_rows].at[:, -2:].add(back)
    tok = both[:, :block_rows].astype(wide)
    scale = lax.rsqrt(jnp.sum(tok * tok, axis=(0, 2)) / D + norm_eps)[None, :, None]
    weighted = g_n1 * gains[0]
    inner = jnp.sum(weighted * tok, axis=(0, 2))[None, :, None]
    gain_one_grad = jnp.sum(g_n1 * tok * scale, axis=1)
    tok_half = (g_res + (scale * weighted - tok * (scale * scale * scale * inner / D))).astype(low)
    token_grad = jnp.where(home, tok_half[0], home_to_away(tok_half[1]))
    ffn = jnp.stack([mul(act, downs[h]) for h in range(2)])
    out_half = (res + (ffn + sibling_to_home(ffn.astype(low)).astype(wide))).astype(low)
    output = jnp.where(home, out_half[0], home_to_away(out_half[1]))

    small = jnp.concatenate(
        [conv_grad]
        + [part for h in range(2) for part in (gain_one_grad[h : h + 1], gain_two_grad[h])]
    )
    small = tie(small, seen["i"][3])
    for bit in range((lax.axis_size("dp") - 1).bit_length()):
        small = small + flip(small, bit)
    small_more = swap(small, "col")
    conv_grad = small[:3] + small_more[:3]
    gains_grad = small[3:5] + small_more[5:]

    conv_m, conv_v, conv_u = lamb_moments(conv_weight, conv_grad, conv_first, conv_second, 0.0)
    gain_m, gain_v, gain_u = lamb_moments(norm_gains, gains_grad, gain_first, gain_second, 0.0)

    def in_flat(values):
        return jnp.transpose(values, (1, 0, 2)).reshape(3 * feat_cols, branch_cols)

    def in_back(values):
        return jnp.transpose(values.reshape(3, feat_cols, branch_cols), (1, 0, 2))

    def gu_back(values):
        return from_linear(values, feat_cols, 2)

    (down_m, down_v, down_u), down_norms = lamb_dense(
        (down_projection_weight, down_first, down_second),
        [(sums["Dd"[k]], 0, k * down_half, down_half) for k in (0, 1)],
        384,
    )
    gu_state = (gu_weight, to_linear(gu_first), to_linear(gu_second))
    pairs = 2 * hidden_cols // 128
    gu_rows = 32
    gu_new, gu_norms = None, 0.0
    for k in (0, 1, 3, 2):
        grad = sums["abce"[k]]
        blocks = grad.shape[0] // 2 // gu_rows
        gu_new, squares = lamb_call(
            lamb_pairs,
            gu_state,
            [(grad, gu_rows, 0), (grad, gu_rows, blocks)],
            gu_rows * pairs,
            k * blocks,
            blocks,
            gu_new,
            [pltpu.VMEM((gu_rows * pairs, 128), wide)],
        )
        gu_norms = gu_norms + squares
    gu_m, gu_v, gu_u = gu_new
    in_weight = in_flat(input_projection_weight)
    (in_m, in_v, in_u), in_norms = lamb_dense(
        (in_weight, in_flat(in_first), in_flat(in_second)),
        [
            (sums["I"], 0, 0, 2 * feat_cols),
            (sums["i"], 0, 2 * feat_cols, feat_cols),
        ],
        256,
    )
    (out_m, out_v, out_u), out_norms = lamb_dense(
        (output_projection_weight, out_first, out_second),
        [(sums["i"], feat_cols, 0, branch_cols)],
        256,
    )
    col_first = (col_pos == 0).astype(wide)
    row_first = (row_pos == 0).astype(wide)
    partial_sums = jnp.stack(
        [
            in_norms,
            square_pair(conv_weight, conv_u) * col_first,
            out_norms,
            square_pair(norm_gains[0], gain_u[0]) * row_first,
            square_pair(norm_gains[1], gain_u[1]) * row_first,
            gu_norms,
            down_norms,
        ]
    )
    trust_norms = jnp.sqrt(lax.psum(partial_sums, ("row", "col")))
    gains_new = jnp.stack(
        [
            apply_trust(norm_gains[0], gain_u[0], trust_norms[3]),
            apply_trust(norm_gains[1], gain_u[1], trust_norms[4]),
        ]
    )
    return (
        output,
        token_grad,
        in_back(apply_trust(in_weight, in_u, trust_norms[0])),
        in_back(in_m),
        in_back(in_v),
        apply_trust(conv_weight, conv_u, trust_norms[1]),
        conv_m,
        conv_v,
        apply_trust(output_projection_weight, out_u, trust_norms[2]),
        out_m,
        out_v,
        gains_new,
        gain_m,
        gain_v,
        gu_back(apply_trust(gu_weight, gu_u, trust_norms[5])),
        gu_back(gu_m),
        gu_back(gu_v),
        apply_trust(down_projection_weight, down_u, trust_norms[6]),
        down_m,
        down_v,
        trust_norms,
    )


def solution(mesh):
    in_specs = (
        P(("dp", "row"), "col"),
        P(("dp", "row"), "col"),
        P("col", None, "row"),
        P(None, "row"),
        P("row", "col"),
        P(None, "col"),
        P("col", None, "row"),
        P("row", "col"),
        P("col", None, "row"),
        P("col", None, "row"),
        P(None, "row"),
        P(None, "row"),
        P("row", "col"),
        P("row", "col"),
        P(None, "col"),
        P(None, "col"),
        P("col", None, "row"),
        P("col", None, "row"),
        P("row", "col"),
        P("row", "col"),
    )
    out_specs = (
        P(("dp", "row"), "col"),
        P(("dp", "row"), "col"),
        P("col", None, "row"),
        P("col", None, "row"),
        P("col", None, "row"),
        P(None, "row"),
        P(None, "row"),
        P(None, "row"),
        P("row", "col"),
        P("row", "col"),
        P("row", "col"),
        P(None, "col"),
        P(None, "col"),
        P(None, "col"),
        P("col", None, "row"),
        P("col", None, "row"),
        P("col", None, "row"),
        P("row", "col"),
        P("row", "col"),
        P("row", "col"),
        P(),
    )
    return jax.shard_map(shards, mesh=mesh, in_specs=in_specs, out_specs=out_specs, check_vma=False)
```

```python
import jax
import jax.numpy as jnp
from jax import lax
from jax.experimental import pallas as pl
from jax.experimental.layout import Layout, with_layout_constraint
from jax.experimental.pallas import tpu as pltpu
from jax.sharding import PartitionSpec as P

D = 1024
SEQ_LEAST = 4096
STEP = 5
MIB = 1024 * 1024


norm_eps = 1e-05
adam_eps = 1e-06
beta_one = 0.5
beta_two = 0.6
learn_rate = 0.5
decay_rate = 0.01
low = jnp.bfloat16
wide = jnp.float32


def from_behind(block, axis, distance):
    devices = range(lax.axis_size(axis))
    route = [(i - distance, i) for i in devices if i - distance in devices]
    return lax.ppermute(block, axis, route)


def swap(values, axis):
    return lax.ppermute(values, axis, [(0, 1), (1, 0)])


def swap_halves(halves):
    return [swap(half, "row") for half in halves]


def to_home(values):
    return lax.ppermute(values, ("row", "col"), [(1, 0), (2, 3)])


def home_to_sibling(values):
    return lax.ppermute(values, ("row", "col"), [(0, 2), (3, 1)])


def home_to_away(values):
    return lax.ppermute(values, ("row", "col"), [(0, 1), (3, 2)])


def sibling_to_home(values):
    return lax.ppermute(values, ("row", "col"), [(2, 0), (1, 3)])


def contract(left, right, left_dim, right_dim):
    return lax.dot_general(
        left, right, (((left_dim,), (right_dim,)), ((), ())), preferred_element_type=wide
    )


def mul(left, right):
    return contract(left, right, 1, 0)


def mul_t(left, right):
    return contract(left, right, 1, 1)


def t_mul(left, right):
    return contract(left, right, 0, 0)


def lamb_moments(weight, grad, first, second, decay):
    first_new = beta_one * first + (1.0 - beta_one) * grad
    second_new = beta_two * second + (1.0 - beta_two) * grad * grad
    direction = (
        first_new
        / (1.0 - beta_one**STEP)
        / (jnp.sqrt(second_new / (1.0 - beta_two**STEP)) + adam_eps)
        + decay * weight
    )
    return (first_new, second_new, direction)


def square_pair(weight, direction):
    return jnp.stack([jnp.sum(weight * weight), jnp.sum(direction * direction)])


def lamb_rows(p, g, m, v, m_out, v_out, u_out):
    weight = p[...]
    grad = g[...].astype(wide)
    first_new, second_new, direction = lamb_moments(weight, grad, m[...], v[...], decay_rate)
    m_out[...] = first_new
    v_out[...] = second_new
    u_out[...] = direction
    return weight * weight, direction * direction


def lamb_loop(refs, sums, rows, step):
    lanes = sums.shape[2]

    @pl.when(pl.program_id(0) == 0)
    def _():
        sums[...] = jnp.zeros_like(sums)

    def body(at, total):
        here = pl.ds(pl.multiple_of(at * step, step), step)
        squares = lamb_rows(*[ref.at[here, :] for ref in refs])
        return tuple(
            t + jnp.sum(sq.reshape(step // 8, 8, lanes), axis=0) for t, sq in zip(total, squares)
        )

    zero = jnp.zeros((8, lanes), wide)
    total = lax.fori_loop(0, rows // step, body, (zero, zero))
    sums[0] += total[0]
    sums[1] += total[1]


def lamb_plain(p, g, m, v, m_out, v_out, u_out, sums):
    lamb_loop((p, g, m, v, m_out, v_out, u_out), sums, p.shape[0], 16)


def lamb_pairs(p, gate, up, m, v, m_out, v_out, u_out, sums, mixed):
    rows, cols = gate.shape
    tiles = cols // 128
    for tile in range(tiles):
        for side, ref in enumerate((gate, up)):
            mixed[pl.ds(2 * tile + side, rows, stride=2 * tiles), :] = ref[
                :, tile * 128 : (tile + 1) * 128
            ].astype(wide)
    lamb_loop((p, mixed, m, v, m_out, v_out, u_out), sums, p.shape[0], 64)


def lamb_call(kernel, state, grads, block, start, count, before, scratch):
    rows, cols = state[0].shape
    flat = pl.BlockSpec((block, cols), lambda i: (i + start, 0))
    whole = jax.ShapeDtypeStruct((rows, cols), wide)
    grad_specs = [
        pl.BlockSpec((size, grad.shape[1]), lambda i, at=at: (i + at, 0)) for grad, size, at in grads
    ]
    weight, first, second = state
    args = [weight, *[grad for grad, _, _ in grads], first, second]
    specs = [flat] + grad_specs + [flat, flat]
    aliases = {}
    run = kernel
    if before is not None:
        aliases = {len(args) + k: k for k in range(3)}

        def run(*refs):
            kernel(*refs[: len(args)], *refs[len(args) + 3 :])

    call = pl.pallas_call(
        run,
        grid=(count,),
        in_specs=specs + [pl.BlockSpec(memory_space=pl.ANY)] * len(aliases),
        out_specs=[flat, flat, flat, pl.BlockSpec((2, 8, cols), lambda i: (0, 0, 0))],
        out_shape=[whole, whole, whole, jax.ShapeDtypeStruct((2, 8, cols), wide)],
        scratch_shapes=scratch,
        input_output_aliases=aliases,
        compiler_params=pltpu.CompilerParams(vmem_limit_bytes=60 * MIB),
        cost_estimate=pl.CostEstimate(
            flops=20 * count * block * cols,
            bytes_accessed=26 * count * block * cols,
            transcendentals=2 * count * block * cols,
        ),
    )
    m_new, v_new, direction, sums = call(*args, *(before or []))
    return [m_new, v_new, direction], jnp.sum(sums, axis=(1, 2))


def lamb_dense(state, parts, block):
    before, norms = None, 0.0
    for grad, grad_at, at, rows in parts:
        before, sums = lamb_call(
            lamb_plain,
            state,
            [(grad, block, grad_at // block)],
            block,
            at // block,
            rows // block,
            before,
            [],
        )
        norms = norms + sums
    return before, norms


def to_linear(values):
    rows, sides, cols = values.shape
    split = with_layout_constraint(
        values.reshape(rows, sides, cols // 128, 128), Layout(major_to_minor=(0, 2, 1, 3))
    )
    return split.transpose(0, 2, 1, 3).reshape(rows * sides * cols // 128, 128)


def from_linear(values, rows, sides):
    cols = values.size // (rows * sides)
    split = values.reshape(rows, cols // 128, sides, 128).transpose(0, 2, 1, 3)
    split = with_layout_constraint(split, Layout(major_to_minor=(0, 2, 1, 3)))
    return split.reshape(rows, sides, cols)


def apply_trust(weight, direction, norms):
    return weight - learn_rate * (norms[0] / (norms[1] + adam_eps)) * direction


def flip(values, bit):
    size = lax.axis_size("dp")
    return lax.ppermute(values, "dp", [(i, i ^ (1 << bit)) for i in range(size)])


def dp_bit(bit):
    return (lax.axis_index("dp") >> bit) & 1


def rows_of(values, start, rows):
    return lax.dynamic_slice_in_dim(values, start, rows, 0)


def total_of(pieces):
    total = pieces[0].astype(wide)
    for piece in pieces[1:]:
        total = total + piece.astype(wide)
    return total


def tie(values, *deps):
    return lax.optimization_barrier((values, *deps))[0]


def low_total(pieces):
    return total_of(pieces).astype(low)


def keep_or_join(bit, part, other):
    return jnp.where(
        dp_bit(bit) == 0,
        jnp.concatenate([part, other]),
        jnp.concatenate([other, part]),
    )


def share_of(weight, order):
    rows = weight.shape[0] // (1 << len(order))
    index = 0
    for bit in order:
        index = 2 * index + dp_bit(bit)
    return rows_of(weight, index * rows, rows)


def half_of(piece, place):
    rows = piece.shape[-2] // 2
    return lax.dynamic_slice_in_dim(piece, place * rows, rows, piece.ndim - 2)


def chunk_sum(chunk, order):
    bits = {"y": 0, "l": 1}
    steps = [name if name == "x" else bits[name] for name in order]
    pieces = [chunk]
    for step in steps:
        if step == "x":
            got = yield step, low_total([piece[1] for piece in pieces])
            pieces = [piece[0] for piece in pieces] + [got]
        else:
            here = dp_bit(step)
            got = yield step, low_total([half_of(piece, 1 - here) for piece in pieces])
            pieces = [half_of(piece, here) for piece in pieces] + [got]
    part = low_total(pieces)
    for step in range((lax.axis_size("dp") - 1).bit_length()):
        if step not in steps:
            got = yield step, part
            part = low_total([part, got])
    for step in reversed(steps):
        if step != "x":
            got = yield step, part
            part = keep_or_join(step, part, got)
    return part


def move(step, send):
    return swap(send, "col") if step == "x" else flip(send, step)


class Turns:
    def __init__(self):
        self.chunks = {}
        self.arrivals = {}
        self.seen = {}
        self.done = {}
        self.after = ()

    def add(self, name, chunk, order):
        self.chunks[name] = chunk_sum(chunk, order)

    def turn(self, name):
        got = self.arrivals.get(name)
        try:
            if got is None:
                self.seen[name] = []
                step, send = next(self.chunks[name])
                send = tie(send, *self.after)
            else:
                got = tie(got, *self.after)
                self.seen[name].append(got)
                step, send = self.chunks[name].send(got)
        except StopIteration as end:
            self.done[name] = end.value
            return
        self.arrivals[name] = move(step, send)
        self.after = (send,)

    def run(self, names):
        for name in names:
            if name not in self.done:
                self.turn(name)

    def finish(self):
        while len(self.done) < len(self.chunks):
            self.run(self.chunks)


def deinterleave(pairs, gate, up):
    rows, cols = gate.shape
    tiles = cols // 128
    for tile in range(tiles):
        for side, out in enumerate((gate, up)):
            out[:, tile * 128 : (tile + 1) * 128] = pairs[
                pl.ds(2 * tile + side, rows, stride=2 * tiles), :
            ].astype(low)


def split_pairs(linear, rows, cols):
    block = 64
    half = jax.ShapeDtypeStruct((rows, cols), low)
    out_spec = pl.BlockSpec((block, cols), lambda i: (i, 0))
    return pl.pallas_call(
        deinterleave,
        grid=(rows // block,),
        in_specs=[pl.BlockSpec((block * 2 * cols // 128, 128), lambda i: (i, 0))],
        out_specs=[out_spec, out_spec],
        out_shape=[half, half],
        compiler_params=pltpu.CompilerParams(vmem_limit_bytes=24 * MIB),
        cost_estimate=pl.CostEstimate(
            flops=rows * cols, bytes_accessed=12 * rows * cols, transcendentals=0
        ),
    )(linear)


def dot_of(left, right, left_dim, right_dim):
    return lax.dot_general(
        left, right, (((left_dim,), (right_dim,)), ((), ())), preferred_element_type=wide
    )


def local_call(kernel, grid, in_specs, out_specs, out_shape, scratch, args, prefetch=0, mib=1):
    return pl.pallas_call(
        kernel,
        grid_spec=pltpu.PrefetchScalarGridSpec(
            num_scalar_prefetch=prefetch,
            grid=grid,
            in_specs=in_specs,
            out_specs=out_specs,
            scratch_shapes=scratch,
        ),
        out_shape=out_shape,
        compiler_params=pltpu.CompilerParams(vmem_limit_bytes=48 * MIB),
        cost_estimate=pl.CostEstimate(flops=0, bytes_accessed=mib * MIB, transcendentals=0),
    )(*args)


def whole_spec(shape):
    return pl.BlockSpec(shape, lambda *_: (0,) * len(shape))


def shape_of(dims, kind):
    return jax.ShapeDtypeStruct(dims, kind)


def row_scale(halves):
    total = sum(jnp.sum(half * half, axis=1, keepdims=True) for half in halves)
    return lax.rsqrt(total / D + norm_eps)


def branch_kernel(tok, gains, taps, own, other, n1, gate_b, gate_c, gate_x, conv, hidden, part0, part1, ext):
    long, width = n1.shape[1:]
    rows = conv.shape[0]
    step = long // 3

    def gates(at, carry):
        here = pl.ds(pl.multiple_of(at * step, step), step)
        halves = [tok[h, here, :].astype(wide) for h in range(2)]
        scale = row_scale(halves)
        for h in range(2):
            n1[h, here, :] = (halves[h] * scale * gains[h]).astype(low)
        for g, out in enumerate((gate_b, gate_c, gate_x)):
            w = slice(g * width, (g + 1) * width)
            out[here, :] = dot_of(n1[0, here, :], own[w, :], 1, 0) + dot_of(
                n1[1, here, :], other[w, :], 1, 0
            )
        return carry

    lax.fori_loop(0, 3, gates, 0)
    ext[8 : 8 + rows, :] = gate_b[:rows, :] * gate_x[:rows, :]
    ext[6:8, :] = gate_b[rows : rows + 2, :] * gate_x[rows : rows + 2, :]
    w_out = slice(3 * width, 4 * width)
    quarter = rows // 4
    for at in range(4):
        start = at * quarter
        taken = slice(start, start + quarter)
        value = sum(taps[k] * ext[start + 6 + k : start + 6 + k + quarter, :] for k in range(3))
        conv[taken, :] = value
        low_hidden = (gate_c[taken, :] * value).astype(low)
        hidden[taken, :] = low_hidden
        for part, weight in ((part0, own), (part1, other)):
            part[taken, :] = dot_of(low_hidden, weight[w_out, :], 1, 0).astype(low)


def branch_forward(tok, rows, tails, gains, taps, own, other):
    width = tok.shape[2]
    gate = shape_of((rows + tails, width), wide)
    outs = [
        shape_of((2, rows + tails, width), low),
        gate,
        gate,
        gate,
        shape_of((rows, width), wide),
        shape_of((rows, width), low),
        shape_of((rows, width), low),
        shape_of((rows, width), low),
    ]
    args = (tok, gains, taps, own, other)
    return local_call(
        branch_kernel,
        (1,),
        [whole_spec(a.shape) for a in args],
        [whole_spec(o.shape) for o in outs],
        outs,
        [pltpu.VMEM((rows + 8, width), wide)],
        args,
    )


def piece_at(bits, which, piece, width):
    place = bits[which] if piece == 0 else 1 - bits[which]
    return pl.ds(pl.multiple_of(place * width, width), width)


def ffn_kernel(bits, tok, mine0, mine1, theirs0, theirs1, gains, g0, g1, g2, u0, u1, u2, n2, res, gate, up, act):
    width = g1.shape[0]

    @pl.when(pl.program_id(0) == 0)
    def _():
        for h, (mine, theirs) in enumerate(((mine0, theirs0), (mine1, theirs1))):
            res[h] = tok[h, : res.shape[1], :].astype(wide) + (
                mine[...].astype(wide) + theirs[...].astype(wide)
            )
        scale = row_scale([res[0], res[1]])
        for h in range(2):
            n2[h] = (res[h] * scale * gains[h]).astype(low)

    for which, (out, w0, w1, w2) in enumerate(((gate, g0, g1, g2), (up, u0, u1, u2))):
        total = dot_of(n2[0], w0[...], 1, 0)
        for piece, w in enumerate((w1, w2)):
            total += dot_of(n2[1, :, piece_at(bits, which, piece, width)], w[...], 1, 0)
        out[...] = total
    value = gate[...]
    act[...] = (value * jax.nn.sigmoid(value) * up[...]).astype(low)


def ffn_forward(bits, tok, mine, theirs, gains, weights):
    rows, width = mine[0].shape
    cols = weights[0].shape[1]
    tile = cols // 3
    both = (2, rows, width)
    full = whole_spec(both)
    wide_tile = pl.BlockSpec((rows, tile), lambda i, *_: (0, i))
    weight_specs = [pl.BlockSpec((w.shape[0], tile), lambda i, *_: (0, i)) for w in weights]
    return local_call(
        ffn_kernel,
        (3,),
        [whole_spec(tok.shape)]
        + [whole_spec((rows, width))] * 4
        + [whole_spec(gains.shape)]
        + weight_specs,
        [full, full, wide_tile, wide_tile, wide_tile],
        [
            shape_of(both, low),
            shape_of(both, wide),
            shape_of((rows, cols), wide),
            shape_of((rows, cols), wide),
            shape_of((rows, cols), low),
        ],
        [],
        (bits, tok, *mine, *theirs, gains, *weights),
        prefetch=1,
    )


def ffn_back_kernel(
    bits, cot, d_own, d_other, gate, up, g0, g1, g2, u0, u1, u2, g_gate, g_up, part0, part1, total
):
    width = g1.shape[0]

    @pl.when(pl.program_id(0) == 0)
    def _():
        total[...] = jnp.zeros_like(total)

    start = cot.shape[1] - gate.shape[0]
    g_act = dot_of(cot[0, start:, :], d_own[...], 1, 1) + dot_of(cot[1, start:, :], d_other[...], 1, 1)
    value = gate[...]
    sigma = jax.nn.sigmoid(value)
    g_gate[...] = (g_act * up[...] * sigma * (1.0 + value * (1.0 - sigma))).astype(low)
    g_up[...] = (g_act * (value * sigma)).astype(low)
    total[0] += dot_of(g_gate[...], g0[...], 1, 1) + dot_of(g_up[...], u0[...], 1, 1)
    for which, (grad, w1, w2) in enumerate(((g_gate, g1, g2), (g_up, u1, u2))):
        for piece, w in enumerate((w1, w2)):
            total[1, :, piece_at(bits, which, piece, width)] += dot_of(grad[...], w[...], 1, 1)

    @pl.when(pl.program_id(0) == pl.num_programs(0) - 1)
    def _():
        part0[...] = total[0].astype(low)
        part1[...] = total[1].astype(low)


def ffn_backward(bits, cot, downs, gate, up, weights):
    rows, cols = gate.shape
    tile = cols // 3
    part = (rows, cot.shape[2])
    wide_tile = pl.BlockSpec((rows, tile), lambda i, *_: (0, i))
    weight_specs = [pl.BlockSpec((w.shape[0], tile), lambda i, *_: (0, i)) for w in weights]
    down_spec = pl.BlockSpec((tile, downs[0].shape[1]), lambda i, *_: (i, 0))
    return local_call(
        ffn_back_kernel,
        (3,),
        [whole_spec(cot.shape), down_spec, down_spec, wide_tile, wide_tile] + weight_specs,
        [wide_tile, wide_tile, whole_spec(part), whole_spec(part)],
        [shape_of((rows, cols), low)] * 2 + [shape_of(part, low)] * 2,
        [pltpu.VMEM((2, *part), wide)],
        (bits, cot, *downs, gate, up, *weights),
        prefetch=1,
    )


def pair_grad_kernel(n2, g_gate, g_up, out):
    rows = n2.shape[2]
    for side, grad in enumerate((g_gate, g_up)):
        out[0, 0, side * rows : (side + 1) * rows, :] = dot_of(n2[0], grad[...], 0, 0).astype(low)


def pair_grads(n2, g_gate, g_up, chunks):
    _, rows, width = n2.shape
    cols = g_gate.shape[1]
    part = width // chunks
    return local_call(
        pair_grad_kernel,
        (chunks, 2),
        [
            pl.BlockSpec((1, rows, part), lambda q, h: (h, 0, q)),
            whole_spec(g_gate.shape),
            whole_spec(g_up.shape),
        ],
        pl.BlockSpec((1, 1, 2 * part, cols), lambda q, h: (q, h, 0, 0)),
        shape_of((chunks, 2, 2 * part, cols), low),
        [],
        (n2, g_gate, g_up),
        mib=16,
    )


def down_grad_kernel(act, cot, out):
    start = cot.shape[1] - act.shape[0]
    out[0, 0] = dot_of(act[...], cot[0, start:, :], 0, 0).astype(low)


def down_grads(act, cot, chunks):
    rows, cols = act.shape
    _, long, width = cot.shape
    part = cols // chunks
    return local_call(
        down_grad_kernel,
        (chunks, 2),
        [
            pl.BlockSpec((rows, part), lambda q, h: (0, q)),
            pl.BlockSpec((1, long, width), lambda q, h: (h, 0, 0)),
        ],
        pl.BlockSpec((1, 1, part, width), lambda q, h: (q, h, 0, 0)),
        shape_of((chunks, 2, part, width), low),
        [],
        (act, cot),
    )


def branch_back_kernel(
    mine0, mine1, theirs0, theirs1, res, cot, gains, taps, own, other, gate_b, gate_c, gate_x, conv,
    g_res, g_low, g_proj, gain_grad, tap_grad, ext, ext_grad,
):
    _, rows, width = res.shape
    scale = row_scale([res[0], res[1]])
    grads = [
        mine[...].astype(wide) + theirs[...].astype(wide)
        for mine, theirs in ((mine0, theirs0), (mine1, theirs1))
    ]
    inner = sum(
        jnp.sum(grads[h] * gains[h] * res[h], axis=1, keepdims=True) for h in range(2)
    )
    factor = scale * scale * scale * inner / D
    for h in range(2):
        gain_grad[h] = jnp.sum(grads[h] * res[h] * scale, axis=0, keepdims=True)
        value = cot[h, cot.shape[1] - rows :, :].astype(wide) + (scale * (grads[h] * gains[h]) - res[h] * factor)
        g_res[h] = value
        g_low[h] = value.astype(low)
    g_hidden = dot_of(g_low[0], own[...], 1, 1) + dot_of(g_low[1], other[...], 1, 1)
    g_proj[1, :rows, :] = (g_hidden * conv[...]).astype(low)
    g_conv = g_hidden * gate_c[:rows, :]
    ext_grad[:rows, :] = g_conv
    ext_grad[rows:, :] = jnp.zeros((8, width), wide)
    ext[8 : 8 + rows, :] = gate_b[:rows, :] * gate_x[:rows, :]
    ext[6:8, :] = gate_b[rows : rows + 2, :] * gate_x[rows : rows + 2, :]
    for k in range(3):
        tap_grad[k : k + 1, :] = jnp.sum(
            g_conv * ext[6 + k : 6 + k + rows, :], axis=0, keepdims=True
        )
    g_mixed = sum(taps[2 - k] * ext_grad[k : k + rows, :] for k in range(3))
    g_proj[0, :rows, :] = (g_mixed * gate_x[:rows, :]).astype(low)
    g_proj[2, :rows, :] = (g_mixed * gate_b[:rows, :]).astype(low)
    tails = g_proj.shape[1] - rows
    row = lax.broadcasted_iota(jnp.int32, (tails, width), 0)
    first, second = ext_grad[0:1, :], ext_grad[1:2, :]
    g_before = jnp.where(
        row == 0,
        taps[0] * first,
        jnp.where(row == 1, taps[1] * first + taps[0] * second, 0.0),
    )
    g_proj[0, rows:, :] = (g_before * gate_x[rows:, :]).astype(low)
    g_proj[1, rows:, :] = jnp.zeros((tails, width), low)
    g_proj[2, rows:, :] = (g_before * gate_b[rows:, :]).astype(low)


def branch_backward(mine, theirs, res, cot, gains, taps, own, other, gates, conv):
    _, rows, width = res.shape
    long = gates[0].shape[0]
    out_weight = pl.BlockSpec((width, width), lambda i, *_: (3, 0))
    outs = [
        shape_of(res.shape, wide),
        shape_of(res.shape, low),
        shape_of((3, long, width), low),
        shape_of((2, 1, width), wide),
        shape_of((3, width), wide),
    ]
    full = whole_spec(res.shape)
    return local_call(
        branch_back_kernel,
        (1,),
        [whole_spec((rows, width))] * 4
        + [full, whole_spec(cot.shape), whole_spec(gains.shape), whole_spec(taps.shape)]
        + [out_weight, out_weight]
        + [whole_spec(g.shape) for g in gates]
        + [whole_spec(conv.shape)],
        [whole_spec(o.shape) for o in outs],
        outs,
        [pltpu.VMEM((rows + 8, width), wide), pltpu.VMEM((rows + 8, width), wide)],
        (*mine, *theirs, res, cot, gains, taps, own, other, *gates, conv),
    )


def branch_grad_kernel(n1, g_proj, hidden, g_low, out):
    kind = pl.program_id(1)

    @pl.when(kind < 3)
    def _():
        out[0, 0, 0] = dot_of(n1[0], g_proj[0], 0, 0).astype(low)

    @pl.when(kind == 3)
    def _():
        out[0, 0, 0] = dot_of(hidden[...], g_low[0], 0, 0).astype(low)


def branch_grads(n1, g_proj, hidden, g_low):
    _, long, width = n1.shape
    rows = hidden.shape[0]
    return local_call(
        branch_grad_kernel,
        (2, 4),
        [
            pl.BlockSpec((1, long, width), lambda h, k: (h, 0, 0)),
            pl.BlockSpec((1, long, width), lambda h, k: (jnp.minimum(k, 2), 0, 0)),
            whole_spec(hidden.shape),
            pl.BlockSpec((1, rows, width), lambda h, k: (h, 0, 0)),
        ],
        pl.BlockSpec((1, 1, 1, width, width), lambda h, k: (k // 2, h, k % 2, 0, 0)),
        shape_of((2, 2, 2, width, width), low),
        [],
        (n1, g_proj, hidden, g_low),
    )


def shards(
    tokens,
    cotangent,
    input_projection_weight,
    conv_weight,
    output_projection_weight,
    norm_gains,
    gate_up_weight,
    down_projection_weight,
    in_first,
    in_second,
    conv_first,
    conv_second,
    out_first,
    out_second,
    gain_first,
    gain_second,
    gu_first,
    gu_second,
    down_first,
    down_second,
):
    feat_cols = tokens.shape[1]
    branch_cols = conv_weight.shape[1]
    hidden_cols = down_projection_weight.shape[0]
    block_rows = tokens.shape[0]
    seq_len = max(SEQ_LEAST, block_rows * lax.axis_size("dp") * lax.axis_size("col"))
    data_pos = lax.axis_index("dp")
    row_pos = lax.axis_index("row")
    col_pos = lax.axis_index("col")
    home = row_pos == col_pos
    tail_rows = 16

    row_start = (data_pos * lax.axis_size("row") + row_pos) * block_rows
    tail = from_behind(tokens[-2:], ("dp", "row"), 1)
    tail = jnp.where(row_start % seq_len != 0, tail, jnp.zeros_like(tail))
    spare = jnp.zeros((tail_rows - 8, feat_cols), low)
    gain_parts = []
    left = norm_gains
    for _ in range(3):
        gain_parts.append(lax.reduce_precision(left, 8, 7))
        left = left - gain_parts[-1]
    gain_parts = jnp.concatenate(gain_parts).astype(low)
    block = jnp.concatenate([tokens, tail, gain_parts, spare, cotangent])
    away = to_home(block)
    in_low = jnp.transpose(input_projection_weight, (1, 0, 2)).astype(low).reshape(-1, branch_cols)
    io_low = jnp.concatenate([in_low, output_projection_weight.astype(low)])
    io_got = swap(share_of(io_low, (1, 0)), "col")
    gu_weight = to_linear(gate_up_weight)
    gate_low, up_low = split_pairs(gu_weight, feat_cols, hidden_cols)
    down_low = down_projection_weight.astype(low)
    both = jnp.stack([block, away])
    both = jnp.where(home, both, home_to_sibling(both))
    gains = both[:, block_rows + 2 : block_rows + 8].astype(wide)
    gains = gains[:, 0:2] + gains[:, 2:4] + gains[:, 4:6]
    gains = [gains[:, k : k + 1] for k in range(2)]
    gate_got = swap(tie(share_of(gate_low, (1, 0)), io_got), "col")
    up_got = swap(tie(share_of(up_low, (0, 1)), away), "col")
    down_got = swap(tie(down_low, gate_got), "col")
    io_pair = keep_or_join(0, io_got, flip(io_got, 0))
    io_other = keep_or_join(1, io_pair, flip(io_pair, 1))
    gate_pair = keep_or_join(0, gate_got, flip(tie(gate_got, io_pair), 0))
    up_pair = keep_or_join(1, up_got, flip(tie(up_got, io_pair), 1))
    gate_more = flip(gate_pair, 1)
    up_more = flip(up_pair, 0)
    weights = [gate_low, gate_pair, gate_more, up_low, up_pair, up_more]
    bits = jnp.stack([dp_bit(1), dp_bit(0)]).astype(jnp.int32)
    downs = [down_low, down_got]

    n1, gate_b, gate_c, gate_x, conv, hidden, *branch = branch_forward(
        both, block_rows, tail_rows, gains[0], conv_weight, io_low, io_other
    )
    n2, res, gate, upper, act = ffn_forward(
        bits, both, branch, swap_halves(branch), gains[1], weights
    )

    turns = Turns()
    down_half = hidden_cols // 2
    down_part = down_grads(act, both, 2)
    for k, order in enumerate(('ylx', 'lyx')):
        turns.add("Dd"[k], down_part[k], order)
    turns.run("Dd")
    g_gate, g_up, *part_two = ffn_backward(bits, tie(both, down_part), downs, gate, upper, weights)
    pair_part = pair_grads(n2, g_gate, g_up, 4)
    for k, order in enumerate(('xyl', 'xyl', 'xyl', 'xyl')):
        turns.add("abce"[k], pair_part[k], order)
    turns.run("abDd")
    g_res, g_branch, g_proj, gain_two_grad, conv_grad = branch_backward(
        part_two,
        swap_halves(part_two),
        tie(res, *turns.after),
        both,
        gains[1],
        conv_weight,
        io_low,
        io_other,
        (gate_b, gate_c, gate_x),
        conv,
    )
    io_part = branch_grads(n1, g_proj, hidden, g_branch).reshape(2, 2, 2 * feat_cols, branch_cols)
    for k, order in enumerate(('xly', 'xyl')):
        turns.add("Ii"[k], io_part[k], order)
    turns.after += (io_part,)
    turns.run("acDdababcaDebdIacDabeidcDeIbdcDeiIbdicIeicIeiIeiIi")
    turns.finish()
    sums, seen = turns.done, turns.seen

    late = seen["i"][0]
    act = tie(act, late)
    g_proj = tie(g_proj, late)
    io_half = [half.reshape(4, feat_cols, branch_cols) for half in (io_low, io_other)]
    g_part = jnp.stack(
        [sum(mul_t(g_proj[g], io_half[h][g]) for g in range(3)).astype(low) for h in range(2)]
    )
    g_long = g_part.astype(wide) + swap(g_part, "row").astype(wide)
    back = from_behind(g_long[::-1, block_rows : block_rows + 2], ("dp", "col"), -1)
    g_n1 = g_long[:, :block_rows].at[:, -2:].add(back)
    tok = both[:, :block_rows].astype(wide)
    scale = lax.rsqrt(jnp.sum(tok * tok, axis=(0, 2)) / D + norm_eps)[None, :, None]
    weighted = g_n1 * gains[0]
    inner = jnp.sum(weighted * tok, axis=(0, 2))[None, :, None]
    gain_one_grad = jnp.sum(g_n1 * tok * scale, axis=1)
    tok_half = (g_res + (scale * weighted - tok * (scale * scale * scale * inner / D))).astype(low)
    token_grad = jnp.where(home, tok_half[0], home_to_away(tok_half[1]))
    ffn = jnp.stack([mul(act, downs[h]) for h in range(2)])
    out_half = (res + (ffn + sibling_to_home(ffn.astype(low)).astype(wide))).astype(low)
    output = jnp.where(home, out_half[0], home_to_away(out_half[1]))

    small = jnp.concatenate(
        [conv_grad]
        + [part for h in range(2) for part in (gain_one_grad[h : h + 1], gain_two_grad[h])]
    )
    small = tie(small, seen["i"][3])
    for bit in range((lax.axis_size("dp") - 1).bit_length()):
        small = small + flip(small, bit)
    small_more = swap(small, "col")
    conv_grad = small[:3] + small_more[:3]
    gains_grad = small[3:5] + small_more[5:]

    conv_m, conv_v, conv_u = lamb_moments(conv_weight, conv_grad, conv_first, conv_second, 0.0)
    gain_m, gain_v, gain_u = lamb_moments(norm_gains, gains_grad, gain_first, gain_second, 0.0)

    def in_flat(values):
        return jnp.transpose(values, (1, 0, 2)).reshape(3 * feat_cols, branch_cols)

    def in_back(values):
        return jnp.transpose(values.reshape(3, feat_cols, branch_cols), (1, 0, 2))

    def gu_back(values):
        return from_linear(values, feat_cols, 2)

    (down_m, down_v, down_u), down_norms = lamb_dense(
        (down_projection_weight, down_first, down_second),
        [(sums["Dd"[k]], 0, k * down_half, down_half) for k in (0, 1)],
        384,
    )
    gu_state = (gu_weight, to_linear(gu_first), to_linear(gu_second))
    pairs = 2 * hidden_cols // 128
    gu_rows = 32
    gu_new, gu_norms = None, 0.0
    for k in (0, 1, 2, 3):
        grad = sums["abce"[k]]
        blocks = grad.shape[0] // 2 // gu_rows
        gu_new, squares = lamb_call(
            lamb_pairs,
            gu_state,
            [(grad, gu_rows, 0), (grad, gu_rows, blocks)],
            gu_rows * pairs,
            k * blocks,
            blocks,
            gu_new,
            [pltpu.VMEM((gu_rows * pairs, 128), wide)],
        )
        gu_norms = gu_norms + squares
    gu_m, gu_v, gu_u = gu_new
    in_weight = in_flat(input_projection_weight)
    (in_m, in_v, in_u), in_norms = lamb_dense(
        (in_weight, in_flat(in_first), in_flat(in_second)),
        [
            (sums["I"], 0, 0, 2 * feat_cols),
            (sums["i"], 0, 2 * feat_cols, feat_cols),
        ],
        256,
    )
    (out_m, out_v, out_u), out_norms = lamb_dense(
        (output_projection_weight, out_first, out_second),
        [(sums["i"], feat_cols, 0, branch_cols)],
        256,
    )
    col_first = (col_pos == 0).astype(wide)
    row_first = (row_pos == 0).astype(wide)
    partial_sums = jnp.stack(
        [
            in_norms,
            square_pair(conv_weight, conv_u) * col_first,
            out_norms,
            square_pair(norm_gains[0], gain_u[0]) * row_first,
            square_pair(norm_gains[1], gain_u[1]) * row_first,
            gu_norms,
            down_norms,
        ]
    )
    trust_norms = jnp.sqrt(lax.psum(partial_sums, ("row", "col")))
    gains_new = jnp.stack(
        [
            apply_trust(norm_gains[0], gain_u[0], trust_norms[3]),
            apply_trust(norm_gains[1], gain_u[1], trust_norms[4]),
        ]
    )
    return (
        output,
        token_grad,
        in_back(apply_trust(in_weight, in_u, trust_norms[0])),
        in_back(in_m),
        in_back(in_v),
        apply_trust(conv_weight, conv_u, trust_norms[1]),
        conv_m,
        conv_v,
        apply_trust(output_projection_weight, out_u, trust_norms[2]),
        out_m,
        out_v,
        gains_new,
        gain_m,
        gain_v,
        gu_back(apply_trust(gu_weight, gu_u, trust_norms[5])),
        gu_back(gu_m),
        gu_back(gu_v),
        apply_trust(down_projection_weight, down_u, trust_norms[6]),
        down_m,
        down_v,
        trust_norms,
    )


def solution(mesh):
    in_specs = (
        P(("dp", "row"), "col"),
        P(("dp", "row"), "col"),
        P("col", None, "row"),
        P(None, "row"),
        P("row", "col"),
        P(None, "col"),
        P("col", None, "row"),
        P("row", "col"),
        P("col", None, "row"),
        P("col", None, "row"),
        P(None, "row"),
        P(None, "row"),
        P("row", "col"),
        P("row", "col"),
        P(None, "col"),
        P(None, "col"),
        P("col", None, "row"),
        P("col", None, "row"),
        P("row", "col"),
        P("row", "col"),
    )
    out_specs = (
        P(("dp", "row"), "col"),
        P(("dp", "row"), "col"),
        P("col", None, "row"),
        P("col", None, "row"),
        P("col", None, "row"),
        P(None, "row"),
        P(None, "row"),
        P(None, "row"),
        P("row", "col"),
        P("row", "col"),
        P("row", "col"),
        P(None, "col"),
        P(None, "col"),
        P(None, "col"),
        P("col", None, "row"),
        P("col", None, "row"),
        P("col", None, "row"),
        P("row", "col"),
        P("row", "col"),
        P("row", "col"),
        P(),
    )
    return jax.shard_map(shards, mesh=mesh, in_specs=in_specs, out_specs=out_specs, check_vma=False)
```

```python
import jax
import jax.numpy as jnp
from jax import lax
from jax.experimental import pallas as pl
from jax.experimental.layout import Layout, with_layout_constraint
from jax.experimental.pallas import tpu as pltpu
from jax.sharding import PartitionSpec as P

D = 1024
SEQ_LEAST = 4096
STEP = 5
MIB = 1024 * 1024


norm_eps = 1e-05
adam_eps = 1e-06
beta_one = 0.5
beta_two = 0.6
learn_rate = 0.5
decay_rate = 0.01
low = jnp.bfloat16
wide = jnp.float32


def from_behind(block, axis, distance):
    devices = range(lax.axis_size(axis))
    route = [(i - distance, i) for i in devices if i - distance in devices]
    return lax.ppermute(block, axis, route)


def swap(values, axis):
    return lax.ppermute(values, axis, [(0, 1), (1, 0)])


def swap_halves(halves):
    return [swap(half, "row") for half in halves]


def to_home(values):
    return lax.ppermute(values, ("row", "col"), [(1, 0), (2, 3)])


def home_to_sibling(values):
    return lax.ppermute(values, ("row", "col"), [(0, 2), (3, 1)])


def home_to_away(values):
    return lax.ppermute(values, ("row", "col"), [(0, 1), (3, 2)])


def sibling_to_home(values):
    return lax.ppermute(values, ("row", "col"), [(2, 0), (1, 3)])


def contract(left, right, left_dim, right_dim):
    return lax.dot_general(
        left, right, (((left_dim,), (right_dim,)), ((), ())), preferred_element_type=wide
    )


def mul(left, right):
    return contract(left, right, 1, 0)


def mul_t(left, right):
    return contract(left, right, 1, 1)


def t_mul(left, right):
    return contract(left, right, 0, 0)


def lamb_moments(weight, grad, first, second, decay):
    first_new = beta_one * first + (1.0 - beta_one) * grad
    second_new = beta_two * second + (1.0 - beta_two) * grad * grad
    direction = (
        first_new
        / (1.0 - beta_one**STEP)
        / (jnp.sqrt(second_new / (1.0 - beta_two**STEP)) + adam_eps)
        + decay * weight
    )
    return (first_new, second_new, direction)


def square_pair(weight, direction):
    return jnp.stack([jnp.sum(weight * weight), jnp.sum(direction * direction)])


def lamb_rows(p, g, m, v, m_out, v_out, u_out):
    weight = p[...]
    grad = g[...].astype(wide)
    first_new, second_new, direction = lamb_moments(weight, grad, m[...], v[...], decay_rate)
    m_out[...] = first_new
    v_out[...] = second_new
    u_out[...] = direction
    return weight * weight, direction * direction


def lamb_loop(refs, sums, rows, step):
    lanes = sums.shape[2]

    @pl.when(pl.program_id(0) == 0)
    def _():
        sums[...] = jnp.zeros_like(sums)

    def body(at, total):
        here = pl.ds(pl.multiple_of(at * step, step), step)
        squares = lamb_rows(*[ref.at[here, :] for ref in refs])
        return tuple(
            t + jnp.sum(sq.reshape(step // 8, 8, lanes), axis=0) for t, sq in zip(total, squares)
        )

    zero = jnp.zeros((8, lanes), wide)
    total = lax.fori_loop(0, rows // step, body, (zero, zero))
    sums[0] += total[0]
    sums[1] += total[1]


def lamb_plain(p, g, m, v, m_out, v_out, u_out, sums):
    lamb_loop((p, g, m, v, m_out, v_out, u_out), sums, p.shape[0], 16)


def lamb_pairs(p, gate, up, m, v, m_out, v_out, u_out, sums, mixed):
    rows, cols = gate.shape
    tiles = cols // 128
    for tile in range(tiles):
        for side, ref in enumerate((gate, up)):
            mixed[pl.ds(2 * tile + side, rows, stride=2 * tiles), :] = ref[
                :, tile * 128 : (tile + 1) * 128
            ].astype(wide)
    lamb_loop((p, mixed, m, v, m_out, v_out, u_out), sums, p.shape[0], 64)


def lamb_call(kernel, state, grads, block, start, count, before, scratch):
    rows, cols = state[0].shape
    flat = pl.BlockSpec((block, cols), lambda i: (i + start, 0))
    whole = jax.ShapeDtypeStruct((rows, cols), wide)
    grad_specs = [
        pl.BlockSpec((size, grad.shape[1]), lambda i, at=at: (i + at, 0)) for grad, size, at in grads
    ]
    weight, first, second = state
    args = [weight, *[grad for grad, _, _ in grads], first, second]
    specs = [flat] + grad_specs + [flat, flat]
    aliases = {}
    run = kernel
    if before is not None:
        aliases = {len(args) + k: k for k in range(3)}

        def run(*refs):
            kernel(*refs[: len(args)], *refs[len(args) + 3 :])

    call = pl.pallas_call(
        run,
        grid=(count,),
        in_specs=specs + [pl.BlockSpec(memory_space=pl.ANY)] * len(aliases),
        out_specs=[flat, flat, flat, pl.BlockSpec((2, 8, cols), lambda i: (0, 0, 0))],
        out_shape=[whole, whole, whole, jax.ShapeDtypeStruct((2, 8, cols), wide)],
        scratch_shapes=scratch,
        input_output_aliases=aliases,
        compiler_params=pltpu.CompilerParams(vmem_limit_bytes=60 * MIB),
        cost_estimate=pl.CostEstimate(
            flops=20 * count * block * cols,
            bytes_accessed=26 * count * block * cols,
            transcendentals=2 * count * block * cols,
        ),
    )
    m_new, v_new, direction, sums = call(*args, *(before or []))
    return [m_new, v_new, direction], jnp.sum(sums, axis=(1, 2))


def lamb_dense(state, parts, block):
    before, norms = None, 0.0
    for grad, grad_at, at, rows in parts:
        before, sums = lamb_call(
            lamb_plain,
            state,
            [(grad, block, grad_at // block)],
            block,
            at // block,
            rows // block,
            before,
            [],
        )
        norms = norms + sums
    return before, norms


def to_linear(values):
    rows, sides, cols = values.shape
    split = with_layout_constraint(
        values.reshape(rows, sides, cols // 128, 128), Layout(major_to_minor=(0, 2, 1, 3))
    )
    return split.transpose(0, 2, 1, 3).reshape(rows * sides * cols // 128, 128)


def from_linear(values, rows, sides):
    cols = values.size // (rows * sides)
    split = values.reshape(rows, cols // 128, sides, 128).transpose(0, 2, 1, 3)
    split = with_layout_constraint(split, Layout(major_to_minor=(0, 2, 1, 3)))
    return split.reshape(rows, sides, cols)


def apply_trust(weight, direction, norms):
    return weight - learn_rate * (norms[0] / (norms[1] + adam_eps)) * direction


def flip(values, bit):
    size = lax.axis_size("dp")
    return lax.ppermute(values, "dp", [(i, i ^ (1 << bit)) for i in range(size)])


def dp_bit(bit):
    return (lax.axis_index("dp") >> bit) & 1


def rows_of(values, start, rows):
    return lax.dynamic_slice_in_dim(values, start, rows, 0)


def total_of(pieces):
    total = pieces[0].astype(wide)
    for piece in pieces[1:]:
        total = total + piece.astype(wide)
    return total


def tie(values, *deps):
    return lax.optimization_barrier((values, *deps))[0]


def low_total(pieces):
    return total_of(pieces).astype(low)


def keep_or_join(bit, part, other):
    return jnp.where(
        dp_bit(bit) == 0,
        jnp.concatenate([part, other]),
        jnp.concatenate([other, part]),
    )


def share_of(weight, order):
    rows = weight.shape[0] // (1 << len(order))
    index = 0
    for bit in order:
        index = 2 * index + dp_bit(bit)
    return rows_of(weight, index * rows, rows)


def half_of(piece, place):
    rows = piece.shape[-2] // 2
    return lax.dynamic_slice_in_dim(piece, place * rows, rows, piece.ndim - 2)


def chunk_sum(chunk, order):
    bits = {"y": 0, "l": 1}
    steps = [name if name == "x" else bits[name] for name in order]
    pieces = [chunk]
    for step in steps:
        if step == "x":
            whole = len(pieces) == 1
            got = yield step, pieces[0][1] if whole else low_total([piece[1] for piece in pieces])
            pieces = [piece[0] for piece in pieces] + [got]
        else:
            here = dp_bit(step)
            got = yield step, low_total([half_of(piece, 1 - here) for piece in pieces])
            pieces = [half_of(piece, here) for piece in pieces] + [got]
    part = low_total(pieces)
    for step in range((lax.axis_size("dp") - 1).bit_length()):
        if step not in steps:
            got = yield step, part
            part = low_total([part, got])
    for step in reversed(steps):
        if step != "x":
            got = yield step, part
            part = keep_or_join(step, part, got)
    return part


def move(step, send):
    return swap(send, "col") if step == "x" else flip(send, step)


class Turns:
    def __init__(self):
        self.chunks = {}
        self.arrivals = {}
        self.seen = {}
        self.done = {}
        self.after = ()

    def add(self, name, chunk, order):
        self.chunks[name] = chunk_sum(chunk, order)

    def turn(self, name):
        got = self.arrivals.get(name)
        try:
            if got is None:
                self.seen[name] = []
                step, send = next(self.chunks[name])
                send = tie(send, *self.after)
            else:
                got = tie(got, *self.after)
                self.seen[name].append(got)
                step, send = self.chunks[name].send(got)
        except StopIteration as end:
            self.done[name] = end.value
            return
        self.arrivals[name] = move(step, send)
        self.after = (send,)

    def run(self, names):
        for name in names:
            if name not in self.done:
                self.turn(name)

    def finish(self):
        while len(self.done) < len(self.chunks):
            self.run(self.chunks)


def deinterleave(pairs, gate, up):
    rows, cols = gate.shape
    tiles = cols // 128
    for tile in range(tiles):
        for side, out in enumerate((gate, up)):
            out[:, tile * 128 : (tile + 1) * 128] = pairs[
                pl.ds(2 * tile + side, rows, stride=2 * tiles), :
            ].astype(low)


def split_pairs(linear, rows, cols):
    block = 64
    half = jax.ShapeDtypeStruct((rows, cols), low)
    out_spec = pl.BlockSpec((block, cols), lambda i: (i, 0))
    return pl.pallas_call(
        deinterleave,
        grid=(rows // block,),
        in_specs=[pl.BlockSpec((block * 2 * cols // 128, 128), lambda i: (i, 0))],
        out_specs=[out_spec, out_spec],
        out_shape=[half, half],
        compiler_params=pltpu.CompilerParams(vmem_limit_bytes=24 * MIB),
        cost_estimate=pl.CostEstimate(
            flops=rows * cols, bytes_accessed=12 * rows * cols, transcendentals=0
        ),
    )(linear)


def dot_of(left, right, left_dim, right_dim):
    return lax.dot_general(
        left, right, (((left_dim,), (right_dim,)), ((), ())), preferred_element_type=wide
    )


def local_call(kernel, grid, in_specs, out_specs, out_shape, scratch, args, prefetch=0):
    return pl.pallas_call(
        kernel,
        grid_spec=pltpu.PrefetchScalarGridSpec(
            num_scalar_prefetch=prefetch,
            grid=grid,
            in_specs=in_specs,
            out_specs=out_specs,
            scratch_shapes=scratch,
        ),
        out_shape=out_shape,
        compiler_params=pltpu.CompilerParams(vmem_limit_bytes=48 * MIB),
        cost_estimate=pl.CostEstimate(flops=0, bytes_accessed=MIB, transcendentals=0),
    )(*args)


def whole_spec(shape):
    return pl.BlockSpec(shape, lambda *_: (0,) * len(shape))


def shape_of(dims, kind):
    return jax.ShapeDtypeStruct(dims, kind)


def row_scale(halves):
    total = sum(jnp.sum(half * half, axis=1, keepdims=True) for half in halves)
    return lax.rsqrt(total / D + norm_eps)


def branch_kernel(tok, gains, taps, own, other, n1, gate_b, gate_c, gate_x, conv, hidden, part0, part1, ext):
    long, width = n1.shape[1:]
    rows = conv.shape[0]
    step = long // 3

    def gates(at, carry):
        here = pl.ds(pl.multiple_of(at * step, step), step)
        halves = [tok[h, here, :].astype(wide) for h in range(2)]
        scale = row_scale(halves)
        for h in range(2):
            n1[h, here, :] = (halves[h] * scale * gains[h]).astype(low)
        for g, out in enumerate((gate_b, gate_c, gate_x)):
            w = slice(g * width, (g + 1) * width)
            out[here, :] = dot_of(n1[0, here, :], own[w, :], 1, 0) + dot_of(
                n1[1, here, :], other[w, :], 1, 0
            )
        return carry

    lax.fori_loop(0, 3, gates, 0)
    ext[8 : 8 + rows, :] = gate_b[:rows, :] * gate_x[:rows, :]
    ext[6:8, :] = gate_b[rows : rows + 2, :] * gate_x[rows : rows + 2, :]
    w_out = slice(3 * width, 4 * width)
    quarter = rows // 4
    for at in range(4):
        start = at * quarter
        taken = slice(start, start + quarter)
        value = sum(taps[k] * ext[start + 6 + k : start + 6 + k + quarter, :] for k in range(3))
        conv[taken, :] = value
        low_hidden = (gate_c[taken, :] * value).astype(low)
        hidden[taken, :] = low_hidden
        for part, weight in ((part0, own), (part1, other)):
            part[taken, :] = dot_of(low_hidden, weight[w_out, :], 1, 0).astype(low)


def branch_forward(tok, rows, tails, gains, taps, own, other):
    width = tok.shape[2]
    gate = shape_of((rows + tails, width), wide)
    outs = [
        shape_of((2, rows + tails, width), low),
        gate,
        gate,
        gate,
        shape_of((rows, width), wide),
        shape_of((rows, width), low),
        shape_of((rows, width), low),
        shape_of((rows, width), low),
    ]
    args = (tok, gains, taps, own, other)
    return local_call(
        branch_kernel,
        (1,),
        [whole_spec(a.shape) for a in args],
        [whole_spec(o.shape) for o in outs],
        outs,
        [pltpu.VMEM((rows + 8, width), wide)],
        args,
    )


def piece_at(bits, which, piece, width):
    place = bits[which] if piece == 0 else 1 - bits[which]
    return pl.ds(pl.multiple_of(place * width, width), width)


def ffn_kernel(bits, tok, mine0, mine1, theirs0, theirs1, gains, g0, g1, g2, u0, u1, u2, n2, res, gate, up, act):
    width = g1.shape[0]

    @pl.when(pl.program_id(0) == 0)
    def _():
        for h, (mine, theirs) in enumerate(((mine0, theirs0), (mine1, theirs1))):
            res[h] = tok[h, : res.shape[1], :].astype(wide) + (
                mine[...].astype(wide) + theirs[...].astype(wide)
            )
        scale = row_scale([res[0], res[1]])
        for h in range(2):
            n2[h] = (res[h] * scale * gains[h]).astype(low)

    for which, (out, w0, w1, w2) in enumerate(((gate, g0, g1, g2), (up, u0, u1, u2))):
        total = dot_of(n2[0], w0[...], 1, 0)
        for piece, w in enumerate((w1, w2)):
            total += dot_of(n2[1, :, piece_at(bits, which, piece, width)], w[...], 1, 0)
        out[...] = total
    value = gate[...]
    act[...] = (value * jax.nn.sigmoid(value) * up[...]).astype(low)


def ffn_forward(bits, tok, mine, theirs, gains, weights):
    rows, width = mine[0].shape
    cols = weights[0].shape[1]
    tile = cols // 3
    both = (2, rows, width)
    full = whole_spec(both)
    wide_tile = pl.BlockSpec((rows, tile), lambda i, *_: (0, i))
    weight_specs = [pl.BlockSpec((w.shape[0], tile), lambda i, *_: (0, i)) for w in weights]
    return local_call(
        ffn_kernel,
        (3,),
        [whole_spec(tok.shape)]
        + [whole_spec((rows, width))] * 4
        + [whole_spec(gains.shape)]
        + weight_specs,
        [full, full, wide_tile, wide_tile, wide_tile],
        [
            shape_of(both, low),
            shape_of(both, wide),
            shape_of((rows, cols), wide),
            shape_of((rows, cols), wide),
            shape_of((rows, cols), low),
        ],
        [],
        (bits, tok, *mine, *theirs, gains, *weights),
        prefetch=1,
    )


def ffn_back_kernel(
    bits, cot, d_own, d_other, gate, up, g0, g1, g2, u0, u1, u2, g_gate, g_up, part0, part1, total
):
    width = g1.shape[0]

    @pl.when(pl.program_id(0) == 0)
    def _():
        total[...] = jnp.zeros_like(total)

    start = cot.shape[1] - gate.shape[0]
    g_act = dot_of(cot[0, start:, :], d_own[...], 1, 1) + dot_of(cot[1, start:, :], d_other[...], 1, 1)
    value = gate[...]
    sigma = jax.nn.sigmoid(value)
    g_gate[...] = (g_act * up[...] * sigma * (1.0 + value * (1.0 - sigma))).astype(low)
    g_up[...] = (g_act * (value * sigma)).astype(low)
    total[0] += dot_of(g_gate[...], g0[...], 1, 1) + dot_of(g_up[...], u0[...], 1, 1)
    for which, (grad, w1, w2) in enumerate(((g_gate, g1, g2), (g_up, u1, u2))):
        for piece, w in enumerate((w1, w2)):
            total[1, :, piece_at(bits, which, piece, width)] += dot_of(grad[...], w[...], 1, 1)

    @pl.when(pl.program_id(0) == pl.num_programs(0) - 1)
    def _():
        part0[...] = total[0].astype(low)
        part1[...] = total[1].astype(low)


def ffn_backward(bits, cot, downs, gate, up, weights):
    rows, cols = gate.shape
    tile = cols // 3
    part = (rows, cot.shape[2])
    wide_tile = pl.BlockSpec((rows, tile), lambda i, *_: (0, i))
    weight_specs = [pl.BlockSpec((w.shape[0], tile), lambda i, *_: (0, i)) for w in weights]
    down_spec = pl.BlockSpec((tile, downs[0].shape[1]), lambda i, *_: (i, 0))
    return local_call(
        ffn_back_kernel,
        (3,),
        [whole_spec(cot.shape), down_spec, down_spec, wide_tile, wide_tile] + weight_specs,
        [wide_tile, wide_tile, whole_spec(part), whole_spec(part)],
        [shape_of((rows, cols), low)] * 2 + [shape_of(part, low)] * 2,
        [pltpu.VMEM((2, *part), wide)],
        (bits, cot, *downs, gate, up, *weights),
        prefetch=1,
    )


def put(outs, half, rows, value):
    if len(outs) == 2:
        outs[half][rows, :] = value.astype(low)
    else:
        outs[0][half, rows, :] = value.astype(low)


def chunk_outs(split, rows, cols):
    if split:
        return [whole_spec((rows, cols))] * 2, [shape_of((rows, cols), low)] * 2
    return [whole_spec((2, rows, cols))], [shape_of((2, rows, cols), low)]


def pair_grad_kernel(n2, g_gate, g_up, *outs):
    rows = n2.shape[2]
    for h in range(2):
        for side, grad in enumerate((g_gate, g_up)):
            put(outs, h, slice(side * rows, (side + 1) * rows), dot_of(n2[h], grad[...], 0, 0))


def pair_grads(n2, g_gate, g_up, at, rows, split):
    specs, shapes = chunk_outs(split, 2 * rows, g_gate.shape[1])
    outs = local_call(
        pair_grad_kernel,
        (1,),
        [
            pl.BlockSpec((2, n2.shape[1], rows), lambda i: (0, 0, at)),
            whole_spec(g_gate.shape),
            whole_spec(g_up.shape),
        ],
        specs,
        shapes,
        [],
        (n2, g_gate, g_up),
    )
    return tuple(outs) if split else outs[0]


def down_grad_kernel(act, cot, *outs):
    start = cot.shape[1] - act.shape[0]
    for h in range(2):
        put(outs, h, slice(None), dot_of(act[...], cot[h, start:, :], 0, 0))


def down_grads(act, cot, at, rows, split):
    specs, shapes = chunk_outs(split, rows, cot.shape[2])
    outs = local_call(
        down_grad_kernel,
        (1,),
        [pl.BlockSpec((act.shape[0], rows), lambda i: (0, at)), whole_spec(cot.shape)],
        specs,
        shapes,
        [],
        (act, cot),
    )
    return tuple(outs) if split else outs[0]


def branch_back_kernel(
    mine0, mine1, theirs0, theirs1, res, cot, gains, taps, own, other, gate_b, gate_c, gate_x, conv,
    g_res, g_low, g_proj, gain_grad, tap_grad, ext, ext_grad,
):
    _, rows, width = res.shape
    scale = row_scale([res[0], res[1]])
    grads = [
        mine[...].astype(wide) + theirs[...].astype(wide)
        for mine, theirs in ((mine0, theirs0), (mine1, theirs1))
    ]
    inner = sum(
        jnp.sum(grads[h] * gains[h] * res[h], axis=1, keepdims=True) for h in range(2)
    )
    factor = scale * scale * scale * inner / D
    for h in range(2):
        gain_grad[h] = jnp.sum(grads[h] * res[h] * scale, axis=0, keepdims=True)
        value = cot[h, cot.shape[1] - rows :, :].astype(wide) + (scale * (grads[h] * gains[h]) - res[h] * factor)
        g_res[h] = value
        g_low[h] = value.astype(low)
    g_hidden = dot_of(g_low[0], own[...], 1, 1) + dot_of(g_low[1], other[...], 1, 1)
    g_proj[1, :rows, :] = (g_hidden * conv[...]).astype(low)
    g_conv = g_hidden * gate_c[:rows, :]
    ext_grad[:rows, :] = g_conv
    ext_grad[rows:, :] = jnp.zeros((8, width), wide)
    ext[8 : 8 + rows, :] = gate_b[:rows, :] * gate_x[:rows, :]
    ext[6:8, :] = gate_b[rows : rows + 2, :] * gate_x[rows : rows + 2, :]
    for k in range(3):
        tap_grad[k : k + 1, :] = jnp.sum(
            g_conv * ext[6 + k : 6 + k + rows, :], axis=0, keepdims=True
        )
    g_mixed = sum(taps[2 - k] * ext_grad[k : k + rows, :] for k in range(3))
    g_proj[0, :rows, :] = (g_mixed * gate_x[:rows, :]).astype(low)
    g_proj[2, :rows, :] = (g_mixed * gate_b[:rows, :]).astype(low)
    tails = g_proj.shape[1] - rows
    row = lax.broadcasted_iota(jnp.int32, (tails, width), 0)
    first, second = ext_grad[0:1, :], ext_grad[1:2, :]
    g_before = jnp.where(
        row == 0,
        taps[0] * first,
        jnp.where(row == 1, taps[1] * first + taps[0] * second, 0.0),
    )
    g_proj[0, rows:, :] = (g_before * gate_x[rows:, :]).astype(low)
    g_proj[1, rows:, :] = jnp.zeros((tails, width), low)
    g_proj[2, rows:, :] = (g_before * gate_b[rows:, :]).astype(low)


def branch_backward(mine, theirs, res, cot, gains, taps, own, other, gates, conv):
    _, rows, width = res.shape
    long = gates[0].shape[0]
    out_weight = pl.BlockSpec((width, width), lambda i, *_: (3, 0))
    outs = [
        shape_of(res.shape, wide),
        shape_of(res.shape, low),
        shape_of((3, long, width), low),
        shape_of((2, 1, width), wide),
        shape_of((3, width), wide),
    ]
    full = whole_spec(res.shape)
    return local_call(
        branch_back_kernel,
        (1,),
        [whole_spec((rows, width))] * 4
        + [full, whole_spec(cot.shape), whole_spec(gains.shape), whole_spec(taps.shape)]
        + [out_weight, out_weight]
        + [whole_spec(g.shape) for g in gates]
        + [whole_spec(conv.shape)],
        [whole_spec(o.shape) for o in outs],
        outs,
        [pltpu.VMEM((rows + 8, width), wide), pltpu.VMEM((rows + 8, width), wide)],
        (*mine, *theirs, res, cot, gains, taps, own, other, *gates, conv),
    )


def branch_grad_kernel(left0, left1, right0, right1, own, other):
    rows = own.shape[0] // 2
    for h, out in enumerate((own, other)):
        for k, (left, right) in enumerate(((left0, right0), (left1, right1))):
            one = left[h] if len(left.shape) == 3 else left[...]
            two = right[h] if k == 1 and len(left.shape) == 2 else right[0]
            out[k * rows : (k + 1) * rows, :] = dot_of(one, two, 0, 0).astype(low)


def branch_grads(n1, g_proj, gate, second):
    width = n1.shape[2]
    gate_spec = pl.BlockSpec((1, *g_proj.shape[1:]), lambda i: (gate, 0, 0))
    if second is None:
        left, right = n1, g_proj
        right_spec = pl.BlockSpec((1, *g_proj.shape[1:]), lambda i: (gate + 1, 0, 0))
    else:
        left, right = second
        right_spec = whole_spec(right.shape)
    specs, shapes = chunk_outs(True, 2 * width, width)
    return local_call(
        branch_grad_kernel,
        (1,),
        [whole_spec(n1.shape), whole_spec(left.shape), gate_spec, right_spec],
        specs,
        shapes,
        [],
        (n1, left, g_proj, right),
    )


def shards(
    tokens,
    cotangent,
    input_projection_weight,
    conv_weight,
    output_projection_weight,
    norm_gains,
    gate_up_weight,
    down_projection_weight,
    in_first,
    in_second,
    conv_first,
    conv_second,
    out_first,
    out_second,
    gain_first,
    gain_second,
    gu_first,
    gu_second,
    down_first,
    down_second,
):
    feat_cols = tokens.shape[1]
    branch_cols = conv_weight.shape[1]
    hidden_cols = down_projection_weight.shape[0]
    block_rows = tokens.shape[0]
    seq_len = max(SEQ_LEAST, block_rows * lax.axis_size("dp") * lax.axis_size("col"))
    data_pos = lax.axis_index("dp")
    row_pos = lax.axis_index("row")
    col_pos = lax.axis_index("col")
    home = row_pos == col_pos
    tail_rows = 16

    in_low = jnp.transpose(input_projection_weight, (1, 0, 2)).astype(low).reshape(-1, branch_cols)
    io_low = jnp.concatenate([in_low, output_projection_weight.astype(low)])
    io_share = share_of(io_low, (1, 0))
    io_got = swap(io_share, "col")
    row_start = (data_pos * lax.axis_size("row") + row_pos) * block_rows
    tail = from_behind(tokens[-2:], ("dp", "row"), 1)
    tail = jnp.where(row_start % seq_len != 0, tail, jnp.zeros_like(tail))
    spare = jnp.zeros((tail_rows - 8, feat_cols), low)
    gain_parts = []
    left = norm_gains
    for _ in range(3):
        gain_parts.append(lax.reduce_precision(left, 8, 7))
        left = left - gain_parts[-1]
    gain_parts = jnp.concatenate(gain_parts).astype(low)
    extra = tie(jnp.concatenate([tail, gain_parts, spare]))
    block = jnp.concatenate([tie(tokens, io_share), extra, cotangent])
    away = to_home(block)
    gu_weight = to_linear(gate_up_weight)
    gate_low, up_low = split_pairs(gu_weight, feat_cols, hidden_cols)
    down_low = down_projection_weight.astype(low)
    both = jnp.stack([block, away])
    both = jnp.where(home, both, home_to_sibling(both))
    gains = both[:, block_rows + 2 : block_rows + 8].astype(wide)
    gains = gains[:, 0:2] + gains[:, 2:4] + gains[:, 4:6]
    gains = [gains[:, k : k + 1] for k in range(2)]
    gate_got = swap(tie(share_of(gate_low, (1, 0)), io_got), "col")
    up_got = swap(tie(share_of(up_low, (0, 1)), away), "col")
    down_got = swap(tie(down_low, gate_got), "col")
    io_pair = keep_or_join(0, io_got, flip(io_got, 0))
    io_other = keep_or_join(1, io_pair, flip(io_pair, 1))
    gate_pair = keep_or_join(0, gate_got, flip(tie(gate_got, io_pair), 0))
    up_pair = keep_or_join(1, up_got, flip(tie(up_got, io_pair), 1))
    gate_more = flip(gate_pair, 1)
    up_more = flip(up_pair, 0)
    weights = [gate_low, gate_pair, gate_more, up_low, up_pair, up_more]
    bits = jnp.stack([dp_bit(1), dp_bit(0)]).astype(jnp.int32)
    downs = [down_low, down_got]

    n1, gate_b, gate_c, gate_x, conv, hidden, *branch = branch_forward(
        both, block_rows, tail_rows, gains[0], conv_weight, io_low, io_other
    )
    n2, res, gate, upper, act = ffn_forward(
        bits, both, branch, swap_halves(branch), gains[1], weights
    )

    turns = Turns()
    orders = dict(D="xyl", d="ylx", a="xyl", b="lyx", c="xyl", e="lyx", I="xyl", i="xyl")
    down_half = hidden_cols // 2
    for k, name in enumerate("Dd"):
        split = orders[name][0] == "x"
        turns.add(name, down_grads(act, both, k, down_half, split), orders[name])
    turns.run("Dd")
    g_gate, g_up, *part_two = ffn_backward(
        bits, tie(both, *turns.after), downs, gate, upper, weights
    )
    quarter = feat_cols // 4
    for k, name in enumerate("abce"):
        split = orders[name][0] == "x"
        turns.add(name, pair_grads(n2, g_gate, g_up, k, quarter, split), orders[name])
    turns.run("abcDe")
    g_res, g_branch, g_proj, gain_two_grad, conv_grad = branch_backward(
        part_two,
        swap_halves(part_two),
        tie(res, *turns.after),
        both,
        gains[1],
        conv_weight,
        io_low,
        io_other,
        (gate_b, gate_c, gate_x),
        conv,
    )
    turns.add("I", branch_grads(n1, g_proj, 0, None), orders["I"])
    io_last = branch_grads(n1, g_proj, 2, (hidden, g_branch))
    turns.after += tuple(io_last)
    turns.run("IdabD")

    g_late = tie(g_proj, *turns.after)
    io_half = [half.reshape(4, feat_cols, branch_cols) for half in (io_low, io_other)]
    g_part = jnp.stack(
        [sum(mul_t(g_late[g], io_half[h][g]) for g in range(3)).astype(low) for h in range(2)]
    )
    g_long = g_part.astype(wide) + swap(g_part, "row").astype(wide)
    tok = both[:, : block_rows + 2].astype(wide)
    scale = lax.rsqrt(jnp.sum(tok * tok, axis=(0, 2)) / D + norm_eps)[None, :, None]
    gain_one_grad = jnp.sum(g_long[:, : block_rows + 2] * tok * scale, axis=1)
    small = [
        jnp.concatenate([conv_grad, gain_one_grad[h : h + 1], gain_two_grad[h]]) for h in range(2)
    ]
    small = [jnp.pad(part, ((0, 59), (0, 0))).astype(low) for part in small]
    turns.add("i", [jnp.concatenate([io_last[h], small[h]]) for h in range(2)], orders["i"])
    turns.run("iacebdDIcaeDciIabDdcieIDabdacibceIdbiedIeiIi")
    turns.finish()
    sums, seen = turns.done, turns.seen

    back = tie(g_long[::-1, block_rows : block_rows + 2], seen["i"][4])
    back = from_behind(back, ("dp", "col"), -1)
    g_n1 = g_long[:, :block_rows].at[:, -2:].add(back)
    tok, scale = tok[:, :block_rows], scale[:, :block_rows]
    weighted = g_n1 * gains[0]
    inner = jnp.sum(weighted * tok, axis=(0, 2))[None, :, None]
    tok_half = (g_res + (scale * weighted - tok * (scale * scale * scale * inner / D))).astype(low)
    token_grad = jnp.where(home, tok_half[0], home_to_away(tok_half[1]))
    act = tie(act, seen["D"][1])
    ffn = jnp.stack([mul(act, downs[h]) for h in range(2)])
    out_half = (res + (ffn + sibling_to_home(ffn.astype(low)).astype(wide))).astype(low)
    output = jnp.where(home, out_half[0], home_to_away(out_half[1]))

    small = sums["i"][2 * feat_cols : 2 * feat_cols + 5].astype(wide)
    conv_grad, gains_grad = small[:3], small[3:]

    conv_m, conv_v, conv_u = lamb_moments(conv_weight, conv_grad, conv_first, conv_second, 0.0)
    gain_m, gain_v, gain_u = lamb_moments(norm_gains, gains_grad, gain_first, gain_second, 0.0)

    def in_flat(values):
        return jnp.transpose(values, (1, 0, 2)).reshape(3 * feat_cols, branch_cols)

    def in_back(values):
        return jnp.transpose(values.reshape(3, feat_cols, branch_cols), (1, 0, 2))

    def gu_back(values):
        return from_linear(values, feat_cols, 2)

    (down_m, down_v, down_u), down_norms = lamb_dense(
        (down_projection_weight, down_first, down_second),
        [(sums["Dd"[k]], 0, k * down_half, down_half) for k in (0, 1)],
        384,
    )
    gu_state = (gu_weight, to_linear(gu_first), to_linear(gu_second))
    pairs = 2 * hidden_cols // 128
    gu_rows = 32
    gu_new, gu_norms = None, 0.0
    for k in (0, 2, 1, 3):
        grad = sums["abce"[k]]
        blocks = grad.shape[0] // 2 // gu_rows
        gu_new, squares = lamb_call(
            lamb_pairs,
            gu_state,
            [(grad, gu_rows, 0), (grad, gu_rows, blocks)],
            gu_rows * pairs,
            k * blocks,
            blocks,
            gu_new,
            [pltpu.VMEM((gu_rows * pairs, 128), wide)],
        )
        gu_norms = gu_norms + squares
    gu_m, gu_v, gu_u = gu_new
    in_weight = in_flat(input_projection_weight)
    (in_m, in_v, in_u), in_norms = lamb_dense(
        (in_weight, in_flat(in_first), in_flat(in_second)),
        [
            (sums["I"], 0, 0, 2 * feat_cols),
            (sums["i"], 0, 2 * feat_cols, feat_cols),
        ],
        256,
    )
    (out_m, out_v, out_u), out_norms = lamb_dense(
        (output_projection_weight, out_first, out_second),
        [(sums["i"], feat_cols, 0, branch_cols)],
        256,
    )
    col_first = (col_pos == 0).astype(wide)
    row_first = (row_pos == 0).astype(wide)
    partial_sums = jnp.stack(
        [
            in_norms,
            square_pair(conv_weight, conv_u) * col_first,
            out_norms,
            square_pair(norm_gains[0], gain_u[0]) * row_first,
            square_pair(norm_gains[1], gain_u[1]) * row_first,
            gu_norms,
            down_norms,
        ]
    )
    trust_norms = jnp.sqrt(lax.psum(partial_sums, ("row", "col")))
    gains_new = jnp.stack(
        [
            apply_trust(norm_gains[0], gain_u[0], trust_norms[3]),
            apply_trust(norm_gains[1], gain_u[1], trust_norms[4]),
        ]
    )
    return (
        output,
        token_grad,
        in_back(apply_trust(in_weight, in_u, trust_norms[0])),
        in_back(in_m),
        in_back(in_v),
        apply_trust(conv_weight, conv_u, trust_norms[1]),
        conv_m,
        conv_v,
        apply_trust(output_projection_weight, out_u, trust_norms[2]),
        out_m,
        out_v,
        gains_new,
        gain_m,
        gain_v,
        gu_back(apply_trust(gu_weight, gu_u, trust_norms[5])),
        gu_back(gu_m),
        gu_back(gu_v),
        apply_trust(down_projection_weight, down_u, trust_norms[6]),
        down_m,
        down_v,
        trust_norms,
    )


def solution(mesh):
    in_specs = (
        P(("dp", "row"), "col"),
        P(("dp", "row"), "col"),
        P("col", None, "row"),
        P(None, "row"),
        P("row", "col"),
        P(None, "col"),
        P("col", None, "row"),
        P("row", "col"),
        P("col", None, "row"),
        P("col", None, "row"),
        P(None, "row"),
        P(None, "row"),
        P("row", "col"),
        P("row", "col"),
        P(None, "col"),
        P(None, "col"),
        P("col", None, "row"),
        P("col", None, "row"),
        P("row", "col"),
        P("row", "col"),
    )
    out_specs = (
        P(("dp", "row"), "col"),
        P(("dp", "row"), "col"),
        P("col", None, "row"),
        P("col", None, "row"),
        P("col", None, "row"),
        P(None, "row"),
        P(None, "row"),
        P(None, "row"),
        P("row", "col"),
        P("row", "col"),
        P("row", "col"),
        P(None, "col"),
        P(None, "col"),
        P(None, "col"),
        P("col", None, "row"),
        P("col", None, "row"),
        P("col", None, "row"),
        P("row", "col"),
        P("row", "col"),
        P("row", "col"),
        P(),
    )
    return jax.shard_map(shards, mesh=mesh, in_specs=in_specs, out_specs=out_specs, check_vma=False)
```

```python
import functools

import jax
import jax.numpy as jnp
from jax import lax
from jax.experimental import pallas as pl
from jax.experimental.layout import Layout, with_layout_constraint
from jax.experimental.pallas import tpu as pltpu
from jax.sharding import PartitionSpec as P

D = 1024
SEQ_LEAST = 4096
STEP = 5
MIB = 1024 * 1024


norm_eps = 1e-05
adam_eps = 1e-06
beta_one = 0.5
beta_two = 0.6
learn_rate = 0.5
decay_rate = 0.01
low = jnp.bfloat16
wide = jnp.float32


def from_behind(block, axis, distance):
    devices = range(lax.axis_size(axis))
    route = [(i - distance, i) for i in devices if i - distance in devices]
    return lax.ppermute(block, axis, route)


def swap(values, axis):
    return lax.ppermute(values, axis, [(0, 1), (1, 0)])


def swap_halves(halves):
    return [swap(half, "row") for half in halves]


def to_home(values):
    return lax.ppermute(values, ("row", "col"), [(1, 0), (2, 3)])


def home_to_sibling(values):
    return lax.ppermute(values, ("row", "col"), [(0, 2), (3, 1)])


def home_to_away(values):
    return lax.ppermute(values, ("row", "col"), [(0, 1), (3, 2)])


def sibling_to_home(values):
    return lax.ppermute(values, ("row", "col"), [(2, 0), (1, 3)])


def contract(left, right, left_dim, right_dim):
    return lax.dot_general(
        left, right, (((left_dim,), (right_dim,)), ((), ())), preferred_element_type=wide
    )


def mul(left, right):
    return contract(left, right, 1, 0)


def mul_t(left, right):
    return contract(left, right, 1, 1)


def t_mul(left, right):
    return contract(left, right, 0, 0)


def lamb_moments(weight, grad, first, second, decay):
    first_new = beta_one * first + (1.0 - beta_one) * grad
    second_new = beta_two * second + (1.0 - beta_two) * grad * grad
    direction = (first_new * (1.0 / (1.0 - beta_one**STEP))) / (
        jnp.sqrt(second_new * (1.0 / (1.0 - beta_two**STEP))) + adam_eps
    ) + decay * weight
    return (first_new, second_new, direction)


def square_pair(weight, direction):
    return jnp.stack([jnp.sum(weight * weight), jnp.sum(direction * direction)])


def kernel_call(kernel, grid, in_specs, out_specs, out_shape, scratch, args, aliases=None, mib=1):
    return pl.pallas_call(
        kernel,
        grid_spec=pltpu.PrefetchScalarGridSpec(
            num_scalar_prefetch=1,
            grid=grid,
            in_specs=in_specs,
            out_specs=out_specs,
            scratch_shapes=scratch,
        ),
        out_shape=out_shape,
        input_output_aliases=aliases or {},
        compiler_params=pltpu.CompilerParams(vmem_limit_bytes=48 * MIB),
        cost_estimate=pl.CostEstimate(flops=0, bytes_accessed=mib * MIB, transcendentals=0),
    )(*args)


SCALARS = pl.BlockSpec(memory_space=pltpu.SMEM)


def norm_kernel(where, grad, *refs):
    sums = refs[-1]
    groups = [refs[:3], refs[3:6]][: len(refs) // 3]
    rows = groups[0][0].shape[0]
    zero = jnp.zeros((8, groups[0][0].shape[1]), wide)
    for k, (p, m, v) in enumerate(groups):

        def body(at, total):
            here = pl.ds(pl.multiple_of(at * 16, 16), 16)
            weight = p[here, :]
            direction = lamb_moments(
                weight, grad[here, :].astype(wide), m[here, :], v[here, :], decay_rate
            )[2]
            return tuple(
                t + (sq[:8] + sq[8:])
                for t, sq in zip(total, (weight * weight, direction * direction))
            )

        total = lax.fori_loop(0, rows // 16, body, (zero, zero))
        mine = 1.0 if len(groups) == 1 else ((where[0] >> 1) == k).astype(wide)
        for j in range(2):
            sums[2 * k + j] = jnp.sum(total[j]) * mine


def norm_pairs_kernel(where, grad, p, m, v, sums):
    rows, cols = grad.shape
    tiles = cols // 128
    side = where[0] >> 1
    zero = jnp.zeros((8, 128), wide)
    total = [zero, zero]
    for tile in range(tiles):
        here = pl.ds(2 * tile + side, rows, stride=2 * tiles)
        weight = p[here, :]
        direction = lamb_moments(
            weight, grad[:, tile * 128 : (tile + 1) * 128].astype(wide), m[here, :], v[here, :], decay_rate
        )[2]
        for j, sq in enumerate((weight * weight, direction * direction)):
            total[j] = total[j] + jnp.sum((sq).reshape(rows // 8, 8, 128), axis=0)
    for j in range(2):
        sums[j] = jnp.sum(total[j])


def share_norms(where, grad, states, rows, pairs=False):
    specs, args = [], []
    for state, at in states:
        for array in state:
            if pairs:
                spec = pl.BlockSpec(
                    (rows, array.shape[1]), lambda i, w, at=at: (at + (w[0] & 1), 0)
                )
            elif len(states) == 2:
                spec = pl.BlockSpec(
                    (rows, array.shape[1]), lambda i, w, at=at: (at + (w[0] & 1), 0)
                )
            else:
                spec = pl.BlockSpec((rows, array.shape[1]), lambda i, w, at=at: (at + w[0], 0))
            specs.append(spec)
            args.append(array)
    return kernel_call(
        norm_pairs_kernel if pairs else norm_kernel,
        (1,),
        [whole_spec(grad.shape)] + specs,
        SCALARS,
        jax.ShapeDtypeStruct((2 * len(states),), wide),
        [],
        (where, grad, *args),
    )


def lamb_loop(refs, outs, ratio, rows, step, pick):
    p, m, v = refs

    def body(at, carry):
        here = pl.ds(pl.multiple_of(at * step, step), step)
        weight = p[here, :]
        first_new, second_new, direction = lamb_moments(
            weight, pick(here), m[here, :], v[here, :], decay_rate
        )
        outs[0][here, :] = weight - ratio * direction
        outs[1][here, :] = first_new
        outs[2][here, :] = second_new
        return carry

    lax.fori_loop(0, rows // step, body, 0)


def lamb_plain(half_of_block, where, ratio, part, got, p, m, v, *outs):
    use = half_of_block(pl.program_id(0)) == (where[0] >> 1)

    def pick(here):
        return jnp.where(use, part[here, :].astype(wide), got[here, :].astype(wide))

    lamb_loop((p, m, v), outs, ratio[0], p.shape[0], 16, pick)


def lamb_pairs(where, ratio, part, got, p, m, v, p_out, m_out, v_out, mixed):
    rows, cols = part.shape
    tiles = cols // 128
    for value, order in ((0, (part, got)), (1, (got, part))):

        @pl.when((where[0] >> 1) == value)
        def _():
            for tile in range(tiles):
                for side, ref in enumerate(order):
                    mixed[pl.ds(2 * tile + side, rows, stride=2 * tiles), :] = ref[
                        :, tile * 128 : (tile + 1) * 128
                    ].astype(wide)

    lamb_loop(
        (p, m, v), (p_out, m_out, v_out), ratio[0], p.shape[0], 64, lambda here: mixed[here, :]
    )


def lamb_call(kernel, where, ratio, grad, grad_block, grad_at, state, block, start, count, before, scratch):
    rows, cols = state[0].shape
    flat = pl.BlockSpec((block, cols), lambda i, w: (i + start, 0))
    grad_spec = pl.BlockSpec((grad_block, grad[0].shape[1]), lambda i, w: (grad_at(i), 0))
    whole = jax.ShapeDtypeStruct((rows, cols), wide)
    args = [where, ratio, *grad, *state]
    specs = [SCALARS, grad_spec, grad_spec, flat, flat, flat]
    run, aliases = kernel, {}
    if before is not None:
        aliases = {len(args) + k: k for k in range(3)}

        def run(*refs):
            kernel(*refs[: len(args)], *refs[len(args) + 3 :])

    return list(
        kernel_call(
            run,
            (count,),
            specs + [pl.BlockSpec(memory_space=pl.ANY)] * len(aliases),
            [flat, flat, flat],
            [whole, whole, whole],
            scratch,
            (*args, *(before or [])),
            aliases,
            mib=26 * count * block * cols // MIB,
        )
    )


def to_linear(values):
    rows, sides, cols = values.shape
    split = with_layout_constraint(
        values.reshape(rows, sides, cols // 128, 128), Layout(major_to_minor=(0, 2, 1, 3))
    )
    return split.transpose(0, 2, 1, 3).reshape(rows * sides * cols // 128, 128)


def from_linear(values, rows, sides):
    cols = values.size // (rows * sides)
    split = values.reshape(rows, cols // 128, sides, 128).transpose(0, 2, 1, 3)
    split = with_layout_constraint(split, Layout(major_to_minor=(0, 2, 1, 3)))
    return split.reshape(rows, sides, cols)


def apply_trust(weight, direction, norms):
    return weight - learn_rate * (norms[0] / (norms[1] + adam_eps)) * direction


def flip(values, bit):
    size = lax.axis_size("dp")
    return lax.ppermute(values, "dp", [(i, i ^ (1 << bit)) for i in range(size)])


def dp_bit(bit):
    return (lax.axis_index("dp") >> bit) & 1


def rows_of(values, start, rows):
    return lax.dynamic_slice_in_dim(values, start, rows, 0)


def total_of(pieces):
    total = pieces[0].astype(wide)
    for piece in pieces[1:]:
        total = total + piece.astype(wide)
    return total


def tie(values, *deps):
    return lax.optimization_barrier((values, *deps))[0]


def low_total(pieces):
    return total_of(pieces).astype(low)


def keep_or_join(bit, part, other):
    return jnp.where(
        dp_bit(bit) == 0,
        jnp.concatenate([part, other]),
        jnp.concatenate([other, part]),
    )


def share_of(weight, order):
    rows = weight.shape[0] // (1 << len(order))
    index = 0
    for bit in order:
        index = 2 * index + dp_bit(bit)
    return rows_of(weight, index * rows, rows)


def half_of(piece, place):
    rows = piece.shape[-2] // 2
    return lax.dynamic_slice_in_dim(piece, place * rows, rows, piece.ndim - 2)


def chunk_sum(chunk, order):
    bits = {"y": 0, "l": 1}
    steps = [name if name == "x" else bits[name] for name in order]
    pieces = [chunk]
    for step in steps:
        if step == "x":
            whole = len(pieces) == 1
            got = yield step, pieces[0][1] if whole else low_total([piece[1] for piece in pieces])
            pieces = [piece[0] for piece in pieces] + [got]
        else:
            here = dp_bit(step)
            got = yield step, low_total([half_of(piece, 1 - here) for piece in pieces])
            pieces = [half_of(piece, here) for piece in pieces] + [got]
    part = low_total(pieces)
    for step in range((lax.axis_size("dp") - 1).bit_length()):
        if step not in steps:
            got = yield step, part
            part = low_total([part, got])
    share = part
    first, second = [step for step in steps if step != "x"]
    got = yield second, part
    part = keep_or_join(second, part, got)
    got = yield first, part
    return share, part, got


def where_of(order):
    bits = {"y": 0, "l": 1}
    first, second = [bits[name] for name in order if name != "x"]
    return (2 * dp_bit(first) + dp_bit(second)).astype(jnp.int32).reshape(1)


def move(step, send):
    return swap(send, "col") if step == "x" else flip(send, step)


class Turns:
    def __init__(self):
        self.chunks = {}
        self.arrivals = {}
        self.seen = {}
        self.done = {}
        self.after = ()

    def add(self, name, chunk, order):
        self.chunks[name] = chunk_sum(chunk, order)

    def turn(self, name):
        got = self.arrivals.get(name)
        try:
            if got is None:
                self.seen[name] = []
                step, send = next(self.chunks[name])
                send = tie(send, *self.after)
            else:
                got = tie(got, *self.after)
                self.seen[name].append(got)
                step, send = self.chunks[name].send(got)
        except StopIteration as end:
            self.done[name] = end.value
            return
        self.arrivals[name] = move(step, send)
        self.after = (send,)

    def run(self, names):
        for name in names:
            if name not in self.done:
                self.turn(name)

    def finish(self):
        while len(self.done) < len(self.chunks):
            self.run(self.chunks)


def deinterleave(pairs, gate, up):
    rows, cols = gate.shape
    tiles = cols // 128
    for tile in range(tiles):
        for side, out in enumerate((gate, up)):
            out[:, tile * 128 : (tile + 1) * 128] = pairs[
                pl.ds(2 * tile + side, rows, stride=2 * tiles), :
            ].astype(low)


def split_pairs(linear, rows, cols):
    block = 64
    half = jax.ShapeDtypeStruct((rows, cols), low)
    out_spec = pl.BlockSpec((block, cols), lambda i: (i, 0))
    return pl.pallas_call(
        deinterleave,
        grid=(rows // block,),
        in_specs=[pl.BlockSpec((block * 2 * cols // 128, 128), lambda i: (i, 0))],
        out_specs=[out_spec, out_spec],
        out_shape=[half, half],
        compiler_params=pltpu.CompilerParams(vmem_limit_bytes=24 * MIB),
        cost_estimate=pl.CostEstimate(
            flops=rows * cols, bytes_accessed=12 * rows * cols, transcendentals=0
        ),
    )(linear)


def dot_of(left, right, left_dim, right_dim):
    return lax.dot_general(
        left, right, (((left_dim,), (right_dim,)), ((), ())), preferred_element_type=wide
    )


def local_call(kernel, grid, in_specs, out_specs, out_shape, scratch, args, prefetch=0):
    return pl.pallas_call(
        kernel,
        grid_spec=pltpu.PrefetchScalarGridSpec(
            num_scalar_prefetch=prefetch,
            grid=grid,
            in_specs=in_specs,
            out_specs=out_specs,
            scratch_shapes=scratch,
        ),
        out_shape=out_shape,
        compiler_params=pltpu.CompilerParams(vmem_limit_bytes=48 * MIB),
        cost_estimate=pl.CostEstimate(flops=0, bytes_accessed=MIB, transcendentals=0),
    )(*args)


def whole_spec(shape):
    return pl.BlockSpec(shape, lambda *_: (0,) * len(shape))


def shape_of(dims, kind):
    return jax.ShapeDtypeStruct(dims, kind)


def row_scale(halves):
    total = sum(jnp.sum(half * half, axis=1, keepdims=True) for half in halves)
    return lax.rsqrt(total / D + norm_eps)


def branch_kernel(tok, gains, taps, own, other, n1, gate_b, gate_c, gate_x, conv, hidden, part0, part1, ext):
    long, width = n1.shape[1:]
    rows = conv.shape[0]
    step = long // 3

    def gates(at, carry):
        here = pl.ds(pl.multiple_of(at * step, step), step)
        halves = [tok[h, here, :].astype(wide) for h in range(2)]
        scale = row_scale(halves)
        for h in range(2):
            n1[h, here, :] = (halves[h] * scale * gains[h]).astype(low)
        for g, out in enumerate((gate_b, gate_c, gate_x)):
            w = slice(g * width, (g + 1) * width)
            out[here, :] = dot_of(n1[0, here, :], own[w, :], 1, 0) + dot_of(
                n1[1, here, :], other[w, :], 1, 0
            )
        return carry

    lax.fori_loop(0, 3, gates, 0)
    ext[8 : 8 + rows, :] = gate_b[:rows, :] * gate_x[:rows, :]
    ext[6:8, :] = gate_b[rows : rows + 2, :] * gate_x[rows : rows + 2, :]
    w_out = slice(3 * width, 4 * width)
    quarter = rows // 4
    for at in range(4):
        start = at * quarter
        taken = slice(start, start + quarter)
        value = sum(taps[k] * ext[start + 6 + k : start + 6 + k + quarter, :] for k in range(3))
        conv[taken, :] = value
        low_hidden = (gate_c[taken, :] * value).astype(low)
        hidden[taken, :] = low_hidden
        for part, weight in ((part0, own), (part1, other)):
            part[taken, :] = dot_of(low_hidden, weight[w_out, :], 1, 0).astype(low)


def branch_forward(tok, rows, tails, gains, taps, own, other):
    width = tok.shape[2]
    gate = shape_of((rows + tails, width), wide)
    outs = [
        shape_of((2, rows + tails, width), low),
        gate,
        gate,
        gate,
        shape_of((rows, width), wide),
        shape_of((rows, width), low),
        shape_of((rows, width), low),
        shape_of((rows, width), low),
    ]
    args = (tok, gains, taps, own, other)
    return local_call(
        branch_kernel,
        (1,),
        [whole_spec(a.shape) for a in args],
        [whole_spec(o.shape) for o in outs],
        outs,
        [pltpu.VMEM((rows + 8, width), wide)],
        args,
    )


def piece_at(bits, which, piece, width):
    place = bits[which] if piece == 0 else 1 - bits[which]
    return pl.ds(pl.multiple_of(place * width, width), width)


def ffn_kernel(bits, tok, mine0, mine1, theirs0, theirs1, gains, g0, g1, g2, u0, u1, u2, n2, res, gate, up, act):
    width = g1.shape[0]

    @pl.when(pl.program_id(0) == 0)
    def _():
        for h, (mine, theirs) in enumerate(((mine0, theirs0), (mine1, theirs1))):
            res[h] = tok[h, : res.shape[1], :].astype(wide) + (
                mine[...].astype(wide) + theirs[...].astype(wide)
            )
        scale = row_scale([res[0], res[1]])
        for h in range(2):
            n2[h] = (res[h] * scale * gains[h]).astype(low)

    for which, (out, w0, w1, w2) in enumerate(((gate, g0, g1, g2), (up, u0, u1, u2))):
        total = dot_of(n2[0], w0[...], 1, 0)
        for piece, w in enumerate((w1, w2)):
            total += dot_of(n2[1, :, piece_at(bits, which, piece, width)], w[...], 1, 0)
        out[...] = total
    value = gate[...]
    act[...] = (value * jax.nn.sigmoid(value) * up[...]).astype(low)


def ffn_forward(bits, tok, mine, theirs, gains, weights):
    rows, width = mine[0].shape
    cols = weights[0].shape[1]
    tile = cols // 3
    both = (2, rows, width)
    full = whole_spec(both)
    wide_tile = pl.BlockSpec((rows, tile), lambda i, *_: (0, i))
    weight_specs = [pl.BlockSpec((w.shape[0], tile), lambda i, *_: (0, i)) for w in weights]
    return local_call(
        ffn_kernel,
        (3,),
        [whole_spec(tok.shape)]
        + [whole_spec((rows, width))] * 4
        + [whole_spec(gains.shape)]
        + weight_specs,
        [full, full, wide_tile, wide_tile, wide_tile],
        [
            shape_of(both, low),
            shape_of(both, wide),
            shape_of((rows, cols), wide),
            shape_of((rows, cols), wide),
            shape_of((rows, cols), low),
        ],
        [],
        (bits, tok, *mine, *theirs, gains, *weights),
        prefetch=1,
    )


def ffn_back_kernel(
    bits, cot, d_own, d_other, gate, up, g0, g1, g2, u0, u1, u2, g_gate, g_up, part0, part1, total
):
    width = g1.shape[0]

    @pl.when(pl.program_id(0) == 0)
    def _():
        total[...] = jnp.zeros_like(total)

    start = cot.shape[1] - gate.shape[0]
    g_act = dot_of(cot[0, start:, :], d_own[...], 1, 1) + dot_of(cot[1, start:, :], d_other[...], 1, 1)
    value = gate[...]
    sigma = jax.nn.sigmoid(value)
    g_gate[...] = (g_act * up[...] * sigma * (1.0 + value * (1.0 - sigma))).astype(low)
    g_up[...] = (g_act * (value * sigma)).astype(low)
    total[0] += dot_of(g_gate[...], g0[...], 1, 1) + dot_of(g_up[...], u0[...], 1, 1)
    for which, (grad, w1, w2) in enumerate(((g_gate, g1, g2), (g_up, u1, u2))):
        for piece, w in enumerate((w1, w2)):
            total[1, :, piece_at(bits, which, piece, width)] += dot_of(grad[...], w[...], 1, 1)

    @pl.when(pl.program_id(0) == pl.num_programs(0) - 1)
    def _():
        part0[...] = total[0].astype(low)
        part1[...] = total[1].astype(low)


def ffn_backward(bits, cot, downs, gate, up, weights):
    rows, cols = gate.shape
    tile = cols // 3
    part = (rows, cot.shape[2])
    wide_tile = pl.BlockSpec((rows, tile), lambda i, *_: (0, i))
    weight_specs = [pl.BlockSpec((w.shape[0], tile), lambda i, *_: (0, i)) for w in weights]
    down_spec = pl.BlockSpec((tile, downs[0].shape[1]), lambda i, *_: (i, 0))
    return local_call(
        ffn_back_kernel,
        (3,),
        [whole_spec(cot.shape), down_spec, down_spec, wide_tile, wide_tile] + weight_specs,
        [wide_tile, wide_tile, whole_spec(part), whole_spec(part)],
        [shape_of((rows, cols), low)] * 2 + [shape_of(part, low)] * 2,
        [pltpu.VMEM((2, *part), wide)],
        (bits, cot, *downs, gate, up, *weights),
        prefetch=1,
    )


def put(outs, half, rows, value):
    if len(outs) == 2:
        outs[half][rows, :] = value.astype(low)
    else:
        outs[0][half, rows, :] = value.astype(low)


def chunk_outs(split, rows, cols):
    if split:
        return [whole_spec((rows, cols))] * 2, [shape_of((rows, cols), low)] * 2
    return [whole_spec((2, rows, cols))], [shape_of((2, rows, cols), low)]


def pair_grad_kernel(n2, g_gate, g_up, *outs):
    rows = n2.shape[2]
    for h in range(2):
        for side, grad in enumerate((g_gate, g_up)):
            put(outs, h, slice(side * rows, (side + 1) * rows), dot_of(n2[h], grad[...], 0, 0))


def pair_grads(n2, g_gate, g_up, at, rows, split):
    specs, shapes = chunk_outs(split, 2 * rows, g_gate.shape[1])
    outs = local_call(
        pair_grad_kernel,
        (1,),
        [
            pl.BlockSpec((2, n2.shape[1], rows), lambda i: (0, 0, at)),
            whole_spec(g_gate.shape),
            whole_spec(g_up.shape),
        ],
        specs,
        shapes,
        [],
        (n2, g_gate, g_up),
    )
    return tuple(outs) if split else outs[0]


def down_grad_kernel(act, cot, *outs):
    start = cot.shape[1] - act.shape[0]
    for h in range(2):
        put(outs, h, slice(None), dot_of(act[...], cot[h, start:, :], 0, 0))


def down_grads(act, cot, at, rows, split):
    specs, shapes = chunk_outs(split, rows, cot.shape[2])
    outs = local_call(
        down_grad_kernel,
        (1,),
        [pl.BlockSpec((act.shape[0], rows), lambda i: (0, at)), whole_spec(cot.shape)],
        specs,
        shapes,
        [],
        (act, cot),
    )
    return tuple(outs) if split else outs[0]


def branch_back_kernel(
    mine0, mine1, theirs0, theirs1, res, cot, gains, taps, own, other, gate_b, gate_c, gate_x, conv,
    g_res, g_low, g_proj, gain_grad, tap_grad, ext, ext_grad,
):
    _, rows, width = res.shape
    scale = row_scale([res[0], res[1]])
    grads = [
        mine[...].astype(wide) + theirs[...].astype(wide)
        for mine, theirs in ((mine0, theirs0), (mine1, theirs1))
    ]
    inner = sum(
        jnp.sum(grads[h] * gains[h] * res[h], axis=1, keepdims=True) for h in range(2)
    )
    factor = scale * scale * scale * inner / D
    for h in range(2):
        gain_grad[h] = jnp.sum(grads[h] * res[h] * scale, axis=0, keepdims=True)
        value = cot[h, cot.shape[1] - rows :, :].astype(wide) + (scale * (grads[h] * gains[h]) - res[h] * factor)
        g_res[h] = value
        g_low[h] = value.astype(low)
    g_hidden = dot_of(g_low[0], own[...], 1, 1) + dot_of(g_low[1], other[...], 1, 1)
    g_proj[1, :rows, :] = (g_hidden * conv[...]).astype(low)
    g_conv = g_hidden * gate_c[:rows, :]
    ext_grad[:rows, :] = g_conv
    ext_grad[rows:, :] = jnp.zeros((8, width), wide)
    ext[8 : 8 + rows, :] = gate_b[:rows, :] * gate_x[:rows, :]
    ext[6:8, :] = gate_b[rows : rows + 2, :] * gate_x[rows : rows + 2, :]
    for k in range(3):
        tap_grad[k : k + 1, :] = jnp.sum(
            g_conv * ext[6 + k : 6 + k + rows, :], axis=0, keepdims=True
        )
    g_mixed = sum(taps[2 - k] * ext_grad[k : k + rows, :] for k in range(3))
    g_proj[0, :rows, :] = (g_mixed * gate_x[:rows, :]).astype(low)
    g_proj[2, :rows, :] = (g_mixed * gate_b[:rows, :]).astype(low)
    tails = g_proj.shape[1] - rows
    row = lax.broadcasted_iota(jnp.int32, (tails, width), 0)
    first, second = ext_grad[0:1, :], ext_grad[1:2, :]
    g_before = jnp.where(
        row == 0,
        taps[0] * first,
        jnp.where(row == 1, taps[1] * first + taps[0] * second, 0.0),
    )
    g_proj[0, rows:, :] = (g_before * gate_x[rows:, :]).astype(low)
    g_proj[1, rows:, :] = jnp.zeros((tails, width), low)
    g_proj[2, rows:, :] = (g_before * gate_b[rows:, :]).astype(low)


def branch_backward(mine, theirs, res, cot, gains, taps, own, other, gates, conv):
    _, rows, width = res.shape
    long = gates[0].shape[0]
    out_weight = pl.BlockSpec((width, width), lambda i, *_: (3, 0))
    outs = [
        shape_of(res.shape, wide),
        shape_of(res.shape, low),
        shape_of((3, long, width), low),
        shape_of((2, 1, width), wide),
        shape_of((3, width), wide),
    ]
    full = whole_spec(res.shape)
    return local_call(
        branch_back_kernel,
        (1,),
        [whole_spec((rows, width))] * 4
        + [full, whole_spec(cot.shape), whole_spec(gains.shape), whole_spec(taps.shape)]
        + [out_weight, out_weight]
        + [whole_spec(g.shape) for g in gates]
        + [whole_spec(conv.shape)],
        [whole_spec(o.shape) for o in outs],
        outs,
        [pltpu.VMEM((rows + 8, width), wide), pltpu.VMEM((rows + 8, width), wide)],
        (*mine, *theirs, res, cot, gains, taps, own, other, *gates, conv),
    )


def branch_grad_kernel(left0, left1, right0, right1, own, other):
    rows = own.shape[0] // 2
    for h, out in enumerate((own, other)):
        for k, (left, right) in enumerate(((left0, right0), (left1, right1))):
            one = left[h] if len(left.shape) == 3 else left[...]
            two = right[h] if k == 1 and len(left.shape) == 2 else right[0]
            out[k * rows : (k + 1) * rows, :] = dot_of(one, two, 0, 0).astype(low)


def branch_grads(n1, g_proj, gate, second):
    width = n1.shape[2]
    gate_spec = pl.BlockSpec((1, *g_proj.shape[1:]), lambda i: (gate, 0, 0))
    if second is None:
        left, right = n1, g_proj
        right_spec = pl.BlockSpec((1, *g_proj.shape[1:]), lambda i: (gate + 1, 0, 0))
    else:
        left, right = second
        right_spec = whole_spec(right.shape)
    specs, shapes = chunk_outs(True, 2 * width, width)
    return local_call(
        branch_grad_kernel,
        (1,),
        [whole_spec(n1.shape), whole_spec(left.shape), gate_spec, right_spec],
        specs,
        shapes,
        [],
        (n1, left, g_proj, right),
    )


def shards(
    tokens,
    cotangent,
    input_projection_weight,
    conv_weight,
    output_projection_weight,
    norm_gains,
    gate_up_weight,
    down_projection_weight,
    in_first,
    in_second,
    conv_first,
    conv_second,
    out_first,
    out_second,
    gain_first,
    gain_second,
    gu_first,
    gu_second,
    down_first,
    down_second,
):
    feat_cols = tokens.shape[1]
    branch_cols = conv_weight.shape[1]
    hidden_cols = down_projection_weight.shape[0]
    block_rows = tokens.shape[0]
    seq_len = max(SEQ_LEAST, block_rows * lax.axis_size("dp") * lax.axis_size("col"))
    data_pos = lax.axis_index("dp")
    row_pos = lax.axis_index("row")
    col_pos = lax.axis_index("col")
    home = row_pos == col_pos
    tail_rows = 16

    in_low = jnp.transpose(input_projection_weight, (1, 0, 2)).astype(low).reshape(-1, branch_cols)
    io_low = jnp.concatenate([in_low, output_projection_weight.astype(low)])
    io_share = share_of(io_low, (1, 0))
    io_got = swap(io_share, "col")
    row_start = (data_pos * lax.axis_size("row") + row_pos) * block_rows
    tail = from_behind(tokens[-2:], ("dp", "row"), 1)
    tail = jnp.where(row_start % seq_len != 0, tail, jnp.zeros_like(tail))
    spare = jnp.zeros((tail_rows - 8, feat_cols), low)
    gain_parts = []
    left = norm_gains
    for _ in range(3):
        gain_parts.append(lax.reduce_precision(left, 8, 7))
        left = left - gain_parts[-1]
    gain_parts = jnp.concatenate(gain_parts).astype(low)
    extra = tie(jnp.concatenate([tail, gain_parts, spare]))
    block = jnp.concatenate([tie(tokens, io_got), extra, cotangent])
    away = to_home(block)
    gu_weight = to_linear(gate_up_weight)
    gate_low, up_low = split_pairs(gu_weight, feat_cols, hidden_cols)
    down_low = down_projection_weight.astype(low)
    both = jnp.stack([block, away])
    both = jnp.where(home, both, home_to_sibling(both))
    gains = both[:, block_rows + 2 : block_rows + 8].astype(wide)
    gains = gains[:, 0:2] + gains[:, 2:4] + gains[:, 4:6]
    gains = [gains[:, k : k + 1] for k in range(2)]
    gate_got = swap(tie(share_of(gate_low, (1, 0)), io_got), "col")
    up_got = swap(tie(share_of(up_low, (0, 1)), gate_got), "col")
    down_got = swap(tie(down_low, up_got), "col")
    io_pair = keep_or_join(0, io_got, flip(io_got, 0))
    io_other = keep_or_join(1, io_pair, flip(io_pair, 1))
    gate_pair = keep_or_join(0, gate_got, flip(tie(gate_got, io_pair), 0))
    up_pair = keep_or_join(1, up_got, flip(tie(up_got, io_pair), 1))
    gate_more = flip(gate_pair, 1)
    up_more = flip(up_pair, 0)
    weights = [gate_low, gate_pair, gate_more, up_low, up_pair, up_more]
    bits = jnp.stack([dp_bit(1), dp_bit(0)]).astype(jnp.int32)
    downs = [down_low, down_got]

    n1, gate_b, gate_c, gate_x, conv, hidden, *branch = branch_forward(
        both, block_rows, tail_rows, gains[0], conv_weight, io_low, io_other
    )
    n2, res, gate, upper, act = ffn_forward(
        bits, both, branch, swap_halves(branch), gains[1], weights
    )

    turns = Turns()
    orders = dict(D="xyl", d="ylx", a="xyl", b="lyx", c="xyl", e="lyx", I="xyl", i="xyl")
    down_half = hidden_cols // 2
    for k, name in enumerate("Dd"):
        split = orders[name][0] == "x"
        turns.add(name, down_grads(act, both, k, down_half, split), orders[name])
    turns.run("Dd")
    g_gate, g_up, *part_two = ffn_backward(
        bits, tie(both, *turns.after), downs, gate, upper, weights
    )
    quarter = feat_cols // 4
    for k, name in enumerate("abce"):
        split = orders[name][0] == "x"
        turns.add(name, pair_grads(n2, g_gate, g_up, k, quarter, split), orders[name])
    turns.run("abcDe")
    g_res, g_branch, g_proj, gain_two_grad, conv_grad = branch_backward(
        part_two,
        swap_halves(part_two),
        tie(res, *turns.after),
        both,
        gains[1],
        conv_weight,
        io_low,
        io_other,
        (gate_b, gate_c, gate_x),
        conv,
    )
    turns.add("I", branch_grads(n1, g_proj, 0, None), orders["I"])
    io_last = branch_grads(n1, g_proj, 2, (hidden, g_branch))
    turns.after += tuple(io_last)
    turns.run("IdabD")

    g_late = tie(g_proj, *turns.after)
    io_half = [half.reshape(4, feat_cols, branch_cols) for half in (io_low, io_other)]
    g_part = jnp.stack(
        [sum(mul_t(g_late[g], io_half[h][g]) for g in range(3)).astype(low) for h in range(2)]
    )
    g_long = g_part.astype(wide) + swap(g_part, "row").astype(wide)
    tok = both[:, : block_rows + 2].astype(wide)
    scale = lax.rsqrt(jnp.sum(tok * tok, axis=(0, 2)) / D + norm_eps)[None, :, None]
    gain_one_grad = jnp.sum(g_long[:, : block_rows + 2] * tok * scale, axis=1)
    small = [
        jnp.concatenate([conv_grad, gain_one_grad[h : h + 1], gain_two_grad[h]]) for h in range(2)
    ]
    spare = jnp.zeros((16, feat_cols), low)
    small = [jnp.pad(part, ((0, 11), (0, 0))).astype(low) for part in small]
    io_long = []
    for h in range(2):
        pieces = jnp.split(io_last[h], 4)
        io_long.append(
            jnp.concatenate(
                [pieces[0], small[h], pieces[1], spare, pieces[2], spare, pieces[3], spare]
            )
        )
    turns.add("i", io_long, orders["i"])
    turns.run("iacebdDIcaeDciIabDdcieIDabdacibceIdbiedIeiIi")
    turns.finish()
    sums, seen = turns.done, turns.seen

    back = tie(g_long[::-1, block_rows : block_rows + 2], seen["i"][4])
    back = from_behind(back, ("dp", "col"), -1)
    g_n1 = g_long[:, :block_rows].at[:, -2:].add(back)
    tok, scale = tok[:, :block_rows], scale[:, :block_rows]
    weighted = g_n1 * gains[0]
    inner = jnp.sum(weighted * tok, axis=(0, 2))[None, :, None]
    tok_half = (g_res + (scale * weighted - tok * (scale * scale * scale * inner / D))).astype(low)
    token_grad = jnp.where(home, tok_half[0], home_to_away(tok_half[1]))
    act = tie(act, seen["D"][1])
    ffn = jnp.stack([mul(act, downs[h]) for h in range(2)])
    out_half = (res + (ffn + sibling_to_home(ffn.astype(low)).astype(wide))).astype(low)
    output = jnp.where(home, out_half[0], home_to_away(out_half[1]))

    def in_flat(values):
        return jnp.transpose(values, (1, 0, 2)).reshape(3 * feat_cols, branch_cols)

    def in_back(values):
        return jnp.transpose(values.reshape(3, feat_cols, branch_cols), (1, 0, 2))

    def gu_back(values):
        return from_linear(values, feat_cols, 2)

    wheres = {name: where_of(orders[name]) for name in orders}
    down_state = (down_projection_weight, down_first, down_second)
    gu_state = (gu_weight, to_linear(gu_first), to_linear(gu_second))
    in_state = (in_flat(input_projection_weight), in_flat(in_first), in_flat(in_second))
    out_state = (output_projection_weight, out_first, out_second)
    pairs = 2 * hidden_cols // 128

    shares = {name: sums[name][0] for name in sums}
    down_norms = sum(
        share_norms(wheres[n], shares[n], [(down_state, 4 * k)], down_half // 4)
        for k, n in enumerate("Dd")
    )
    gu_norms = sum(
        share_norms(wheres[n], shares[n], [(gu_state, 2 * k)], quarter // 2 * pairs, pairs=True)
        for k, n in enumerate("abce")
    )
    part_rows = feat_cols // 2
    io_norms = share_norms(
        wheres["i"], shares["i"], [(in_state, 4), (out_state, 0)], part_rows
    )
    in_norms = io_norms[:2] + share_norms(wheres["I"], shares["I"], [(in_state, 0)], part_rows)
    matrix_norms = jnp.stack([in_norms, io_norms[2:], gu_norms, down_norms])
    copies = lax.axis_size("dp") // 4
    matrix_norms = jnp.sqrt(lax.psum(matrix_norms, ("dp", "row", "col")) * (1.0 / copies))
    ratios = learn_rate * (matrix_norms[:, 0] / (matrix_norms[:, 1] + adam_eps))
    ratios = [ratios[k : k + 1] for k in range(4)]

    def later_half(count):
        return functools.partial(lamb_plain, lambda i: (i >= count // 2).astype(jnp.int32))

    def fixed_half(half):
        return functools.partial(lamb_plain, lambda i: half)

    down_new = None
    for k in (0, 1):
        name = "Dd"[k]
        block = down_half // 6
        down_new = lamb_call(
            later_half(6), wheres[name], ratios[3], sums[name][1:], block, lambda i: i % 3,
            down_state, block, 6 * k, 6, down_new, [],
        )
    gu_new = None
    gu_rows = 32
    for k in (0, 2, 1, 3):
        name = "abce"[k]
        blocks = quarter // gu_rows
        gu_new = lamb_call(
            lamb_pairs, wheres[name], ratios[2], sums[name][1:], gu_rows, lambda i: i,
            gu_state, gu_rows * pairs, k * blocks, blocks, gu_new,
            [pltpu.VMEM((gu_rows * pairs, 128), wide)],
        )
    in_new = lamb_call(
        later_half(4), wheres["I"], ratios[0], sums["I"][1:], part_rows, lambda i: i % 2,
        in_state, part_rows, 0, 4, None, [],
    )
    last = sums["i"][1:]
    in_new = lamb_call(
        fixed_half(0), wheres["i"], ratios[0], last, part_rows + 16, lambda i: i,
        in_state, part_rows, 4, 2, in_new, [],
    )
    out_new = lamb_call(
        fixed_half(1), wheres["i"], ratios[1], last, part_rows + 16, lambda i: i,
        out_state, part_rows, 0, 2, None, [],
    )

    small = [part[part_rows : part_rows + 5] for part in last]
    small = jnp.where((wheres["i"][0] >> 1) == 0, small[0], small[1]).astype(wide)
    conv_grad, gains_grad = small[:3], small[3:]
    conv_m, conv_v, conv_u = lamb_moments(conv_weight, conv_grad, conv_first, conv_second, 0.0)
    gain_m, gain_v, gain_u = lamb_moments(norm_gains, gains_grad, gain_first, gain_second, 0.0)
    col_first = (col_pos == 0).astype(wide)
    row_first = (row_pos == 0).astype(wide)
    small_norms = jnp.stack(
        [
            square_pair(conv_weight, conv_u) * col_first,
            square_pair(norm_gains[0], gain_u[0]) * row_first,
            square_pair(norm_gains[1], gain_u[1]) * row_first,
        ]
    )
    small_norms = small_norms + swap(small_norms, "row")
    small_norms = jnp.sqrt(small_norms + swap(small_norms, "col"))
    trust_norms = jnp.stack(
        [
            matrix_norms[0],
            small_norms[0],
            matrix_norms[1],
            small_norms[1],
            small_norms[2],
            matrix_norms[2],
            matrix_norms[3],
        ]
    )
    gains_new = jnp.stack(
        [
            apply_trust(norm_gains[0], gain_u[0], small_norms[1]),
            apply_trust(norm_gains[1], gain_u[1], small_norms[2]),
        ]
    )
    return (
        output,
        token_grad,
        *[in_back(values) for values in in_new],
        apply_trust(conv_weight, conv_u, small_norms[0]),
        conv_m,
        conv_v,
        *out_new,
        gains_new,
        gain_m,
        gain_v,
        *[gu_back(values) for values in gu_new],
        *down_new,
        trust_norms,
    )


def solution(mesh):
    in_specs = (
        P(("dp", "row"), "col"),
        P(("dp", "row"), "col"),
        P("col", None, "row"),
        P(None, "row"),
        P("row", "col"),
        P(None, "col"),
        P("col", None, "row"),
        P("row", "col"),
        P("col", None, "row"),
        P("col", None, "row"),
        P(None, "row"),
        P(None, "row"),
        P("row", "col"),
        P("row", "col"),
        P(None, "col"),
        P(None, "col"),
        P("col", None, "row"),
        P("col", None, "row"),
        P("row", "col"),
        P("row", "col"),
    )
    out_specs = (
        P(("dp", "row"), "col"),
        P(("dp", "row"), "col"),
        P("col", None, "row"),
        P("col", None, "row"),
        P("col", None, "row"),
        P(None, "row"),
        P(None, "row"),
        P(None, "row"),
        P("row", "col"),
        P("row", "col"),
        P("row", "col"),
        P(None, "col"),
        P(None, "col"),
        P(None, "col"),
        P("col", None, "row"),
        P("col", None, "row"),
        P("col", None, "row"),
        P("row", "col"),
        P("row", "col"),
        P("row", "col"),
        P(),
    )
    return jax.shard_map(shards, mesh=mesh, in_specs=in_specs, out_specs=out_specs, check_vma=False)
```

```python
import functools

import jax
import jax.numpy as jnp
from jax import lax
from jax.experimental import pallas as pl
from jax.experimental.layout import Layout, with_layout_constraint
from jax.experimental.pallas import tpu as pltpu
from jax.sharding import PartitionSpec as P

D = 1024
SEQ_LEAST = 4096
STEP = 5
MIB = 1024 * 1024


norm_eps = 1e-05
adam_eps = 1e-06
beta_one = 0.5
beta_two = 0.6
learn_rate = 0.5
decay_rate = 0.01
low = jnp.bfloat16
wide = jnp.float32


def from_behind(block, axis, distance):
    devices = range(lax.axis_size(axis))
    route = [(i - distance, i) for i in devices if i - distance in devices]
    return lax.ppermute(block, axis, route)


def swap(values, axis):
    return lax.ppermute(values, axis, [(0, 1), (1, 0)])


def swap_halves(halves):
    return [swap(half, "row") for half in halves]


def to_home(values):
    return lax.ppermute(values, ("row", "col"), [(1, 0), (2, 3)])


def home_to_sibling(values):
    return lax.ppermute(values, ("row", "col"), [(0, 2), (3, 1)])


def home_to_away(values):
    return lax.ppermute(values, ("row", "col"), [(0, 1), (3, 2)])


def sibling_to_home(values):
    return lax.ppermute(values, ("row", "col"), [(2, 0), (1, 3)])


def contract(left, right, left_dim, right_dim):
    return lax.dot_general(
        left, right, (((left_dim,), (right_dim,)), ((), ())), preferred_element_type=wide
    )


def mul(left, right):
    return contract(left, right, 1, 0)


def mul_t(left, right):
    return contract(left, right, 1, 1)


def t_mul(left, right):
    return contract(left, right, 0, 0)


def lamb_moments(weight, grad, first, second, decay):
    first_new = beta_one * first + (1.0 - beta_one) * grad
    second_new = beta_two * second + (1.0 - beta_two) * grad * grad
    direction = (first_new * (1.0 / (1.0 - beta_one**STEP))) / (
        jnp.sqrt(second_new * (1.0 / (1.0 - beta_two**STEP))) + adam_eps
    ) + decay * weight
    return (first_new, second_new, direction)


def square_pair(weight, direction):
    return jnp.stack([jnp.sum(weight * weight), jnp.sum(direction * direction)])


def kernel_call(kernel, grid, in_specs, out_specs, out_shape, scratch, args, aliases=None, mib=1):
    return pl.pallas_call(
        kernel,
        grid_spec=pltpu.PrefetchScalarGridSpec(
            num_scalar_prefetch=1,
            grid=grid,
            in_specs=in_specs,
            out_specs=out_specs,
            scratch_shapes=scratch,
        ),
        out_shape=out_shape,
        input_output_aliases=aliases or {},
        compiler_params=pltpu.CompilerParams(vmem_limit_bytes=48 * MIB),
        cost_estimate=pl.CostEstimate(flops=0, bytes_accessed=mib * MIB, transcendentals=0),
    )(*args)


SCALARS = pl.BlockSpec(memory_space=pltpu.SMEM)


def norm_kernel(where, grad, *refs):
    sums = refs[-1]
    groups = [refs[:3], refs[3:6]][: len(refs) // 3]
    rows = groups[0][0].shape[0]
    zero = jnp.zeros((8, groups[0][0].shape[1]), wide)
    for k, (p, m, v) in enumerate(groups):

        def body(at, total):
            here = pl.ds(pl.multiple_of(at * 32, 32), 32)
            weight = p[here, :]
            direction = lamb_moments(
                weight, grad[here, :].astype(wide), m[here, :], v[here, :], decay_rate
            )[2]
            return tuple(
                t + (sq[:8] + sq[8:16]) + (sq[16:24] + sq[24:])
                for t, sq in zip(total, (weight * weight, direction * direction))
            )

        total = lax.fori_loop(0, rows // 32, body, (zero, zero))
        mine = 1.0 if len(groups) == 1 else ((where[0] >> 1) == k).astype(wide)
        for j in range(2):
            sums[2 * k + j] = jnp.sum(total[j]) * mine


def norm_pairs_kernel(where, grad, p, m, v, sums):
    rows, cols = grad.shape
    tiles = cols // 128
    side = where[0] >> 1
    zero = jnp.zeros((8, 128), wide)
    total = [zero, zero]
    for tile in range(tiles):
        here = pl.ds(2 * tile + side, rows, stride=2 * tiles)
        weight = p[here, :]
        direction = lamb_moments(
            weight, grad[:, tile * 128 : (tile + 1) * 128].astype(wide), m[here, :], v[here, :], decay_rate
        )[2]
        for j, sq in enumerate((weight * weight, direction * direction)):
            total[j] = total[j] + jnp.sum((sq).reshape(rows // 8, 8, 128), axis=0)
    for j in range(2):
        sums[j] = jnp.sum(total[j])


def share_norms(where, grad, states, rows, pairs=False):
    specs, args = [], []
    for state, at in states:
        for array in state:
            if pairs:
                spec = pl.BlockSpec(
                    (rows, array.shape[1]), lambda i, w, at=at: (at + (w[0] & 1), 0)
                )
            elif len(states) == 2:
                spec = pl.BlockSpec(
                    (rows, array.shape[1]), lambda i, w, at=at: (at + (w[0] & 1), 0)
                )
            else:
                spec = pl.BlockSpec((rows, array.shape[1]), lambda i, w, at=at: (at + w[0], 0))
            specs.append(spec)
            args.append(array)
    return kernel_call(
        norm_pairs_kernel if pairs else norm_kernel,
        (1,),
        [whole_spec(grad.shape)] + specs,
        SCALARS,
        jax.ShapeDtypeStruct((2 * len(states),), wide),
        [],
        (where, grad, *args),
    )


def lamb_loop(refs, outs, ratio, rows, step, pick):
    p, m, v = refs

    def body(at, carry):
        here = pl.ds(pl.multiple_of(at * step, step), step)
        weight = p[here, :]
        first_new, second_new, direction = lamb_moments(
            weight, pick(here), m[here, :], v[here, :], decay_rate
        )
        outs[0][here, :] = weight - ratio * direction
        outs[1][here, :] = first_new
        outs[2][here, :] = second_new
        return carry

    lax.fori_loop(0, rows // step, body, 0)


def lamb_plain(half_of_block, where, ratio, part, got, p, m, v, *outs):
    use = half_of_block(pl.program_id(0)) == (where[0] >> 1)

    def pick(here):
        return jnp.where(use, part[here, :].astype(wide), got[here, :].astype(wide))

    lamb_loop((p, m, v), outs, ratio[0], p.shape[0], 64, pick)


def lamb_pairs(where, ratio, part, got, p, m, v, p_out, m_out, v_out, mixed):
    rows, cols = part.shape
    tiles = cols // 128
    for value, order in ((0, (part, got)), (1, (got, part))):

        @pl.when((where[0] >> 1) == value)
        def _():
            for tile in range(tiles):
                for side, ref in enumerate(order):
                    mixed[pl.ds(2 * tile + side, rows, stride=2 * tiles), :] = ref[
                        :, tile * 128 : (tile + 1) * 128
                    ].astype(wide)

    lamb_loop(
        (p, m, v), (p_out, m_out, v_out), ratio[0], p.shape[0], 192, lambda here: mixed[here, :]
    )


def lamb_call(kernel, where, ratio, grad, grad_block, grad_at, state, block, start, count, before, scratch):
    rows, cols = state[0].shape
    flat = pl.BlockSpec((block, cols), lambda i, w: (i + start, 0))
    grad_spec = pl.BlockSpec((grad_block, grad[0].shape[1]), lambda i, w: (grad_at(i), 0))
    whole = jax.ShapeDtypeStruct((rows, cols), wide)
    args = [where, ratio, *grad, *state]
    specs = [SCALARS, grad_spec, grad_spec, flat, flat, flat]
    run, aliases = kernel, {}
    if before is not None:
        aliases = {len(args) + k: k for k in range(3)}

        def run(*refs):
            kernel(*refs[: len(args)], *refs[len(args) + 3 :])

    return list(
        kernel_call(
            run,
            (count,),
            specs + [pl.BlockSpec(memory_space=pl.ANY)] * len(aliases),
            [flat, flat, flat],
            [whole, whole, whole],
            scratch,
            (*args, *(before or [])),
            aliases,
            mib=26 * count * block * cols // MIB,
        )
    )


def to_linear(values):
    rows, sides, cols = values.shape
    split = with_layout_constraint(
        values.reshape(rows, sides, cols // 128, 128), Layout(major_to_minor=(0, 2, 1, 3))
    )
    return split.transpose(0, 2, 1, 3).reshape(rows * sides * cols // 128, 128)


def from_linear(values, rows, sides):
    cols = values.size // (rows * sides)
    split = values.reshape(rows, cols // 128, sides, 128).transpose(0, 2, 1, 3)
    split = with_layout_constraint(split, Layout(major_to_minor=(0, 2, 1, 3)))
    return split.reshape(rows, sides, cols)


def apply_trust(weight, direction, norms):
    return weight - learn_rate * (norms[0] / (norms[1] + adam_eps)) * direction


def flip(values, bit):
    size = lax.axis_size("dp")
    return lax.ppermute(values, "dp", [(i, i ^ (1 << bit)) for i in range(size)])


def dp_bit(bit):
    return (lax.axis_index("dp") >> bit) & 1


def rows_of(values, start, rows):
    return lax.dynamic_slice_in_dim(values, start, rows, 0)


def total_of(pieces):
    total = pieces[0].astype(wide)
    for piece in pieces[1:]:
        total = total + piece.astype(wide)
    return total


def tie(values, *deps):
    return lax.optimization_barrier((values, *deps))[0]


def low_total(pieces):
    return total_of(pieces).astype(low)


def keep_or_join(bit, part, other):
    return jnp.where(
        dp_bit(bit) == 0,
        jnp.concatenate([part, other]),
        jnp.concatenate([other, part]),
    )


def share_of(weight, order):
    rows = weight.shape[0] // (1 << len(order))
    index = 0
    for bit in order:
        index = 2 * index + dp_bit(bit)
    return rows_of(weight, index * rows, rows)


def half_of(piece, place):
    rows = piece.shape[-2] // 2
    return lax.dynamic_slice_in_dim(piece, place * rows, rows, piece.ndim - 2)


def chunk_sum(chunk, order, keep):
    bits = {"y": 0, "l": 1}
    steps = [name if name == "x" else bits[name] for name in order]
    pieces = [chunk]
    for step in steps:
        if step == "x":
            whole = len(pieces) == 1
            got = yield step, pieces[0][1] if whole else low_total([piece[1] for piece in pieces])
            pieces = [piece[0] for piece in pieces] + [got]
        else:
            here = dp_bit(step)
            got = yield step, low_total([half_of(piece, 1 - here) for piece in pieces])
            pieces = [half_of(piece, here) for piece in pieces] + [got]
    part = low_total(pieces)
    for step in range((lax.axis_size("dp") - 1).bit_length()):
        if step not in steps:
            got = yield step, part
            part = low_total([part, got])
    keep(part)
    first, second = [step for step in steps if step != "x"]
    got = yield second, part
    part = keep_or_join(second, part, got)
    got = yield first, part
    return part, got


def norm_sum(values):
    for step in ("x", "row", 1, 0):
        got = yield step, values
        values = values + got
    return values


def where_of(order):
    bits = {"y": 0, "l": 1}
    first, second = [bits[name] for name in order if name != "x"]
    return (2 * dp_bit(first) + dp_bit(second)).astype(jnp.int32).reshape(1)


def move(step, send):
    if step == "row":
        return swap(send, "row")
    return swap(send, "col") if step == "x" else flip(send, step)


class Turns:
    def __init__(self):
        self.chunks = {}
        self.arrivals = {}
        self.seen = {}
        self.done = {}
        self.shares = {}
        self.after = ()

    def add(self, name, chunk, order):
        self.chunks[name] = chunk_sum(chunk, order, functools.partial(self.shares.__setitem__, name))

    def add_norms(self, name, values):
        self.chunks[name] = norm_sum(values)

    def turn(self, name):
        got = self.arrivals.get(name)
        try:
            if got is None:
                self.seen[name] = []
                step, send = next(self.chunks[name])
                send = tie(send, *self.after)
            else:
                got = tie(got, *self.after)
                self.seen[name].append(got)
                step, send = self.chunks[name].send(got)
        except StopIteration as end:
            self.done[name] = end.value
            return
        self.arrivals[name] = move(step, send)
        self.after = (send,)

    def run(self, names):
        for name in names:
            if name not in self.done:
                self.turn(name)

    def reach_shares(self, names):
        while any(name not in self.shares for name in names):
            self.run([name for name in names if name not in self.shares])

    def finish(self):
        while len(self.done) < len(self.chunks):
            self.run(self.chunks)


def deinterleave(pairs, gate, up):
    rows, cols = gate.shape
    tiles = cols // 128
    for tile in range(tiles):
        for side, out in enumerate((gate, up)):
            out[:, tile * 128 : (tile + 1) * 128] = pairs[
                pl.ds(2 * tile + side, rows, stride=2 * tiles), :
            ].astype(low)


def split_pairs(linear, rows, cols):
    block = 64
    half = jax.ShapeDtypeStruct((rows, cols), low)
    out_spec = pl.BlockSpec((block, cols), lambda i: (i, 0))
    return pl.pallas_call(
        deinterleave,
        grid=(rows // block,),
        in_specs=[pl.BlockSpec((block * 2 * cols // 128, 128), lambda i: (i, 0))],
        out_specs=[out_spec, out_spec],
        out_shape=[half, half],
        compiler_params=pltpu.CompilerParams(vmem_limit_bytes=24 * MIB),
        cost_estimate=pl.CostEstimate(
            flops=rows * cols, bytes_accessed=12 * rows * cols, transcendentals=0
        ),
    )(linear)


def dot_of(left, right, left_dim, right_dim):
    return lax.dot_general(
        left, right, (((left_dim,), (right_dim,)), ((), ())), preferred_element_type=wide
    )


def local_call(kernel, grid, in_specs, out_specs, out_shape, scratch, args, prefetch=0):
    return pl.pallas_call(
        kernel,
        grid_spec=pltpu.PrefetchScalarGridSpec(
            num_scalar_prefetch=prefetch,
            grid=grid,
            in_specs=in_specs,
            out_specs=out_specs,
            scratch_shapes=scratch,
        ),
        out_shape=out_shape,
        compiler_params=pltpu.CompilerParams(vmem_limit_bytes=48 * MIB),
        cost_estimate=pl.CostEstimate(flops=0, bytes_accessed=MIB, transcendentals=0),
    )(*args)


def whole_spec(shape):
    return pl.BlockSpec(shape, lambda *_: (0,) * len(shape))


def shape_of(dims, kind):
    return jax.ShapeDtypeStruct(dims, kind)


def row_scale(halves):
    total = sum(jnp.sum(half * half, axis=1, keepdims=True) for half in halves)
    return lax.rsqrt(total / D + norm_eps)


def branch_kernel(tok, gains, taps, own, other, n1, gate_b, gate_c, gate_x, conv, hidden, part0, part1, ext):
    long, width = n1.shape[1:]
    rows = conv.shape[0]
    step = long // 3

    def gates(at, carry):
        here = pl.ds(pl.multiple_of(at * step, step), step)
        halves = [tok[h, here, :].astype(wide) for h in range(2)]
        scale = row_scale(halves)
        for h in range(2):
            n1[h, here, :] = (halves[h] * scale * gains[h]).astype(low)
        for g, out in enumerate((gate_b, gate_c, gate_x)):
            w = slice(g * width, (g + 1) * width)
            out[here, :] = dot_of(n1[0, here, :], own[w, :], 1, 0) + dot_of(
                n1[1, here, :], other[w, :], 1, 0
            )
        return carry

    lax.fori_loop(0, 3, gates, 0)
    ext[8 : 8 + rows, :] = gate_b[:rows, :] * gate_x[:rows, :]
    ext[6:8, :] = gate_b[rows : rows + 2, :] * gate_x[rows : rows + 2, :]
    w_out = slice(3 * width, 4 * width)
    quarter = rows // 4
    for at in range(4):
        start = at * quarter
        taken = slice(start, start + quarter)
        value = sum(taps[k] * ext[start + 6 + k : start + 6 + k + quarter, :] for k in range(3))
        conv[taken, :] = value
        low_hidden = (gate_c[taken, :] * value).astype(low)
        hidden[taken, :] = low_hidden
        for part, weight in ((part0, own), (part1, other)):
            part[taken, :] = dot_of(low_hidden, weight[w_out, :], 1, 0).astype(low)


def branch_forward(tok, rows, tails, gains, taps, own, other):
    width = tok.shape[2]
    gate = shape_of((rows + tails, width), wide)
    outs = [
        shape_of((2, rows + tails, width), low),
        gate,
        gate,
        gate,
        shape_of((rows, width), wide),
        shape_of((rows, width), low),
        shape_of((rows, width), low),
        shape_of((rows, width), low),
    ]
    args = (tok, gains, taps, own, other)
    return local_call(
        branch_kernel,
        (1,),
        [whole_spec(a.shape) for a in args],
        [whole_spec(o.shape) for o in outs],
        outs,
        [pltpu.VMEM((rows + 8, width), wide)],
        args,
    )


def piece_at(bits, which, piece, width):
    place = bits[which] if piece == 0 else 1 - bits[which]
    return pl.ds(pl.multiple_of(place * width, width), width)


def ffn_kernel(bits, tok, mine0, mine1, theirs0, theirs1, gains, g0, g1, g2, u0, u1, u2, n2, res, gate, up, act):
    width = g1.shape[0]

    @pl.when(pl.program_id(0) == 0)
    def _():
        for h, (mine, theirs) in enumerate(((mine0, theirs0), (mine1, theirs1))):
            res[h] = tok[h, : res.shape[1], :].astype(wide) + (
                mine[...].astype(wide) + theirs[...].astype(wide)
            )
        scale = row_scale([res[0], res[1]])
        for h in range(2):
            n2[h] = (res[h] * scale * gains[h]).astype(low)

    for which, (out, w0, w1, w2) in enumerate(((gate, g0, g1, g2), (up, u0, u1, u2))):
        total = dot_of(n2[0], w0[...], 1, 0)
        for piece, w in enumerate((w1, w2)):
            total += dot_of(n2[1, :, piece_at(bits, which, piece, width)], w[...], 1, 0)
        out[...] = total
    value = gate[...]
    act[...] = (value * jax.nn.sigmoid(value) * up[...]).astype(low)


def ffn_forward(bits, tok, mine, theirs, gains, weights):
    rows, width = mine[0].shape
    cols = weights[0].shape[1]
    tile = cols // 3
    both = (2, rows, width)
    full = whole_spec(both)
    wide_tile = pl.BlockSpec((rows, tile), lambda i, *_: (0, i))
    weight_specs = [pl.BlockSpec((w.shape[0], tile), lambda i, *_: (0, i)) for w in weights]
    return local_call(
        ffn_kernel,
        (3,),
        [whole_spec(tok.shape)]
        + [whole_spec((rows, width))] * 4
        + [whole_spec(gains.shape)]
        + weight_specs,
        [full, full, wide_tile, wide_tile, wide_tile],
        [
            shape_of(both, low),
            shape_of(both, wide),
            shape_of((rows, cols), wide),
            shape_of((rows, cols), wide),
            shape_of((rows, cols), low),
        ],
        [],
        (bits, tok, *mine, *theirs, gains, *weights),
        prefetch=1,
    )


def ffn_back_kernel(
    bits, cot, d_own, d_other, gate, up, g0, g1, g2, u0, u1, u2, g_gate, g_up, part0, part1, total
):
    width = g1.shape[0]

    @pl.when(pl.program_id(0) == 0)
    def _():
        total[...] = jnp.zeros_like(total)

    start = cot.shape[1] - gate.shape[0]
    g_act = dot_of(cot[0, start:, :], d_own[...], 1, 1) + dot_of(cot[1, start:, :], d_other[...], 1, 1)
    value = gate[...]
    sigma = jax.nn.sigmoid(value)
    g_gate[...] = (g_act * up[...] * sigma * (1.0 + value * (1.0 - sigma))).astype(low)
    g_up[...] = (g_act * (value * sigma)).astype(low)
    total[0] += dot_of(g_gate[...], g0[...], 1, 1) + dot_of(g_up[...], u0[...], 1, 1)
    for which, (grad, w1, w2) in enumerate(((g_gate, g1, g2), (g_up, u1, u2))):
        for piece, w in enumerate((w1, w2)):
            total[1, :, piece_at(bits, which, piece, width)] += dot_of(grad[...], w[...], 1, 1)

    @pl.when(pl.program_id(0) == pl.num_programs(0) - 1)
    def _():
        part0[...] = total[0].astype(low)
        part1[...] = total[1].astype(low)


def ffn_backward(bits, cot, downs, gate, up, weights):
    rows, cols = gate.shape
    tile = cols // 3
    part = (rows, cot.shape[2])
    wide_tile = pl.BlockSpec((rows, tile), lambda i, *_: (0, i))
    weight_specs = [pl.BlockSpec((w.shape[0], tile), lambda i, *_: (0, i)) for w in weights]
    down_spec = pl.BlockSpec((tile, downs[0].shape[1]), lambda i, *_: (i, 0))
    return local_call(
        ffn_back_kernel,
        (3,),
        [whole_spec(cot.shape), down_spec, down_spec, wide_tile, wide_tile] + weight_specs,
        [wide_tile, wide_tile, whole_spec(part), whole_spec(part)],
        [shape_of((rows, cols), low)] * 2 + [shape_of(part, low)] * 2,
        [pltpu.VMEM((2, *part), wide)],
        (bits, cot, *downs, gate, up, *weights),
        prefetch=1,
    )


def put(outs, half, rows, value):
    if len(outs) == 2:
        outs[half][rows, :] = value.astype(low)
    else:
        outs[0][half, rows, :] = value.astype(low)


def chunk_outs(split, rows, cols):
    if split:
        return [whole_spec((rows, cols))] * 2, [shape_of((rows, cols), low)] * 2
    return [whole_spec((2, rows, cols))], [shape_of((2, rows, cols), low)]


def pair_grad_kernel(n2, g_gate, g_up, *outs):
    rows = n2.shape[2]
    for h in range(2):
        for side, grad in enumerate((g_gate, g_up)):
            put(outs, h, slice(side * rows, (side + 1) * rows), dot_of(n2[h], grad[...], 0, 0))


def pair_grads(n2, g_gate, g_up, at, rows, split):
    specs, shapes = chunk_outs(split, 2 * rows, g_gate.shape[1])
    outs = local_call(
        pair_grad_kernel,
        (1,),
        [
            pl.BlockSpec((2, n2.shape[1], rows), lambda i: (0, 0, at)),
            whole_spec(g_gate.shape),
            whole_spec(g_up.shape),
        ],
        specs,
        shapes,
        [],
        (n2, g_gate, g_up),
    )
    return tuple(outs) if split else outs[0]


def down_grad_kernel(act, cot, *outs):
    start = cot.shape[1] - act.shape[0]
    for h in range(2):
        put(outs, h, slice(None), dot_of(act[...], cot[h, start:, :], 0, 0))


def down_grads(act, cot, at, rows, split):
    specs, shapes = chunk_outs(split, rows, cot.shape[2])
    outs = local_call(
        down_grad_kernel,
        (1,),
        [pl.BlockSpec((act.shape[0], rows), lambda i: (0, at)), whole_spec(cot.shape)],
        specs,
        shapes,
        [],
        (act, cot),
    )
    return tuple(outs) if split else outs[0]


def branch_back_kernel(
    mine0, mine1, theirs0, theirs1, res, cot, gains, taps, own, other, gate_b, gate_c, gate_x, conv,
    g_res, g_low, g_proj, gain_grad, tap_grad, ext, ext_grad,
):
    _, rows, width = res.shape
    scale = row_scale([res[0], res[1]])
    grads = [
        mine[...].astype(wide) + theirs[...].astype(wide)
        for mine, theirs in ((mine0, theirs0), (mine1, theirs1))
    ]
    inner = sum(
        jnp.sum(grads[h] * gains[h] * res[h], axis=1, keepdims=True) for h in range(2)
    )
    factor = scale * scale * scale * inner / D
    for h in range(2):
        gain_grad[h] = jnp.sum(grads[h] * res[h] * scale, axis=0, keepdims=True)
        value = cot[h, cot.shape[1] - rows :, :].astype(wide) + (scale * (grads[h] * gains[h]) - res[h] * factor)
        g_res[h] = value
        g_low[h] = value.astype(low)
    g_hidden = dot_of(g_low[0], own[...], 1, 1) + dot_of(g_low[1], other[...], 1, 1)
    g_proj[1, :rows, :] = (g_hidden * conv[...]).astype(low)
    g_conv = g_hidden * gate_c[:rows, :]
    ext_grad[:rows, :] = g_conv
    ext_grad[rows:, :] = jnp.zeros((8, width), wide)
    ext[8 : 8 + rows, :] = gate_b[:rows, :] * gate_x[:rows, :]
    ext[6:8, :] = gate_b[rows : rows + 2, :] * gate_x[rows : rows + 2, :]
    for k in range(3):
        tap_grad[k : k + 1, :] = jnp.sum(
            g_conv * ext[6 + k : 6 + k + rows, :], axis=0, keepdims=True
        )
    g_mixed = sum(taps[2 - k] * ext_grad[k : k + rows, :] for k in range(3))
    g_proj[0, :rows, :] = (g_mixed * gate_x[:rows, :]).astype(low)
    g_proj[2, :rows, :] = (g_mixed * gate_b[:rows, :]).astype(low)
    tails = g_proj.shape[1] - rows
    row = lax.broadcasted_iota(jnp.int32, (tails, width), 0)
    first, second = ext_grad[0:1, :], ext_grad[1:2, :]
    g_before = jnp.where(
        row == 0,
        taps[0] * first,
        jnp.where(row == 1, taps[1] * first + taps[0] * second, 0.0),
    )
    g_proj[0, rows:, :] = (g_before * gate_x[rows:, :]).astype(low)
    g_proj[1, rows:, :] = jnp.zeros((tails, width), low)
    g_proj[2, rows:, :] = (g_before * gate_b[rows:, :]).astype(low)


def branch_backward(mine, theirs, res, cot, gains, taps, own, other, gates, conv):
    _, rows, width = res.shape
    long = gates[0].shape[0]
    out_weight = pl.BlockSpec((width, width), lambda i, *_: (3, 0))
    outs = [
        shape_of(res.shape, wide),
        shape_of(res.shape, low),
        shape_of((3, long, width), low),
        shape_of((2, 1, width), wide),
        shape_of((3, width), wide),
    ]
    full = whole_spec(res.shape)
    return local_call(
        branch_back_kernel,
        (1,),
        [whole_spec((rows, width))] * 4
        + [full, whole_spec(cot.shape), whole_spec(gains.shape), whole_spec(taps.shape)]
        + [out_weight, out_weight]
        + [whole_spec(g.shape) for g in gates]
        + [whole_spec(conv.shape)],
        [whole_spec(o.shape) for o in outs],
        outs,
        [pltpu.VMEM((rows + 8, width), wide), pltpu.VMEM((rows + 8, width), wide)],
        (*mine, *theirs, res, cot, gains, taps, own, other, *gates, conv),
    )


def branch_grad_kernel(left0, left1, right0, right1, own, other):
    rows = own.shape[0] // 2
    for h, out in enumerate((own, other)):
        for k, (left, right) in enumerate(((left0, right0), (left1, right1))):
            one = left[h] if len(left.shape) == 3 else left[...]
            two = right[h] if k == 1 and len(left.shape) == 2 else right[0]
            out[k * rows : (k + 1) * rows, :] = dot_of(one, two, 0, 0).astype(low)


def branch_grads(n1, g_proj, gate, second):
    width = n1.shape[2]
    gate_spec = pl.BlockSpec((1, *g_proj.shape[1:]), lambda i: (gate, 0, 0))
    if second is None:
        left, right = n1, g_proj
        right_spec = pl.BlockSpec((1, *g_proj.shape[1:]), lambda i: (gate + 1, 0, 0))
    else:
        left, right = second
        right_spec = whole_spec(right.shape)
    specs, shapes = chunk_outs(True, 2 * width, width)
    return local_call(
        branch_grad_kernel,
        (1,),
        [whole_spec(n1.shape), whole_spec(left.shape), gate_spec, right_spec],
        specs,
        shapes,
        [],
        (n1, left, g_proj, right),
    )


def shards(
    tokens,
    cotangent,
    input_projection_weight,
    conv_weight,
    output_projection_weight,
    norm_gains,
    gate_up_weight,
    down_projection_weight,
    in_first,
    in_second,
    conv_first,
    conv_second,
    out_first,
    out_second,
    gain_first,
    gain_second,
    gu_first,
    gu_second,
    down_first,
    down_second,
):
    feat_cols = tokens.shape[1]
    branch_cols = conv_weight.shape[1]
    hidden_cols = down_projection_weight.shape[0]
    block_rows = tokens.shape[0]
    seq_len = max(SEQ_LEAST, block_rows * lax.axis_size("dp") * lax.axis_size("col"))
    data_pos = lax.axis_index("dp")
    row_pos = lax.axis_index("row")
    col_pos = lax.axis_index("col")
    home = row_pos == col_pos
    tail_rows = 16

    in_low = jnp.transpose(input_projection_weight, (1, 0, 2)).astype(low).reshape(-1, branch_cols)
    io_low = jnp.concatenate([in_low, output_projection_weight.astype(low)])
    io_share = share_of(io_low, (1, 0))
    io_got = swap(io_share, "col")
    row_start = (data_pos * lax.axis_size("row") + row_pos) * block_rows
    tail = from_behind(tokens[-2:], ("dp", "row"), 1)
    tail = jnp.where(row_start % seq_len != 0, tail, jnp.zeros_like(tail))
    spare = jnp.zeros((tail_rows - 8, feat_cols), low)
    gain_parts = []
    left = norm_gains
    for _ in range(3):
        gain_parts.append(lax.reduce_precision(left, 8, 7))
        left = left - gain_parts[-1]
    gain_parts = jnp.concatenate(gain_parts).astype(low)
    extra = tie(jnp.concatenate([tail, gain_parts, spare]))
    block = jnp.concatenate([tie(tokens, io_got), extra, cotangent])
    away = to_home(block)
    gu_weight = to_linear(gate_up_weight)
    gate_low, up_low = split_pairs(gu_weight, feat_cols, hidden_cols)
    down_low = down_projection_weight.astype(low)
    both = jnp.stack([block, away])
    both = jnp.where(home, both, home_to_sibling(both))
    gains = both[:, block_rows + 2 : block_rows + 8].astype(wide)
    gains = gains[:, 0:2] + gains[:, 2:4] + gains[:, 4:6]
    gains = [gains[:, k : k + 1] for k in range(2)]
    gate_got = swap(tie(share_of(gate_low, (1, 0)), io_got), "col")
    up_got = swap(tie(share_of(up_low, (0, 1)), gate_got), "col")
    down_got = swap(tie(down_low, up_got), "col")
    io_pair = keep_or_join(0, io_got, flip(io_got, 0))
    io_other = keep_or_join(1, io_pair, flip(io_pair, 1))
    gate_pair = keep_or_join(0, gate_got, flip(tie(gate_got, io_pair), 0))
    up_pair = keep_or_join(1, up_got, flip(tie(up_got, io_pair), 1))
    gate_more = flip(gate_pair, 1)
    up_more = flip(up_pair, 0)
    weights = [gate_low, gate_pair, gate_more, up_low, up_pair, up_more]
    bits = jnp.stack([dp_bit(1), dp_bit(0)]).astype(jnp.int32)
    downs = [down_low, down_got]

    n1, gate_b, gate_c, gate_x, conv, hidden, *branch = branch_forward(
        both, block_rows, tail_rows, gains[0], conv_weight, io_low, io_other
    )
    n2, res, gate, upper, act = ffn_forward(
        bits, both, branch, swap_halves(branch), gains[1], weights
    )

    turns = Turns()
    orders = dict(D="xyl", d="ylx", a="xyl", b="lyx", c="xyl", e="lyx", I="xyl", i="xyl")
    down_half = hidden_cols // 2
    for k, name in enumerate("Dd"):
        split = orders[name][0] == "x"
        turns.add(name, down_grads(act, both, k, down_half, split), orders[name])
    turns.run("Dd")
    g_gate, g_up, *part_two = ffn_backward(
        bits, tie(both, *turns.after), downs, gate, upper, weights
    )
    quarter = feat_cols // 4
    for k, name in enumerate("abce"):
        split = orders[name][0] == "x"
        turns.add(name, pair_grads(n2, g_gate, g_up, k, quarter, split), orders[name])
    turns.run("abcDe")
    g_res, g_branch, g_proj, gain_two_grad, conv_grad = branch_backward(
        part_two,
        swap_halves(part_two),
        tie(res, *turns.after),
        both,
        gains[1],
        conv_weight,
        io_low,
        io_other,
        (gate_b, gate_c, gate_x),
        conv,
    )
    turns.add("I", branch_grads(n1, g_proj, 0, None), orders["I"])
    io_last = branch_grads(n1, g_proj, 2, (hidden, g_branch))
    turns.after += tuple(io_last)
    turns.run("IdabD")

    g_late = tie(g_proj, *turns.after)
    io_half = [half.reshape(4, feat_cols, branch_cols) for half in (io_low, io_other)]
    g_part = jnp.stack(
        [sum(mul_t(g_late[g], io_half[h][g]) for g in range(3)).astype(low) for h in range(2)]
    )
    g_long = g_part.astype(wide) + swap(g_part, "row").astype(wide)
    tok = both[:, : block_rows + 2].astype(wide)
    scale = lax.rsqrt(jnp.sum(tok * tok, axis=(0, 2)) / D + norm_eps)[None, :, None]
    gain_one_grad = jnp.sum(g_long[:, : block_rows + 2] * tok * scale, axis=1)
    small = [
        jnp.concatenate([conv_grad, gain_one_grad[h : h + 1], gain_two_grad[h]]) for h in range(2)
    ]
    spare = jnp.zeros((16, feat_cols), low)
    small = [jnp.pad(part, ((0, 11), (0, 0))).astype(low) for part in small]
    io_long = []
    for h in range(2):
        pieces = jnp.split(io_last[h], 4)
        io_long.append(
            jnp.concatenate(
                [pieces[0], small[h], pieces[1], spare, pieces[2], spare, pieces[3], spare]
            )
        )
    turns.add("i", io_long, orders["i"])
    turns.run("iacebdDIcaeDciIabDdcieIDabdacibce")

    def in_flat(values):
        return jnp.transpose(values, (1, 0, 2)).reshape(3 * feat_cols, branch_cols)

    def in_back(values):
        return jnp.transpose(values.reshape(3, feat_cols, branch_cols), (1, 0, 2))

    wheres = {name: where_of(orders[name]) for name in orders}
    down_state = (down_projection_weight, down_first, down_second)
    gu_state = (gu_weight, to_linear(gu_first), to_linear(gu_second))
    in_state = (in_flat(input_projection_weight), in_flat(in_first), in_flat(in_second))
    out_state = (output_projection_weight, out_first, out_second)
    pairs = 2 * hidden_cols // 128

    turns.reach_shares("Ddabce")
    shares = turns.shares
    down_squares = sum(
        share_norms(wheres[n], shares[n], [(down_state, 4 * k)], down_half // 4)
        for k, n in enumerate("Dd")
    )
    gu_squares = sum(
        share_norms(wheres[n], shares[n], [(gu_state, 2 * k)], quarter // 2 * pairs, pairs=True)
        for k, n in enumerate("abce")
    )
    turns.add_norms("n", jnp.concatenate([gu_squares, down_squares]))
    turns.run("nIdnbin")
    turns.reach_shares("Ii")
    part_rows = feat_cols // 2
    io_squares = share_norms(wheres["i"], shares["i"], [(in_state, 4), (out_state, 0)], part_rows)
    in_squares = share_norms(wheres["I"], shares["I"], [(in_state, 0)], part_rows)
    turns.add_norms("m", io_squares + jnp.pad(in_squares, (0, 2)))
    turns.run("mendnImemimImi")
    turns.finish()
    sums, seen = turns.done, turns.seen

    back = tie(g_long[::-1, block_rows : block_rows + 2], seen["i"][4])
    back = from_behind(back, ("dp", "col"), -1)
    g_n1 = g_long[:, :block_rows].at[:, -2:].add(back)
    tok, scale = tok[:, :block_rows], scale[:, :block_rows]
    weighted = g_n1 * gains[0]
    inner = jnp.sum(weighted * tok, axis=(0, 2))[None, :, None]
    tok_half = (g_res + (scale * weighted - tok * (scale * scale * scale * inner / D))).astype(low)
    token_grad = jnp.where(home, tok_half[0], home_to_away(tok_half[1]))
    act = tie(act, seen["D"][1])
    ffn = jnp.stack([mul(act, downs[h]) for h in range(2)])
    out_half = (res + (ffn + sibling_to_home(ffn.astype(low)).astype(wide))).astype(low)
    output = jnp.where(home, out_half[0], home_to_away(out_half[1]))

    def gu_back(values):
        return from_linear(values, feat_cols, 2)

    def ratio_of(norms):
        norms = jnp.sqrt(norms)
        return norms, (learn_rate * (norms[0] / (norms[1] + adam_eps))).reshape(1)

    (gu_norms, gu_ratio), (down_norms, down_ratio) = [ratio_of(sums["n"][k : k + 2]) for k in (0, 2)]
    (in_norms, in_ratio), (out_norms, out_ratio) = [ratio_of(sums["m"][k : k + 2]) for k in (0, 2)]

    def later_half(count):
        return functools.partial(lamb_plain, lambda i: (i >= count // 2).astype(jnp.int32))

    def fixed_half(half):
        return functools.partial(lamb_plain, lambda i: half)

    down_new = None
    for k in (0, 1):
        name = "Dd"[k]
        block = down_half // 6
        down_new = lamb_call(
            later_half(6), wheres[name], down_ratio, sums[name], block, lambda i: i % 3,
            down_state, block, 6 * k, 6, down_new, [],
        )
    gu_new = None
    gu_rows = 32
    for k in (0, 2, 1, 3):
        name = "abce"[k]
        blocks = quarter // gu_rows
        gu_new = lamb_call(
            lamb_pairs, wheres[name], gu_ratio, sums[name], gu_rows, lambda i: i,
            gu_state, gu_rows * pairs, k * blocks, blocks, gu_new,
            [pltpu.VMEM((gu_rows * pairs, 128), wide)],
        )
    in_new = lamb_call(
        later_half(4), wheres["I"], in_ratio, sums["I"], part_rows, lambda i: i % 2,
        in_state, part_rows, 0, 4, None, [],
    )
    last = sums["i"]
    in_new = lamb_call(
        fixed_half(0), wheres["i"], in_ratio, last, part_rows + 16, lambda i: i,
        in_state, part_rows, 4, 2, in_new, [],
    )
    out_new = lamb_call(
        fixed_half(1), wheres["i"], out_ratio, last, part_rows + 16, lambda i: i,
        out_state, part_rows, 0, 2, None, [],
    )

    small = [part[part_rows : part_rows + 5] for part in last]
    small = jnp.where((wheres["i"][0] >> 1) == 0, small[0], small[1]).astype(wide)
    conv_grad, gains_grad = small[:3], small[3:]
    conv_m, conv_v, conv_u = lamb_moments(conv_weight, conv_grad, conv_first, conv_second, 0.0)
    gain_m, gain_v, gain_u = lamb_moments(norm_gains, gains_grad, gain_first, gain_second, 0.0)
    col_first = (col_pos == 0).astype(wide)
    row_first = (row_pos == 0).astype(wide)
    small_norms = jnp.stack(
        [
            square_pair(conv_weight, conv_u) * col_first,
            square_pair(norm_gains[0], gain_u[0]) * row_first,
            square_pair(norm_gains[1], gain_u[1]) * row_first,
        ]
    )
    small_norms = small_norms + swap(small_norms, "row")
    small_norms = jnp.sqrt(small_norms + swap(small_norms, "col"))
    trust_norms = jnp.stack(
        [
            in_norms,
            small_norms[0],
            out_norms,
            small_norms[1],
            small_norms[2],
            gu_norms,
            down_norms,
        ]
    )
    gains_new = jnp.stack(
        [
            apply_trust(norm_gains[0], gain_u[0], small_norms[1]),
            apply_trust(norm_gains[1], gain_u[1], small_norms[2]),
        ]
    )
    return (
        output,
        token_grad,
        *[in_back(values) for values in in_new],
        apply_trust(conv_weight, conv_u, small_norms[0]),
        conv_m,
        conv_v,
        *out_new,
        gains_new,
        gain_m,
        gain_v,
        *[gu_back(values) for values in gu_new],
        *down_new,
        trust_norms,
    )


def solution(mesh):
    in_specs = (
        P(("dp", "row"), "col"),
        P(("dp", "row"), "col"),
        P("col", None, "row"),
        P(None, "row"),
        P("row", "col"),
        P(None, "col"),
        P("col", None, "row"),
        P("row", "col"),
        P("col", None, "row"),
        P("col", None, "row"),
        P(None, "row"),
        P(None, "row"),
        P("row", "col"),
        P("row", "col"),
        P(None, "col"),
        P(None, "col"),
        P("col", None, "row"),
        P("col", None, "row"),
        P("row", "col"),
        P("row", "col"),
    )
    out_specs = (
        P(("dp", "row"), "col"),
        P(("dp", "row"), "col"),
        P("col", None, "row"),
        P("col", None, "row"),
        P("col", None, "row"),
        P(None, "row"),
        P(None, "row"),
        P(None, "row"),
        P("row", "col"),
        P("row", "col"),
        P("row", "col"),
        P(None, "col"),
        P(None, "col"),
        P(None, "col"),
        P("col", None, "row"),
        P("col", None, "row"),
        P("col", None, "row"),
        P("row", "col"),
        P("row", "col"),
        P("row", "col"),
        P(),
    )
    return jax.shard_map(shards, mesh=mesh, in_specs=in_specs, out_specs=out_specs, check_vma=False)
```

```python
import functools

import jax
import jax.numpy as jnp
from jax import lax
from jax.experimental import pallas as pl
from jax.experimental.layout import Layout, with_layout_constraint
from jax.experimental.pallas import tpu as pltpu
from jax.sharding import PartitionSpec as P

D = 1024
SEQ_LEAST = 4096
STEP = 5
MIB = 1024 * 1024


norm_eps = 1e-05
adam_eps = 1e-06
beta_one = 0.5
beta_two = 0.6
learn_rate = 0.5
decay_rate = 0.01
low = jnp.bfloat16
wide = jnp.float32


def from_behind(block, axis, distance):
    devices = range(lax.axis_size(axis))
    route = [(i - distance, i) for i in devices if i - distance in devices]
    return lax.ppermute(block, axis, route)


def swap(values, axis):
    return lax.ppermute(values, axis, [(0, 1), (1, 0)])


def swap_halves(halves):
    return [swap(half, "row") for half in halves]


def to_home(values):
    return lax.ppermute(values, ("row", "col"), [(1, 0), (2, 3)])


def home_to_sibling(values):
    return lax.ppermute(values, ("row", "col"), [(0, 2), (3, 1)])


def home_to_away(values):
    return lax.ppermute(values, ("row", "col"), [(0, 1), (3, 2)])


def sibling_to_home(values):
    return lax.ppermute(values, ("row", "col"), [(2, 0), (1, 3)])


def contract(left, right, left_dim, right_dim):
    return lax.dot_general(
        left, right, (((left_dim,), (right_dim,)), ((), ())), preferred_element_type=wide
    )


def mul(left, right):
    return contract(left, right, 1, 0)


def mul_t(left, right):
    return contract(left, right, 1, 1)


def t_mul(left, right):
    return contract(left, right, 0, 0)


def lamb_moments(weight, grad, first, second, decay):
    first_new = beta_one * first + (1.0 - beta_one) * grad
    second_new = beta_two * second + (1.0 - beta_two) * grad * grad
    direction = (first_new * (1.0 / (1.0 - beta_one**STEP))) / (
        jnp.sqrt(second_new * (1.0 / (1.0 - beta_two**STEP))) + adam_eps
    ) + decay * weight
    return (first_new, second_new, direction)


def square_pair(weight, direction):
    return jnp.stack([jnp.sum(weight * weight), jnp.sum(direction * direction)])


def kernel_call(kernel, grid, in_specs, out_specs, out_shape, scratch, args, aliases=None, mib=1):
    return pl.pallas_call(
        kernel,
        grid_spec=pltpu.PrefetchScalarGridSpec(
            num_scalar_prefetch=1,
            grid=grid,
            in_specs=in_specs,
            out_specs=out_specs,
            scratch_shapes=scratch,
        ),
        out_shape=out_shape,
        input_output_aliases=aliases or {},
        compiler_params=pltpu.CompilerParams(vmem_limit_bytes=48 * MIB),
        cost_estimate=pl.CostEstimate(flops=0, bytes_accessed=mib * MIB, transcendentals=0),
    )(*args)


SCALARS = pl.BlockSpec(memory_space=pltpu.SMEM)


def norm_kernel(where, grad, *refs):
    sums = refs[-1]
    groups = [refs[:3], refs[3:6]][: len(refs) // 3]
    rows = groups[0][0].shape[0]
    zero = jnp.zeros((8, groups[0][0].shape[1]), wide)
    for k, (p, m, v) in enumerate(groups):

        def body(at, total):
            here = pl.ds(pl.multiple_of(at * 32, 32), 32)
            weight = p[here, :]
            direction = lamb_moments(
                weight, grad[here, :].astype(wide), m[here, :], v[here, :], decay_rate
            )[2]
            return tuple(
                t + (sq[:8] + sq[8:16]) + (sq[16:24] + sq[24:])
                for t, sq in zip(total, (weight * weight, direction * direction))
            )

        total = lax.fori_loop(0, rows // 32, body, (zero, zero))
        mine = 1.0 if len(groups) == 1 else ((where[0] >> 1) == k).astype(wide)
        for j in range(2):
            sums[2 * k + j] = jnp.sum(total[j]) * mine


def norm_pairs_kernel(where, grad, p, m, v, sums):
    rows, cols = grad.shape
    tiles = cols // 128
    side = where[0] >> 1
    zero = jnp.zeros((8, 128), wide)
    total = [zero, zero]
    for tile in range(tiles):
        here = pl.ds(2 * tile + side, rows, stride=2 * tiles)
        weight = p[here, :]
        direction = lamb_moments(
            weight, grad[:, tile * 128 : (tile + 1) * 128].astype(wide), m[here, :], v[here, :], decay_rate
        )[2]
        for j, sq in enumerate((weight * weight, direction * direction)):
            total[j] = total[j] + jnp.sum((sq).reshape(rows // 8, 8, 128), axis=0)
    for j in range(2):
        sums[j] = jnp.sum(total[j])


def share_norms(where, grad, states, rows, pairs=False):
    specs, args = [], []
    for state, at in states:
        for array in state:
            if pairs:
                spec = pl.BlockSpec(
                    (rows, array.shape[1]), lambda i, w, at=at: (at + (w[0] & 1), 0)
                )
            elif len(states) == 2:
                spec = pl.BlockSpec(
                    (rows, array.shape[1]), lambda i, w, at=at: (at + (w[0] & 1), 0)
                )
            else:
                spec = pl.BlockSpec((rows, array.shape[1]), lambda i, w, at=at: (at + w[0], 0))
            specs.append(spec)
            args.append(array)
    return kernel_call(
        norm_pairs_kernel if pairs else norm_kernel,
        (1,),
        [whole_spec(grad.shape)] + specs,
        SCALARS,
        jax.ShapeDtypeStruct((2 * len(states),), wide),
        [],
        (where, grad, *args),
    )


def lamb_loop(refs, outs, ratio, rows, step, pick):
    p, m, v = refs

    def body(at, carry):
        here = pl.ds(pl.multiple_of(at * step, step), step)
        weight = p[here, :]
        first_new, second_new, direction = lamb_moments(
            weight, pick(here), m[here, :], v[here, :], decay_rate
        )
        outs[0][here, :] = weight - ratio * direction
        outs[1][here, :] = first_new
        outs[2][here, :] = second_new
        return carry

    lax.fori_loop(0, rows // step, body, 0)


def lamb_plain(half_of_block, where, ratio, part, got, p, m, v, *outs):
    use = half_of_block(pl.program_id(0)) == (where[0] >> 1)

    def pick(here):
        return jnp.where(use, part[here, :].astype(wide), got[here, :].astype(wide))

    lamb_loop((p, m, v), outs, ratio[0], p.shape[0], 64, pick)


def lamb_pairs(where, ratio, part, got, p, m, v, p_out, m_out, v_out, mixed):
    rows, cols = part.shape
    tiles = cols // 128
    for value, order in ((0, (part, got)), (1, (got, part))):

        @pl.when((where[0] >> 1) == value)
        def _():
            for tile in range(tiles):
                for side, ref in enumerate(order):
                    mixed[pl.ds(2 * tile + side, rows, stride=2 * tiles), :] = ref[
                        :, tile * 128 : (tile + 1) * 128
                    ].astype(wide)

    lamb_loop(
        (p, m, v), (p_out, m_out, v_out), ratio[0], p.shape[0], 192, lambda here: mixed[here, :]
    )


def lamb_call(kernel, where, ratio, grad, grad_block, grad_at, state, block, start, count, before, scratch):
    rows, cols = state[0].shape
    flat = pl.BlockSpec((block, cols), lambda i, w: (i + start, 0))
    grad_spec = pl.BlockSpec((grad_block, grad[0].shape[1]), lambda i, w: (grad_at(i), 0))
    whole = jax.ShapeDtypeStruct((rows, cols), wide)
    args = [where, ratio, *grad, *state]
    specs = [SCALARS, grad_spec, grad_spec, flat, flat, flat]
    run, aliases = kernel, {}
    if before is not None:
        aliases = {len(args) + k: k for k in range(3)}

        def run(*refs):
            kernel(*refs[: len(args)], *refs[len(args) + 3 :])

    return list(
        kernel_call(
            run,
            (count,),
            specs + [pl.BlockSpec(memory_space=pl.ANY)] * len(aliases),
            [flat, flat, flat],
            [whole, whole, whole],
            scratch,
            (*args, *(before or [])),
            aliases,
            mib=26 * count * block * cols // MIB,
        )
    )


def to_linear(values):
    rows, sides, cols = values.shape
    split = with_layout_constraint(
        values.reshape(rows, sides, cols // 128, 128), Layout(major_to_minor=(0, 2, 1, 3))
    )
    return split.transpose(0, 2, 1, 3).reshape(rows * sides * cols // 128, 128)


def from_linear(values, rows, sides):
    cols = values.size // (rows * sides)
    split = values.reshape(rows, cols // 128, sides, 128).transpose(0, 2, 1, 3)
    split = with_layout_constraint(split, Layout(major_to_minor=(0, 2, 1, 3)))
    return split.reshape(rows, sides, cols)


def apply_trust(weight, direction, norms):
    return weight - learn_rate * (norms[0] / (norms[1] + adam_eps)) * direction


def flip(values, bit):
    size = lax.axis_size("dp")
    return lax.ppermute(values, "dp", [(i, i ^ (1 << bit)) for i in range(size)])


def dp_bit(bit):
    return (lax.axis_index("dp") >> bit) & 1


def rows_of(values, start, rows):
    return lax.dynamic_slice_in_dim(values, start, rows, 0)


def total_of(pieces):
    total = pieces[0].astype(wide)
    for piece in pieces[1:]:
        total = total + piece.astype(wide)
    return total


def tie(values, *deps):
    return lax.optimization_barrier((values, *deps))[0]


def low_total(pieces):
    return total_of(pieces).astype(low)


def keep_or_join(bit, part, other):
    return jnp.where(
        dp_bit(bit) == 0,
        jnp.concatenate([part, other]),
        jnp.concatenate([other, part]),
    )


def share_of(weight, order):
    rows = weight.shape[0] // (1 << len(order))
    index = 0
    for bit in order:
        index = 2 * index + dp_bit(bit)
    return rows_of(weight, index * rows, rows)


def half_of(piece, place):
    rows = piece.shape[-2] // 2
    return lax.dynamic_slice_in_dim(piece, place * rows, rows, piece.ndim - 2)


def chunk_sum(chunk, order, keep):
    bits = {"y": 0, "l": 1}
    steps = [name if name == "x" else bits[name] for name in order]
    pieces = [chunk]
    for step in steps:
        if step == "x":
            whole = len(pieces) == 1
            got = yield step, pieces[0][1] if whole else low_total([piece[1] for piece in pieces])
            pieces = [piece[0] for piece in pieces] + [got]
        else:
            here = dp_bit(step)
            got = yield step, low_total([half_of(piece, 1 - here) for piece in pieces])
            pieces = [half_of(piece, here) for piece in pieces] + [got]
    part = low_total(pieces)
    for step in range((lax.axis_size("dp") - 1).bit_length()):
        if step not in steps:
            got = yield step, part
            part = low_total([part, got])
    keep(part)
    first, second = [step for step in steps if step != "x"]
    got = yield second, part
    part = keep_or_join(second, part, got)
    got = yield first, part
    return part, got


def norm_sum(values):
    for step in ("x", "row", 1, 0):
        got = yield step, values
        values = values + got
    return values


def where_of(order):
    bits = {"y": 0, "l": 1}
    first, second = [bits[name] for name in order if name != "x"]
    return (2 * dp_bit(first) + dp_bit(second)).astype(jnp.int32).reshape(1)


def move(step, send):
    if step == "row":
        return swap(send, "row")
    return swap(send, "col") if step == "x" else flip(send, step)


class Turns:
    def __init__(self):
        self.chunks = {}
        self.arrivals = {}
        self.seen = {}
        self.done = {}
        self.shares = {}
        self.after = ()

    def add(self, name, chunk, order):
        self.chunks[name] = chunk_sum(chunk, order, functools.partial(self.shares.__setitem__, name))

    def add_norms(self, name, values):
        self.chunks[name] = norm_sum(values)

    def turn(self, name):
        got = self.arrivals.get(name)
        try:
            if got is None:
                self.seen[name] = []
                step, send = next(self.chunks[name])
                send = tie(send, *self.after)
            else:
                got = tie(got, *self.after)
                self.seen[name].append(got)
                step, send = self.chunks[name].send(got)
        except StopIteration as end:
            self.done[name] = end.value
            return
        self.arrivals[name] = move(step, send)
        self.after = (send,)

    def run(self, names):
        for name in names:
            if name not in self.done:
                self.turn(name)

    def reach_shares(self, names):
        while any(name not in self.shares for name in names):
            self.run([name for name in names if name not in self.shares])

    def finish(self):
        while len(self.done) < len(self.chunks):
            self.run(self.chunks)


def deinterleave(pairs, gate, up):
    rows, cols = gate.shape
    tiles = cols // 128
    for tile in range(tiles):
        for side, out in enumerate((gate, up)):
            out[:, tile * 128 : (tile + 1) * 128] = pairs[
                pl.ds(2 * tile + side, rows, stride=2 * tiles), :
            ].astype(low)


def split_pairs(linear, rows, cols):
    block = 64
    half = jax.ShapeDtypeStruct((rows, cols), low)
    out_spec = pl.BlockSpec((block, cols), lambda i: (i, 0))
    return pl.pallas_call(
        deinterleave,
        grid=(rows // block,),
        in_specs=[pl.BlockSpec((block * 2 * cols // 128, 128), lambda i: (i, 0))],
        out_specs=[out_spec, out_spec],
        out_shape=[half, half],
        compiler_params=pltpu.CompilerParams(vmem_limit_bytes=24 * MIB),
        cost_estimate=pl.CostEstimate(
            flops=rows * cols, bytes_accessed=12 * rows * cols, transcendentals=0
        ),
    )(linear)


def dot_of(left, right, left_dim, right_dim):
    return lax.dot_general(
        left, right, (((left_dim,), (right_dim,)), ((), ())), preferred_element_type=wide
    )


def local_call(kernel, grid, in_specs, out_specs, out_shape, scratch, args, prefetch=0):
    return pl.pallas_call(
        kernel,
        grid_spec=pltpu.PrefetchScalarGridSpec(
            num_scalar_prefetch=prefetch,
            grid=grid,
            in_specs=in_specs,
            out_specs=out_specs,
            scratch_shapes=scratch,
        ),
        out_shape=out_shape,
        compiler_params=pltpu.CompilerParams(vmem_limit_bytes=48 * MIB),
        cost_estimate=pl.CostEstimate(flops=0, bytes_accessed=MIB, transcendentals=0),
    )(*args)


def whole_spec(shape):
    return pl.BlockSpec(shape, lambda *_: (0,) * len(shape))


def shape_of(dims, kind):
    return jax.ShapeDtypeStruct(dims, kind)


def row_scale(halves):
    total = sum(jnp.sum(half * half, axis=1, keepdims=True) for half in halves)
    return lax.rsqrt(total / D + norm_eps)


def branch_kernel(tok, gains, taps, own, other, n1, gate_b, gate_c, gate_x, conv, hidden, part0, part1, ext):
    long, width = n1.shape[1:]
    rows = conv.shape[0]
    step = long // 3

    def gates(at, carry):
        here = pl.ds(pl.multiple_of(at * step, step), step)
        halves = [tok[h, here, :].astype(wide) for h in range(2)]
        scale = row_scale(halves)
        for h in range(2):
            n1[h, here, :] = (halves[h] * scale * gains[h]).astype(low)
        for g, out in enumerate((gate_b, gate_c, gate_x)):
            w = slice(g * width, (g + 1) * width)
            out[here, :] = dot_of(n1[0, here, :], own[w, :], 1, 0) + dot_of(
                n1[1, here, :], other[w, :], 1, 0
            )
        return carry

    lax.fori_loop(0, 3, gates, 0)
    ext[8 : 8 + rows, :] = gate_b[:rows, :] * gate_x[:rows, :]
    ext[6:8, :] = gate_b[rows : rows + 2, :] * gate_x[rows : rows + 2, :]
    w_out = slice(3 * width, 4 * width)
    quarter = rows // 4
    for at in range(4):
        start = at * quarter
        taken = slice(start, start + quarter)
        value = sum(taps[k] * ext[start + 6 + k : start + 6 + k + quarter, :] for k in range(3))
        conv[taken, :] = value
        low_hidden = (gate_c[taken, :] * value).astype(low)
        hidden[taken, :] = low_hidden
        for part, weight in ((part0, own), (part1, other)):
            part[taken, :] = dot_of(low_hidden, weight[w_out, :], 1, 0).astype(low)


def branch_forward(tok, rows, tails, gains, taps, own, other):
    width = tok.shape[2]
    gate = shape_of((rows + tails, width), wide)
    outs = [
        shape_of((2, rows + tails, width), low),
        gate,
        gate,
        gate,
        shape_of((rows, width), wide),
        shape_of((rows, width), low),
        shape_of((rows, width), low),
        shape_of((rows, width), low),
    ]
    args = (tok, gains, taps, own, other)
    return local_call(
        branch_kernel,
        (1,),
        [whole_spec(a.shape) for a in args],
        [whole_spec(o.shape) for o in outs],
        outs,
        [pltpu.VMEM((rows + 8, width), wide)],
        args,
    )


def piece_at(bits, which, piece, width):
    place = bits[which] if piece == 0 else 1 - bits[which]
    return pl.ds(pl.multiple_of(place * width, width), width)


def ffn_kernel(bits, tok, mine0, mine1, theirs0, theirs1, gains, g0, g1, g2, u0, u1, u2, n2, res, gate, up, act):
    width = g1.shape[0]

    @pl.when(pl.program_id(0) == 0)
    def _():
        for h, (mine, theirs) in enumerate(((mine0, theirs0), (mine1, theirs1))):
            res[h] = tok[h, : res.shape[1], :].astype(wide) + (
                mine[...].astype(wide) + theirs[...].astype(wide)
            )
        scale = row_scale([res[0], res[1]])
        for h in range(2):
            n2[h] = (res[h] * scale * gains[h]).astype(low)

    for which, (out, w0, w1, w2) in enumerate(((gate, g0, g1, g2), (up, u0, u1, u2))):
        total = dot_of(n2[0], w0[...], 1, 0)
        for piece, w in enumerate((w1, w2)):
            total += dot_of(n2[1, :, piece_at(bits, which, piece, width)], w[...], 1, 0)
        out[...] = total
    value = gate[...]
    act[...] = (value * jax.nn.sigmoid(value) * up[...]).astype(low)


def ffn_forward(bits, tok, mine, theirs, gains, weights):
    rows, width = mine[0].shape
    cols = weights[0].shape[1]
    tile = cols // 3
    both = (2, rows, width)
    full = whole_spec(both)
    wide_tile = pl.BlockSpec((rows, tile), lambda i, *_: (0, i))
    weight_specs = [pl.BlockSpec((w.shape[0], tile), lambda i, *_: (0, i)) for w in weights]
    return local_call(
        ffn_kernel,
        (3,),
        [whole_spec(tok.shape)]
        + [whole_spec((rows, width))] * 4
        + [whole_spec(gains.shape)]
        + weight_specs,
        [full, full, wide_tile, wide_tile, wide_tile],
        [
            shape_of(both, low),
            shape_of(both, wide),
            shape_of((rows, cols), wide),
            shape_of((rows, cols), wide),
            shape_of((rows, cols), low),
        ],
        [],
        (bits, tok, *mine, *theirs, gains, *weights),
        prefetch=1,
    )


def ffn_back_kernel(
    bits, cot, d_own, d_other, gate, up, g0, g1, g2, u0, u1, u2, g_gate, g_up, part0, part1, total
):
    width = g1.shape[0]

    @pl.when(pl.program_id(0) == 0)
    def _():
        total[...] = jnp.zeros_like(total)

    start = cot.shape[1] - gate.shape[0]
    g_act = dot_of(cot[0, start:, :], d_own[...], 1, 1) + dot_of(cot[1, start:, :], d_other[...], 1, 1)
    value = gate[...]
    sigma = jax.nn.sigmoid(value)
    g_gate[...] = (g_act * up[...] * sigma * (1.0 + value * (1.0 - sigma))).astype(low)
    g_up[...] = (g_act * (value * sigma)).astype(low)
    total[0] += dot_of(g_gate[...], g0[...], 1, 1) + dot_of(g_up[...], u0[...], 1, 1)
    for which, (grad, w1, w2) in enumerate(((g_gate, g1, g2), (g_up, u1, u2))):
        for piece, w in enumerate((w1, w2)):
            total[1, :, piece_at(bits, which, piece, width)] += dot_of(grad[...], w[...], 1, 1)

    @pl.when(pl.program_id(0) == pl.num_programs(0) - 1)
    def _():
        part0[...] = total[0].astype(low)
        part1[...] = total[1].astype(low)


def ffn_backward(bits, cot, downs, gate, up, weights):
    rows, cols = gate.shape
    tile = cols // 3
    part = (rows, cot.shape[2])
    wide_tile = pl.BlockSpec((rows, tile), lambda i, *_: (0, i))
    weight_specs = [pl.BlockSpec((w.shape[0], tile), lambda i, *_: (0, i)) for w in weights]
    down_spec = pl.BlockSpec((tile, downs[0].shape[1]), lambda i, *_: (i, 0))
    return local_call(
        ffn_back_kernel,
        (3,),
        [whole_spec(cot.shape), down_spec, down_spec, wide_tile, wide_tile] + weight_specs,
        [wide_tile, wide_tile, whole_spec(part), whole_spec(part)],
        [shape_of((rows, cols), low)] * 2 + [shape_of(part, low)] * 2,
        [pltpu.VMEM((2, *part), wide)],
        (bits, cot, *downs, gate, up, *weights),
        prefetch=1,
    )


def put(outs, half, rows, value):
    if len(outs) == 2:
        outs[half][rows, :] = value.astype(low)
    else:
        outs[0][half, rows, :] = value.astype(low)


def chunk_outs(split, rows, cols):
    if split:
        return [whole_spec((rows, cols))] * 2, [shape_of((rows, cols), low)] * 2
    return [whole_spec((2, rows, cols))], [shape_of((2, rows, cols), low)]


def pair_grad_kernel(n2, g_gate, g_up, *outs):
    rows = n2.shape[2]
    for h in range(2):
        for side, grad in enumerate((g_gate, g_up)):
            put(outs, h, slice(side * rows, (side + 1) * rows), dot_of(n2[h], grad[...], 0, 0))


def pair_grads(n2, g_gate, g_up, at, rows, split):
    specs, shapes = chunk_outs(split, 2 * rows, g_gate.shape[1])
    outs = local_call(
        pair_grad_kernel,
        (1,),
        [
            pl.BlockSpec((2, n2.shape[1], rows), lambda i: (0, 0, at)),
            whole_spec(g_gate.shape),
            whole_spec(g_up.shape),
        ],
        specs,
        shapes,
        [],
        (n2, g_gate, g_up),
    )
    return tuple(outs) if split else outs[0]


def down_grad_kernel(act, cot, *outs):
    start = cot.shape[1] - act.shape[0]
    for h in range(2):
        put(outs, h, slice(None), dot_of(act[...], cot[h, start:, :], 0, 0))


def down_grads(act, cot, at, rows, split):
    specs, shapes = chunk_outs(split, rows, cot.shape[2])
    outs = local_call(
        down_grad_kernel,
        (1,),
        [pl.BlockSpec((act.shape[0], rows), lambda i: (0, at)), whole_spec(cot.shape)],
        specs,
        shapes,
        [],
        (act, cot),
    )
    return tuple(outs) if split else outs[0]


def branch_back_kernel(
    mine0, mine1, theirs0, theirs1, res, cot, gains, taps, own, other, gate_b, gate_c, gate_x, conv,
    g_res, g_low, g_proj, gain_grad, tap_grad, ext, ext_grad,
):
    _, rows, width = res.shape
    scale = row_scale([res[0], res[1]])
    grads = [
        mine[...].astype(wide) + theirs[...].astype(wide)
        for mine, theirs in ((mine0, theirs0), (mine1, theirs1))
    ]
    inner = sum(
        jnp.sum(grads[h] * gains[h] * res[h], axis=1, keepdims=True) for h in range(2)
    )
    factor = scale * scale * scale * inner / D
    for h in range(2):
        gain_grad[h] = jnp.sum(grads[h] * res[h] * scale, axis=0, keepdims=True)
        value = cot[h, cot.shape[1] - rows :, :].astype(wide) + (scale * (grads[h] * gains[h]) - res[h] * factor)
        g_res[h] = value
        g_low[h] = value.astype(low)
    g_hidden = dot_of(g_low[0], own[...], 1, 1) + dot_of(g_low[1], other[...], 1, 1)
    g_proj[1, :rows, :] = (g_hidden * conv[...]).astype(low)
    g_conv = g_hidden * gate_c[:rows, :]
    ext_grad[:rows, :] = g_conv
    ext_grad[rows:, :] = jnp.zeros((8, width), wide)
    ext[8 : 8 + rows, :] = gate_b[:rows, :] * gate_x[:rows, :]
    ext[6:8, :] = gate_b[rows : rows + 2, :] * gate_x[rows : rows + 2, :]
    for k in range(3):
        tap_grad[k : k + 1, :] = jnp.sum(
            g_conv * ext[6 + k : 6 + k + rows, :], axis=0, keepdims=True
        )
    g_mixed = sum(taps[2 - k] * ext_grad[k : k + rows, :] for k in range(3))
    g_proj[0, :rows, :] = (g_mixed * gate_x[:rows, :]).astype(low)
    g_proj[2, :rows, :] = (g_mixed * gate_b[:rows, :]).astype(low)
    tails = g_proj.shape[1] - rows
    row = lax.broadcasted_iota(jnp.int32, (tails, width), 0)
    first, second = ext_grad[0:1, :], ext_grad[1:2, :]
    g_before = jnp.where(
        row == 0,
        taps[0] * first,
        jnp.where(row == 1, taps[1] * first + taps[0] * second, 0.0),
    )
    g_proj[0, rows:, :] = (g_before * gate_x[rows:, :]).astype(low)
    g_proj[1, rows:, :] = jnp.zeros((tails, width), low)
    g_proj[2, rows:, :] = (g_before * gate_b[rows:, :]).astype(low)


def branch_backward(mine, theirs, res, cot, gains, taps, own, other, gates, conv):
    _, rows, width = res.shape
    long = gates[0].shape[0]
    out_weight = pl.BlockSpec((width, width), lambda i, *_: (3, 0))
    outs = [
        shape_of(res.shape, wide),
        shape_of(res.shape, low),
        shape_of((3, long, width), low),
        shape_of((2, 1, width), wide),
        shape_of((3, width), wide),
    ]
    full = whole_spec(res.shape)
    return local_call(
        branch_back_kernel,
        (1,),
        [whole_spec((rows, width))] * 4
        + [full, whole_spec(cot.shape), whole_spec(gains.shape), whole_spec(taps.shape)]
        + [out_weight, out_weight]
        + [whole_spec(g.shape) for g in gates]
        + [whole_spec(conv.shape)],
        [whole_spec(o.shape) for o in outs],
        outs,
        [pltpu.VMEM((rows + 8, width), wide), pltpu.VMEM((rows + 8, width), wide)],
        (*mine, *theirs, res, cot, gains, taps, own, other, *gates, conv),
    )


def branch_grad_kernel(left0, left1, right0, right1, own, other):
    rows = own.shape[0] // 2
    for h, out in enumerate((own, other)):
        for k, (left, right) in enumerate(((left0, right0), (left1, right1))):
            one = left[h] if len(left.shape) == 3 else left[...]
            two = right[h] if k == 1 and len(left.shape) == 2 else right[0]
            out[k * rows : (k + 1) * rows, :] = dot_of(one, two, 0, 0).astype(low)


def branch_grads(n1, g_proj, gate, second):
    width = n1.shape[2]
    gate_spec = pl.BlockSpec((1, *g_proj.shape[1:]), lambda i: (gate, 0, 0))
    if second is None:
        left, right = n1, g_proj
        right_spec = pl.BlockSpec((1, *g_proj.shape[1:]), lambda i: (gate + 1, 0, 0))
    else:
        left, right = second
        right_spec = whole_spec(right.shape)
    specs, shapes = chunk_outs(True, 2 * width, width)
    return local_call(
        branch_grad_kernel,
        (1,),
        [whole_spec(n1.shape), whole_spec(left.shape), gate_spec, right_spec],
        specs,
        shapes,
        [],
        (n1, left, g_proj, right),
    )


def shards(
    tokens,
    cotangent,
    input_projection_weight,
    conv_weight,
    output_projection_weight,
    norm_gains,
    gate_up_weight,
    down_projection_weight,
    in_first,
    in_second,
    conv_first,
    conv_second,
    out_first,
    out_second,
    gain_first,
    gain_second,
    gu_first,
    gu_second,
    down_first,
    down_second,
):
    feat_cols = tokens.shape[1]
    branch_cols = conv_weight.shape[1]
    hidden_cols = down_projection_weight.shape[0]
    block_rows = tokens.shape[0]
    seq_len = max(SEQ_LEAST, block_rows * lax.axis_size("dp") * lax.axis_size("col"))
    data_pos = lax.axis_index("dp")
    row_pos = lax.axis_index("row")
    col_pos = lax.axis_index("col")
    home = row_pos == col_pos
    tail_rows = 16

    in_low = jnp.transpose(input_projection_weight, (1, 0, 2)).astype(low).reshape(-1, branch_cols)
    io_low = jnp.concatenate([in_low, output_projection_weight.astype(low)])
    io_share = share_of(io_low, (1, 0))
    io_got = swap(io_share, "col")
    io_pair = keep_or_join(0, io_got, flip(io_got, 0))
    row_start = (data_pos * lax.axis_size("row") + row_pos) * block_rows
    tail = from_behind(tokens[-2:], ("dp", "row"), 1)
    tail = jnp.where(row_start % seq_len != 0, tail, jnp.zeros_like(tail))
    spare = jnp.zeros((tail_rows - 8, feat_cols), low)
    gain_parts = []
    left = norm_gains
    for _ in range(3):
        gain_parts.append(lax.reduce_precision(left, 8, 7))
        left = left - gain_parts[-1]
    gain_parts = jnp.concatenate(gain_parts).astype(low)
    extra = tie(jnp.concatenate([tail, gain_parts, spare]))
    block = jnp.concatenate([tie(tokens, io_pair), extra, cotangent])
    away = to_home(block)
    gu_weight = to_linear(gate_up_weight)
    gate_low, up_low = split_pairs(gu_weight, feat_cols, hidden_cols)
    down_low = down_projection_weight.astype(low)
    both = jnp.stack([block, away])
    both = jnp.where(home, both, home_to_sibling(both))
    gains = both[:, block_rows + 2 : block_rows + 8].astype(wide)
    gains = gains[:, 0:2] + gains[:, 2:4] + gains[:, 4:6]
    gains = [gains[:, k : k + 1] for k in range(2)]
    gate_got = swap(tie(share_of(gate_low, (1, 0)), io_got), "col")
    up_got = swap(tie(share_of(up_low, (0, 1)), gate_got), "col")
    down_got = swap(tie(down_low, up_got), "col")
    io_other = keep_or_join(1, io_pair, flip(io_pair, 1))
    gate_pair = keep_or_join(0, gate_got, flip(tie(gate_got, io_pair), 0))
    up_pair = keep_or_join(1, up_got, flip(tie(up_got, io_other), 1))
    gate_more = flip(tie(gate_pair, io_other), 1)
    up_more = flip(up_pair, 0)
    weights = [gate_low, gate_pair, gate_more, up_low, up_pair, up_more]
    bits = jnp.stack([dp_bit(1), dp_bit(0)]).astype(jnp.int32)
    downs = [down_low, down_got]

    n1, gate_b, gate_c, gate_x, conv, hidden, *branch = branch_forward(
        both, block_rows, tail_rows, gains[0], conv_weight, io_low, io_other
    )
    n2, res, gate, upper, act = ffn_forward(
        bits, both, branch, swap_halves(branch), gains[1], weights
    )

    turns = Turns()
    orders = dict(D="xyl", d="ylx", a="xyl", b="lyx", c="xyl", e="lyx", I="xyl", i="xyl")
    down_half = hidden_cols // 2
    for k, name in enumerate("Dd"):
        split = orders[name][0] == "x"
        turns.add(name, down_grads(act, both, k, down_half, split), orders[name])
    turns.run("Dd")
    g_gate, g_up, *part_two = ffn_backward(
        bits, tie(both, *turns.after), downs, gate, upper, weights
    )
    quarter = feat_cols // 4
    for k, name in enumerate("abce"):
        split = orders[name][0] == "x"
        turns.add(name, pair_grads(n2, g_gate, g_up, k, quarter, split), orders[name])
    turns.run("abcDe")
    g_res, g_branch, g_proj, gain_two_grad, conv_grad = branch_backward(
        part_two,
        swap_halves(part_two),
        tie(res, *turns.after),
        both,
        gains[1],
        conv_weight,
        io_low,
        io_other,
        (gate_b, gate_c, gate_x),
        conv,
    )
    turns.add("I", branch_grads(n1, g_proj, 0, None), orders["I"])
    io_last = branch_grads(n1, g_proj, 2, (hidden, g_branch))
    turns.after += tuple(io_last)
    turns.run("IdabD")

    g_late = tie(g_proj, *turns.after)
    io_half = [half.reshape(4, feat_cols, branch_cols) for half in (io_low, io_other)]
    g_part = jnp.stack(
        [sum(mul_t(g_late[g], io_half[h][g]) for g in range(3)).astype(low) for h in range(2)]
    )
    g_long = g_part.astype(wide) + swap(g_part, "row").astype(wide)
    tok = both[:, : block_rows + 2].astype(wide)
    scale = lax.rsqrt(jnp.sum(tok * tok, axis=(0, 2)) / D + norm_eps)[None, :, None]
    gain_one_grad = jnp.sum(g_long[:, : block_rows + 2] * tok * scale, axis=1)
    small = [
        jnp.concatenate([conv_grad, gain_one_grad[h : h + 1], gain_two_grad[h]]) for h in range(2)
    ]
    spare = jnp.zeros((16, feat_cols), low)
    small = [jnp.pad(part, ((0, 11), (0, 0))).astype(low) for part in small]
    io_long = []
    for h in range(2):
        pieces = jnp.split(io_last[h], 4)
        io_long.append(
            jnp.concatenate(
                [pieces[0], small[h], pieces[1], spare, pieces[2], spare, pieces[3], spare]
            )
        )
    turns.add("i", io_long, orders["i"])
    turns.run("iacebdDIcaeDciIabDdcieIDabd")

    def in_flat(values):
        return jnp.transpose(values, (1, 0, 2)).reshape(3 * feat_cols, branch_cols)

    def in_back(values):
        return jnp.transpose(values.reshape(3, feat_cols, branch_cols), (1, 0, 2))

    wheres = {name: where_of(orders[name]) for name in orders}
    down_state = (down_projection_weight, down_first, down_second)
    gu_state = (gu_weight, to_linear(gu_first), to_linear(gu_second))
    in_state = (in_flat(input_projection_weight), in_flat(in_first), in_flat(in_second))
    out_state = (output_projection_weight, out_first, out_second)
    pairs = 2 * hidden_cols // 128

    shares = turns.shares
    part_rows = feat_cols // 2
    turns.reach_shares("Dd")
    down_squares = sum(
        share_norms(wheres[n], shares[n], [(down_state, 4 * k)], down_half // 4)
        for k, n in enumerate("Dd")
    )
    turns.add_norms("p", down_squares)
    turns.run("pacpibpcep")
    turns.reach_shares("abce")
    gu_squares = sum(
        share_norms(wheres[n], shares[n], [(gu_state, 2 * k)], quarter // 2 * pairs, pairs=True)
        for k, n in enumerate("abce")
    )
    turns.add_norms("n", gu_squares)
    turns.run("nIdpnbin")
    turns.reach_shares("Ii")
    io_squares = share_norms(wheres["i"], shares["i"], [(in_state, 4), (out_state, 0)], part_rows)
    in_squares = share_norms(wheres["I"], shares["I"], [(in_state, 0)], part_rows)
    turns.add_norms("m", io_squares + jnp.pad(in_squares, (0, 2)))
    turns.run("memdnmImenmiIi")
    turns.finish()
    sums, seen = turns.done, turns.seen

    back = tie(g_long[::-1, block_rows : block_rows + 2], seen["i"][4])
    back = from_behind(back, ("dp", "col"), -1)
    g_n1 = g_long[:, :block_rows].at[:, -2:].add(back)
    tok, scale = tok[:, :block_rows], scale[:, :block_rows]
    weighted = g_n1 * gains[0]
    inner = jnp.sum(weighted * tok, axis=(0, 2))[None, :, None]
    tok_half = (g_res + (scale * weighted - tok * (scale * scale * scale * inner / D))).astype(low)
    token_grad = jnp.where(home, tok_half[0], home_to_away(tok_half[1]))
    act = tie(act, seen["D"][1])
    ffn = jnp.stack([mul(act, downs[h]) for h in range(2)])
    out_half = (res + (ffn + sibling_to_home(ffn.astype(low)).astype(wide))).astype(low)
    output = jnp.where(home, out_half[0], home_to_away(out_half[1]))

    def gu_back(values):
        return from_linear(values, feat_cols, 2)

    def ratio_of(norms):
        norms = jnp.sqrt(norms)
        return norms, (learn_rate * (norms[0] / (norms[1] + adam_eps))).reshape(1)

    (gu_norms, gu_ratio), (down_norms, down_ratio) = [ratio_of(sums[name]) for name in "np"]
    (in_norms, in_ratio), (out_norms, out_ratio) = [ratio_of(sums["m"][k : k + 2]) for k in (0, 2)]

    def later_half(count):
        return functools.partial(lamb_plain, lambda i: (i >= count // 2).astype(jnp.int32))

    def fixed_half(half):
        return functools.partial(lamb_plain, lambda i: half)

    down_new = None
    for k in (0, 1):
        name = "Dd"[k]
        block = down_half // 6
        down_new = lamb_call(
            later_half(6), wheres[name], down_ratio, sums[name], block, lambda i: i % 3,
            down_state, block, 6 * k, 6, down_new, [],
        )
    gu_new = None
    gu_rows = 32
    for k in (0, 2, 1, 3):
        name = "abce"[k]
        blocks = quarter // gu_rows
        gu_new = lamb_call(
            lamb_pairs, wheres[name], gu_ratio, sums[name], gu_rows, lambda i: i,
            gu_state, gu_rows * pairs, k * blocks, blocks, gu_new,
            [pltpu.VMEM((gu_rows * pairs, 128), wide)],
        )
    last = sums["i"]
    small = [part[part_rows : part_rows + 5] for part in last]
    small = jnp.where((wheres["i"][0] >> 1) == 0, small[0], small[1]).astype(wide)
    conv_grad, gains_grad = small[:3], small[3:]
    conv_m, conv_v, conv_u = lamb_moments(conv_weight, conv_grad, conv_first, conv_second, 0.0)
    gain_m, gain_v, gain_u = lamb_moments(norm_gains, gains_grad, gain_first, gain_second, 0.0)
    col_first = (col_pos == 0).astype(wide)
    row_first = (row_pos == 0).astype(wide)
    small_norms = jnp.stack(
        [
            square_pair(conv_weight, conv_u) * col_first,
            square_pair(norm_gains[0], gain_u[0]) * row_first,
            square_pair(norm_gains[1], gain_u[1]) * row_first,
        ]
    )
    last = [tie(part, small_norms) for part in last]
    small_norms = small_norms + swap(small_norms, "row")
    in_new = lamb_call(
        later_half(4), wheres["I"], in_ratio, sums["I"], part_rows, lambda i: i % 2,
        in_state, part_rows, 0, 4, None, [],
    )
    in_new = lamb_call(
        fixed_half(0), wheres["i"], in_ratio, last, part_rows + 16, lambda i: i,
        in_state, part_rows, 4, 2, in_new, [],
    )
    out_new = lamb_call(
        fixed_half(1), wheres["i"], out_ratio, last, part_rows + 16, lambda i: i,
        out_state, part_rows, 0, 2, None, [],
    )

    small_norms = jnp.sqrt(small_norms + swap(small_norms, "col"))
    trust_norms = jnp.stack(
        [
            in_norms,
            small_norms[0],
            out_norms,
            small_norms[1],
            small_norms[2],
            gu_norms,
            down_norms,
        ]
    )
    gains_new = jnp.stack(
        [
            apply_trust(norm_gains[0], gain_u[0], small_norms[1]),
            apply_trust(norm_gains[1], gain_u[1], small_norms[2]),
        ]
    )
    return (
        output,
        token_grad,
        *[in_back(values) for values in in_new],
        apply_trust(conv_weight, conv_u, small_norms[0]),
        conv_m,
        conv_v,
        *out_new,
        gains_new,
        gain_m,
        gain_v,
        *[gu_back(values) for values in gu_new],
        *down_new,
        trust_norms,
    )


def solution(mesh):
    in_specs = (
        P(("dp", "row"), "col"),
        P(("dp", "row"), "col"),
        P("col", None, "row"),
        P(None, "row"),
        P("row", "col"),
        P(None, "col"),
        P("col", None, "row"),
        P("row", "col"),
        P("col", None, "row"),
        P("col", None, "row"),
        P(None, "row"),
        P(None, "row"),
        P("row", "col"),
        P("row", "col"),
        P(None, "col"),
        P(None, "col"),
        P("col", None, "row"),
        P("col", None, "row"),
        P("row", "col"),
        P("row", "col"),
    )
    out_specs = (
        P(("dp", "row"), "col"),
        P(("dp", "row"), "col"),
        P("col", None, "row"),
        P("col", None, "row"),
        P("col", None, "row"),
        P(None, "row"),
        P(None, "row"),
        P(None, "row"),
        P("row", "col"),
        P("row", "col"),
        P("row", "col"),
        P(None, "col"),
        P(None, "col"),
        P(None, "col"),
        P("col", None, "row"),
        P("col", None, "row"),
        P("col", None, "row"),
        P("row", "col"),
        P("row", "col"),
        P("row", "col"),
        P(),
    )
    return jax.shard_map(shards, mesh=mesh, in_specs=in_specs, out_specs=out_specs, check_vma=False)
```

```python
import functools

import jax
import jax.numpy as jnp
from jax import lax
from jax.experimental import pallas as pl
from jax.experimental.layout import Layout, with_layout_constraint
from jax.experimental.pallas import tpu as pltpu
from jax.sharding import PartitionSpec as P

D = 1024
SEQ_LEAST = 4096
STEP = 5
MIB = 1024 * 1024


norm_eps = 1e-05
adam_eps = 1e-06
beta_one = 0.5
beta_two = 0.6
learn_rate = 0.5
decay_rate = 0.01
low = jnp.bfloat16
wide = jnp.float32


def from_behind(block, axis, distance):
    devices = range(lax.axis_size(axis))
    route = [(i - distance, i) for i in devices if i - distance in devices]
    return lax.ppermute(block, axis, route)


def swap(values, axis):
    return lax.ppermute(values, axis, [(0, 1), (1, 0)])


def swap_halves(halves):
    return [swap(half, "row") for half in halves]


def to_home(values):
    return lax.ppermute(values, ("row", "col"), [(1, 0), (2, 3)])


def home_to_sibling(values):
    return lax.ppermute(values, ("row", "col"), [(0, 2), (3, 1)])


def home_to_away(values):
    return lax.ppermute(values, ("row", "col"), [(0, 1), (3, 2)])


def sibling_to_home(values):
    return lax.ppermute(values, ("row", "col"), [(2, 0), (1, 3)])


def contract(left, right, left_dim, right_dim):
    return lax.dot_general(
        left, right, (((left_dim,), (right_dim,)), ((), ())), preferred_element_type=wide
    )


def mul(left, right):
    return contract(left, right, 1, 0)


def mul_t(left, right):
    return contract(left, right, 1, 1)


def t_mul(left, right):
    return contract(left, right, 0, 0)


def lamb_moments(weight, grad, first, second, decay):
    first_new = beta_one * first + (1.0 - beta_one) * grad
    second_new = beta_two * second + (1.0 - beta_two) * grad * grad
    direction = (first_new * (1.0 / (1.0 - beta_one**STEP))) / (
        jnp.sqrt(second_new * (1.0 / (1.0 - beta_two**STEP))) + adam_eps
    ) + decay * weight
    return (first_new, second_new, direction)


def square_pair(weight, direction):
    return jnp.stack([jnp.sum(weight * weight), jnp.sum(direction * direction)])


def kernel_call(kernel, grid, in_specs, out_specs, out_shape, scratch, args, aliases=None, mib=1):
    return pl.pallas_call(
        kernel,
        grid_spec=pltpu.PrefetchScalarGridSpec(
            num_scalar_prefetch=1,
            grid=grid,
            in_specs=in_specs,
            out_specs=out_specs,
            scratch_shapes=scratch,
        ),
        out_shape=out_shape,
        input_output_aliases=aliases or {},
        compiler_params=pltpu.CompilerParams(vmem_limit_bytes=48 * MIB),
        cost_estimate=pl.CostEstimate(flops=0, bytes_accessed=mib * MIB, transcendentals=0),
    )(*args)


SCALARS = pl.BlockSpec(memory_space=pltpu.SMEM)


def norm_kernel(where, grad, *refs):
    sums = refs[-1]
    groups = [refs[:3], refs[3:6]][: len(refs) // 3]
    rows = groups[0][0].shape[0]
    zero = jnp.zeros((8, groups[0][0].shape[1]), wide)
    for k, (p, m, v) in enumerate(groups):

        def body(at, total):
            here = pl.ds(pl.multiple_of(at * 32, 32), 32)
            weight = p[here, :]
            direction = lamb_moments(
                weight, grad[here, :].astype(wide), m[here, :], v[here, :], decay_rate
            )[2]
            return tuple(
                t + (sq[:8] + sq[8:16]) + (sq[16:24] + sq[24:])
                for t, sq in zip(total, (weight * weight, direction * direction))
            )

        total = lax.fori_loop(0, rows // 32, body, (zero, zero))
        mine = 1.0 if len(groups) == 1 else ((where[0] >> 1) == k).astype(wide)
        for j in range(2):
            sums[2 * k + j] = jnp.sum(total[j]) * mine


def norm_pairs_kernel(where, grad, p, m, v, sums):
    rows, cols = grad.shape
    tiles = cols // 128
    side = where[0] >> 1
    zero = jnp.zeros((8, 128), wide)
    total = [zero, zero]
    for tile in range(tiles):
        here = pl.ds(2 * tile + side, rows, stride=2 * tiles)
        weight = p[here, :]
        direction = lamb_moments(
            weight, grad[:, tile * 128 : (tile + 1) * 128].astype(wide), m[here, :], v[here, :], decay_rate
        )[2]
        for j, sq in enumerate((weight * weight, direction * direction)):
            total[j] = total[j] + jnp.sum((sq).reshape(rows // 8, 8, 128), axis=0)
    for j in range(2):
        sums[j] = jnp.sum(total[j])


def share_norms(where, grad, states, rows, pairs=False):
    specs, args = [], []
    for state, at in states:
        for array in state:
            if pairs:
                spec = pl.BlockSpec(
                    (rows, array.shape[1]), lambda i, w, at=at: (at + (w[0] & 1), 0)
                )
            elif len(states) == 2:
                spec = pl.BlockSpec(
                    (rows, array.shape[1]), lambda i, w, at=at: (at + (w[0] & 1), 0)
                )
            else:
                spec = pl.BlockSpec((rows, array.shape[1]), lambda i, w, at=at: (at + w[0], 0))
            specs.append(spec)
            args.append(array)
    return kernel_call(
        norm_pairs_kernel if pairs else norm_kernel,
        (1,),
        [whole_spec(grad.shape)] + specs,
        SCALARS,
        jax.ShapeDtypeStruct((2 * len(states),), wide),
        [],
        (where, grad, *args),
    )


def lamb_loop(refs, outs, ratio, rows, step, pick):
    p, m, v = refs

    def body(at, carry):
        here = pl.ds(pl.multiple_of(at * step, step), step)
        weight = p[here, :]
        first_new, second_new, direction = lamb_moments(
            weight, pick(here), m[here, :], v[here, :], decay_rate
        )
        outs[0][here, :] = weight - ratio * direction
        outs[1][here, :] = first_new
        outs[2][here, :] = second_new
        return carry

    lax.fori_loop(0, rows // step, body, 0)


def lamb_plain(half_of_block, where, ratio, part, got, p, m, v, *outs):
    use = half_of_block(pl.program_id(0)) == (where[0] >> 1)

    def pick(here):
        return jnp.where(use, part[here, :].astype(wide), got[here, :].astype(wide))

    lamb_loop((p, m, v), outs, ratio[0], p.shape[0], 64, pick)


def lamb_pairs(where, ratio, part, got, p, m, v, p_out, m_out, v_out, mixed):
    rows, cols = part.shape
    tiles = cols // 128
    for value, order in ((0, (part, got)), (1, (got, part))):

        @pl.when((where[0] >> 1) == value)
        def _():
            for tile in range(tiles):
                for side, ref in enumerate(order):
                    mixed[pl.ds(2 * tile + side, rows, stride=2 * tiles), :] = ref[
                        :, tile * 128 : (tile + 1) * 128
                    ].astype(wide)

    lamb_loop(
        (p, m, v), (p_out, m_out, v_out), ratio[0], p.shape[0], 192, lambda here: mixed[here, :]
    )


def lamb_call(kernel, where, ratio, grad, grad_block, grad_at, state, block, start, count, before, scratch):
    rows, cols = state[0].shape
    flat = pl.BlockSpec((block, cols), lambda i, w: (i + start, 0))
    grad_spec = pl.BlockSpec((grad_block, grad[0].shape[1]), lambda i, w: (grad_at(i), 0))
    whole = jax.ShapeDtypeStruct((rows, cols), wide)
    args = [where, ratio, *grad, *state]
    specs = [SCALARS, grad_spec, grad_spec, flat, flat, flat]
    run, aliases = kernel, {}
    if before is not None:
        aliases = {len(args) + k: k for k in range(3)}

        def run(*refs):
            kernel(*refs[: len(args)], *refs[len(args) + 3 :])

    return list(
        kernel_call(
            run,
            (count,),
            specs + [pl.BlockSpec(memory_space=pl.ANY)] * len(aliases),
            [flat, flat, flat],
            [whole, whole, whole],
            scratch,
            (*args, *(before or [])),
            aliases,
            mib=26 * count * block * cols // MIB,
        )
    )


def to_linear(values):
    rows, sides, cols = values.shape
    split = with_layout_constraint(
        values.reshape(rows, sides, cols // 128, 128), Layout(major_to_minor=(0, 2, 1, 3))
    )
    return split.transpose(0, 2, 1, 3).reshape(rows * sides * cols // 128, 128)


def from_linear(values, rows, sides):
    cols = values.size // (rows * sides)
    split = values.reshape(rows, cols // 128, sides, 128).transpose(0, 2, 1, 3)
    split = with_layout_constraint(split, Layout(major_to_minor=(0, 2, 1, 3)))
    return split.reshape(rows, sides, cols)


def apply_trust(weight, direction, norms):
    return weight - learn_rate * (norms[0] / (norms[1] + adam_eps)) * direction


def flip(values, bit):
    size = lax.axis_size("dp")
    return lax.ppermute(values, "dp", [(i, i ^ (1 << bit)) for i in range(size)])


def dp_bit(bit):
    return (lax.axis_index("dp") >> bit) & 1


def rows_of(values, start, rows):
    return lax.dynamic_slice_in_dim(values, start, rows, 0)


def total_of(pieces):
    total = pieces[0].astype(wide)
    for piece in pieces[1:]:
        total = total + piece.astype(wide)
    return total


def tie(values, *deps):
    return lax.optimization_barrier((values, *deps))[0]


def low_total(pieces):
    return total_of(pieces).astype(low)


def keep_or_join(bit, part, other):
    return jnp.where(
        dp_bit(bit) == 0,
        jnp.concatenate([part, other]),
        jnp.concatenate([other, part]),
    )


def share_of(weight, order):
    rows = weight.shape[0] // (1 << len(order))
    index = 0
    for bit in order:
        index = 2 * index + dp_bit(bit)
    return rows_of(weight, index * rows, rows)


def half_of(piece, place):
    rows = piece.shape[-2] // 2
    return lax.dynamic_slice_in_dim(piece, place * rows, rows, piece.ndim - 2)


def chunk_sum(chunk, order, keep):
    bits = {"y": 0, "l": 1}
    steps = [name if name == "x" else bits[name] for name in order]
    pieces = [chunk]
    for step in steps:
        if step == "x":
            whole = len(pieces) == 1
            got = yield step, pieces[0][1] if whole else low_total([piece[1] for piece in pieces])
            pieces = [piece[0] for piece in pieces] + [got]
        else:
            here = dp_bit(step)
            got = yield step, low_total([half_of(piece, 1 - here) for piece in pieces])
            pieces = [half_of(piece, here) for piece in pieces] + [got]
    part = low_total(pieces)
    for step in range((lax.axis_size("dp") - 1).bit_length()):
        if step not in steps:
            got = yield step, part
            part = low_total([part, got])
    keep(part)
    first, second = [step for step in steps if step != "x"]
    got = yield second, part
    part = keep_or_join(second, part, got)
    got = yield first, part
    return part, got


def norm_sum(values):
    for step in ("x", "row", 1, 0):
        got = yield step, values
        values = values + got
    return values


def where_of(order):
    bits = {"y": 0, "l": 1}
    first, second = [bits[name] for name in order if name != "x"]
    return (2 * dp_bit(first) + dp_bit(second)).astype(jnp.int32).reshape(1)


def move(step, send):
    if step == "row":
        return swap(send, "row")
    return swap(send, "col") if step == "x" else flip(send, step)


class Turns:
    def __init__(self):
        self.chunks = {}
        self.arrivals = {}
        self.seen = {}
        self.done = {}
        self.shares = {}
        self.after = ()

    def add(self, name, chunk, order):
        self.chunks[name] = chunk_sum(chunk, order, functools.partial(self.shares.__setitem__, name))

    def add_norms(self, name, values):
        self.chunks[name] = norm_sum(values)

    def turn(self, name):
        got = self.arrivals.get(name)
        try:
            if got is None:
                self.seen[name] = []
                step, send = next(self.chunks[name])
                send = tie(send, *self.after)
            else:
                got = tie(got, *self.after)
                self.seen[name].append(got)
                step, send = self.chunks[name].send(got)
        except StopIteration as end:
            self.done[name] = end.value
            return
        self.arrivals[name] = move(step, send)
        self.after = (send,)

    def run(self, names):
        for name in names:
            if name not in self.done:
                self.turn(name)

    def reach_shares(self, names):
        while any(name not in self.shares for name in names):
            self.run([name for name in names if name not in self.shares])

    def finish(self):
        while len(self.done) < len(self.chunks):
            self.run(self.chunks)


def deinterleave(pairs, gate, up):
    rows, cols = gate.shape
    tiles = cols // 128
    for tile in range(tiles):
        for side, out in enumerate((gate, up)):
            out[:, tile * 128 : (tile + 1) * 128] = pairs[
                pl.ds(2 * tile + side, rows, stride=2 * tiles), :
            ].astype(low)


def split_pairs(linear, rows, cols):
    block = 64
    half = jax.ShapeDtypeStruct((rows, cols), low)
    out_spec = pl.BlockSpec((block, cols), lambda i: (i, 0))
    return pl.pallas_call(
        deinterleave,
        grid=(rows // block,),
        in_specs=[pl.BlockSpec((block * 2 * cols // 128, 128), lambda i: (i, 0))],
        out_specs=[out_spec, out_spec],
        out_shape=[half, half],
        compiler_params=pltpu.CompilerParams(vmem_limit_bytes=24 * MIB),
        cost_estimate=pl.CostEstimate(
            flops=rows * cols, bytes_accessed=12 * rows * cols, transcendentals=0
        ),
    )(linear)


def dot_of(left, right, left_dim, right_dim):
    return lax.dot_general(
        left, right, (((left_dim,), (right_dim,)), ((), ())), preferred_element_type=wide
    )


def local_call(kernel, grid, in_specs, out_specs, out_shape, scratch, args, prefetch=0):
    return pl.pallas_call(
        kernel,
        grid_spec=pltpu.PrefetchScalarGridSpec(
            num_scalar_prefetch=prefetch,
            grid=grid,
            in_specs=in_specs,
            out_specs=out_specs,
            scratch_shapes=scratch,
        ),
        out_shape=out_shape,
        compiler_params=pltpu.CompilerParams(vmem_limit_bytes=48 * MIB),
        cost_estimate=pl.CostEstimate(flops=0, bytes_accessed=MIB, transcendentals=0),
    )(*args)


def whole_spec(shape):
    return pl.BlockSpec(shape, lambda *_: (0,) * len(shape))


def shape_of(dims, kind):
    return jax.ShapeDtypeStruct(dims, kind)


def row_scale(halves):
    total = sum(jnp.sum(half * half, axis=1, keepdims=True) for half in halves)
    return lax.rsqrt(total / D + norm_eps)


def branch_kernel(tok, gains, taps, own, other, n1, gate_b, gate_c, gate_x, conv, hidden, part0, part1, ext):
    long, width = n1.shape[1:]
    rows = conv.shape[0]
    step = long // 3

    def gates(at, carry):
        here = pl.ds(pl.multiple_of(at * step, step), step)
        halves = [tok[h, here, :].astype(wide) for h in range(2)]
        scale = row_scale(halves)
        for h in range(2):
            n1[h, here, :] = (halves[h] * scale * gains[h]).astype(low)
        for g, out in enumerate((gate_b, gate_c, gate_x)):
            w = slice(g * width, (g + 1) * width)
            out[here, :] = dot_of(n1[0, here, :], own[w, :], 1, 0) + dot_of(
                n1[1, here, :], other[w, :], 1, 0
            )
        return carry

    lax.fori_loop(0, 3, gates, 0)
    ext[8 : 8 + rows, :] = gate_b[:rows, :] * gate_x[:rows, :]
    ext[6:8, :] = gate_b[rows : rows + 2, :] * gate_x[rows : rows + 2, :]
    w_out = slice(3 * width, 4 * width)
    quarter = rows // 4
    for at in range(4):
        start = at * quarter
        taken = slice(start, start + quarter)
        value = sum(taps[k] * ext[start + 6 + k : start + 6 + k + quarter, :] for k in range(3))
        conv[taken, :] = value
        low_hidden = (gate_c[taken, :] * value).astype(low)
        hidden[taken, :] = low_hidden
        for part, weight in ((part0, own), (part1, other)):
            part[taken, :] = dot_of(low_hidden, weight[w_out, :], 1, 0).astype(low)


def branch_forward(tok, rows, tails, gains, taps, own, other):
    width = tok.shape[2]
    gate = shape_of((rows + tails, width), wide)
    outs = [
        shape_of((2, rows + tails, width), low),
        gate,
        gate,
        gate,
        shape_of((rows, width), wide),
        shape_of((rows, width), low),
        shape_of((rows, width), low),
        shape_of((rows, width), low),
    ]
    args = (tok, gains, taps, own, other)
    return local_call(
        branch_kernel,
        (1,),
        [whole_spec(a.shape) for a in args],
        [whole_spec(o.shape) for o in outs],
        outs,
        [pltpu.VMEM((rows + 8, width), wide)],
        args,
    )


def piece_at(bits, which, piece, width):
    place = bits[which] if piece == 0 else 1 - bits[which]
    return pl.ds(pl.multiple_of(place * width, width), width)


def ffn_kernel(bits, tok, mine0, mine1, theirs0, theirs1, gains, g0, g1, g2, u0, u1, u2, n2, res, gate, up, act):
    width = g1.shape[0]

    @pl.when(pl.program_id(0) == 0)
    def _():
        for h, (mine, theirs) in enumerate(((mine0, theirs0), (mine1, theirs1))):
            res[h] = tok[h, : res.shape[1], :].astype(wide) + (
                mine[...].astype(wide) + theirs[...].astype(wide)
            )
        scale = row_scale([res[0], res[1]])
        for h in range(2):
            n2[h] = (res[h] * scale * gains[h]).astype(low)

    for which, (out, w0, w1, w2) in enumerate(((gate, g0, g1, g2), (up, u0, u1, u2))):
        total = dot_of(n2[0], w0[...], 1, 0)
        for piece, w in enumerate((w1, w2)):
            total += dot_of(n2[1, :, piece_at(bits, which, piece, width)], w[...], 1, 0)
        out[...] = total
    value = gate[...]
    act[...] = (value * jax.nn.sigmoid(value) * up[...]).astype(low)


def ffn_forward(bits, tok, mine, theirs, gains, weights):
    rows, width = mine[0].shape
    cols = weights[0].shape[1]
    tile = cols // 3
    both = (2, rows, width)
    full = whole_spec(both)
    wide_tile = pl.BlockSpec((rows, tile), lambda i, *_: (0, i))
    weight_specs = [pl.BlockSpec((w.shape[0], tile), lambda i, *_: (0, i)) for w in weights]
    return local_call(
        ffn_kernel,
        (3,),
        [whole_spec(tok.shape)]
        + [whole_spec((rows, width))] * 4
        + [whole_spec(gains.shape)]
        + weight_specs,
        [full, full, wide_tile, wide_tile, wide_tile],
        [
            shape_of(both, low),
            shape_of(both, wide),
            shape_of((rows, cols), wide),
            shape_of((rows, cols), wide),
            shape_of((rows, cols), low),
        ],
        [],
        (bits, tok, *mine, *theirs, gains, *weights),
        prefetch=1,
    )


def ffn_back_kernel(
    bits, cot, d_own, d_other, gate, up, g0, g1, g2, u0, u1, u2, g_gate, g_up, part0, part1, total
):
    width = g1.shape[0]

    @pl.when(pl.program_id(0) == 0)
    def _():
        total[...] = jnp.zeros_like(total)

    start = cot.shape[1] - gate.shape[0]
    g_act = dot_of(cot[0, start:, :], d_own[...], 1, 1) + dot_of(cot[1, start:, :], d_other[...], 1, 1)
    value = gate[...]
    sigma = jax.nn.sigmoid(value)
    g_gate[...] = (g_act * up[...] * sigma * (1.0 + value * (1.0 - sigma))).astype(low)
    g_up[...] = (g_act * (value * sigma)).astype(low)
    total[0] += dot_of(g_gate[...], g0[...], 1, 1) + dot_of(g_up[...], u0[...], 1, 1)
    for which, (grad, w1, w2) in enumerate(((g_gate, g1, g2), (g_up, u1, u2))):
        for piece, w in enumerate((w1, w2)):
            total[1, :, piece_at(bits, which, piece, width)] += dot_of(grad[...], w[...], 1, 1)

    @pl.when(pl.program_id(0) == pl.num_programs(0) - 1)
    def _():
        part0[...] = total[0].astype(low)
        part1[...] = total[1].astype(low)


def ffn_backward(bits, cot, downs, gate, up, weights):
    rows, cols = gate.shape
    tile = cols // 3
    part = (rows, cot.shape[2])
    wide_tile = pl.BlockSpec((rows, tile), lambda i, *_: (0, i))
    weight_specs = [pl.BlockSpec((w.shape[0], tile), lambda i, *_: (0, i)) for w in weights]
    down_spec = pl.BlockSpec((tile, downs[0].shape[1]), lambda i, *_: (i, 0))
    return local_call(
        ffn_back_kernel,
        (3,),
        [whole_spec(cot.shape), down_spec, down_spec, wide_tile, wide_tile] + weight_specs,
        [wide_tile, wide_tile, whole_spec(part), whole_spec(part)],
        [shape_of((rows, cols), low)] * 2 + [shape_of(part, low)] * 2,
        [pltpu.VMEM((2, *part), wide)],
        (bits, cot, *downs, gate, up, *weights),
        prefetch=1,
    )


def put(outs, half, rows, value):
    if len(outs) == 2:
        outs[half][rows, :] = value.astype(low)
    else:
        outs[0][half, rows, :] = value.astype(low)


def chunk_outs(split, rows, cols):
    if split:
        return [whole_spec((rows, cols))] * 2, [shape_of((rows, cols), low)] * 2
    return [whole_spec((2, rows, cols))], [shape_of((2, rows, cols), low)]


def pair_grad_kernel(n2, g_gate, g_up, *outs):
    rows = n2.shape[2]
    for h in range(2):
        for side, grad in enumerate((g_gate, g_up)):
            put(outs, h, slice(side * rows, (side + 1) * rows), dot_of(n2[h], grad[...], 0, 0))


def pair_grads(n2, g_gate, g_up, at, rows, split):
    specs, shapes = chunk_outs(split, 2 * rows, g_gate.shape[1])
    outs = local_call(
        pair_grad_kernel,
        (1,),
        [
            pl.BlockSpec((2, n2.shape[1], rows), lambda i: (0, 0, at)),
            whole_spec(g_gate.shape),
            whole_spec(g_up.shape),
        ],
        specs,
        shapes,
        [],
        (n2, g_gate, g_up),
    )
    return tuple(outs) if split else outs[0]


def down_grad_kernel(act, cot, *outs):
    start = cot.shape[1] - act.shape[0]
    for h in range(2):
        put(outs, h, slice(None), dot_of(act[...], cot[h, start:, :], 0, 0))


def down_grads(act, cot, at, rows, split):
    specs, shapes = chunk_outs(split, rows, cot.shape[2])
    outs = local_call(
        down_grad_kernel,
        (1,),
        [pl.BlockSpec((act.shape[0], rows), lambda i: (0, at)), whole_spec(cot.shape)],
        specs,
        shapes,
        [],
        (act, cot),
    )
    return tuple(outs) if split else outs[0]


def branch_back_kernel(
    mine0, mine1, theirs0, theirs1, res, cot, gains, taps, own, other, gate_b, gate_c, gate_x, conv,
    g_res, g_low, g_proj, gain_grad, tap_grad, ext, ext_grad,
):
    _, rows, width = res.shape
    scale = row_scale([res[0], res[1]])
    grads = [
        mine[...].astype(wide) + theirs[...].astype(wide)
        for mine, theirs in ((mine0, theirs0), (mine1, theirs1))
    ]
    inner = sum(
        jnp.sum(grads[h] * gains[h] * res[h], axis=1, keepdims=True) for h in range(2)
    )
    factor = scale * scale * scale * inner / D
    for h in range(2):
        gain_grad[h] = jnp.sum(grads[h] * res[h] * scale, axis=0, keepdims=True)
        value = cot[h, cot.shape[1] - rows :, :].astype(wide) + (scale * (grads[h] * gains[h]) - res[h] * factor)
        g_res[h] = value
        g_low[h] = value.astype(low)
    g_hidden = dot_of(g_low[0], own[...], 1, 1) + dot_of(g_low[1], other[...], 1, 1)
    g_proj[1, :rows, :] = (g_hidden * conv[...]).astype(low)
    g_conv = g_hidden * gate_c[:rows, :]
    ext_grad[:rows, :] = g_conv
    ext_grad[rows:, :] = jnp.zeros((8, width), wide)
    ext[8 : 8 + rows, :] = gate_b[:rows, :] * gate_x[:rows, :]
    ext[6:8, :] = gate_b[rows : rows + 2, :] * gate_x[rows : rows + 2, :]
    for k in range(3):
        tap_grad[k : k + 1, :] = jnp.sum(
            g_conv * ext[6 + k : 6 + k + rows, :], axis=0, keepdims=True
        )
    g_mixed = sum(taps[2 - k] * ext_grad[k : k + rows, :] for k in range(3))
    g_proj[0, :rows, :] = (g_mixed * gate_x[:rows, :]).astype(low)
    g_proj[2, :rows, :] = (g_mixed * gate_b[:rows, :]).astype(low)
    tails = g_proj.shape[1] - rows
    row = lax.broadcasted_iota(jnp.int32, (tails, width), 0)
    first, second = ext_grad[0:1, :], ext_grad[1:2, :]
    g_before = jnp.where(
        row == 0,
        taps[0] * first,
        jnp.where(row == 1, taps[1] * first + taps[0] * second, 0.0),
    )
    g_proj[0, rows:, :] = (g_before * gate_x[rows:, :]).astype(low)
    g_proj[1, rows:, :] = jnp.zeros((tails, width), low)
    g_proj[2, rows:, :] = (g_before * gate_b[rows:, :]).astype(low)


def branch_backward(mine, theirs, res, cot, gains, taps, own, other, gates, conv):
    _, rows, width = res.shape
    long = gates[0].shape[0]
    out_weight = pl.BlockSpec((width, width), lambda i, *_: (3, 0))
    outs = [
        shape_of(res.shape, wide),
        shape_of(res.shape, low),
        shape_of((3, long, width), low),
        shape_of((2, 1, width), wide),
        shape_of((3, width), wide),
    ]
    full = whole_spec(res.shape)
    return local_call(
        branch_back_kernel,
        (1,),
        [whole_spec((rows, width))] * 4
        + [full, whole_spec(cot.shape), whole_spec(gains.shape), whole_spec(taps.shape)]
        + [out_weight, out_weight]
        + [whole_spec(g.shape) for g in gates]
        + [whole_spec(conv.shape)],
        [whole_spec(o.shape) for o in outs],
        outs,
        [pltpu.VMEM((rows + 8, width), wide), pltpu.VMEM((rows + 8, width), wide)],
        (*mine, *theirs, res, cot, gains, taps, own, other, *gates, conv),
    )


def branch_grad_kernel(left0, left1, right0, right1, own, other):
    rows = own.shape[0] // 2
    for h, out in enumerate((own, other)):
        for k, (left, right) in enumerate(((left0, right0), (left1, right1))):
            one = left[h] if len(left.shape) == 3 else left[...]
            two = right[h] if k == 1 and len(left.shape) == 2 else right[0]
            out[k * rows : (k + 1) * rows, :] = dot_of(one, two, 0, 0).astype(low)


def branch_grads(n1, g_proj, gate, second):
    width = n1.shape[2]
    gate_spec = pl.BlockSpec((1, *g_proj.shape[1:]), lambda i: (gate, 0, 0))
    if second is None:
        left, right = n1, g_proj
        right_spec = pl.BlockSpec((1, *g_proj.shape[1:]), lambda i: (gate + 1, 0, 0))
    else:
        left, right = second
        right_spec = whole_spec(right.shape)
    specs, shapes = chunk_outs(True, 2 * width, width)
    return local_call(
        branch_grad_kernel,
        (1,),
        [whole_spec(n1.shape), whole_spec(left.shape), gate_spec, right_spec],
        specs,
        shapes,
        [],
        (n1, left, g_proj, right),
    )


def shards(
    tokens,
    cotangent,
    input_projection_weight,
    conv_weight,
    output_projection_weight,
    norm_gains,
    gate_up_weight,
    down_projection_weight,
    in_first,
    in_second,
    conv_first,
    conv_second,
    out_first,
    out_second,
    gain_first,
    gain_second,
    gu_first,
    gu_second,
    down_first,
    down_second,
):
    feat_cols = tokens.shape[1]
    branch_cols = conv_weight.shape[1]
    hidden_cols = down_projection_weight.shape[0]
    block_rows = tokens.shape[0]
    seq_len = max(SEQ_LEAST, block_rows * lax.axis_size("dp") * lax.axis_size("col"))
    data_pos = lax.axis_index("dp")
    row_pos = lax.axis_index("row")
    col_pos = lax.axis_index("col")
    home = row_pos == col_pos
    tail_rows = 16

    in_low = jnp.transpose(input_projection_weight, (1, 0, 2)).astype(low).reshape(-1, branch_cols)
    io_low = jnp.concatenate([in_low, output_projection_weight.astype(low)])
    io_share = share_of(io_low, (1, 0))
    io_got = swap(io_share, "col")
    gu_weight = to_linear(gate_up_weight)
    gate_low, up_low = split_pairs(gu_weight, feat_cols, hidden_cols)
    gate_got = swap(tie(share_of(gate_low, (1, 0)), io_got), "col")
    up_got = swap(tie(share_of(up_low, (0, 1)), gate_got), "col")
    down_low = down_projection_weight.astype(low)
    row_start = (data_pos * lax.axis_size("row") + row_pos) * block_rows
    tail = from_behind(tokens[-2:], ("dp", "row"), 1)
    tail = jnp.where(row_start % seq_len != 0, tail, jnp.zeros_like(tail))
    spare = jnp.zeros((tail_rows - 8, feat_cols), low)
    gain_parts = []
    left = norm_gains
    for _ in range(3):
        gain_parts.append(lax.reduce_precision(left, 8, 7))
        left = left - gain_parts[-1]
    gain_parts = jnp.concatenate(gain_parts).astype(low)
    extra = tie(jnp.concatenate([tail, gain_parts, spare]))
    block = jnp.concatenate([tie(tokens, gate_got), extra, cotangent])
    away = to_home(block)
    both = jnp.stack([block, away])
    both = jnp.where(home, both, home_to_sibling(both))
    gains = both[:, block_rows + 2 : block_rows + 8].astype(wide)
    gains = gains[:, 0:2] + gains[:, 2:4] + gains[:, 4:6]
    gains = [gains[:, k : k + 1] for k in range(2)]
    down_got = swap(tie(down_low, up_got), "col")
    io_pair = keep_or_join(0, io_got, flip(io_got, 0))
    io_other = keep_or_join(1, io_pair, flip(io_pair, 1))
    gate_pair = keep_or_join(0, gate_got, flip(tie(gate_got, io_pair), 0))
    up_pair = keep_or_join(1, up_got, flip(tie(up_got, io_pair), 1))
    gate_more = flip(gate_pair, 1)
    up_more = flip(up_pair, 0)
    weights = [gate_low, gate_pair, gate_more, up_low, up_pair, up_more]
    bits = jnp.stack([dp_bit(1), dp_bit(0)]).astype(jnp.int32)
    downs = [down_low, down_got]

    n1, gate_b, gate_c, gate_x, conv, hidden, *branch = branch_forward(
        both, block_rows, tail_rows, gains[0], conv_weight, io_low, io_other
    )
    n2, res, gate, upper, act = ffn_forward(
        bits, both, branch, swap_halves(branch), gains[1], weights
    )

    turns = Turns()
    orders = dict(D="xyl", d="ylx", a="xyl", b="lyx", c="xyl", e="lyx", I="xyl", i="xyl")
    down_half = hidden_cols // 2
    for k, name in enumerate("Dd"):
        split = orders[name][0] == "x"
        turns.add(name, down_grads(act, both, k, down_half, split), orders[name])
    turns.run("Dd")
    g_gate, g_up, *part_two = ffn_backward(
        bits, tie(both, *turns.after), downs, gate, upper, weights
    )
    quarter = feat_cols // 4
    for k, name in enumerate("abce"):
        split = orders[name][0] == "x"
        turns.add(name, pair_grads(n2, g_gate, g_up, k, quarter, split), orders[name])
    turns.run("abcDe")
    g_res, g_branch, g_proj, gain_two_grad, conv_grad = branch_backward(
        part_two,
        swap_halves(part_two),
        tie(res, *turns.after),
        both,
        gains[1],
        conv_weight,
        io_low,
        io_other,
        (gate_b, gate_c, gate_x),
        conv,
    )
    turns.add("I", branch_grads(n1, g_proj, 0, None), orders["I"])
    io_last = branch_grads(n1, g_proj, 2, (hidden, g_branch))
    turns.after += tuple(io_last)
    turns.run("IdabD")

    g_late = tie(g_proj, *turns.after)
    io_half = [half.reshape(4, feat_cols, branch_cols) for half in (io_low, io_other)]
    g_part = jnp.stack(
        [sum(mul_t(g_late[g], io_half[h][g]) for g in range(3)).astype(low) for h in range(2)]
    )
    g_long = g_part.astype(wide) + swap(g_part, "row").astype(wide)
    tok = both[:, : block_rows + 2].astype(wide)
    scale = lax.rsqrt(jnp.sum(tok * tok, axis=(0, 2)) / D + norm_eps)[None, :, None]
    gain_one_grad = jnp.sum(g_long[:, : block_rows + 2] * tok * scale, axis=1)
    small = [
        jnp.concatenate([conv_grad, gain_one_grad[h : h + 1], gain_two_grad[h]]) for h in range(2)
    ]
    spare = jnp.zeros((16, feat_cols), low)
    small = [jnp.pad(part, ((0, 11), (0, 0))).astype(low) for part in small]
    io_long = []
    for h in range(2):
        pieces = jnp.split(io_last[h], 4)
        io_long.append(
            jnp.concatenate(
                [pieces[0], small[h], pieces[1], spare, pieces[2], spare, pieces[3], spare]
            )
        )
    turns.add("i", io_long, orders["i"])
    turns.run("eiacbdDIcaeDciIabDdcieIDabd")

    def in_flat(values):
        return jnp.transpose(values, (1, 0, 2)).reshape(3 * feat_cols, branch_cols)

    def in_back(values):
        return jnp.transpose(values.reshape(3, feat_cols, branch_cols), (1, 0, 2))

    wheres = {name: where_of(orders[name]) for name in orders}
    down_state = (down_projection_weight, down_first, down_second)
    gu_state = (gu_weight, to_linear(gu_first), to_linear(gu_second))
    in_state = (in_flat(input_projection_weight), in_flat(in_first), in_flat(in_second))
    out_state = (output_projection_weight, out_first, out_second)
    pairs = 2 * hidden_cols // 128

    shares = turns.shares
    part_rows = feat_cols // 2
    turns.reach_shares("Dd")
    down_squares = sum(
        share_norms(wheres[n], shares[n], [(down_state, 4 * k)], down_half // 4)
        for k, n in enumerate("Dd")
    )
    turns.add_norms("p", down_squares)
    turns.run("pacpibpcep")
    turns.reach_shares("abce")
    gu_squares = sum(
        share_norms(wheres[n], shares[n], [(gu_state, 2 * k)], quarter // 2 * pairs, pairs=True)
        for k, n in enumerate("abce")
    )
    turns.add_norms("n", gu_squares)
    turns.run("nIdpnbin")
    turns.reach_shares("Ii")
    io_squares = share_norms(wheres["i"], shares["i"], [(in_state, 4), (out_state, 0)], part_rows)
    in_squares = share_norms(wheres["I"], shares["I"], [(in_state, 0)], part_rows)
    turns.add_norms("m", io_squares + jnp.pad(in_squares, (0, 2)))
    turns.run("memdnmImenmiIi")
    turns.finish()
    sums, seen = turns.done, turns.seen

    back = tie(g_long[::-1, block_rows : block_rows + 2], seen["i"][4])
    back = from_behind(back, ("dp", "col"), -1)
    g_n1 = g_long[:, :block_rows].at[:, -2:].add(back)
    tok, scale = tok[:, :block_rows], scale[:, :block_rows]
    weighted = g_n1 * gains[0]
    inner = jnp.sum(weighted * tok, axis=(0, 2))[None, :, None]
    tok_half = (g_res + (scale * weighted - tok * (scale * scale * scale * inner / D))).astype(low)
    token_grad = jnp.where(home, tok_half[0], home_to_away(tok_half[1]))
    act = tie(act, seen["D"][1])
    ffn = jnp.stack([mul(act, downs[h]) for h in range(2)])
    out_half = (res + (ffn + sibling_to_home(ffn.astype(low)).astype(wide))).astype(low)
    output = jnp.where(home, out_half[0], home_to_away(out_half[1]))

    def gu_back(values):
        return from_linear(values, feat_cols, 2)

    def ratio_of(norms):
        norms = jnp.sqrt(norms)
        return norms, (learn_rate * (norms[0] / (norms[1] + adam_eps))).reshape(1)

    (gu_norms, gu_ratio), (down_norms, down_ratio) = [ratio_of(sums[name]) for name in "np"]
    (in_norms, in_ratio), (out_norms, out_ratio) = [ratio_of(sums["m"][k : k + 2]) for k in (0, 2)]

    def later_half(count):
        return functools.partial(lamb_plain, lambda i: (i >= count // 2).astype(jnp.int32))

    def fixed_half(half):
        return functools.partial(lamb_plain, lambda i: half)

    down_new = None
    for k in (0, 1):
        name = "Dd"[k]
        block = down_half // 6
        down_new = lamb_call(
            later_half(6), wheres[name], down_ratio, sums[name], block, lambda i: i % 3,
            down_state, block, 6 * k, 6, down_new, [],
        )
    gu_new = None
    gu_rows = 32
    for k in (0, 2, 1, 3):
        name = "abce"[k]
        blocks = quarter // gu_rows
        gu_new = lamb_call(
            lamb_pairs, wheres[name], gu_ratio, sums[name], gu_rows, lambda i: i,
            gu_state, gu_rows * pairs, k * blocks, blocks, gu_new,
            [pltpu.VMEM((gu_rows * pairs, 128), wide)],
        )
    last = sums["i"]
    small = [part[part_rows : part_rows + 5] for part in last]
    small = jnp.where((wheres["i"][0] >> 1) == 0, small[0], small[1]).astype(wide)
    conv_grad, gains_grad = small[:3], small[3:]
    conv_m, conv_v, conv_u = lamb_moments(conv_weight, conv_grad, conv_first, conv_second, 0.0)
    gain_m, gain_v, gain_u = lamb_moments(norm_gains, gains_grad, gain_first, gain_second, 0.0)
    col_first = (col_pos == 0).astype(wide)
    row_first = (row_pos == 0).astype(wide)
    small_norms = jnp.stack(
        [
            square_pair(conv_weight, conv_u) * col_first,
            square_pair(norm_gains[0], gain_u[0]) * row_first,
            square_pair(norm_gains[1], gain_u[1]) * row_first,
        ]
    )
    small_norms = small_norms + swap(small_norms, "row")
    small_norms = jnp.sqrt(small_norms + swap(small_norms, "col"))
    last = [tie(part, small_norms) for part in last]
    first_io = [tie(part, small_norms) for part in sums["I"]]
    in_new = lamb_call(
        later_half(4), wheres["I"], in_ratio, first_io, part_rows, lambda i: i % 2,
        in_state, part_rows, 0, 4, None, [],
    )
    in_new = lamb_call(
        fixed_half(0), wheres["i"], in_ratio, last, part_rows + 16, lambda i: i,
        in_state, part_rows, 4, 2, in_new, [],
    )
    out_new = lamb_call(
        fixed_half(1), wheres["i"], out_ratio, last, part_rows + 16, lambda i: i,
        out_state, part_rows, 0, 2, None, [],
    )

    trust_norms = jnp.stack(
        [
            in_norms,
            small_norms[0],
            out_norms,
            small_norms[1],
            small_norms[2],
            gu_norms,
            down_norms,
        ]
    )
    gains_new = jnp.stack(
        [
            apply_trust(norm_gains[0], gain_u[0], small_norms[1]),
            apply_trust(norm_gains[1], gain_u[1], small_norms[2]),
        ]
    )
    return (
        output,
        token_grad,
        *[in_back(values) for values in in_new],
        apply_trust(conv_weight, conv_u, small_norms[0]),
        conv_m,
        conv_v,
        *out_new,
        gains_new,
        gain_m,
        gain_v,
        *[gu_back(values) for values in gu_new],
        *down_new,
        trust_norms,
    )


def solution(mesh):
    in_specs = (
        P(("dp", "row"), "col"),
        P(("dp", "row"), "col"),
        P("col", None, "row"),
        P(None, "row"),
        P("row", "col"),
        P(None, "col"),
        P("col", None, "row"),
        P("row", "col"),
        P("col", None, "row"),
        P("col", None, "row"),
        P(None, "row"),
        P(None, "row"),
        P("row", "col"),
        P("row", "col"),
        P(None, "col"),
        P(None, "col"),
        P("col", None, "row"),
        P("col", None, "row"),
        P("row", "col"),
        P("row", "col"),
    )
    out_specs = (
        P(("dp", "row"), "col"),
        P(("dp", "row"), "col"),
        P("col", None, "row"),
        P("col", None, "row"),
        P("col", None, "row"),
        P(None, "row"),
        P(None, "row"),
        P(None, "row"),
        P("row", "col"),
        P("row", "col"),
        P("row", "col"),
        P(None, "col"),
        P(None, "col"),
        P(None, "col"),
        P("col", None, "row"),
        P("col", None, "row"),
        P("col", None, "row"),
        P("row", "col"),
        P("row", "col"),
        P("row", "col"),
        P(),
    )
    return jax.shard_map(shards, mesh=mesh, in_specs=in_specs, out_specs=out_specs, check_vma=False)
```

```python
import functools

import jax
import jax.numpy as jnp
from jax import lax
from jax.experimental import pallas as pl
from jax.experimental.layout import Layout, with_layout_constraint
from jax.experimental.pallas import tpu as pltpu
from jax.sharding import PartitionSpec as P

D = 1024
SEQ_LEAST = 4096
STEP = 5
MIB = 1024 * 1024


norm_eps = 1e-05
adam_eps = 1e-06
beta_one = 0.5
beta_two = 0.6
learn_rate = 0.5
decay_rate = 0.01
low = jnp.bfloat16
wide = jnp.float32


def from_behind(block, axis, distance):
    devices = range(lax.axis_size(axis))
    route = [(i - distance, i) for i in devices if i - distance in devices]
    return lax.ppermute(block, axis, route)


def swap(values, axis):
    return lax.ppermute(values, axis, [(0, 1), (1, 0)])


def swap_halves(halves):
    return [swap(half, "row") for half in halves]


def to_home(values):
    return lax.ppermute(values, ("row", "col"), [(1, 0), (2, 3)])


def home_to_sibling(values):
    return lax.ppermute(values, ("row", "col"), [(0, 2), (3, 1)])


def home_to_away(values):
    return lax.ppermute(values, ("row", "col"), [(0, 1), (3, 2)])


def sibling_to_home(values):
    return lax.ppermute(values, ("row", "col"), [(2, 0), (1, 3)])


def contract(left, right, left_dim, right_dim):
    return lax.dot_general(
        left, right, (((left_dim,), (right_dim,)), ((), ())), preferred_element_type=wide
    )


def mul(left, right):
    return contract(left, right, 1, 0)


def mul_t(left, right):
    return contract(left, right, 1, 1)


def t_mul(left, right):
    return contract(left, right, 0, 0)


def lamb_moments(weight, grad, first, second, decay):
    first_new = beta_one * first + (1.0 - beta_one) * grad
    second_new = beta_two * second + (1.0 - beta_two) * grad * grad
    direction = (first_new * (1.0 / (1.0 - beta_one**STEP))) / (
        jnp.sqrt(second_new * (1.0 / (1.0 - beta_two**STEP))) + adam_eps
    ) + decay * weight
    return (first_new, second_new, direction)


def square_pair(weight, direction):
    return jnp.stack([jnp.sum(weight * weight), jnp.sum(direction * direction)])


def kernel_call(kernel, grid, in_specs, out_specs, out_shape, scratch, args, aliases=None, mib=1):
    return pl.pallas_call(
        kernel,
        grid_spec=pltpu.PrefetchScalarGridSpec(
            num_scalar_prefetch=1,
            grid=grid,
            in_specs=in_specs,
            out_specs=out_specs,
            scratch_shapes=scratch,
        ),
        out_shape=out_shape,
        input_output_aliases=aliases or {},
        compiler_params=pltpu.CompilerParams(vmem_limit_bytes=48 * MIB),
        cost_estimate=pl.CostEstimate(flops=0, bytes_accessed=mib * MIB, transcendentals=0),
    )(*args)


SCALARS = pl.BlockSpec(memory_space=pltpu.SMEM)


def norm_kernel(where, grad, *refs):
    sums = refs[-1]
    groups = [refs[:3], refs[3:6]][: len(refs) // 3]
    rows = groups[0][0].shape[0]
    zero = jnp.zeros((8, groups[0][0].shape[1]), wide)
    for k, (p, m, v) in enumerate(groups):

        def body(at, total):
            here = pl.ds(pl.multiple_of(at * 32, 32), 32)
            weight = p[here, :]
            direction = lamb_moments(
                weight, grad[here, :].astype(wide), m[here, :], v[here, :], decay_rate
            )[2]
            return tuple(
                t + (sq[:8] + sq[8:16]) + (sq[16:24] + sq[24:])
                for t, sq in zip(total, (weight * weight, direction * direction))
            )

        total = lax.fori_loop(0, rows // 32, body, (zero, zero))
        mine = 1.0 if len(groups) == 1 else ((where[0] >> 1) == k).astype(wide)
        for j in range(2):
            sums[2 * k + j] = jnp.sum(total[j]) * mine


def norm_pairs_kernel(where, grad, p, m, v, sums):
    rows, cols = grad.shape
    tiles = cols // 128
    side = where[0] >> 1
    zero = jnp.zeros((8, 128), wide)
    total = [zero, zero]
    for tile in range(tiles):
        here = pl.ds(2 * tile + side, rows, stride=2 * tiles)
        weight = p[here, :]
        direction = lamb_moments(
            weight, grad[:, tile * 128 : (tile + 1) * 128].astype(wide), m[here, :], v[here, :], decay_rate
        )[2]
        for j, sq in enumerate((weight * weight, direction * direction)):
            total[j] = total[j] + jnp.sum((sq).reshape(rows // 8, 8, 128), axis=0)
    for j in range(2):
        sums[j] = jnp.sum(total[j])


def share_norms(where, grad, states, rows, pairs=False):
    specs, args = [], []
    for state, at in states:
        for array in state:
            if pairs:
                spec = pl.BlockSpec(
                    (rows, array.shape[1]), lambda i, w, at=at: (at + (w[0] & 1), 0)
                )
            elif len(states) == 2:
                spec = pl.BlockSpec(
                    (rows, array.shape[1]), lambda i, w, at=at: (at + (w[0] & 1), 0)
                )
            else:
                spec = pl.BlockSpec((rows, array.shape[1]), lambda i, w, at=at: (at + w[0], 0))
            specs.append(spec)
            args.append(array)
    return kernel_call(
        norm_pairs_kernel if pairs else norm_kernel,
        (1,),
        [whole_spec(grad.shape)] + specs,
        SCALARS,
        jax.ShapeDtypeStruct((2 * len(states),), wide),
        [],
        (where, grad, *args),
    )


def lamb_loop(refs, outs, ratio, rows, step, pick):
    p, m, v = refs

    def body(at, carry):
        here = pl.ds(pl.multiple_of(at * step, step), step)
        weight = p[here, :]
        first_new, second_new, direction = lamb_moments(
            weight, pick(here), m[here, :], v[here, :], decay_rate
        )
        outs[0][here, :] = weight - ratio * direction
        outs[1][here, :] = first_new
        outs[2][here, :] = second_new
        return carry

    lax.fori_loop(0, rows // step, body, 0)


def lamb_plain(half_of_block, where, ratio, part, got, p, m, v, *outs):
    use = half_of_block(pl.program_id(0)) == (where[0] >> 1)

    def pick(here):
        return jnp.where(use, part[here, :].astype(wide), got[here, :].astype(wide))

    lamb_loop((p, m, v), outs, ratio[0], p.shape[0], 32, pick)


def lamb_pairs(where, ratio, part, got, p, m, v, p_out, m_out, v_out, mixed):
    rows, cols = part.shape
    tiles = cols // 128
    for value, order in ((0, (part, got)), (1, (got, part))):

        @pl.when((where[0] >> 1) == value)
        def _():
            for tile in range(tiles):
                for side, ref in enumerate(order):
                    mixed[pl.ds(2 * tile + side, rows, stride=2 * tiles), :] = ref[
                        :, tile * 128 : (tile + 1) * 128
                    ].astype(wide)

    lamb_loop(
        (p, m, v), (p_out, m_out, v_out), ratio[0], p.shape[0], 192, lambda here: mixed[here, :]
    )


def lamb_call(kernel, where, ratio, grad, grad_block, grad_at, state, block, start, count, before, scratch):
    rows, cols = state[0].shape
    flat = pl.BlockSpec((block, cols), lambda i, w: (i + start, 0))
    grad_spec = pl.BlockSpec((grad_block, grad[0].shape[1]), lambda i, w: (grad_at(i), 0))
    whole = jax.ShapeDtypeStruct((rows, cols), wide)
    args = [where, ratio, *grad, *state]
    specs = [SCALARS, grad_spec, grad_spec, flat, flat, flat]
    run, aliases = kernel, {}
    if before is not None:
        aliases = {len(args) + k: k for k in range(3)}

        def run(*refs):
            kernel(*refs[: len(args)], *refs[len(args) + 3 :])

    return list(
        kernel_call(
            run,
            (count,),
            specs + [pl.BlockSpec(memory_space=pl.ANY)] * len(aliases),
            [flat, flat, flat],
            [whole, whole, whole],
            scratch,
            (*args, *(before or [])),
            aliases,
            mib=26 * count * block * cols // MIB,
        )
    )


def to_linear(values):
    rows, sides, cols = values.shape
    split = with_layout_constraint(
        values.reshape(rows, sides, cols // 128, 128), Layout(major_to_minor=(0, 2, 1, 3))
    )
    return split.transpose(0, 2, 1, 3).reshape(rows * sides * cols // 128, 128)


def from_linear(values, rows, sides):
    cols = values.size // (rows * sides)
    split = values.reshape(rows, cols // 128, sides, 128).transpose(0, 2, 1, 3)
    split = with_layout_constraint(split, Layout(major_to_minor=(0, 2, 1, 3)))
    return split.reshape(rows, sides, cols)


def apply_trust(weight, direction, norms):
    return weight - learn_rate * (norms[0] / (norms[1] + adam_eps)) * direction


def flip(values, bit):
    size = lax.axis_size("dp")
    return lax.ppermute(values, "dp", [(i, i ^ (1 << bit)) for i in range(size)])


def dp_bit(bit):
    return (lax.axis_index("dp") >> bit) & 1


def rows_of(values, start, rows):
    return lax.dynamic_slice_in_dim(values, start, rows, 0)


def total_of(pieces):
    total = pieces[0].astype(wide)
    for piece in pieces[1:]:
        total = total + piece.astype(wide)
    return total


def tie(values, *deps):
    return lax.optimization_barrier((values, *deps))[0]


def low_total(pieces):
    return total_of(pieces).astype(low)


def keep_or_join(bit, part, other):
    return jnp.where(
        dp_bit(bit) == 0,
        jnp.concatenate([part, other]),
        jnp.concatenate([other, part]),
    )


def share_of(weight, order):
    rows = weight.shape[0] // (1 << len(order))
    index = 0
    for bit in order:
        index = 2 * index + dp_bit(bit)
    return rows_of(weight, index * rows, rows)


def half_of(piece, place):
    rows = piece.shape[-2] // 2
    return lax.dynamic_slice_in_dim(piece, place * rows, rows, piece.ndim - 2)


def chunk_sum(chunk, order, keep):
    bits = {"y": 0, "l": 1}
    steps = [name if name == "x" else bits[name] for name in order]
    pieces = [chunk]
    for step in steps:
        if step == "x":
            whole = len(pieces) == 1
            got = yield step, pieces[0][1] if whole else low_total([piece[1] for piece in pieces])
            pieces = [piece[0] for piece in pieces] + [got]
        else:
            here = dp_bit(step)
            got = yield step, low_total([half_of(piece, 1 - here) for piece in pieces])
            pieces = [half_of(piece, here) for piece in pieces] + [got]
    part = low_total(pieces)
    for step in range((lax.axis_size("dp") - 1).bit_length()):
        if step not in steps:
            got = yield step, part
            part = low_total([part, got])
    keep(part)
    first, second = [step for step in steps if step != "x"]
    got = yield second, part
    part = keep_or_join(second, part, got)
    got = yield first, part
    return part, got


def norm_sum(values):
    for step in ("x", "row", 1, 0):
        got = yield step, values
        values = values + got
    return values


def where_of(order):
    bits = {"y": 0, "l": 1}
    first, second = [bits[name] for name in order if name != "x"]
    return (2 * dp_bit(first) + dp_bit(second)).astype(jnp.int32).reshape(1)


def move(step, send):
    if step == "row":
        return swap(send, "row")
    return swap(send, "col") if step == "x" else flip(send, step)


class Turns:
    def __init__(self):
        self.chunks = {}
        self.arrivals = {}
        self.seen = {}
        self.done = {}
        self.shares = {}
        self.after = ()

    def add(self, name, chunk, order):
        self.chunks[name] = chunk_sum(chunk, order, functools.partial(self.shares.__setitem__, name))

    def add_norms(self, name, values):
        self.chunks[name] = norm_sum(values)

    def turn(self, name):
        got = self.arrivals.get(name)
        try:
            if got is None:
                self.seen[name] = []
                step, send = next(self.chunks[name])
                send = tie(send, *self.after)
            else:
                got = tie(got, *self.after)
                self.seen[name].append(got)
                step, send = self.chunks[name].send(got)
        except StopIteration as end:
            self.done[name] = end.value
            return
        self.arrivals[name] = move(step, send)
        self.after = (send,)

    def run(self, names):
        for name in names:
            if name not in self.done:
                self.turn(name)

    def reach_shares(self, names):
        while any(name not in self.shares for name in names):
            self.run([name for name in names if name not in self.shares])

    def finish(self):
        while len(self.done) < len(self.chunks):
            self.run(self.chunks)


def deinterleave(pairs, gate, up):
    rows, cols = gate.shape
    tiles = cols // 128
    for tile in range(tiles):
        for side, out in enumerate((gate, up)):
            out[:, tile * 128 : (tile + 1) * 128] = pairs[
                pl.ds(2 * tile + side, rows, stride=2 * tiles), :
            ].astype(low)


def split_pairs(linear, rows, cols):
    block = 64
    half = jax.ShapeDtypeStruct((rows, cols), low)
    out_spec = pl.BlockSpec((block, cols), lambda i: (i, 0))
    return pl.pallas_call(
        deinterleave,
        grid=(rows // block,),
        in_specs=[pl.BlockSpec((block * 2 * cols // 128, 128), lambda i: (i, 0))],
        out_specs=[out_spec, out_spec],
        out_shape=[half, half],
        compiler_params=pltpu.CompilerParams(vmem_limit_bytes=24 * MIB),
        cost_estimate=pl.CostEstimate(
            flops=rows * cols, bytes_accessed=12 * rows * cols, transcendentals=0
        ),
    )(linear)


def dot_of(left, right, left_dim, right_dim):
    return lax.dot_general(
        left, right, (((left_dim,), (right_dim,)), ((), ())), preferred_element_type=wide
    )


def local_call(kernel, grid, in_specs, out_specs, out_shape, scratch, args, prefetch=0):
    return pl.pallas_call(
        kernel,
        grid_spec=pltpu.PrefetchScalarGridSpec(
            num_scalar_prefetch=prefetch,
            grid=grid,
            in_specs=in_specs,
            out_specs=out_specs,
            scratch_shapes=scratch,
        ),
        out_shape=out_shape,
        compiler_params=pltpu.CompilerParams(vmem_limit_bytes=48 * MIB),
        cost_estimate=pl.CostEstimate(flops=0, bytes_accessed=MIB, transcendentals=0),
    )(*args)


def whole_spec(shape):
    return pl.BlockSpec(shape, lambda *_: (0,) * len(shape))


def shape_of(dims, kind):
    return jax.ShapeDtypeStruct(dims, kind)


def row_scale(halves):
    total = sum(jnp.sum(half * half, axis=1, keepdims=True) for half in halves)
    return lax.rsqrt(total / D + norm_eps)


def branch_kernel(tok, gains, taps, own, other, n1, gate_b, gate_c, gate_x, conv, hidden, part0, part1, ext):
    long, width = n1.shape[1:]
    rows = conv.shape[0]
    step = long // 3

    def gates(at, carry):
        here = pl.ds(pl.multiple_of(at * step, step), step)
        halves = [tok[h, here, :].astype(wide) for h in range(2)]
        scale = row_scale(halves)
        for h in range(2):
            n1[h, here, :] = (halves[h] * scale * gains[h]).astype(low)
        for g, out in enumerate((gate_b, gate_c, gate_x)):
            w = slice(g * width, (g + 1) * width)
            out[here, :] = dot_of(n1[0, here, :], own[w, :], 1, 0) + dot_of(
                n1[1, here, :], other[w, :], 1, 0
            )
        return carry

    lax.fori_loop(0, 3, gates, 0)
    ext[8 : 8 + rows, :] = gate_b[:rows, :] * gate_x[:rows, :]
    ext[6:8, :] = gate_b[rows : rows + 2, :] * gate_x[rows : rows + 2, :]
    w_out = slice(3 * width, 4 * width)
    quarter = rows // 4
    for at in range(4):
        start = at * quarter
        taken = slice(start, start + quarter)
        value = sum(taps[k] * ext[start + 6 + k : start + 6 + k + quarter, :] for k in range(3))
        conv[taken, :] = value
        low_hidden = (gate_c[taken, :] * value).astype(low)
        hidden[taken, :] = low_hidden
        for part, weight in ((part0, own), (part1, other)):
            part[taken, :] = dot_of(low_hidden, weight[w_out, :], 1, 0).astype(low)


def branch_forward(tok, rows, tails, gains, taps, own, other):
    width = tok.shape[2]
    gate = shape_of((rows + tails, width), wide)
    outs = [
        shape_of((2, rows + tails, width), low),
        gate,
        gate,
        gate,
        shape_of((rows, width), wide),
        shape_of((rows, width), low),
        shape_of((rows, width), low),
        shape_of((rows, width), low),
    ]
    args = (tok, gains, taps, own, other)
    return local_call(
        branch_kernel,
        (1,),
        [whole_spec(a.shape) for a in args],
        [whole_spec(o.shape) for o in outs],
        outs,
        [pltpu.VMEM((rows + 8, width), wide)],
        args,
    )


def piece_at(bits, which, piece, width):
    place = bits[which] if piece == 0 else 1 - bits[which]
    return pl.ds(pl.multiple_of(place * width, width), width)


def ffn_kernel(bits, tok, mine0, mine1, theirs0, theirs1, gains, g0, g1, g2, u0, u1, u2, n2, res, gate, up, act):
    width = g1.shape[0]

    @pl.when(pl.program_id(0) == 0)
    def _():
        for h, (mine, theirs) in enumerate(((mine0, theirs0), (mine1, theirs1))):
            res[h] = tok[h, : res.shape[1], :].astype(wide) + (
                mine[...].astype(wide) + theirs[...].astype(wide)
            )
        scale = row_scale([res[0], res[1]])
        for h in range(2):
            n2[h] = (res[h] * scale * gains[h]).astype(low)

    for which, (out, w0, w1, w2) in enumerate(((gate, g0, g1, g2), (up, u0, u1, u2))):
        total = dot_of(n2[0], w0[...], 1, 0)
        for piece, w in enumerate((w1, w2)):
            total += dot_of(n2[1, :, piece_at(bits, which, piece, width)], w[...], 1, 0)
        out[...] = total
    value = gate[...]
    act[...] = (value * jax.nn.sigmoid(value) * up[...]).astype(low)


def ffn_forward(bits, tok, mine, theirs, gains, weights):
    rows, width = mine[0].shape
    cols = weights[0].shape[1]
    tile = cols // 3
    both = (2, rows, width)
    full = whole_spec(both)
    wide_tile = pl.BlockSpec((rows, tile), lambda i, *_: (0, i))
    weight_specs = [pl.BlockSpec((w.shape[0], tile), lambda i, *_: (0, i)) for w in weights]
    return local_call(
        ffn_kernel,
        (3,),
        [whole_spec(tok.shape)]
        + [whole_spec((rows, width))] * 4
        + [whole_spec(gains.shape)]
        + weight_specs,
        [full, full, wide_tile, wide_tile, wide_tile],
        [
            shape_of(both, low),
            shape_of(both, wide),
            shape_of((rows, cols), wide),
            shape_of((rows, cols), wide),
            shape_of((rows, cols), low),
        ],
        [],
        (bits, tok, *mine, *theirs, gains, *weights),
        prefetch=1,
    )


def ffn_back_kernel(
    bits, cot, d_own, d_other, gate, up, g0, g1, g2, u0, u1, u2, g_gate, g_up, part0, part1, total
):
    width = g1.shape[0]

    @pl.when(pl.program_id(0) == 0)
    def _():
        total[...] = jnp.zeros_like(total)

    start = cot.shape[1] - gate.shape[0]
    g_act = dot_of(cot[0, start:, :], d_own[...], 1, 1) + dot_of(cot[1, start:, :], d_other[...], 1, 1)
    value = gate[...]
    sigma = jax.nn.sigmoid(value)
    g_gate[...] = (g_act * up[...] * sigma * (1.0 + value * (1.0 - sigma))).astype(low)
    g_up[...] = (g_act * (value * sigma)).astype(low)
    total[0] += dot_of(g_gate[...], g0[...], 1, 1) + dot_of(g_up[...], u0[...], 1, 1)
    for which, (grad, w1, w2) in enumerate(((g_gate, g1, g2), (g_up, u1, u2))):
        for piece, w in enumerate((w1, w2)):
            total[1, :, piece_at(bits, which, piece, width)] += dot_of(grad[...], w[...], 1, 1)

    @pl.when(pl.program_id(0) == pl.num_programs(0) - 1)
    def _():
        part0[...] = total[0].astype(low)
        part1[...] = total[1].astype(low)


def ffn_backward(bits, cot, downs, gate, up, weights):
    rows, cols = gate.shape
    tile = cols // 3
    part = (rows, cot.shape[2])
    wide_tile = pl.BlockSpec((rows, tile), lambda i, *_: (0, i))
    weight_specs = [pl.BlockSpec((w.shape[0], tile), lambda i, *_: (0, i)) for w in weights]
    down_spec = pl.BlockSpec((tile, downs[0].shape[1]), lambda i, *_: (i, 0))
    return local_call(
        ffn_back_kernel,
        (3,),
        [whole_spec(cot.shape), down_spec, down_spec, wide_tile, wide_tile] + weight_specs,
        [wide_tile, wide_tile, whole_spec(part), whole_spec(part)],
        [shape_of((rows, cols), low)] * 2 + [shape_of(part, low)] * 2,
        [pltpu.VMEM((2, *part), wide)],
        (bits, cot, *downs, gate, up, *weights),
        prefetch=1,
    )


def put(outs, half, rows, value):
    if len(outs) == 2:
        outs[half][rows, :] = value.astype(low)
    else:
        outs[0][half, rows, :] = value.astype(low)


def chunk_outs(split, rows, cols):
    if split:
        return [whole_spec((rows, cols))] * 2, [shape_of((rows, cols), low)] * 2
    return [whole_spec((2, rows, cols))], [shape_of((2, rows, cols), low)]


def pair_grad_kernel(n2, g_gate, g_up, *outs):
    rows = n2.shape[2]
    for h in range(2):
        for side, grad in enumerate((g_gate, g_up)):
            put(outs, h, slice(side * rows, (side + 1) * rows), dot_of(n2[h], grad[...], 0, 0))


def pair_grads(n2, g_gate, g_up, at, rows, split):
    specs, shapes = chunk_outs(split, 2 * rows, g_gate.shape[1])
    outs = local_call(
        pair_grad_kernel,
        (1,),
        [
            pl.BlockSpec((2, n2.shape[1], rows), lambda i: (0, 0, at)),
            whole_spec(g_gate.shape),
            whole_spec(g_up.shape),
        ],
        specs,
        shapes,
        [],
        (n2, g_gate, g_up),
    )
    return tuple(outs) if split else outs[0]


def down_grad_kernel(act, cot, *outs):
    start = cot.shape[1] - act.shape[0]
    for h in range(2):
        put(outs, h, slice(None), dot_of(act[...], cot[h, start:, :], 0, 0))


def down_grads(act, cot, at, rows, split):
    specs, shapes = chunk_outs(split, rows, cot.shape[2])
    outs = local_call(
        down_grad_kernel,
        (1,),
        [pl.BlockSpec((act.shape[0], rows), lambda i: (0, at)), whole_spec(cot.shape)],
        specs,
        shapes,
        [],
        (act, cot),
    )
    return tuple(outs) if split else outs[0]


def branch_back_kernel(
    mine0, mine1, theirs0, theirs1, res, cot, gains, taps, own, other, gate_b, gate_c, gate_x, conv,
    g_res, g_low, g_proj, gain_grad, tap_grad, ext, ext_grad,
):
    _, rows, width = res.shape
    scale = row_scale([res[0], res[1]])
    grads = [
        mine[...].astype(wide) + theirs[...].astype(wide)
        for mine, theirs in ((mine0, theirs0), (mine1, theirs1))
    ]
    inner = sum(
        jnp.sum(grads[h] * gains[h] * res[h], axis=1, keepdims=True) for h in range(2)
    )
    factor = scale * scale * scale * inner / D
    for h in range(2):
        gain_grad[h] = jnp.sum(grads[h] * res[h] * scale, axis=0, keepdims=True)
        value = cot[h, cot.shape[1] - rows :, :].astype(wide) + (scale * (grads[h] * gains[h]) - res[h] * factor)
        g_res[h] = value
        g_low[h] = value.astype(low)
    g_hidden = dot_of(g_low[0], own[...], 1, 1) + dot_of(g_low[1], other[...], 1, 1)
    g_proj[1, :rows, :] = (g_hidden * conv[...]).astype(low)
    g_conv = g_hidden * gate_c[:rows, :]
    ext_grad[:rows, :] = g_conv
    ext_grad[rows:, :] = jnp.zeros((8, width), wide)
    ext[8 : 8 + rows, :] = gate_b[:rows, :] * gate_x[:rows, :]
    ext[6:8, :] = gate_b[rows : rows + 2, :] * gate_x[rows : rows + 2, :]
    for k in range(3):
        tap_grad[k : k + 1, :] = jnp.sum(
            g_conv * ext[6 + k : 6 + k + rows, :], axis=0, keepdims=True
        )
    g_mixed = sum(taps[2 - k] * ext_grad[k : k + rows, :] for k in range(3))
    g_proj[0, :rows, :] = (g_mixed * gate_x[:rows, :]).astype(low)
    g_proj[2, :rows, :] = (g_mixed * gate_b[:rows, :]).astype(low)
    tails = g_proj.shape[1] - rows
    row = lax.broadcasted_iota(jnp.int32, (tails, width), 0)
    first, second = ext_grad[0:1, :], ext_grad[1:2, :]
    g_before = jnp.where(
        row == 0,
        taps[0] * first,
        jnp.where(row == 1, taps[1] * first + taps[0] * second, 0.0),
    )
    g_proj[0, rows:, :] = (g_before * gate_x[rows:, :]).astype(low)
    g_proj[1, rows:, :] = jnp.zeros((tails, width), low)
    g_proj[2, rows:, :] = (g_before * gate_b[rows:, :]).astype(low)


def branch_backward(mine, theirs, res, cot, gains, taps, own, other, gates, conv):
    _, rows, width = res.shape
    long = gates[0].shape[0]
    out_weight = pl.BlockSpec((width, width), lambda i, *_: (3, 0))
    outs = [
        shape_of(res.shape, wide),
        shape_of(res.shape, low),
        shape_of((3, long, width), low),
        shape_of((2, 1, width), wide),
        shape_of((3, width), wide),
    ]
    full = whole_spec(res.shape)
    return local_call(
        branch_back_kernel,
        (1,),
        [whole_spec((rows, width))] * 4
        + [full, whole_spec(cot.shape), whole_spec(gains.shape), whole_spec(taps.shape)]
        + [out_weight, out_weight]
        + [whole_spec(g.shape) for g in gates]
        + [whole_spec(conv.shape)],
        [whole_spec(o.shape) for o in outs],
        outs,
        [pltpu.VMEM((rows + 8, width), wide), pltpu.VMEM((rows + 8, width), wide)],
        (*mine, *theirs, res, cot, gains, taps, own, other, *gates, conv),
    )


def branch_grad_kernel(left0, left1, right0, right1, own, other):
    rows = own.shape[0] // 2
    for h, out in enumerate((own, other)):
        for k, (left, right) in enumerate(((left0, right0), (left1, right1))):
            one = left[h] if len(left.shape) == 3 else left[...]
            two = right[h] if k == 1 and len(left.shape) == 2 else right[0]
            out[k * rows : (k + 1) * rows, :] = dot_of(one, two, 0, 0).astype(low)


def branch_grads(n1, g_proj, gate, second):
    width = n1.shape[2]
    gate_spec = pl.BlockSpec((1, *g_proj.shape[1:]), lambda i: (gate, 0, 0))
    if second is None:
        left, right = n1, g_proj
        right_spec = pl.BlockSpec((1, *g_proj.shape[1:]), lambda i: (gate + 1, 0, 0))
    else:
        left, right = second
        right_spec = whole_spec(right.shape)
    specs, shapes = chunk_outs(True, 2 * width, width)
    return local_call(
        branch_grad_kernel,
        (1,),
        [whole_spec(n1.shape), whole_spec(left.shape), gate_spec, right_spec],
        specs,
        shapes,
        [],
        (n1, left, g_proj, right),
    )


def shards(
    tokens,
    cotangent,
    input_projection_weight,
    conv_weight,
    output_projection_weight,
    norm_gains,
    gate_up_weight,
    down_projection_weight,
    in_first,
    in_second,
    conv_first,
    conv_second,
    out_first,
    out_second,
    gain_first,
    gain_second,
    gu_first,
    gu_second,
    down_first,
    down_second,
):
    feat_cols = tokens.shape[1]
    branch_cols = conv_weight.shape[1]
    hidden_cols = down_projection_weight.shape[0]
    block_rows = tokens.shape[0]
    seq_len = max(SEQ_LEAST, block_rows * lax.axis_size("dp") * lax.axis_size("col"))
    data_pos = lax.axis_index("dp")
    row_pos = lax.axis_index("row")
    col_pos = lax.axis_index("col")
    home = row_pos == col_pos
    tail_rows = 16

    in_low = jnp.transpose(input_projection_weight, (1, 0, 2)).astype(low).reshape(-1, branch_cols)
    io_low = jnp.concatenate([in_low, output_projection_weight.astype(low)])
    io_share = share_of(io_low, (1, 0))
    io_got = swap(io_share, "col")
    row_start = (data_pos * lax.axis_size("row") + row_pos) * block_rows
    tail = from_behind(tokens[-2:], ("dp", "row"), 1)
    tail = jnp.where(row_start % seq_len != 0, tail, jnp.zeros_like(tail))
    spare = jnp.zeros((tail_rows - 8, feat_cols), low)
    gain_parts = []
    left = norm_gains
    for _ in range(3):
        gain_parts.append(lax.reduce_precision(left, 8, 7))
        left = left - gain_parts[-1]
    gain_parts = jnp.concatenate(gain_parts).astype(low)
    extra = tie(jnp.concatenate([tail, gain_parts, spare]))
    block = jnp.concatenate([tie(tokens, io_got), extra, cotangent])
    away = to_home(block)
    gu_weight = to_linear(gate_up_weight)
    gate_low, up_low = split_pairs(gu_weight, feat_cols, hidden_cols)
    down_low = down_projection_weight.astype(low)
    both = jnp.stack([block, away])
    both = jnp.where(home, both, home_to_sibling(both))
    gains = both[:, block_rows + 2 : block_rows + 8].astype(wide)
    gains = gains[:, 0:2] + gains[:, 2:4] + gains[:, 4:6]
    gains = [gains[:, k : k + 1] for k in range(2)]
    gate_got = swap(tie(share_of(gate_low, (1, 0)), io_got), "col")
    up_got = swap(tie(share_of(up_low, (0, 1)), gate_got), "col")
    down_got = swap(tie(down_low, up_got), "col")
    io_pair = keep_or_join(0, io_got, flip(io_got, 0))
    io_other = keep_or_join(1, io_pair, flip(io_pair, 1))
    gate_pair = keep_or_join(0, gate_got, flip(tie(gate_got, io_pair), 0))
    up_pair = keep_or_join(1, up_got, flip(tie(up_got, io_pair), 1))
    gate_more = flip(gate_pair, 1)
    up_more = flip(up_pair, 0)
    weights = [gate_low, gate_pair, gate_more, up_low, up_pair, up_more]
    bits = jnp.stack([dp_bit(1), dp_bit(0)]).astype(jnp.int32)
    downs = [down_low, down_got]

    n1, gate_b, gate_c, gate_x, conv, hidden, *branch = branch_forward(
        both, block_rows, tail_rows, gains[0], conv_weight, io_low, io_other
    )
    n2, res, gate, upper, act = ffn_forward(
        bits, both, branch, swap_halves(branch), gains[1], weights
    )

    turns = Turns()
    orders = dict(D="xyl", d="ylx", a="xyl", b="lyx", c="xyl", e="lyx", I="xyl", i="xyl")
    down_half = hidden_cols // 2
    for k, name in enumerate("Dd"):
        split = orders[name][0] == "x"
        turns.add(name, down_grads(act, both, k, down_half, split), orders[name])
    turns.run("Dd")
    g_gate, g_up, *part_two = ffn_backward(
        bits, tie(both, *turns.after), downs, gate, upper, weights
    )
    quarter = feat_cols // 4
    for k, name in enumerate("abce"):
        split = orders[name][0] == "x"
        turns.add(name, pair_grads(n2, g_gate, g_up, k, quarter, split), orders[name])
    turns.run("abcDe")
    g_res, g_branch, g_proj, gain_two_grad, conv_grad = branch_backward(
        part_two,
        swap_halves(part_two),
        tie(res, *turns.after),
        both,
        gains[1],
        conv_weight,
        io_low,
        io_other,
        (gate_b, gate_c, gate_x),
        conv,
    )
    turns.add("I", branch_grads(n1, g_proj, 0, None), orders["I"])
    io_last = branch_grads(n1, g_proj, 2, (hidden, g_branch))
    turns.after += tuple(io_last)
    turns.run("IdabD")

    g_late = tie(g_proj, *turns.after)
    io_half = [half.reshape(4, feat_cols, branch_cols) for half in (io_low, io_other)]
    g_part = jnp.stack(
        [sum(mul_t(g_late[g], io_half[h][g]) for g in range(3)).astype(low) for h in range(2)]
    )
    g_long = g_part.astype(wide) + swap(g_part, "row").astype(wide)
    tok = both[:, : block_rows + 2].astype(wide)
    scale = lax.rsqrt(jnp.sum(tok * tok, axis=(0, 2)) / D + norm_eps)[None, :, None]
    gain_one_grad = jnp.sum(g_long[:, : block_rows + 2] * tok * scale, axis=1)
    small = [
        jnp.concatenate([conv_grad, gain_one_grad[h : h + 1], gain_two_grad[h]]) for h in range(2)
    ]
    spare = jnp.zeros((16, feat_cols), low)
    small = [jnp.pad(part, ((0, 11), (0, 0))).astype(low) for part in small]
    io_long = []
    for h in range(2):
        pieces = jnp.split(io_last[h], 4)
        io_long.append(
            jnp.concatenate(
                [pieces[0], small[h], pieces[1], spare, pieces[2], spare, pieces[3], spare]
            )
        )
    turns.add("i", io_long, orders["i"])
    turns.run("eiacbdDIcaeDciIabDdcieIDabd")

    def in_flat(values):
        return jnp.transpose(values, (1, 0, 2)).reshape(3 * feat_cols, branch_cols)

    def in_back(values):
        return jnp.transpose(values.reshape(3, feat_cols, branch_cols), (1, 0, 2))

    wheres = {name: where_of(orders[name]) for name in orders}
    down_state = (down_projection_weight, down_first, down_second)
    gu_state = (gu_weight, to_linear(gu_first), to_linear(gu_second))
    in_state = (in_flat(input_projection_weight), in_flat(in_first), in_flat(in_second))
    out_state = (output_projection_weight, out_first, out_second)
    pairs = 2 * hidden_cols // 128

    shares = turns.shares
    part_rows = feat_cols // 2
    turns.reach_shares("Dd")
    down_squares = sum(
        share_norms(wheres[n], shares[n], [(down_state, 4 * k)], down_half // 4)
        for k, n in enumerate("Dd")
    )
    turns.add_norms("p", down_squares)
    turns.run("pacpibpcep")
    turns.reach_shares("abce")
    gu_squares = sum(
        share_norms(wheres[n], shares[n], [(gu_state, 2 * k)], quarter // 2 * pairs, pairs=True)
        for k, n in enumerate("abce")
    )
    turns.add_norms("n", gu_squares)
    turns.run("nIdpnbin")
    turns.reach_shares("Ii")
    io_squares = share_norms(wheres["i"], shares["i"], [(in_state, 4), (out_state, 0)], part_rows)
    in_squares = share_norms(wheres["I"], shares["I"], [(in_state, 0)], part_rows)
    turns.add_norms("m", io_squares + jnp.pad(in_squares, (0, 2)))
    turns.run("memdnmImenmiIi")
    turns.finish()
    sums, seen = turns.done, turns.seen

    back = tie(g_long[::-1, block_rows : block_rows + 2], seen["i"][4])
    back = from_behind(back, ("dp", "col"), -1)
    g_n1 = g_long[:, :block_rows].at[:, -2:].add(back)
    tok, scale = tok[:, :block_rows], scale[:, :block_rows]
    weighted = g_n1 * gains[0]
    inner = jnp.sum(weighted * tok, axis=(0, 2))[None, :, None]
    tok_half = (g_res + (scale * weighted - tok * (scale * scale * scale * inner / D))).astype(low)
    token_grad = jnp.where(home, tok_half[0], home_to_away(tok_half[1]))
    act = tie(act, seen["D"][1])
    ffn = jnp.stack([mul(act, downs[h]) for h in range(2)])
    out_half = (res + (ffn + sibling_to_home(ffn.astype(low)).astype(wide))).astype(low)
    output = jnp.where(home, out_half[0], home_to_away(out_half[1]))

    def gu_back(values):
        return from_linear(values, feat_cols, 2)

    def ratio_of(norms):
        norms = jnp.sqrt(norms)
        return norms, (learn_rate * (norms[0] / (norms[1] + adam_eps))).reshape(1)

    (gu_norms, gu_ratio), (down_norms, down_ratio) = [ratio_of(sums[name]) for name in "np"]
    (in_norms, in_ratio), (out_norms, out_ratio) = [ratio_of(sums["m"][k : k + 2]) for k in (0, 2)]

    def later_half(count):
        return functools.partial(lamb_plain, lambda i: (i >= count // 2).astype(jnp.int32))

    def fixed_half(half):
        return functools.partial(lamb_plain, lambda i: half)

    last = sums["i"]
    small = [part[part_rows : part_rows + 5] for part in last]
    small = jnp.where((wheres["i"][0] >> 1) == 0, small[0], small[1]).astype(wide)
    conv_grad, gains_grad = small[:3], small[3:]
    conv_m, conv_v, conv_u = lamb_moments(conv_weight, conv_grad, conv_first, conv_second, 0.0)
    gain_m, gain_v, gain_u = lamb_moments(norm_gains, gains_grad, gain_first, gain_second, 0.0)
    col_first = (col_pos == 0).astype(wide)
    row_first = (row_pos == 0).astype(wide)
    small_norms = jnp.stack(
        [
            square_pair(conv_weight, conv_u) * col_first,
            square_pair(norm_gains[0], gain_u[0]) * row_first,
            square_pair(norm_gains[1], gain_u[1]) * row_first,
        ]
    )
    down_sums = [sums[name] for name in "Dd"]
    pair_sums = [sums[name] for name in "abce"]
    row_norms = small_norms + swap(small_norms, "row")
    pair_sums[1] = [tie(part, small_norms) for part in pair_sums[1]]
    pair_sums[3] = [tie(part, row_norms) for part in pair_sums[3]]
    down_sums[1] = [tie(part, row_norms) for part in down_sums[1]]
    down_new = None
    for k in (0, 1):
        name = "Dd"[k]
        block = down_half // 12
        down_new = lamb_call(
            later_half(12), wheres[name], down_ratio, down_sums[k], block, lambda i: i % 6,
            down_state, block, 12 * k, 12, down_new, [],
        )
    gu_new = None
    gu_rows = 16
    for k in (0, 2, 1, 3):
        name = "abce"[k]
        blocks = quarter // gu_rows
        gu_new = lamb_call(
            lamb_pairs, wheres[name], gu_ratio, pair_sums[k], gu_rows, lambda i: i,
            gu_state, gu_rows * pairs, k * blocks, blocks, gu_new,
            [pltpu.VMEM((gu_rows * pairs, 128), wide)],
        )
    small_norms = jnp.sqrt(row_norms + swap(row_norms, "col"))
    last = [tie(part, small_norms) for part in last]
    first_io = [tie(part, small_norms) for part in sums["I"]]
    in_new = lamb_call(
        later_half(8), wheres["I"], in_ratio, first_io, part_rows // 2, lambda i: i % 4,
        in_state, part_rows // 2, 0, 8, None, [],
    )
    in_new = lamb_call(
        fixed_half(0), wheres["i"], in_ratio, last, part_rows + 16, lambda i: i,
        in_state, part_rows, 4, 2, in_new, [],
    )
    out_new = lamb_call(
        fixed_half(1), wheres["i"], out_ratio, last, part_rows + 16, lambda i: i,
        out_state, part_rows, 0, 2, None, [],
    )

    trust_norms = jnp.stack(
        [
            in_norms,
            small_norms[0],
            out_norms,
            small_norms[1],
            small_norms[2],
            gu_norms,
            down_norms,
        ]
    )
    gains_new = jnp.stack(
        [
            apply_trust(norm_gains[0], gain_u[0], small_norms[1]),
            apply_trust(norm_gains[1], gain_u[1], small_norms[2]),
        ]
    )
    return (
        output,
        token_grad,
        *[in_back(values) for values in in_new],
        apply_trust(conv_weight, conv_u, small_norms[0]),
        conv_m,
        conv_v,
        *out_new,
        gains_new,
        gain_m,
        gain_v,
        *[gu_back(values) for values in gu_new],
        *down_new,
        trust_norms,
    )


def solution(mesh):
    in_specs = (
        P(("dp", "row"), "col"),
        P(("dp", "row"), "col"),
        P("col", None, "row"),
        P(None, "row"),
        P("row", "col"),
        P(None, "col"),
        P("col", None, "row"),
        P("row", "col"),
        P("col", None, "row"),
        P("col", None, "row"),
        P(None, "row"),
        P(None, "row"),
        P("row", "col"),
        P("row", "col"),
        P(None, "col"),
        P(None, "col"),
        P("col", None, "row"),
        P("col", None, "row"),
        P("row", "col"),
        P("row", "col"),
    )
    out_specs = (
        P(("dp", "row"), "col"),
        P(("dp", "row"), "col"),
        P("col", None, "row"),
        P("col", None, "row"),
        P("col", None, "row"),
        P(None, "row"),
        P(None, "row"),
        P(None, "row"),
        P("row", "col"),
        P("row", "col"),
        P("row", "col"),
        P(None, "col"),
        P(None, "col"),
        P(None, "col"),
        P("col", None, "row"),
        P("col", None, "row"),
        P("col", None, "row"),
        P("row", "col"),
        P("row", "col"),
        P("row", "col"),
        P(),
    )
    return jax.shard_map(shards, mesh=mesh, in_specs=in_specs, out_specs=out_specs, check_vma=False)
```

```python
import functools

import jax
import jax.numpy as jnp
from jax import lax
from jax.experimental import pallas as pl
from jax.experimental.layout import Layout, with_layout_constraint
from jax.experimental.pallas import tpu as pltpu
from jax.sharding import PartitionSpec as P

D = 1024
SEQ_LEAST = 4096
STEP = 5
MIB = 1024 * 1024


norm_eps = 1e-05
adam_eps = 1e-06
beta_one = 0.5
beta_two = 0.6
learn_rate = 0.5
decay_rate = 0.01
low = jnp.bfloat16
wide = jnp.float32


def from_behind(block, axis, distance):
    devices = range(lax.axis_size(axis))
    route = [(i - distance, i) for i in devices if i - distance in devices]
    return lax.ppermute(block, axis, route)


def swap(values, axis):
    return lax.ppermute(values, axis, [(0, 1), (1, 0)])


def swap_halves(halves):
    return [swap(half, "row") for half in halves]


def to_home(values):
    return lax.ppermute(values, ("row", "col"), [(1, 0), (2, 3)])


def home_to_sibling(values):
    return lax.ppermute(values, ("row", "col"), [(0, 2), (3, 1)])


def home_to_away(values):
    return lax.ppermute(values, ("row", "col"), [(0, 1), (3, 2)])


def sibling_to_home(values):
    return lax.ppermute(values, ("row", "col"), [(2, 0), (1, 3)])


def contract(left, right, left_dim, right_dim):
    return lax.dot_general(
        left, right, (((left_dim,), (right_dim,)), ((), ())), preferred_element_type=wide
    )


def mul(left, right):
    return contract(left, right, 1, 0)


def mul_t(left, right):
    return contract(left, right, 1, 1)


def t_mul(left, right):
    return contract(left, right, 0, 0)


def lamb_moments(weight, grad, first, second, decay):
    first_new = beta_one * first + (1.0 - beta_one) * grad
    second_new = beta_two * second + (1.0 - beta_two) * grad * grad
    direction = (first_new * (1.0 / (1.0 - beta_one**STEP))) / (
        jnp.sqrt(second_new * (1.0 / (1.0 - beta_two**STEP))) + adam_eps
    ) + decay * weight
    return (first_new, second_new, direction)


def square_pair(weight, direction):
    return jnp.stack([jnp.sum(weight * weight), jnp.sum(direction * direction)])


def kernel_call(kernel, grid, in_specs, out_specs, out_shape, scratch, args, aliases=None, mib=1):
    return pl.pallas_call(
        kernel,
        grid_spec=pltpu.PrefetchScalarGridSpec(
            num_scalar_prefetch=1,
            grid=grid,
            in_specs=in_specs,
            out_specs=out_specs,
            scratch_shapes=scratch,
        ),
        out_shape=out_shape,
        input_output_aliases=aliases or {},
        compiler_params=pltpu.CompilerParams(vmem_limit_bytes=48 * MIB),
        cost_estimate=pl.CostEstimate(flops=0, bytes_accessed=mib * MIB, transcendentals=0),
    )(*args)


SCALARS = pl.BlockSpec(memory_space=pltpu.SMEM)


def norm_kernel(where, grad, *refs):
    sums = refs[-1]
    groups = [refs[:3], refs[3:6]][: len(refs) // 3]
    rows = groups[0][0].shape[0]
    zero = jnp.zeros((8, groups[0][0].shape[1]), wide)
    for k, (p, m, v) in enumerate(groups):

        def body(at, total):
            here = pl.ds(pl.multiple_of(at * 32, 32), 32)
            weight = p[here, :]
            direction = lamb_moments(
                weight, grad[here, :].astype(wide), m[here, :], v[here, :], decay_rate
            )[2]
            return tuple(
                t + (sq[:8] + sq[8:16]) + (sq[16:24] + sq[24:])
                for t, sq in zip(total, (weight * weight, direction * direction))
            )

        total = lax.fori_loop(0, rows // 32, body, (zero, zero))
        mine = 1.0 if len(groups) == 1 else ((where[0] >> 1) == k).astype(wide)
        for j in range(2):
            sums[2 * k + j] = jnp.sum(total[j]) * mine


def norm_pairs_kernel(where, grad, p, m, v, sums):
    rows, cols = grad.shape
    tiles = cols // 128
    side = where[0] >> 1
    zero = jnp.zeros((8, 128), wide)
    total = [zero, zero]
    for tile in range(tiles):
        here = pl.ds(2 * tile + side, rows, stride=2 * tiles)
        weight = p[here, :]
        direction = lamb_moments(
            weight, grad[:, tile * 128 : (tile + 1) * 128].astype(wide), m[here, :], v[here, :], decay_rate
        )[2]
        for j, sq in enumerate((weight * weight, direction * direction)):
            total[j] = total[j] + jnp.sum((sq).reshape(rows // 8, 8, 128), axis=0)
    for j in range(2):
        sums[j] = jnp.sum(total[j])


def share_norms(where, grad, states, rows, pairs=False):
    specs, args = [], []
    for state, at in states:
        for array in state:
            if pairs:
                spec = pl.BlockSpec(
                    (rows, array.shape[1]), lambda i, w, at=at: (at + (w[0] & 1), 0)
                )
            elif len(states) == 2:
                spec = pl.BlockSpec(
                    (rows, array.shape[1]), lambda i, w, at=at: (at + (w[0] & 1), 0)
                )
            else:
                spec = pl.BlockSpec((rows, array.shape[1]), lambda i, w, at=at: (at + w[0], 0))
            specs.append(spec)
            args.append(array)
    return kernel_call(
        norm_pairs_kernel if pairs else norm_kernel,
        (1,),
        [whole_spec(grad.shape)] + specs,
        SCALARS,
        jax.ShapeDtypeStruct((2 * len(states),), wide),
        [],
        (where, grad, *args),
    )


def lamb_loop(refs, outs, ratio, rows, step, pick):
    p, m, v = refs

    def body(at, carry):
        here = pl.ds(pl.multiple_of(at * step, step), step)
        weight = p[here, :]
        first_new, second_new, direction = lamb_moments(
            weight, pick(here), m[here, :], v[here, :], decay_rate
        )
        outs[0][here, :] = weight - ratio * direction
        outs[1][here, :] = first_new
        outs[2][here, :] = second_new
        return carry

    lax.fori_loop(0, rows // step, body, 0)


def lamb_plain(half_of_block, where, ratio, part, got, p, m, v, *outs):
    use = half_of_block(pl.program_id(0)) == (where[0] >> 1)

    def pick(here):
        return jnp.where(use, part[here, :].astype(wide), got[here, :].astype(wide))

    lamb_loop((p, m, v), outs, ratio[0], p.shape[0], 64, pick)


def lamb_pairs(where, ratio, part, got, p, m, v, p_out, m_out, v_out, mixed):
    rows, cols = part.shape
    tiles = cols // 128
    for value, order in ((0, (part, got)), (1, (got, part))):

        @pl.when((where[0] >> 1) == value)
        def _():
            for tile in range(tiles):
                for side, ref in enumerate(order):
                    mixed[pl.ds(2 * tile + side, rows, stride=2 * tiles), :] = ref[
                        :, tile * 128 : (tile + 1) * 128
                    ].astype(wide)

    lamb_loop(
        (p, m, v), (p_out, m_out, v_out), ratio[0], p.shape[0], 192, lambda here: mixed[here, :]
    )


def lamb_call(kernel, where, ratio, grad, grad_block, grad_at, state, block, start, count, before, scratch):
    rows, cols = state[0].shape
    flat = pl.BlockSpec((block, cols), lambda i, w: (i + start, 0))
    grad_spec = pl.BlockSpec((grad_block, grad[0].shape[1]), lambda i, w: (grad_at(i), 0))
    whole = jax.ShapeDtypeStruct((rows, cols), wide)
    args = [where, ratio, *grad, *state]
    specs = [SCALARS, grad_spec, grad_spec, flat, flat, flat]
    run, aliases = kernel, {}
    if before is not None:
        aliases = {len(args) + k: k for k in range(3)}

        def run(*refs):
            kernel(*refs[: len(args)], *refs[len(args) + 3 :])

    return list(
        kernel_call(
            run,
            (count,),
            specs + [pl.BlockSpec(memory_space=pl.ANY)] * len(aliases),
            [flat, flat, flat],
            [whole, whole, whole],
            scratch,
            (*args, *(before or [])),
            aliases,
            mib=26 * count * block * cols // MIB,
        )
    )


def to_linear(values):
    rows, sides, cols = values.shape
    split = with_layout_constraint(
        values.reshape(rows, sides, cols // 128, 128), Layout(major_to_minor=(0, 2, 1, 3))
    )
    return split.transpose(0, 2, 1, 3).reshape(rows * sides * cols // 128, 128)


def from_linear(values, rows, sides):
    cols = values.size // (rows * sides)
    split = values.reshape(rows, cols // 128, sides, 128).transpose(0, 2, 1, 3)
    split = with_layout_constraint(split, Layout(major_to_minor=(0, 2, 1, 3)))
    return split.reshape(rows, sides, cols)


def apply_trust(weight, direction, norms):
    return weight - learn_rate * (norms[0] / (norms[1] + adam_eps)) * direction


def flip(values, bit):
    size = lax.axis_size("dp")
    return lax.ppermute(values, "dp", [(i, i ^ (1 << bit)) for i in range(size)])


def dp_bit(bit):
    return (lax.axis_index("dp") >> bit) & 1


def rows_of(values, start, rows):
    return lax.dynamic_slice_in_dim(values, start, rows, 0)


def total_of(pieces):
    total = pieces[0].astype(wide)
    for piece in pieces[1:]:
        total = total + piece.astype(wide)
    return total


def tie(values, *deps):
    return lax.optimization_barrier((values, *deps))[0]


def low_total(pieces):
    return total_of(pieces).astype(low)


def keep_or_join(bit, part, other):
    return jnp.where(
        dp_bit(bit) == 0,
        jnp.concatenate([part, other]),
        jnp.concatenate([other, part]),
    )


def share_of(weight, order):
    rows = weight.shape[0] // (1 << len(order))
    index = 0
    for bit in order:
        index = 2 * index + dp_bit(bit)
    return rows_of(weight, index * rows, rows)


def half_of(piece, place):
    rows = piece.shape[-2] // 2
    return lax.dynamic_slice_in_dim(piece, place * rows, rows, piece.ndim - 2)


def chunk_sum(chunk, order, keep):
    bits = {"y": 0, "l": 1}
    steps = [name if name == "x" else bits[name] for name in order]
    pieces = [chunk]
    for step in steps:
        if step == "x":
            whole = len(pieces) == 1
            got = yield step, pieces[0][1] if whole else low_total([piece[1] for piece in pieces])
            pieces = [piece[0] for piece in pieces] + [got]
        else:
            here = dp_bit(step)
            got = yield step, low_total([half_of(piece, 1 - here) for piece in pieces])
            pieces = [half_of(piece, here) for piece in pieces] + [got]
    part = low_total(pieces)
    for step in range((lax.axis_size("dp") - 1).bit_length()):
        if step not in steps:
            got = yield step, part
            part = low_total([part, got])
    keep(part)
    first, second = [step for step in steps if step != "x"]
    got = yield second, part
    part = keep_or_join(second, part, got)
    got = yield first, part
    return part, got


def norm_sum(values):
    for step in ("x", "row", 1, 0):
        got = yield step, values
        values = values + got
    return values


def where_of(order):
    bits = {"y": 0, "l": 1}
    first, second = [bits[name] for name in order if name != "x"]
    return (2 * dp_bit(first) + dp_bit(second)).astype(jnp.int32).reshape(1)


def move(step, send):
    if step == "row":
        return swap(send, "row")
    return swap(send, "col") if step == "x" else flip(send, step)


class Turns:
    def __init__(self):
        self.chunks = {}
        self.arrivals = {}
        self.seen = {}
        self.done = {}
        self.shares = {}
        self.after = ()

    def add(self, name, chunk, order):
        self.chunks[name] = chunk_sum(chunk, order, functools.partial(self.shares.__setitem__, name))

    def add_norms(self, name, values):
        self.chunks[name] = norm_sum(values)

    def turn(self, name):
        got = self.arrivals.get(name)
        try:
            if got is None:
                self.seen[name] = []
                step, send = next(self.chunks[name])
                send = tie(send, *self.after)
            else:
                got = tie(got, *self.after)
                self.seen[name].append(got)
                step, send = self.chunks[name].send(got)
        except StopIteration as end:
            self.done[name] = end.value
            return
        self.arrivals[name] = move(step, send)
        self.after = (send,)

    def run(self, names):
        for name in names:
            if name not in self.done:
                self.turn(name)

    def reach_shares(self, names):
        while any(name not in self.shares for name in names):
            self.run([name for name in names if name not in self.shares])

    def finish(self):
        while len(self.done) < len(self.chunks):
            self.run(self.chunks)


def deinterleave(pairs, gate, up):
    rows, cols = gate.shape
    tiles = cols // 128
    for tile in range(tiles):
        for side, out in enumerate((gate, up)):
            out[:, tile * 128 : (tile + 1) * 128] = pairs[
                pl.ds(2 * tile + side, rows, stride=2 * tiles), :
            ].astype(low)


def split_pairs(linear, rows, cols):
    block = 64
    half = jax.ShapeDtypeStruct((rows, cols), low)
    out_spec = pl.BlockSpec((block, cols), lambda i: (i, 0))
    return pl.pallas_call(
        deinterleave,
        grid=(rows // block,),
        in_specs=[pl.BlockSpec((block * 2 * cols // 128, 128), lambda i: (i, 0))],
        out_specs=[out_spec, out_spec],
        out_shape=[half, half],
        compiler_params=pltpu.CompilerParams(vmem_limit_bytes=24 * MIB),
        cost_estimate=pl.CostEstimate(
            flops=rows * cols, bytes_accessed=12 * rows * cols, transcendentals=0
        ),
    )(linear)


def dot_of(left, right, left_dim, right_dim):
    return lax.dot_general(
        left, right, (((left_dim,), (right_dim,)), ((), ())), preferred_element_type=wide
    )


def local_call(kernel, grid, in_specs, out_specs, out_shape, scratch, args, prefetch=0):
    return pl.pallas_call(
        kernel,
        grid_spec=pltpu.PrefetchScalarGridSpec(
            num_scalar_prefetch=prefetch,
            grid=grid,
            in_specs=in_specs,
            out_specs=out_specs,
            scratch_shapes=scratch,
        ),
        out_shape=out_shape,
        compiler_params=pltpu.CompilerParams(vmem_limit_bytes=48 * MIB),
        cost_estimate=pl.CostEstimate(flops=0, bytes_accessed=MIB, transcendentals=0),
    )(*args)


def whole_spec(shape):
    return pl.BlockSpec(shape, lambda *_: (0,) * len(shape))


def shape_of(dims, kind):
    return jax.ShapeDtypeStruct(dims, kind)


def row_scale(halves):
    total = sum(jnp.sum(half * half, axis=1, keepdims=True) for half in halves)
    return lax.rsqrt(total / D + norm_eps)


def branch_kernel(tok, gains, taps, own, other, n1, gate_b, gate_c, gate_x, conv, hidden, part0, part1, ext):
    long, width = n1.shape[1:]
    rows = conv.shape[0]
    step = long // 3

    def gates(at, carry):
        here = pl.ds(pl.multiple_of(at * step, step), step)
        halves = [tok[h, here, :].astype(wide) for h in range(2)]
        scale = row_scale(halves)
        for h in range(2):
            n1[h, here, :] = (halves[h] * scale * gains[h]).astype(low)
        for g, out in enumerate((gate_b, gate_c, gate_x)):
            w = slice(g * width, (g + 1) * width)
            out[here, :] = dot_of(n1[0, here, :], own[w, :], 1, 0) + dot_of(
                n1[1, here, :], other[w, :], 1, 0
            )
        return carry

    lax.fori_loop(0, 3, gates, 0)
    ext[8 : 8 + rows, :] = gate_b[:rows, :] * gate_x[:rows, :]
    ext[6:8, :] = gate_b[rows : rows + 2, :] * gate_x[rows : rows + 2, :]
    w_out = slice(3 * width, 4 * width)
    quarter = rows // 4
    for at in range(4):
        start = at * quarter
        taken = slice(start, start + quarter)
        value = sum(taps[k] * ext[start + 6 + k : start + 6 + k + quarter, :] for k in range(3))
        conv[taken, :] = value
        low_hidden = (gate_c[taken, :] * value).astype(low)
        hidden[taken, :] = low_hidden
        for part, weight in ((part0, own), (part1, other)):
            part[taken, :] = dot_of(low_hidden, weight[w_out, :], 1, 0).astype(low)


def branch_forward(tok, rows, tails, gains, taps, own, other):
    width = tok.shape[2]
    gate = shape_of((rows + tails, width), wide)
    outs = [
        shape_of((2, rows + tails, width), low),
        gate,
        gate,
        gate,
        shape_of((rows, width), wide),
        shape_of((rows, width), low),
        shape_of((rows, width), low),
        shape_of((rows, width), low),
    ]
    args = (tok, gains, taps, own, other)
    return local_call(
        branch_kernel,
        (1,),
        [whole_spec(a.shape) for a in args],
        [whole_spec(o.shape) for o in outs],
        outs,
        [pltpu.VMEM((rows + 8, width), wide)],
        args,
    )


def piece_at(bits, which, piece, width):
    place = bits[which] if piece == 0 else 1 - bits[which]
    return pl.ds(pl.multiple_of(place * width, width), width)


def ffn_kernel(bits, tok, mine0, mine1, theirs0, theirs1, gains, g0, g1, g2, u0, u1, u2, n2, res, gate, up, act):
    width = g1.shape[0]

    @pl.when(pl.program_id(0) == 0)
    def _():
        for h, (mine, theirs) in enumerate(((mine0, theirs0), (mine1, theirs1))):
            res[h] = tok[h, : res.shape[1], :].astype(wide) + (
                mine[...].astype(wide) + theirs[...].astype(wide)
            )
        scale = row_scale([res[0], res[1]])
        for h in range(2):
            n2[h] = (res[h] * scale * gains[h]).astype(low)

    for which, (out, w0, w1, w2) in enumerate(((gate, g0, g1, g2), (up, u0, u1, u2))):
        total = dot_of(n2[0], w0[...], 1, 0)
        for piece, w in enumerate((w1, w2)):
            total += dot_of(n2[1, :, piece_at(bits, which, piece, width)], w[...], 1, 0)
        out[...] = total
    value = gate[...]
    act[...] = (value * jax.nn.sigmoid(value) * up[...]).astype(low)


def ffn_forward(bits, tok, mine, theirs, gains, weights):
    rows, width = mine[0].shape
    cols = weights[0].shape[1]
    tile = cols // 3
    both = (2, rows, width)
    full = whole_spec(both)
    wide_tile = pl.BlockSpec((rows, tile), lambda i, *_: (0, i))
    weight_specs = [pl.BlockSpec((w.shape[0], tile), lambda i, *_: (0, i)) for w in weights]
    return local_call(
        ffn_kernel,
        (3,),
        [whole_spec(tok.shape)]
        + [whole_spec((rows, width))] * 4
        + [whole_spec(gains.shape)]
        + weight_specs,
        [full, full, wide_tile, wide_tile, wide_tile],
        [
            shape_of(both, low),
            shape_of(both, wide),
            shape_of((rows, cols), wide),
            shape_of((rows, cols), wide),
            shape_of((rows, cols), low),
        ],
        [],
        (bits, tok, *mine, *theirs, gains, *weights),
        prefetch=1,
    )


def ffn_back_kernel(
    bits, cot, d_own, d_other, gate, up, g0, g1, g2, u0, u1, u2, g_gate, g_up, part0, part1, total
):
    width = g1.shape[0]

    @pl.when(pl.program_id(0) == 0)
    def _():
        total[...] = jnp.zeros_like(total)

    start = cot.shape[1] - gate.shape[0]
    g_act = dot_of(cot[0, start:, :], d_own[...], 1, 1) + dot_of(cot[1, start:, :], d_other[...], 1, 1)
    value = gate[...]
    sigma = jax.nn.sigmoid(value)
    g_gate[...] = (g_act * up[...] * sigma * (1.0 + value * (1.0 - sigma))).astype(low)
    g_up[...] = (g_act * (value * sigma)).astype(low)
    total[0] += dot_of(g_gate[...], g0[...], 1, 1) + dot_of(g_up[...], u0[...], 1, 1)
    for which, (grad, w1, w2) in enumerate(((g_gate, g1, g2), (g_up, u1, u2))):
        for piece, w in enumerate((w1, w2)):
            total[1, :, piece_at(bits, which, piece, width)] += dot_of(grad[...], w[...], 1, 1)

    @pl.when(pl.program_id(0) == pl.num_programs(0) - 1)
    def _():
        part0[...] = total[0].astype(low)
        part1[...] = total[1].astype(low)


def ffn_backward(bits, cot, downs, gate, up, weights):
    rows, cols = gate.shape
    tile = cols // 3
    part = (rows, cot.shape[2])
    wide_tile = pl.BlockSpec((rows, tile), lambda i, *_: (0, i))
    weight_specs = [pl.BlockSpec((w.shape[0], tile), lambda i, *_: (0, i)) for w in weights]
    down_spec = pl.BlockSpec((tile, downs[0].shape[1]), lambda i, *_: (i, 0))
    return local_call(
        ffn_back_kernel,
        (3,),
        [whole_spec(cot.shape), down_spec, down_spec, wide_tile, wide_tile] + weight_specs,
        [wide_tile, wide_tile, whole_spec(part), whole_spec(part)],
        [shape_of((rows, cols), low)] * 2 + [shape_of(part, low)] * 2,
        [pltpu.VMEM((2, *part), wide)],
        (bits, cot, *downs, gate, up, *weights),
        prefetch=1,
    )


def put(outs, half, rows, value):
    if len(outs) == 2:
        outs[half][rows, :] = value.astype(low)
    else:
        outs[0][half, rows, :] = value.astype(low)


def chunk_outs(split, rows, cols):
    if split:
        return [whole_spec((rows, cols))] * 2, [shape_of((rows, cols), low)] * 2
    return [whole_spec((2, rows, cols))], [shape_of((2, rows, cols), low)]


def pair_grad_kernel(n2, g_gate, g_up, *outs):
    rows = n2.shape[2]
    for h in range(2):
        for side, grad in enumerate((g_gate, g_up)):
            put(outs, h, slice(side * rows, (side + 1) * rows), dot_of(n2[h], grad[...], 0, 0))


def pair_grads(n2, g_gate, g_up, at, rows, split):
    specs, shapes = chunk_outs(split, 2 * rows, g_gate.shape[1])
    outs = local_call(
        pair_grad_kernel,
        (1,),
        [
            pl.BlockSpec((2, n2.shape[1], rows), lambda i: (0, 0, at)),
            whole_spec(g_gate.shape),
            whole_spec(g_up.shape),
        ],
        specs,
        shapes,
        [],
        (n2, g_gate, g_up),
    )
    return tuple(outs) if split else outs[0]


def down_grad_kernel(act, cot, *outs):
    start = cot.shape[1] - act.shape[0]
    for h in range(2):
        put(outs, h, slice(None), dot_of(act[...], cot[h, start:, :], 0, 0))


def down_grads(act, cot, at, rows, split):
    specs, shapes = chunk_outs(split, rows, cot.shape[2])
    outs = local_call(
        down_grad_kernel,
        (1,),
        [pl.BlockSpec((act.shape[0], rows), lambda i: (0, at)), whole_spec(cot.shape)],
        specs,
        shapes,
        [],
        (act, cot),
    )
    return tuple(outs) if split else outs[0]


def branch_back_kernel(
    mine0, mine1, theirs0, theirs1, res, cot, gains, taps, own, other, gate_b, gate_c, gate_x, conv,
    g_res, g_low, g_proj, gain_grad, tap_grad, ext, ext_grad,
):
    _, rows, width = res.shape
    scale = row_scale([res[0], res[1]])
    grads = [
        mine[...].astype(wide) + theirs[...].astype(wide)
        for mine, theirs in ((mine0, theirs0), (mine1, theirs1))
    ]
    inner = sum(
        jnp.sum(grads[h] * gains[h] * res[h], axis=1, keepdims=True) for h in range(2)
    )
    factor = scale * scale * scale * inner / D
    for h in range(2):
        gain_grad[h] = jnp.sum(grads[h] * res[h] * scale, axis=0, keepdims=True)
        value = cot[h, cot.shape[1] - rows :, :].astype(wide) + (scale * (grads[h] * gains[h]) - res[h] * factor)
        g_res[h] = value
        g_low[h] = value.astype(low)
    g_hidden = dot_of(g_low[0], own[...], 1, 1) + dot_of(g_low[1], other[...], 1, 1)
    g_proj[1, :rows, :] = (g_hidden * conv[...]).astype(low)
    g_conv = g_hidden * gate_c[:rows, :]
    ext_grad[:rows, :] = g_conv
    ext_grad[rows:, :] = jnp.zeros((8, width), wide)
    ext[8 : 8 + rows, :] = gate_b[:rows, :] * gate_x[:rows, :]
    ext[6:8, :] = gate_b[rows : rows + 2, :] * gate_x[rows : rows + 2, :]
    for k in range(3):
        tap_grad[k : k + 1, :] = jnp.sum(
            g_conv * ext[6 + k : 6 + k + rows, :], axis=0, keepdims=True
        )
    g_mixed = sum(taps[2 - k] * ext_grad[k : k + rows, :] for k in range(3))
    g_proj[0, :rows, :] = (g_mixed * gate_x[:rows, :]).astype(low)
    g_proj[2, :rows, :] = (g_mixed * gate_b[:rows, :]).astype(low)
    tails = g_proj.shape[1] - rows
    row = lax.broadcasted_iota(jnp.int32, (tails, width), 0)
    first, second = ext_grad[0:1, :], ext_grad[1:2, :]
    g_before = jnp.where(
        row == 0,
        taps[0] * first,
        jnp.where(row == 1, taps[1] * first + taps[0] * second, 0.0),
    )
    g_proj[0, rows:, :] = (g_before * gate_x[rows:, :]).astype(low)
    g_proj[1, rows:, :] = jnp.zeros((tails, width), low)
    g_proj[2, rows:, :] = (g_before * gate_b[rows:, :]).astype(low)


def branch_backward(mine, theirs, res, cot, gains, taps, own, other, gates, conv):
    _, rows, width = res.shape
    long = gates[0].shape[0]
    out_weight = pl.BlockSpec((width, width), lambda i, *_: (3, 0))
    outs = [
        shape_of(res.shape, wide),
        shape_of(res.shape, low),
        shape_of((3, long, width), low),
        shape_of((2, 1, width), wide),
        shape_of((3, width), wide),
    ]
    full = whole_spec(res.shape)
    return local_call(
        branch_back_kernel,
        (1,),
        [whole_spec((rows, width))] * 4
        + [full, whole_spec(cot.shape), whole_spec(gains.shape), whole_spec(taps.shape)]
        + [out_weight, out_weight]
        + [whole_spec(g.shape) for g in gates]
        + [whole_spec(conv.shape)],
        [whole_spec(o.shape) for o in outs],
        outs,
        [pltpu.VMEM((rows + 8, width), wide), pltpu.VMEM((rows + 8, width), wide)],
        (*mine, *theirs, res, cot, gains, taps, own, other, *gates, conv),
    )


def branch_grad_kernel(left0, left1, right0, right1, own, other):
    rows = own.shape[0] // 2
    for h, out in enumerate((own, other)):
        for k, (left, right) in enumerate(((left0, right0), (left1, right1))):
            one = left[h] if len(left.shape) == 3 else left[...]
            two = right[h] if k == 1 and len(left.shape) == 2 else right[0]
            out[k * rows : (k + 1) * rows, :] = dot_of(one, two, 0, 0).astype(low)


def branch_grads(n1, g_proj, gate, second):
    width = n1.shape[2]
    gate_spec = pl.BlockSpec((1, *g_proj.shape[1:]), lambda i: (gate, 0, 0))
    if second is None:
        left, right = n1, g_proj
        right_spec = pl.BlockSpec((1, *g_proj.shape[1:]), lambda i: (gate + 1, 0, 0))
    else:
        left, right = second
        right_spec = whole_spec(right.shape)
    specs, shapes = chunk_outs(True, 2 * width, width)
    return local_call(
        branch_grad_kernel,
        (1,),
        [whole_spec(n1.shape), whole_spec(left.shape), gate_spec, right_spec],
        specs,
        shapes,
        [],
        (n1, left, g_proj, right),
    )


def shards(
    tokens,
    cotangent,
    input_projection_weight,
    conv_weight,
    output_projection_weight,
    norm_gains,
    gate_up_weight,
    down_projection_weight,
    in_first,
    in_second,
    conv_first,
    conv_second,
    out_first,
    out_second,
    gain_first,
    gain_second,
    gu_first,
    gu_second,
    down_first,
    down_second,
):
    feat_cols = tokens.shape[1]
    branch_cols = conv_weight.shape[1]
    hidden_cols = down_projection_weight.shape[0]
    block_rows = tokens.shape[0]
    seq_len = max(SEQ_LEAST, block_rows * lax.axis_size("dp") * lax.axis_size("col"))
    data_pos = lax.axis_index("dp")
    row_pos = lax.axis_index("row")
    col_pos = lax.axis_index("col")
    home = row_pos == col_pos
    tail_rows = 16

    in_low = jnp.transpose(input_projection_weight, (1, 0, 2)).astype(low).reshape(-1, branch_cols)
    io_low = jnp.concatenate([in_low, output_projection_weight.astype(low)])
    io_share = share_of(io_low, (1, 0))
    io_got = swap(io_share, "col")
    row_start = (data_pos * lax.axis_size("row") + row_pos) * block_rows
    tail = from_behind(tokens[-2:], ("dp", "row"), 1)
    tail = jnp.where(row_start % seq_len != 0, tail, jnp.zeros_like(tail))
    spare = jnp.zeros((tail_rows - 8, feat_cols), low)
    gain_parts = []
    left = norm_gains
    for _ in range(3):
        gain_parts.append(lax.reduce_precision(left, 8, 7))
        left = left - gain_parts[-1]
    gain_parts = jnp.concatenate(gain_parts).astype(low)
    extra = tie(jnp.concatenate([tail, gain_parts, spare]))
    block = jnp.concatenate([tie(tokens, io_got), extra, cotangent])
    away = to_home(block)
    gu_weight = to_linear(gate_up_weight)
    gate_low, up_low = split_pairs(gu_weight, feat_cols, hidden_cols)
    down_low = down_projection_weight.astype(low)
    both = jnp.stack([block, away])
    both = jnp.where(home, both, home_to_sibling(both))
    gains = both[:, block_rows + 2 : block_rows + 8].astype(wide)
    gains = gains[:, 0:2] + gains[:, 2:4] + gains[:, 4:6]
    gains = [gains[:, k : k + 1] for k in range(2)]
    gate_got = swap(tie(share_of(gate_low, (1, 0)), io_got), "col")
    up_got = swap(tie(share_of(up_low, (0, 1)), gate_got), "col")
    down_got = swap(tie(down_low, up_got), "col")
    io_pair = keep_or_join(0, io_got, flip(io_got, 0))
    io_other = keep_or_join(1, io_pair, flip(io_pair, 1))
    gate_pair = keep_or_join(0, gate_got, flip(tie(gate_got, io_pair), 0))
    up_pair = keep_or_join(1, up_got, flip(tie(up_got, io_pair), 1))
    gate_more = flip(gate_pair, 1)
    up_more = flip(up_pair, 0)
    weights = [gate_low, gate_pair, gate_more, up_low, up_pair, up_more]
    bits = jnp.stack([dp_bit(1), dp_bit(0)]).astype(jnp.int32)
    downs = [down_low, down_got]

    n1, gate_b, gate_c, gate_x, conv, hidden, *branch = branch_forward(
        both, block_rows, tail_rows, gains[0], conv_weight, io_low, io_other
    )
    n2, res, gate, upper, act = ffn_forward(
        bits, both, branch, swap_halves(branch), gains[1], weights
    )

    turns = Turns()
    orders = dict(D="xyl", d="ylx", a="xyl", b="lyx", c="xyl", e="lyx", I="xyl", i="xyl")
    down_half = hidden_cols // 2
    for k, name in enumerate("Dd"):
        split = orders[name][0] == "x"
        turns.add(name, down_grads(act, both, k, down_half, split), orders[name])
    turns.run("Dd")
    g_gate, g_up, *part_two = ffn_backward(
        bits, tie(both, *turns.after), downs, gate, upper, weights
    )
    quarter = feat_cols // 4
    for k, name in enumerate("abce"):
        split = orders[name][0] == "x"
        turns.add(name, pair_grads(n2, g_gate, g_up, k, quarter, split), orders[name])
    turns.run("abcDe")
    g_res, g_branch, g_proj, gain_two_grad, conv_grad = branch_backward(
        part_two,
        swap_halves(part_two),
        tie(res, *turns.after),
        both,
        gains[1],
        conv_weight,
        io_low,
        io_other,
        (gate_b, gate_c, gate_x),
        conv,
    )
    turns.add("I", branch_grads(n1, g_proj, 0, None), orders["I"])
    io_last = branch_grads(n1, g_proj, 2, (hidden, g_branch))
    turns.after += tuple(io_last)
    turns.run("IdabD")

    g_late = tie(g_proj, *turns.after)
    io_half = [half.reshape(4, feat_cols, branch_cols) for half in (io_low, io_other)]
    g_part = jnp.stack(
        [sum(mul_t(g_late[g], io_half[h][g]) for g in range(3)).astype(low) for h in range(2)]
    )
    g_long = g_part.astype(wide) + swap(g_part, "row").astype(wide)
    tok = both[:, : block_rows + 2].astype(wide)
    scale = lax.rsqrt(jnp.sum(tok * tok, axis=(0, 2)) / D + norm_eps)[None, :, None]
    gain_one_grad = jnp.sum(g_long[:, : block_rows + 2] * tok * scale, axis=1)
    small = [
        jnp.concatenate([conv_grad, gain_one_grad[h : h + 1], gain_two_grad[h]]) for h in range(2)
    ]
    spare = jnp.zeros((16, feat_cols), low)
    small = [jnp.pad(part, ((0, 11), (0, 0))).astype(low) for part in small]
    io_long = []
    for h in range(2):
        pieces = jnp.split(io_last[h], 4)
        io_long.append(
            jnp.concatenate(
                [pieces[0], small[h], pieces[1], spare, pieces[2], spare, pieces[3], spare]
            )
        )
    turns.add("i", io_long, orders["i"])
    turns.run("eiacbdDIcaeDciIabDdcieIDabd")

    def in_flat(values):
        return jnp.transpose(values, (1, 0, 2)).reshape(3 * feat_cols, branch_cols)

    def in_back(values):
        return jnp.transpose(values.reshape(3, feat_cols, branch_cols), (1, 0, 2))

    wheres = {name: where_of(orders[name]) for name in orders}
    down_state = (down_projection_weight, down_first, down_second)
    gu_state = (gu_weight, to_linear(gu_first), to_linear(gu_second))
    in_state = (in_flat(input_projection_weight), in_flat(in_first), in_flat(in_second))
    out_state = (output_projection_weight, out_first, out_second)
    pairs = 2 * hidden_cols // 128

    shares = turns.shares
    part_rows = feat_cols // 2
    turns.reach_shares("Dd")
    down_squares = sum(
        share_norms(wheres[n], shares[n], [(down_state, 4 * k)], down_half // 4)
        for k, n in enumerate("Dd")
    )
    turns.add_norms("p", down_squares)
    turns.run("pacpibpcep")
    turns.reach_shares("abce")
    gu_squares = sum(
        share_norms(wheres[n], shares[n], [(gu_state, 2 * k)], quarter // 2 * pairs, pairs=True)
        for k, n in enumerate("abce")
    )
    turns.add_norms("n", gu_squares)
    turns.run("nIdnbipn")
    turns.reach_shares("Ii")
    io_squares = share_norms(wheres["i"], shares["i"], [(in_state, 4), (out_state, 0)], part_rows)
    in_squares = share_norms(wheres["I"], shares["I"], [(in_state, 0)], part_rows)
    turns.add_norms("m", io_squares + jnp.pad(in_squares, (0, 2)))
    turns.run("mednIenimIimmm")
    turns.finish()
    sums, seen = turns.done, turns.seen

    back = tie(g_long[::-1, block_rows : block_rows + 2], seen["i"][4])
    back = from_behind(back, ("dp", "col"), -1)
    g_n1 = g_long[:, :block_rows].at[:, -2:].add(back)
    tok, scale = tok[:, :block_rows], scale[:, :block_rows]
    weighted = g_n1 * gains[0]
    inner = jnp.sum(weighted * tok, axis=(0, 2))[None, :, None]
    tok_half = (g_res + (scale * weighted - tok * (scale * scale * scale * inner / D))).astype(low)
    token_grad = jnp.where(home, tok_half[0], home_to_away(tok_half[1]))
    act = tie(act, seen["D"][1])
    ffn = jnp.stack([mul(act, downs[h]) for h in range(2)])
    out_half = (res + (ffn + sibling_to_home(ffn.astype(low)).astype(wide))).astype(low)
    output = jnp.where(home, out_half[0], home_to_away(out_half[1]))

    def gu_back(values):
        return from_linear(values, feat_cols, 2)

    def ratio_of(norms):
        norms = jnp.sqrt(norms)
        return norms, (learn_rate * (norms[0] / (norms[1] + adam_eps))).reshape(1)

    (gu_norms, gu_ratio), (down_norms, down_ratio) = [ratio_of(sums[name]) for name in "np"]
    (in_norms, in_ratio), (out_norms, out_ratio) = [ratio_of(sums["m"][k : k + 2]) for k in (0, 2)]

    def later_half(count):
        return functools.partial(lamb_plain, lambda i: (i >= count // 2).astype(jnp.int32))

    def fixed_half(half):
        return functools.partial(lamb_plain, lambda i: half)

    last = sums["i"]
    small = [part[part_rows : part_rows + 5] for part in last]
    small = jnp.where((wheres["i"][0] >> 1) == 0, small[0], small[1]).astype(wide)
    conv_grad, gains_grad = small[:3], small[3:]
    conv_m, conv_v, conv_u = lamb_moments(conv_weight, conv_grad, conv_first, conv_second, 0.0)
    gain_m, gain_v, gain_u = lamb_moments(norm_gains, gains_grad, gain_first, gain_second, 0.0)
    col_first = (col_pos == 0).astype(wide)
    row_first = (row_pos == 0).astype(wide)
    small_norms = jnp.stack(
        [
            square_pair(conv_weight, conv_u) * col_first,
            square_pair(norm_gains[0], gain_u[0]) * row_first,
            square_pair(norm_gains[1], gain_u[1]) * row_first,
        ]
    )
    down_sums = [sums[name] for name in "Dd"]
    pair_sums = [sums[name] for name in "abce"]
    row_norms = small_norms + swap(small_norms, "row")
    pair_sums[1] = [tie(part, small_norms) for part in pair_sums[1]]
    pair_sums[3] = [tie(part, row_norms) for part in pair_sums[3]]
    down_sums[1] = [tie(part, row_norms) for part in down_sums[1]]
    down_new = None
    for k in (0, 1):
        name = "Dd"[k]
        block = down_half // 6
        down_new = lamb_call(
            later_half(6), wheres[name], down_ratio, down_sums[k], block, lambda i: i % 3,
            down_state, block, 6 * k, 6, down_new, [],
        )
    gu_new = None
    gu_rows = 32
    for k in (0, 2, 1, 3):
        name = "abce"[k]
        blocks = quarter // gu_rows
        gu_new = lamb_call(
            lamb_pairs, wheres[name], gu_ratio, pair_sums[k], gu_rows, lambda i: i,
            gu_state, gu_rows * pairs, k * blocks, blocks, gu_new,
            [pltpu.VMEM((gu_rows * pairs, 128), wide)],
        )
    small_norms = jnp.sqrt(row_norms + swap(row_norms, "col"))
    last = [tie(part, small_norms) for part in last]
    first_io = [tie(part, small_norms) for part in sums["I"]]
    in_new = lamb_call(
        later_half(4), wheres["I"], in_ratio, first_io, part_rows, lambda i: i % 2,
        in_state, part_rows, 0, 4, None, [],
    )
    in_new = lamb_call(
        fixed_half(0), wheres["i"], in_ratio, last, part_rows + 16, lambda i: i,
        in_state, part_rows, 4, 2, in_new, [],
    )
    out_new = lamb_call(
        fixed_half(1), wheres["i"], out_ratio, last, part_rows + 16, lambda i: i,
        out_state, part_rows, 0, 2, None, [],
    )

    trust_norms = jnp.stack(
        [
            in_norms,
            small_norms[0],
            out_norms,
            small_norms[1],
            small_norms[2],
            gu_norms,
            down_norms,
        ]
    )
    gains_new = jnp.stack(
        [
            apply_trust(norm_gains[0], gain_u[0], small_norms[1]),
            apply_trust(norm_gains[1], gain_u[1], small_norms[2]),
        ]
    )
    return (
        output,
        token_grad,
        *[in_back(values) for values in in_new],
        apply_trust(conv_weight, conv_u, small_norms[0]),
        conv_m,
        conv_v,
        *out_new,
        gains_new,
        gain_m,
        gain_v,
        *[gu_back(values) for values in gu_new],
        *down_new,
        trust_norms,
    )


def solution(mesh):
    in_specs = (
        P(("dp", "row"), "col"),
        P(("dp", "row"), "col"),
        P("col", None, "row"),
        P(None, "row"),
        P("row", "col"),
        P(None, "col"),
        P("col", None, "row"),
        P("row", "col"),
        P("col", None, "row"),
        P("col", None, "row"),
        P(None, "row"),
        P(None, "row"),
        P("row", "col"),
        P("row", "col"),
        P(None, "col"),
        P(None, "col"),
        P("col", None, "row"),
        P("col", None, "row"),
        P("row", "col"),
        P("row", "col"),
    )
    out_specs = (
        P(("dp", "row"), "col"),
        P(("dp", "row"), "col"),
        P("col", None, "row"),
        P("col", None, "row"),
        P("col", None, "row"),
        P(None, "row"),
        P(None, "row"),
        P(None, "row"),
        P("row", "col"),
        P("row", "col"),
        P("row", "col"),
        P(None, "col"),
        P(None, "col"),
        P(None, "col"),
        P("col", None, "row"),
        P("col", None, "row"),
        P("col", None, "row"),
        P("row", "col"),
        P("row", "col"),
        P("row", "col"),
        P(),
    )
    return jax.shard_map(shards, mesh=mesh, in_specs=in_specs, out_specs=out_specs, check_vma=False)
```

```python
import functools

import jax
import jax.numpy as jnp
from jax import lax
from jax.experimental import pallas as pl
from jax.experimental.layout import Layout, with_layout_constraint
from jax.experimental.pallas import tpu as pltpu
from jax.sharding import PartitionSpec as P

D = 1024
SEQ_LEAST = 4096
STEP = 5
MIB = 1024 * 1024


norm_eps = 1e-05
adam_eps = 1e-06
beta_one = 0.5
beta_two = 0.6
learn_rate = 0.5
decay_rate = 0.01
low = jnp.bfloat16
wide = jnp.float32


def from_behind(block, axis, distance):
    devices = range(lax.axis_size(axis))
    route = [(i - distance, i) for i in devices if i - distance in devices]
    return lax.ppermute(block, axis, route)


def swap(values, axis):
    return lax.ppermute(values, axis, [(0, 1), (1, 0)])


def swap_halves(halves):
    return [swap(half, "row") for half in halves]


def to_home(values):
    return lax.ppermute(values, ("row", "col"), [(1, 0), (2, 3)])


def home_to_sibling(values):
    return lax.ppermute(values, ("row", "col"), [(0, 2), (3, 1)])


def home_to_away(values):
    return lax.ppermute(values, ("row", "col"), [(0, 1), (3, 2)])


def sibling_to_home(values):
    return lax.ppermute(values, ("row", "col"), [(2, 0), (1, 3)])


def contract(left, right, left_dim, right_dim):
    return lax.dot_general(
        left, right, (((left_dim,), (right_dim,)), ((), ())), preferred_element_type=wide
    )


def mul(left, right):
    return contract(left, right, 1, 0)


def mul_t(left, right):
    return contract(left, right, 1, 1)


def t_mul(left, right):
    return contract(left, right, 0, 0)


def lamb_moments(weight, grad, first, second, decay):
    first_new = beta_one * first + (1.0 - beta_one) * grad
    second_new = beta_two * second + (1.0 - beta_two) * grad * grad
    direction = (first_new * (1.0 / (1.0 - beta_one**STEP))) / (
        jnp.sqrt(second_new * (1.0 / (1.0 - beta_two**STEP))) + adam_eps
    ) + decay * weight
    return (first_new, second_new, direction)


def square_pair(weight, direction):
    return jnp.stack([jnp.sum(weight * weight), jnp.sum(direction * direction)])


def kernel_call(kernel, grid, in_specs, out_specs, out_shape, scratch, args, aliases=None, mib=1):
    return pl.pallas_call(
        kernel,
        grid_spec=pltpu.PrefetchScalarGridSpec(
            num_scalar_prefetch=1,
            grid=grid,
            in_specs=in_specs,
            out_specs=out_specs,
            scratch_shapes=scratch,
        ),
        out_shape=out_shape,
        input_output_aliases=aliases or {},
        compiler_params=pltpu.CompilerParams(vmem_limit_bytes=48 * MIB),
        cost_estimate=pl.CostEstimate(flops=0, bytes_accessed=mib * MIB, transcendentals=0),
    )(*args)


SCALARS = pl.BlockSpec(memory_space=pltpu.SMEM)


def norm_kernel(where, grad, *refs):
    sums = refs[-1]
    groups = [refs[:3], refs[3:6]][: len(refs) // 3]
    rows = groups[0][0].shape[0]
    zero = jnp.zeros((8, groups[0][0].shape[1]), wide)
    for k, (p, m, v) in enumerate(groups):

        def body(at, total):
            here = pl.ds(pl.multiple_of(at * 32, 32), 32)
            weight = p[here, :]
            direction = lamb_moments(
                weight, grad[here, :].astype(wide), m[here, :], v[here, :], decay_rate
            )[2]
            return tuple(
                t + (sq[:8] + sq[8:16]) + (sq[16:24] + sq[24:])
                for t, sq in zip(total, (weight * weight, direction * direction))
            )

        total = lax.fori_loop(0, rows // 32, body, (zero, zero))
        mine = 1.0 if len(groups) == 1 else ((where[0] >> 1) == k).astype(wide)
        for j in range(2):
            sums[2 * k + j] = jnp.sum(total[j]) * mine


def norm_pairs_kernel(where, grad, p, m, v, sums):
    rows, cols = grad.shape
    tiles = cols // 128
    side = where[0] >> 1
    zero = jnp.zeros((8, 128), wide)
    total = [zero, zero]
    for tile in range(tiles):
        here = pl.ds(2 * tile + side, rows, stride=2 * tiles)
        weight = p[here, :]
        direction = lamb_moments(
            weight, grad[:, tile * 128 : (tile + 1) * 128].astype(wide), m[here, :], v[here, :], decay_rate
        )[2]
        for j, sq in enumerate((weight * weight, direction * direction)):
            total[j] = total[j] + jnp.sum((sq).reshape(rows // 8, 8, 128), axis=0)
    for j in range(2):
        sums[j] = jnp.sum(total[j])


def share_norms(where, grad, states, rows, pairs=False):
    specs, args = [], []
    for state, at in states:
        for array in state:
            if pairs:
                spec = pl.BlockSpec(
                    (rows, array.shape[1]), lambda i, w, at=at: (at + (w[0] & 1), 0)
                )
            elif len(states) == 2:
                spec = pl.BlockSpec(
                    (rows, array.shape[1]), lambda i, w, at=at: (at + (w[0] & 1), 0)
                )
            else:
                spec = pl.BlockSpec((rows, array.shape[1]), lambda i, w, at=at: (at + w[0], 0))
            specs.append(spec)
            args.append(array)
    return kernel_call(
        norm_pairs_kernel if pairs else norm_kernel,
        (1,),
        [whole_spec(grad.shape)] + specs,
        SCALARS,
        jax.ShapeDtypeStruct((2 * len(states),), wide),
        [],
        (where, grad, *args),
    )


def lamb_loop(refs, outs, ratio, rows, step, pick):
    p, m, v = refs

    def body(at, carry):
        here = pl.ds(pl.multiple_of(at * step, step), step)
        weight = p[here, :]
        first_new, second_new, direction = lamb_moments(
            weight, pick(here), m[here, :], v[here, :], decay_rate
        )
        outs[0][here, :] = weight - ratio * direction
        outs[1][here, :] = first_new
        outs[2][here, :] = second_new
        return carry

    lax.fori_loop(0, rows // step, body, 0)


def lamb_plain(half_of_block, where, ratio, part, got, p, m, v, *outs):
    use = half_of_block(pl.program_id(0)) == (where[0] >> 1)

    def pick(here):
        return jnp.where(use, part[here, :].astype(wide), got[here, :].astype(wide))

    lamb_loop((p, m, v), outs, ratio[0], p.shape[0], 64, pick)


def lamb_pairs(where, ratio, part, got, p, m, v, p_out, m_out, v_out, mixed):
    rows, cols = part.shape
    tiles = cols // 128
    for value, order in ((0, (part, got)), (1, (got, part))):

        @pl.when((where[0] >> 1) == value)
        def _():
            for tile in range(tiles):
                for side, ref in enumerate(order):
                    mixed[pl.ds(2 * tile + side, rows, stride=2 * tiles), :] = ref[
                        :, tile * 128 : (tile + 1) * 128
                    ].astype(wide)

    lamb_loop(
        (p, m, v), (p_out, m_out, v_out), ratio[0], p.shape[0], 192, lambda here: mixed[here, :]
    )


def lamb_call(kernel, where, ratio, grad, grad_block, grad_at, state, block, start, count, before, scratch):
    rows, cols = state[0].shape
    flat = pl.BlockSpec((block, cols), lambda i, w: (i + start, 0))
    grad_spec = pl.BlockSpec((grad_block, grad[0].shape[1]), lambda i, w: (grad_at(i), 0))
    whole = jax.ShapeDtypeStruct((rows, cols), wide)
    args = [where, ratio, *grad, *state]
    specs = [SCALARS, grad_spec, grad_spec, flat, flat, flat]
    run, aliases = kernel, {}
    if before is not None:
        aliases = {len(args) + k: k for k in range(3)}

        def run(*refs):
            kernel(*refs[: len(args)], *refs[len(args) + 3 :])

    return list(
        kernel_call(
            run,
            (count,),
            specs + [pl.BlockSpec(memory_space=pl.ANY)] * len(aliases),
            [flat, flat, flat],
            [whole, whole, whole],
            scratch,
            (*args, *(before or [])),
            aliases,
            mib=26 * count * block * cols // MIB,
        )
    )


def to_linear(values):
    rows, sides, cols = values.shape
    split = with_layout_constraint(
        values.reshape(rows, sides, cols // 128, 128), Layout(major_to_minor=(0, 2, 1, 3))
    )
    return split.transpose(0, 2, 1, 3).reshape(rows * sides * cols // 128, 128)


def from_linear(values, rows, sides):
    cols = values.size // (rows * sides)
    split = values.reshape(rows, cols // 128, sides, 128).transpose(0, 2, 1, 3)
    split = with_layout_constraint(split, Layout(major_to_minor=(0, 2, 1, 3)))
    return split.reshape(rows, sides, cols)


def apply_trust(weight, direction, norms):
    return weight - learn_rate * (norms[0] / (norms[1] + adam_eps)) * direction


def flip(values, bit):
    size = lax.axis_size("dp")
    return lax.ppermute(values, "dp", [(i, i ^ (1 << bit)) for i in range(size)])


def dp_bit(bit):
    return (lax.axis_index("dp") >> bit) & 1


def rows_of(values, start, rows):
    return lax.dynamic_slice_in_dim(values, start, rows, 0)


def total_of(pieces):
    total = pieces[0].astype(wide)
    for piece in pieces[1:]:
        total = total + piece.astype(wide)
    return total


def tie(values, *deps):
    return lax.optimization_barrier((values, *deps))[0]


def low_total(pieces):
    return total_of(pieces).astype(low)


def keep_or_join(bit, part, other):
    return jnp.where(
        dp_bit(bit) == 0,
        jnp.concatenate([part, other]),
        jnp.concatenate([other, part]),
    )


def share_of(weight, order):
    rows = weight.shape[0] // (1 << len(order))
    index = 0
    for bit in order:
        index = 2 * index + dp_bit(bit)
    return rows_of(weight, index * rows, rows)


def half_of(piece, place):
    rows = piece.shape[-2] // 2
    return lax.dynamic_slice_in_dim(piece, place * rows, rows, piece.ndim - 2)


def chunk_sum(chunk, order, keep):
    bits = {"y": 0, "l": 1}
    steps = [name if name == "x" else bits[name] for name in order]
    pieces = [chunk]
    for step in steps:
        if step == "x":
            whole = len(pieces) == 1
            got = yield step, pieces[0][1] if whole else low_total([piece[1] for piece in pieces])
            pieces = [piece[0] for piece in pieces] + [got]
        else:
            here = dp_bit(step)
            got = yield step, low_total([half_of(piece, 1 - here) for piece in pieces])
            pieces = [half_of(piece, here) for piece in pieces] + [got]
    part = low_total(pieces)
    for step in range((lax.axis_size("dp") - 1).bit_length()):
        if step not in steps:
            got = yield step, part
            part = low_total([part, got])
    keep(part)
    first, second = [step for step in steps if step != "x"]
    got = yield second, part
    part = keep_or_join(second, part, got)
    got = yield first, part
    return part, got


def norm_sum(values):
    for step in ("x", "row", 1, 0):
        got = yield step, values
        values = values + got
    return values


def where_of(order):
    bits = {"y": 0, "l": 1}
    first, second = [bits[name] for name in order if name != "x"]
    return (2 * dp_bit(first) + dp_bit(second)).astype(jnp.int32).reshape(1)


def move(step, send):
    if step == "row":
        return swap(send, "row")
    return swap(send, "col") if step == "x" else flip(send, step)


class Turns:
    def __init__(self):
        self.chunks = {}
        self.arrivals = {}
        self.seen = {}
        self.done = {}
        self.shares = {}
        self.after = ()

    def add(self, name, chunk, order):
        self.chunks[name] = chunk_sum(chunk, order, functools.partial(self.shares.__setitem__, name))

    def add_norms(self, name, values):
        self.chunks[name] = norm_sum(values)

    def turn(self, name):
        got = self.arrivals.get(name)
        try:
            if got is None:
                self.seen[name] = []
                step, send = next(self.chunks[name])
                send = tie(send, *self.after)
            else:
                got = tie(got, *self.after)
                self.seen[name].append(got)
                step, send = self.chunks[name].send(got)
        except StopIteration as end:
            self.done[name] = end.value
            return
        self.arrivals[name] = move(step, send)
        self.after = (send,)

    def run(self, names):
        for name in names:
            if name not in self.done:
                self.turn(name)

    def reach_shares(self, names):
        while any(name not in self.shares for name in names):
            self.run([name for name in names if name not in self.shares])

    def finish(self):
        while len(self.done) < len(self.chunks):
            self.run(self.chunks)


def deinterleave(pairs, gate, up):
    rows, cols = gate.shape
    tiles = cols // 128
    for tile in range(tiles):
        for side, out in enumerate((gate, up)):
            out[:, tile * 128 : (tile + 1) * 128] = pairs[
                pl.ds(2 * tile + side, rows, stride=2 * tiles), :
            ].astype(low)


def split_pairs(linear, rows, cols):
    block = 64
    half = jax.ShapeDtypeStruct((rows, cols), low)
    out_spec = pl.BlockSpec((block, cols), lambda i: (i, 0))
    return pl.pallas_call(
        deinterleave,
        grid=(rows // block,),
        in_specs=[pl.BlockSpec((block * 2 * cols // 128, 128), lambda i: (i, 0))],
        out_specs=[out_spec, out_spec],
        out_shape=[half, half],
        compiler_params=pltpu.CompilerParams(vmem_limit_bytes=24 * MIB),
        cost_estimate=pl.CostEstimate(
            flops=rows * cols, bytes_accessed=12 * rows * cols, transcendentals=0
        ),
    )(linear)


def dot_of(left, right, left_dim, right_dim):
    return lax.dot_general(
        left, right, (((left_dim,), (right_dim,)), ((), ())), preferred_element_type=wide
    )


def local_call(kernel, grid, in_specs, out_specs, out_shape, scratch, args, prefetch=0):
    return pl.pallas_call(
        kernel,
        grid_spec=pltpu.PrefetchScalarGridSpec(
            num_scalar_prefetch=prefetch,
            grid=grid,
            in_specs=in_specs,
            out_specs=out_specs,
            scratch_shapes=scratch,
        ),
        out_shape=out_shape,
        compiler_params=pltpu.CompilerParams(vmem_limit_bytes=48 * MIB),
        cost_estimate=pl.CostEstimate(flops=0, bytes_accessed=MIB, transcendentals=0),
    )(*args)


def whole_spec(shape):
    return pl.BlockSpec(shape, lambda *_: (0,) * len(shape))


def shape_of(dims, kind):
    return jax.ShapeDtypeStruct(dims, kind)


def row_scale(halves):
    total = sum(jnp.sum(half * half, axis=1, keepdims=True) for half in halves)
    return lax.rsqrt(total / D + norm_eps)


def branch_kernel(tok, gains, taps, own, other, n1, gate_b, gate_c, gate_x, conv, hidden, part0, part1, ext):
    long, width = n1.shape[1:]
    rows = conv.shape[0]
    step = long // 3

    def gates(at, carry):
        here = pl.ds(pl.multiple_of(at * step, step), step)
        halves = [tok[h, here, :].astype(wide) for h in range(2)]
        scale = row_scale(halves)
        for h in range(2):
            n1[h, here, :] = (halves[h] * scale * gains[h]).astype(low)
        for g, out in enumerate((gate_b, gate_c, gate_x)):
            w = slice(g * width, (g + 1) * width)
            out[here, :] = dot_of(n1[0, here, :], own[w, :], 1, 0) + dot_of(
                n1[1, here, :], other[w, :], 1, 0
            )
        return carry

    lax.fori_loop(0, 3, gates, 0)
    ext[8 : 8 + rows, :] = gate_b[:rows, :] * gate_x[:rows, :]
    ext[6:8, :] = gate_b[rows : rows + 2, :] * gate_x[rows : rows + 2, :]
    w_out = slice(3 * width, 4 * width)
    quarter = rows // 4
    for at in range(4):
        start = at * quarter
        taken = slice(start, start + quarter)
        value = sum(taps[k] * ext[start + 6 + k : start + 6 + k + quarter, :] for k in range(3))
        conv[taken, :] = value
        low_hidden = (gate_c[taken, :] * value).astype(low)
        hidden[taken, :] = low_hidden
        for part, weight in ((part0, own), (part1, other)):
            part[taken, :] = dot_of(low_hidden, weight[w_out, :], 1, 0).astype(low)


def branch_forward(tok, rows, tails, gains, taps, own, other):
    width = tok.shape[2]
    gate = shape_of((rows + tails, width), wide)
    outs = [
        shape_of((2, rows + tails, width), low),
        gate,
        gate,
        gate,
        shape_of((rows, width), wide),
        shape_of((rows, width), low),
        shape_of((rows, width), low),
        shape_of((rows, width), low),
    ]
    args = (tok, gains, taps, own, other)
    return local_call(
        branch_kernel,
        (1,),
        [whole_spec(a.shape) for a in args],
        [whole_spec(o.shape) for o in outs],
        outs,
        [pltpu.VMEM((rows + 8, width), wide)],
        args,
    )


def piece_at(bits, which, piece, width):
    place = bits[which] if piece == 0 else 1 - bits[which]
    return pl.ds(pl.multiple_of(place * width, width), width)


def ffn_kernel(bits, tok, mine0, mine1, theirs0, theirs1, gains, g0, g1, g2, u0, u1, u2, n2, res, gate, up, act):
    width = g1.shape[0]

    @pl.when(pl.program_id(0) == 0)
    def _():
        for h, (mine, theirs) in enumerate(((mine0, theirs0), (mine1, theirs1))):
            res[h] = tok[h, : res.shape[1], :].astype(wide) + (
                mine[...].astype(wide) + theirs[...].astype(wide)
            )
        scale = row_scale([res[0], res[1]])
        for h in range(2):
            n2[h] = (res[h] * scale * gains[h]).astype(low)

    for which, (out, w0, w1, w2) in enumerate(((gate, g0, g1, g2), (up, u0, u1, u2))):
        total = dot_of(n2[0], w0[...], 1, 0)
        for piece, w in enumerate((w1, w2)):
            total += dot_of(n2[1, :, piece_at(bits, which, piece, width)], w[...], 1, 0)
        out[...] = total
    value = gate[...]
    act[...] = (value * jax.nn.sigmoid(value) * up[...]).astype(low)


def ffn_forward(bits, tok, mine, theirs, gains, weights):
    rows, width = mine[0].shape
    cols = weights[0].shape[1]
    tile = cols // 3
    both = (2, rows, width)
    full = whole_spec(both)
    wide_tile = pl.BlockSpec((rows, tile), lambda i, *_: (0, i))
    weight_specs = [pl.BlockSpec((w.shape[0], tile), lambda i, *_: (0, i)) for w in weights]
    return local_call(
        ffn_kernel,
        (3,),
        [whole_spec(tok.shape)]
        + [whole_spec((rows, width))] * 4
        + [whole_spec(gains.shape)]
        + weight_specs,
        [full, full, wide_tile, wide_tile, wide_tile],
        [
            shape_of(both, low),
            shape_of(both, wide),
            shape_of((rows, cols), wide),
            shape_of((rows, cols), wide),
            shape_of((rows, cols), low),
        ],
        [],
        (bits, tok, *mine, *theirs, gains, *weights),
        prefetch=1,
    )


def ffn_back_kernel(
    bits, cot, d_own, d_other, gate, up, g0, g1, g2, u0, u1, u2, g_gate, g_up, part0, part1, total
):
    width = g1.shape[0]

    @pl.when(pl.program_id(0) == 0)
    def _():
        total[...] = jnp.zeros_like(total)

    start = cot.shape[1] - gate.shape[0]
    g_act = dot_of(cot[0, start:, :], d_own[...], 1, 1) + dot_of(cot[1, start:, :], d_other[...], 1, 1)
    value = gate[...]
    sigma = jax.nn.sigmoid(value)
    g_gate[...] = (g_act * up[...] * sigma * (1.0 + value * (1.0 - sigma))).astype(low)
    g_up[...] = (g_act * (value * sigma)).astype(low)
    total[0] += dot_of(g_gate[...], g0[...], 1, 1) + dot_of(g_up[...], u0[...], 1, 1)
    for which, (grad, w1, w2) in enumerate(((g_gate, g1, g2), (g_up, u1, u2))):
        for piece, w in enumerate((w1, w2)):
            total[1, :, piece_at(bits, which, piece, width)] += dot_of(grad[...], w[...], 1, 1)

    @pl.when(pl.program_id(0) == pl.num_programs(0) - 1)
    def _():
        part0[...] = total[0].astype(low)
        part1[...] = total[1].astype(low)


def ffn_backward(bits, cot, downs, gate, up, weights):
    rows, cols = gate.shape
    tile = cols // 3
    part = (rows, cot.shape[2])
    wide_tile = pl.BlockSpec((rows, tile), lambda i, *_: (0, i))
    weight_specs = [pl.BlockSpec((w.shape[0], tile), lambda i, *_: (0, i)) for w in weights]
    down_spec = pl.BlockSpec((tile, downs[0].shape[1]), lambda i, *_: (i, 0))
    return local_call(
        ffn_back_kernel,
        (3,),
        [whole_spec(cot.shape), down_spec, down_spec, wide_tile, wide_tile] + weight_specs,
        [wide_tile, wide_tile, whole_spec(part), whole_spec(part)],
        [shape_of((rows, cols), low)] * 2 + [shape_of(part, low)] * 2,
        [pltpu.VMEM((2, *part), wide)],
        (bits, cot, *downs, gate, up, *weights),
        prefetch=1,
    )


def put(outs, half, rows, value):
    if len(outs) == 2:
        outs[half][rows, :] = value.astype(low)
    else:
        outs[0][half, rows, :] = value.astype(low)


def chunk_outs(split, rows, cols):
    if split:
        return [whole_spec((rows, cols))] * 2, [shape_of((rows, cols), low)] * 2
    return [whole_spec((2, rows, cols))], [shape_of((2, rows, cols), low)]


def pair_grad_kernel(items, n2, g_gate, g_up, *outs):
    rows = outs[0].shape[-2] // 2
    for at, split in items:
        count = 2 if split else 1
        mine, outs = outs[:count], outs[count:]
        for h in range(2):
            left = n2[h, :, at * rows : (at + 1) * rows]
            for side, grad in enumerate((g_gate, g_up)):
                put(mine, h, slice(side * rows, (side + 1) * rows), dot_of(left, grad[...], 0, 0))


def pair_grads(n2, g_gate, g_up, items, rows):
    specs, shapes = [], []
    for _, split in items:
        more = chunk_outs(split, 2 * rows, g_gate.shape[1])
        specs += more[0]
        shapes += more[1]
    outs = local_call(
        functools.partial(pair_grad_kernel, items),
        (1,),
        [whole_spec(n2.shape), whole_spec(g_gate.shape), whole_spec(g_up.shape)],
        specs,
        shapes,
        [],
        (n2, g_gate, g_up),
    )
    found = []
    for _, split in items:
        count = 2 if split else 1
        found.append(tuple(outs[:count]) if split else outs[0])
        outs = outs[count:]
    return found


def down_grad_kernel(act, cot, *outs):
    start = cot.shape[1] - act.shape[0]
    for h in range(2):
        put(outs, h, slice(None), dot_of(act[...], cot[h, start:, :], 0, 0))


def down_grads(act, cot, at, rows, split):
    specs, shapes = chunk_outs(split, rows, cot.shape[2])
    outs = local_call(
        down_grad_kernel,
        (1,),
        [pl.BlockSpec((act.shape[0], rows), lambda i: (0, at)), whole_spec(cot.shape)],
        specs,
        shapes,
        [],
        (act, cot),
    )
    return tuple(outs) if split else outs[0]


def branch_back_kernel(
    mine0, mine1, theirs0, theirs1, res, cot, gains, taps, own, other, gate_b, gate_c, gate_x, conv,
    g_res, g_low, g_proj, gain_grad, tap_grad, ext, ext_grad,
):
    _, rows, width = res.shape
    scale = row_scale([res[0], res[1]])
    grads = [
        mine[...].astype(wide) + theirs[...].astype(wide)
        for mine, theirs in ((mine0, theirs0), (mine1, theirs1))
    ]
    inner = sum(
        jnp.sum(grads[h] * gains[h] * res[h], axis=1, keepdims=True) for h in range(2)
    )
    factor = scale * scale * scale * inner / D
    for h in range(2):
        gain_grad[h] = jnp.sum(grads[h] * res[h] * scale, axis=0, keepdims=True)
        value = cot[h, cot.shape[1] - rows :, :].astype(wide) + (scale * (grads[h] * gains[h]) - res[h] * factor)
        g_res[h] = value
        g_low[h] = value.astype(low)
    g_hidden = dot_of(g_low[0], own[...], 1, 1) + dot_of(g_low[1], other[...], 1, 1)
    g_proj[1, :rows, :] = (g_hidden * conv[...]).astype(low)
    g_conv = g_hidden * gate_c[:rows, :]
    ext_grad[:rows, :] = g_conv
    ext_grad[rows:, :] = jnp.zeros((8, width), wide)
    ext[8 : 8 + rows, :] = gate_b[:rows, :] * gate_x[:rows, :]
    ext[6:8, :] = gate_b[rows : rows + 2, :] * gate_x[rows : rows + 2, :]
    for k in range(3):
        tap_grad[k : k + 1, :] = jnp.sum(
            g_conv * ext[6 + k : 6 + k + rows, :], axis=0, keepdims=True
        )
    g_mixed = sum(taps[2 - k] * ext_grad[k : k + rows, :] for k in range(3))
    g_proj[0, :rows, :] = (g_mixed * gate_x[:rows, :]).astype(low)
    g_proj[2, :rows, :] = (g_mixed * gate_b[:rows, :]).astype(low)
    tails = g_proj.shape[1] - rows
    row = lax.broadcasted_iota(jnp.int32, (tails, width), 0)
    first, second = ext_grad[0:1, :], ext_grad[1:2, :]
    g_before = jnp.where(
        row == 0,
        taps[0] * first,
        jnp.where(row == 1, taps[1] * first + taps[0] * second, 0.0),
    )
    g_proj[0, rows:, :] = (g_before * gate_x[rows:, :]).astype(low)
    g_proj[1, rows:, :] = jnp.zeros((tails, width), low)
    g_proj[2, rows:, :] = (g_before * gate_b[rows:, :]).astype(low)


def branch_backward(mine, theirs, res, cot, gains, taps, own, other, gates, conv):
    _, rows, width = res.shape
    long = gates[0].shape[0]
    out_weight = pl.BlockSpec((width, width), lambda i, *_: (3, 0))
    outs = [
        shape_of(res.shape, wide),
        shape_of(res.shape, low),
        shape_of((3, long, width), low),
        shape_of((2, 1, width), wide),
        shape_of((3, width), wide),
    ]
    full = whole_spec(res.shape)
    return local_call(
        branch_back_kernel,
        (1,),
        [whole_spec((rows, width))] * 4
        + [full, whole_spec(cot.shape), whole_spec(gains.shape), whole_spec(taps.shape)]
        + [out_weight, out_weight]
        + [whole_spec(g.shape) for g in gates]
        + [whole_spec(conv.shape)],
        [whole_spec(o.shape) for o in outs],
        outs,
        [pltpu.VMEM((rows + 8, width), wide), pltpu.VMEM((rows + 8, width), wide)],
        (*mine, *theirs, res, cot, gains, taps, own, other, *gates, conv),
    )


def branch_grad_kernel(left0, left1, right0, right1, own, other):
    rows = own.shape[0] // 2
    for h, out in enumerate((own, other)):
        for k, (left, right) in enumerate(((left0, right0), (left1, right1))):
            one = left[h] if len(left.shape) == 3 else left[...]
            two = right[h] if k == 1 and len(left.shape) == 2 else right[0]
            out[k * rows : (k + 1) * rows, :] = dot_of(one, two, 0, 0).astype(low)


def branch_grads(n1, g_proj, gate, second):
    width = n1.shape[2]
    gate_spec = pl.BlockSpec((1, *g_proj.shape[1:]), lambda i: (gate, 0, 0))
    if second is None:
        left, right = n1, g_proj
        right_spec = pl.BlockSpec((1, *g_proj.shape[1:]), lambda i: (gate + 1, 0, 0))
    else:
        left, right = second
        right_spec = whole_spec(right.shape)
    specs, shapes = chunk_outs(True, 2 * width, width)
    return local_call(
        branch_grad_kernel,
        (1,),
        [whole_spec(n1.shape), whole_spec(left.shape), gate_spec, right_spec],
        specs,
        shapes,
        [],
        (n1, left, g_proj, right),
    )


def shards(
    tokens,
    cotangent,
    input_projection_weight,
    conv_weight,
    output_projection_weight,
    norm_gains,
    gate_up_weight,
    down_projection_weight,
    in_first,
    in_second,
    conv_first,
    conv_second,
    out_first,
    out_second,
    gain_first,
    gain_second,
    gu_first,
    gu_second,
    down_first,
    down_second,
):
    feat_cols = tokens.shape[1]
    branch_cols = conv_weight.shape[1]
    hidden_cols = down_projection_weight.shape[0]
    block_rows = tokens.shape[0]
    seq_len = max(SEQ_LEAST, block_rows * lax.axis_size("dp") * lax.axis_size("col"))
    data_pos = lax.axis_index("dp")
    row_pos = lax.axis_index("row")
    col_pos = lax.axis_index("col")
    home = row_pos == col_pos
    tail_rows = 16

    in_low = jnp.transpose(input_projection_weight, (1, 0, 2)).astype(low).reshape(-1, branch_cols)
    io_low = jnp.concatenate([in_low, output_projection_weight.astype(low)])
    io_share = share_of(io_low, (1, 0))
    io_got = swap(io_share, "col")
    row_start = (data_pos * lax.axis_size("row") + row_pos) * block_rows
    tail = from_behind(tokens[-2:], ("dp", "row"), 1)
    tail = jnp.where(row_start % seq_len != 0, tail, jnp.zeros_like(tail))
    spare = jnp.zeros((tail_rows - 8, feat_cols), low)
    gain_parts = []
    left = norm_gains
    for _ in range(3):
        gain_parts.append(lax.reduce_precision(left, 8, 7))
        left = left - gain_parts[-1]
    gain_parts = jnp.concatenate(gain_parts).astype(low)
    extra = tie(jnp.concatenate([tail, gain_parts, spare]))
    block = jnp.concatenate([tie(tokens, io_got), extra, cotangent])
    away = to_home(block)
    gu_weight = to_linear(gate_up_weight)
    gate_low, up_low = split_pairs(gu_weight, feat_cols, hidden_cols)
    down_low = down_projection_weight.astype(low)
    both = jnp.stack([block, away])
    both = jnp.where(home, both, home_to_sibling(both))
    gains = both[:, block_rows + 2 : block_rows + 8].astype(wide)
    gains = gains[:, 0:2] + gains[:, 2:4] + gains[:, 4:6]
    gains = [gains[:, k : k + 1] for k in range(2)]
    gate_got = swap(tie(share_of(gate_low, (1, 0)), io_got), "col")
    up_got = swap(tie(share_of(up_low, (0, 1)), gate_got), "col")
    down_got = swap(tie(down_low, up_got), "col")
    io_pair = keep_or_join(0, io_got, flip(io_got, 0))
    io_other = keep_or_join(1, io_pair, flip(io_pair, 1))
    gate_pair = keep_or_join(0, gate_got, flip(tie(gate_got, io_pair), 0))
    up_pair = keep_or_join(1, up_got, flip(tie(up_got, io_pair), 1))
    gate_more = flip(gate_pair, 1)
    up_more = flip(up_pair, 0)
    weights = [gate_low, gate_pair, gate_more, up_low, up_pair, up_more]
    bits = jnp.stack([dp_bit(1), dp_bit(0)]).astype(jnp.int32)
    downs = [down_low, down_got]

    n1, gate_b, gate_c, gate_x, conv, hidden, *branch = branch_forward(
        both, block_rows, tail_rows, gains[0], conv_weight, io_low, io_other
    )
    n2, res, gate, upper, act = ffn_forward(
        bits, both, branch, swap_halves(branch), gains[1], weights
    )

    turns = Turns()
    orders = dict(D="xyl", d="ylx", a="xyl", b="lyx", c="xyl", e="lyx", I="xyl", i="xyl")
    down_half = hidden_cols // 2
    for k, name in enumerate("Dd"):
        split = orders[name][0] == "x"
        turns.add(name, down_grads(act, both, k, down_half, split), orders[name])
    turns.run("Dd")
    g_gate, g_up, *part_two = ffn_backward(
        bits, tie(both, *turns.after), downs, gate, upper, weights
    )
    quarter = feat_cols // 4
    for names in ("ab", "ce"):
        items = [("abce".index(name), orders[name][0] == "x") for name in names]
        for name, chunk in zip(names, pair_grads(n2, g_gate, g_up, items, quarter)):
            turns.add(name, chunk, orders[name])
    turns.run("abcDe")
    g_res, g_branch, g_proj, gain_two_grad, conv_grad = branch_backward(
        part_two,
        swap_halves(part_two),
        tie(res, *turns.after),
        both,
        gains[1],
        conv_weight,
        io_low,
        io_other,
        (gate_b, gate_c, gate_x),
        conv,
    )
    turns.add("I", branch_grads(n1, g_proj, 0, None), orders["I"])
    io_last = branch_grads(n1, g_proj, 2, (hidden, g_branch))
    turns.after += tuple(io_last)
    turns.run("IdabD")

    g_late = tie(g_proj, *turns.after)
    io_half = [half.reshape(4, feat_cols, branch_cols) for half in (io_low, io_other)]
    g_part = jnp.stack(
        [sum(mul_t(g_late[g], io_half[h][g]) for g in range(3)).astype(low) for h in range(2)]
    )
    g_long = g_part.astype(wide) + swap(g_part, "row").astype(wide)
    tok = both[:, : block_rows + 2].astype(wide)
    scale = lax.rsqrt(jnp.sum(tok * tok, axis=(0, 2)) / D + norm_eps)[None, :, None]
    gain_one_grad = jnp.sum(g_long[:, : block_rows + 2] * tok * scale, axis=1)
    small = [
        jnp.concatenate([conv_grad, gain_one_grad[h : h + 1], gain_two_grad[h]]) for h in range(2)
    ]
    spare = jnp.zeros((16, feat_cols), low)
    small = [jnp.pad(part, ((0, 11), (0, 0))).astype(low) for part in small]
    io_long = []
    for h in range(2):
        pieces = jnp.split(io_last[h], 4)
        io_long.append(
            jnp.concatenate(
                [pieces[0], small[h], pieces[1], spare, pieces[2], spare, pieces[3], spare]
            )
        )
    turns.add("i", io_long, orders["i"])
    turns.run("eiacbdDIcaeDciIabDdcieIDabd")

    def in_flat(values):
        return jnp.transpose(values, (1, 0, 2)).reshape(3 * feat_cols, branch_cols)

    def in_back(values):
        return jnp.transpose(values.reshape(3, feat_cols, branch_cols), (1, 0, 2))

    wheres = {name: where_of(orders[name]) for name in orders}
    down_state = (down_projection_weight, down_first, down_second)
    gu_state = (gu_weight, to_linear(gu_first), to_linear(gu_second))
    in_state = (in_flat(input_projection_weight), in_flat(in_first), in_flat(in_second))
    out_state = (output_projection_weight, out_first, out_second)
    pairs = 2 * hidden_cols // 128

    shares = turns.shares
    part_rows = feat_cols // 2
    turns.reach_shares("Dd")
    down_squares = sum(
        share_norms(wheres[n], shares[n], [(down_state, 4 * k)], down_half // 4)
        for k, n in enumerate("Dd")
    )
    turns.add_norms("p", down_squares)
    turns.run("pacpibpcep")
    turns.reach_shares("abce")
    gu_squares = sum(
        share_norms(wheres[n], shares[n], [(gu_state, 2 * k)], quarter // 2 * pairs, pairs=True)
        for k, n in enumerate("abce")
    )
    turns.add_norms("n", gu_squares)
    turns.run("nIdnbipn")
    turns.reach_shares("Ii")
    io_squares = share_norms(wheres["i"], shares["i"], [(in_state, 4), (out_state, 0)], part_rows)
    in_squares = share_norms(wheres["I"], shares["I"], [(in_state, 0)], part_rows)
    turns.add_norms("m", io_squares + jnp.pad(in_squares, (0, 2)))
    turns.run("mednIenimIimmm")
    turns.finish()
    sums, seen = turns.done, turns.seen

    back = tie(g_long[::-1, block_rows : block_rows + 2], seen["i"][4])
    back = from_behind(back, ("dp", "col"), -1)
    g_n1 = g_long[:, :block_rows].at[:, -2:].add(back)
    tok, scale = tok[:, :block_rows], scale[:, :block_rows]
    weighted = g_n1 * gains[0]
    inner = jnp.sum(weighted * tok, axis=(0, 2))[None, :, None]
    tok_half = (g_res + (scale * weighted - tok * (scale * scale * scale * inner / D))).astype(low)
    token_grad = jnp.where(home, tok_half[0], home_to_away(tok_half[1]))
    act = tie(act, seen["D"][1])
    ffn = jnp.stack([mul(act, downs[h]) for h in range(2)])
    out_half = (res + (ffn + sibling_to_home(ffn.astype(low)).astype(wide))).astype(low)
    output = jnp.where(home, out_half[0], home_to_away(out_half[1]))

    def gu_back(values):
        return from_linear(values, feat_cols, 2)

    def ratio_of(norms):
        norms = jnp.sqrt(norms)
        return norms, (learn_rate * (norms[0] / (norms[1] + adam_eps))).reshape(1)

    (gu_norms, gu_ratio), (down_norms, down_ratio) = [ratio_of(sums[name]) for name in "np"]
    (in_norms, in_ratio), (out_norms, out_ratio) = [ratio_of(sums["m"][k : k + 2]) for k in (0, 2)]

    def later_half(count):
        return functools.partial(lamb_plain, lambda i: (i >= count // 2).astype(jnp.int32))

    def fixed_half(half):
        return functools.partial(lamb_plain, lambda i: half)

    last = sums["i"]
    small = [part[part_rows : part_rows + 5] for part in last]
    small = jnp.where((wheres["i"][0] >> 1) == 0, small[0], small[1]).astype(wide)
    conv_grad, gains_grad = small[:3], small[3:]
    conv_m, conv_v, conv_u = lamb_moments(conv_weight, conv_grad, conv_first, conv_second, 0.0)
    gain_m, gain_v, gain_u = lamb_moments(norm_gains, gains_grad, gain_first, gain_second, 0.0)
    col_first = (col_pos == 0).astype(wide)
    row_first = (row_pos == 0).astype(wide)
    small_weight = jnp.concatenate([conv_weight, norm_gains])
    small_direction = jnp.concatenate([conv_u, gain_u])
    squares = jnp.stack(
        [
            jnp.sum(small_weight * small_weight, axis=1),
            jnp.sum(small_direction * small_direction, axis=1),
        ],
        axis=1,
    )
    small_norms = jnp.concatenate(
        [jnp.sum(squares[:3], axis=0, keepdims=True) * col_first, squares[3:] * row_first]
    )
    down_sums = [sums[name] for name in "Dd"]
    pair_sums = [sums[name] for name in "abce"]
    row_norms = small_norms + swap(small_norms, "row")
    pair_sums[2] = [tie(part, last[1]) for part in pair_sums[2]]
    pair_sums[1] = [tie(part, small_norms) for part in pair_sums[1]]
    pair_sums[3] = [tie(part, row_norms) for part in pair_sums[3]]
    down_sums[1] = [tie(part, row_norms) for part in down_sums[1]]
    down_new = None
    for k in (0, 1):
        name = "Dd"[k]
        block = down_half // 6
        down_new = lamb_call(
            later_half(6), wheres[name], down_ratio, down_sums[k], block, lambda i: i % 3,
            down_state, block, 6 * k, 6, down_new, [],
        )
    gu_new = None
    gu_rows = 32
    for k in (0, 2, 1, 3):
        name = "abce"[k]
        blocks = quarter // gu_rows
        gu_new = lamb_call(
            lamb_pairs, wheres[name], gu_ratio, pair_sums[k], gu_rows, lambda i: i,
            gu_state, gu_rows * pairs, k * blocks, blocks, gu_new,
            [pltpu.VMEM((gu_rows * pairs, 128), wide)],
        )
    small_norms = jnp.sqrt(row_norms + swap(row_norms, "col"))
    last = [tie(part, small_norms) for part in last]
    first_io = [tie(part, small_norms) for part in sums["I"]]
    in_new = lamb_call(
        later_half(4), wheres["I"], in_ratio, first_io, part_rows, lambda i: i % 2,
        in_state, part_rows, 0, 4, None, [],
    )
    in_new = lamb_call(
        fixed_half(0), wheres["i"], in_ratio, last, part_rows + 16, lambda i: i,
        in_state, part_rows, 4, 2, in_new, [],
    )
    out_new = lamb_call(
        fixed_half(1), wheres["i"], out_ratio, last, part_rows + 16, lambda i: i,
        out_state, part_rows, 0, 2, None, [],
    )

    trust_norms = jnp.stack(
        [
            in_norms,
            small_norms[0],
            out_norms,
            small_norms[1],
            small_norms[2],
            gu_norms,
            down_norms,
        ]
    )
    gains_new = jnp.stack(
        [
            apply_trust(norm_gains[0], gain_u[0], small_norms[1]),
            apply_trust(norm_gains[1], gain_u[1], small_norms[2]),
        ]
    )
    return (
        output,
        token_grad,
        *[in_back(values) for values in in_new],
        apply_trust(conv_weight, conv_u, small_norms[0]),
        conv_m,
        conv_v,
        *out_new,
        gains_new,
        gain_m,
        gain_v,
        *[gu_back(values) for values in gu_new],
        *down_new,
        trust_norms,
    )


def solution(mesh):
    in_specs = (
        P(("dp", "row"), "col"),
        P(("dp", "row"), "col"),
        P("col", None, "row"),
        P(None, "row"),
        P("row", "col"),
        P(None, "col"),
        P("col", None, "row"),
        P("row", "col"),
        P("col", None, "row"),
        P("col", None, "row"),
        P(None, "row"),
        P(None, "row"),
        P("row", "col"),
        P("row", "col"),
        P(None, "col"),
        P(None, "col"),
        P("col", None, "row"),
        P("col", None, "row"),
        P("row", "col"),
        P("row", "col"),
    )
    out_specs = (
        P(("dp", "row"), "col"),
        P(("dp", "row"), "col"),
        P("col", None, "row"),
        P("col", None, "row"),
        P("col", None, "row"),
        P(None, "row"),
        P(None, "row"),
        P(None, "row"),
        P("row", "col"),
        P("row", "col"),
        P("row", "col"),
        P(None, "col"),
        P(None, "col"),
        P(None, "col"),
        P("col", None, "row"),
        P("col", None, "row"),
        P("col", None, "row"),
        P("row", "col"),
        P("row", "col"),
        P("row", "col"),
        P(),
    )
    return jax.shard_map(shards, mesh=mesh, in_specs=in_specs, out_specs=out_specs, check_vma=False)
```

```python
import functools

import jax
import jax.numpy as jnp
from jax import lax
from jax.experimental import pallas as pl
from jax.experimental.layout import Layout, with_layout_constraint
from jax.experimental.pallas import tpu as pltpu
from jax.sharding import PartitionSpec as P

D = 1024
SEQ_LEAST = 4096
STEP = 5
MIB = 1024 * 1024


norm_eps = 1e-05
adam_eps = 1e-06
beta_one = 0.5
beta_two = 0.6
learn_rate = 0.5
decay_rate = 0.01
low = jnp.bfloat16
wide = jnp.float32


def from_behind(block, axis, distance):
    devices = range(lax.axis_size(axis))
    route = [(i - distance, i) for i in devices if i - distance in devices]
    return lax.ppermute(block, axis, route)


def swap(values, axis):
    return lax.ppermute(values, axis, [(0, 1), (1, 0)])


def swap_halves(halves):
    return [swap(half, "row") for half in halves]


def to_home(values):
    return lax.ppermute(values, ("row", "col"), [(1, 0), (2, 3)])


def home_to_sibling(values):
    return lax.ppermute(values, ("row", "col"), [(0, 2), (3, 1)])


def home_to_away(values):
    return lax.ppermute(values, ("row", "col"), [(0, 1), (3, 2)])


def sibling_to_home(values):
    return lax.ppermute(values, ("row", "col"), [(2, 0), (1, 3)])


def contract(left, right, left_dim, right_dim):
    return lax.dot_general(
        left, right, (((left_dim,), (right_dim,)), ((), ())), preferred_element_type=wide
    )


def mul(left, right):
    return contract(left, right, 1, 0)


def mul_t(left, right):
    return contract(left, right, 1, 1)


def t_mul(left, right):
    return contract(left, right, 0, 0)


def lamb_moments(weight, grad, first, second, decay):
    first_new = beta_one * first + (1.0 - beta_one) * grad
    second_new = beta_two * second + (1.0 - beta_two) * grad * grad
    direction = (first_new * (1.0 / (1.0 - beta_one**STEP))) / (
        jnp.sqrt(second_new * (1.0 / (1.0 - beta_two**STEP))) + adam_eps
    ) + decay * weight
    return (first_new, second_new, direction)


def square_pair(weight, direction):
    return jnp.stack([jnp.sum(weight * weight), jnp.sum(direction * direction)])


def kernel_call(kernel, grid, in_specs, out_specs, out_shape, scratch, args, aliases=None, mib=1):
    return pl.pallas_call(
        kernel,
        grid_spec=pltpu.PrefetchScalarGridSpec(
            num_scalar_prefetch=1,
            grid=grid,
            in_specs=in_specs,
            out_specs=out_specs,
            scratch_shapes=scratch,
        ),
        out_shape=out_shape,
        input_output_aliases=aliases or {},
        compiler_params=pltpu.CompilerParams(vmem_limit_bytes=48 * MIB),
        cost_estimate=pl.CostEstimate(flops=0, bytes_accessed=mib * MIB, transcendentals=0),
    )(*args)


SCALARS = pl.BlockSpec(memory_space=pltpu.SMEM)


def norm_kernel(where, grad, *refs):
    sums = refs[-1]
    groups = [refs[:3], refs[3:6]][: len(refs) // 3]
    rows = groups[0][0].shape[0]
    zero = jnp.zeros((8, groups[0][0].shape[1]), wide)
    for k, (p, m, v) in enumerate(groups):

        def body(at, total):
            here = pl.ds(pl.multiple_of(at * 32, 32), 32)
            weight = p[here, :]
            direction = lamb_moments(
                weight, grad[here, :].astype(wide), m[here, :], v[here, :], decay_rate
            )[2]
            return tuple(
                t + (sq[:8] + sq[8:16]) + (sq[16:24] + sq[24:])
                for t, sq in zip(total, (weight * weight, direction * direction))
            )

        total = lax.fori_loop(0, rows // 32, body, (zero, zero))
        mine = 1.0 if len(groups) == 1 else ((where[0] >> 1) == k).astype(wide)
        for j in range(2):
            sums[2 * k + j] = jnp.sum(total[j]) * mine


def norm_pairs_kernel(where, grad, p, m, v, sums):
    rows, cols = grad.shape
    tiles = cols // 128
    side = where[0] >> 1
    zero = jnp.zeros((8, 128), wide)
    total = [zero, zero]
    for tile in range(tiles):
        here = pl.ds(2 * tile + side, rows, stride=2 * tiles)
        weight = p[here, :]
        direction = lamb_moments(
            weight, grad[:, tile * 128 : (tile + 1) * 128].astype(wide), m[here, :], v[here, :], decay_rate
        )[2]
        for j, sq in enumerate((weight * weight, direction * direction)):
            total[j] = total[j] + jnp.sum((sq).reshape(rows // 8, 8, 128), axis=0)
    for j in range(2):
        sums[j] = jnp.sum(total[j])


def share_norms(where, grad, states, rows, pairs=False):
    specs, args = [], []
    for state, at in states:
        for array in state:
            if pairs:
                spec = pl.BlockSpec(
                    (rows, array.shape[1]), lambda i, w, at=at: (at + (w[0] & 1), 0)
                )
            elif len(states) == 2:
                spec = pl.BlockSpec(
                    (rows, array.shape[1]), lambda i, w, at=at: (at + (w[0] & 1), 0)
                )
            else:
                spec = pl.BlockSpec((rows, array.shape[1]), lambda i, w, at=at: (at + w[0], 0))
            specs.append(spec)
            args.append(array)
    return kernel_call(
        norm_pairs_kernel if pairs else norm_kernel,
        (1,),
        [whole_spec(grad.shape)] + specs,
        SCALARS,
        jax.ShapeDtypeStruct((2 * len(states),), wide),
        [],
        (where, grad, *args),
    )


def lamb_loop(refs, outs, ratio, rows, step, pick):
    p, m, v = refs

    def body(at, carry):
        here = pl.ds(pl.multiple_of(at * step, step), step)
        weight = p[here, :]
        first_new, second_new, direction = lamb_moments(
            weight, pick(here), m[here, :], v[here, :], decay_rate
        )
        outs[0][here, :] = weight - ratio * direction
        outs[1][here, :] = first_new
        outs[2][here, :] = second_new
        return carry

    lax.fori_loop(0, rows // step, body, 0)


def lamb_plain(half_of_block, where, ratio, part, got, p, m, v, *outs):
    use = half_of_block(pl.program_id(0)) == (where[0] >> 1)

    def pick(here):
        return jnp.where(use, part[here, :].astype(wide), got[here, :].astype(wide))

    lamb_loop((p, m, v), outs, ratio[0], p.shape[0], 64, pick)


def lamb_pairs(where, ratio, part, got, p, m, v, p_out, m_out, v_out, mixed):
    rows, cols = part.shape
    tiles = cols // 128
    for value, order in ((0, (part, got)), (1, (got, part))):

        @pl.when((where[0] >> 1) == value)
        def _():
            for tile in range(tiles):
                for side, ref in enumerate(order):
                    mixed[pl.ds(2 * tile + side, rows, stride=2 * tiles), :] = ref[
                        :, tile * 128 : (tile + 1) * 128
                    ].astype(wide)

    lamb_loop(
        (p, m, v), (p_out, m_out, v_out), ratio[0], p.shape[0], 192, lambda here: mixed[here, :]
    )


def lamb_call(kernel, where, ratio, grad, grad_block, grad_at, state, block, start, count, before, scratch):
    rows, cols = state[0].shape
    flat = pl.BlockSpec((block, cols), lambda i, w: (i + start, 0))
    grad_spec = pl.BlockSpec((grad_block, grad[0].shape[1]), lambda i, w: (grad_at(i), 0))
    whole = jax.ShapeDtypeStruct((rows, cols), wide)
    args = [where, ratio, *grad, *state]
    specs = [SCALARS, grad_spec, grad_spec, flat, flat, flat]
    run, aliases = kernel, {}
    if before is not None:
        aliases = {len(args) + k: k for k in range(3)}

        def run(*refs):
            kernel(*refs[: len(args)], *refs[len(args) + 3 :])

    return list(
        kernel_call(
            run,
            (count,),
            specs + [pl.BlockSpec(memory_space=pl.ANY)] * len(aliases),
            [flat, flat, flat],
            [whole, whole, whole],
            scratch,
            (*args, *(before or [])),
            aliases,
            mib=26 * count * block * cols // MIB,
        )
    )


def to_linear(values):
    rows, sides, cols = values.shape
    split = with_layout_constraint(
        values.reshape(rows, sides, cols // 128, 128), Layout(major_to_minor=(0, 2, 1, 3))
    )
    return split.transpose(0, 2, 1, 3).reshape(rows * sides * cols // 128, 128)


def from_linear(values, rows, sides):
    cols = values.size // (rows * sides)
    split = values.reshape(rows, cols // 128, sides, 128).transpose(0, 2, 1, 3)
    split = with_layout_constraint(split, Layout(major_to_minor=(0, 2, 1, 3)))
    return split.reshape(rows, sides, cols)


def apply_trust(weight, direction, norms):
    return weight - learn_rate * (norms[0] / (norms[1] + adam_eps)) * direction


def flip(values, bit):
    size = lax.axis_size("dp")
    return lax.ppermute(values, "dp", [(i, i ^ (1 << bit)) for i in range(size)])


def dp_bit(bit):
    return (lax.axis_index("dp") >> bit) & 1


def rows_of(values, start, rows):
    return lax.dynamic_slice_in_dim(values, start, rows, 0)


def total_of(pieces):
    total = pieces[0].astype(wide)
    for piece in pieces[1:]:
        total = total + piece.astype(wide)
    return total


def tie(values, *deps):
    return lax.optimization_barrier((values, *deps))[0]


def low_total(pieces):
    return total_of(pieces).astype(low)


def keep_or_join(bit, part, other):
    return jnp.where(
        dp_bit(bit) == 0,
        jnp.concatenate([part, other]),
        jnp.concatenate([other, part]),
    )


def share_of(weight, order):
    rows = weight.shape[0] // (1 << len(order))
    index = 0
    for bit in order:
        index = 2 * index + dp_bit(bit)
    return rows_of(weight, index * rows, rows)


def half_of(piece, place):
    rows = piece.shape[-2] // 2
    return lax.dynamic_slice_in_dim(piece, place * rows, rows, piece.ndim - 2)


def chunk_sum(chunk, order, keep):
    bits = {"y": 0, "l": 1}
    steps = [name if name == "x" else bits[name] for name in order]
    pieces = [chunk]
    for step in steps:
        if step == "x":
            whole = len(pieces) == 1
            got = yield step, pieces[0][1] if whole else low_total([piece[1] for piece in pieces])
            pieces = [piece[0] for piece in pieces] + [got]
        else:
            here = dp_bit(step)
            got = yield step, low_total([half_of(piece, 1 - here) for piece in pieces])
            pieces = [half_of(piece, here) for piece in pieces] + [got]
    part = low_total(pieces)
    for step in range((lax.axis_size("dp") - 1).bit_length()):
        if step not in steps:
            got = yield step, part
            part = low_total([part, got])
    keep(part)
    first, second = [step for step in steps if step != "x"]
    got = yield second, part
    part = keep_or_join(second, part, got)
    got = yield first, part
    return part, got


def norm_sum(values, steps, others=None):
    for step in steps:
        if step == 1 and others is not None:
            values = jnp.concatenate([values, others()])
        got = yield step, values
        values = values + got
    return values


def where_of(order):
    bits = {"y": 0, "l": 1}
    first, second = [bits[name] for name in order if name != "x"]
    return (2 * dp_bit(first) + dp_bit(second)).astype(jnp.int32).reshape(1)


def move(step, send):
    if step == "row":
        return swap(send, "row")
    return swap(send, "col") if step == "x" else flip(send, step)


class Turns:
    def __init__(self):
        self.chunks = {}
        self.arrivals = {}
        self.seen = {}
        self.done = {}
        self.shares = {}
        self.after = ()

    def add(self, name, chunk, order):
        self.chunks[name] = chunk_sum(chunk, order, functools.partial(self.shares.__setitem__, name))

    def add_norms(self, name, values, steps=("x", "row", 1, 0), others=None):
        self.chunks[name] = norm_sum(values, steps, others)

    def turn(self, name):
        got = self.arrivals.get(name)
        try:
            if got is None:
                self.seen[name] = []
                step, send = next(self.chunks[name])
                send = tie(send, *self.after)
            else:
                got = tie(got, *self.after)
                self.seen[name].append(got)
                step, send = self.chunks[name].send(got)
        except StopIteration as end:
            self.done[name] = end.value
            return
        self.arrivals[name] = move(step, send)
        self.after = (send,)

    def run(self, names):
        for name in names:
            if name not in self.done:
                self.turn(name)

    def reach_shares(self, names):
        while any(name not in self.shares for name in names):
            self.run([name for name in names if name not in self.shares])

    def finish(self):
        while len(self.done) < len(self.chunks):
            self.run(self.chunks)


def deinterleave(pairs, gate, up):
    rows, cols = gate.shape
    tiles = cols // 128
    for tile in range(tiles):
        for side, out in enumerate((gate, up)):
            out[:, tile * 128 : (tile + 1) * 128] = pairs[
                pl.ds(2 * tile + side, rows, stride=2 * tiles), :
            ].astype(low)


def split_pairs(linear, rows, cols):
    block = 64
    half = jax.ShapeDtypeStruct((rows, cols), low)
    out_spec = pl.BlockSpec((block, cols), lambda i: (i, 0))
    return pl.pallas_call(
        deinterleave,
        grid=(rows // block,),
        in_specs=[pl.BlockSpec((block * 2 * cols // 128, 128), lambda i: (i, 0))],
        out_specs=[out_spec, out_spec],
        out_shape=[half, half],
        compiler_params=pltpu.CompilerParams(vmem_limit_bytes=24 * MIB),
        cost_estimate=pl.CostEstimate(
            flops=rows * cols, bytes_accessed=12 * rows * cols, transcendentals=0
        ),
    )(linear)


def dot_of(left, right, left_dim, right_dim):
    return lax.dot_general(
        left, right, (((left_dim,), (right_dim,)), ((), ())), preferred_element_type=wide
    )


def local_call(kernel, grid, in_specs, out_specs, out_shape, scratch, args, prefetch=0):
    return pl.pallas_call(
        kernel,
        grid_spec=pltpu.PrefetchScalarGridSpec(
            num_scalar_prefetch=prefetch,
            grid=grid,
            in_specs=in_specs,
            out_specs=out_specs,
            scratch_shapes=scratch,
        ),
        out_shape=out_shape,
        compiler_params=pltpu.CompilerParams(vmem_limit_bytes=48 * MIB),
        cost_estimate=pl.CostEstimate(flops=0, bytes_accessed=MIB, transcendentals=0),
    )(*args)


def whole_spec(shape):
    return pl.BlockSpec(shape, lambda *_: (0,) * len(shape))


def shape_of(dims, kind):
    return jax.ShapeDtypeStruct(dims, kind)


def row_scale(halves):
    total = sum(jnp.sum(half * half, axis=1, keepdims=True) for half in halves)
    return lax.rsqrt(total / D + norm_eps)


def branch_kernel(tok, gains, taps, own, other, n1, gate_b, gate_c, gate_x, conv, hidden, part0, part1, ext):
    long, width = n1.shape[1:]
    rows = conv.shape[0]
    step = long // 3

    def gates(at, carry):
        here = pl.ds(pl.multiple_of(at * step, step), step)
        halves = [tok[h, here, :].astype(wide) for h in range(2)]
        scale = row_scale(halves)
        for h in range(2):
            n1[h, here, :] = (halves[h] * scale * gains[h]).astype(low)
        for g, out in enumerate((gate_b, gate_c, gate_x)):
            w = slice(g * width, (g + 1) * width)
            out[here, :] = dot_of(n1[0, here, :], own[w, :], 1, 0) + dot_of(
                n1[1, here, :], other[w, :], 1, 0
            )
        return carry

    lax.fori_loop(0, 3, gates, 0)
    ext[8 : 8 + rows, :] = gate_b[:rows, :] * gate_x[:rows, :]
    ext[6:8, :] = gate_b[rows : rows + 2, :] * gate_x[rows : rows + 2, :]
    w_out = slice(3 * width, 4 * width)
    quarter = rows // 4
    for at in range(4):
        start = at * quarter
        taken = slice(start, start + quarter)
        value = sum(taps[k] * ext[start + 6 + k : start + 6 + k + quarter, :] for k in range(3))
        conv[taken, :] = value
        low_hidden = (gate_c[taken, :] * value).astype(low)
        hidden[taken, :] = low_hidden
        for part, weight in ((part0, own), (part1, other)):
            part[taken, :] = dot_of(low_hidden, weight[w_out, :], 1, 0).astype(low)


def branch_forward(tok, rows, tails, gains, taps, own, other):
    width = tok.shape[2]
    gate = shape_of((rows + tails, width), wide)
    outs = [
        shape_of((2, rows + tails, width), low),
        gate,
        gate,
        gate,
        shape_of((rows, width), wide),
        shape_of((rows, width), low),
        shape_of((rows, width), low),
        shape_of((rows, width), low),
    ]
    args = (tok, gains, taps, own, other)
    return local_call(
        branch_kernel,
        (1,),
        [whole_spec(a.shape) for a in args],
        [whole_spec(o.shape) for o in outs],
        outs,
        [pltpu.VMEM((rows + 8, width), wide)],
        args,
    )


def piece_at(bits, which, piece, width):
    place = bits[which] if piece == 0 else 1 - bits[which]
    return pl.ds(pl.multiple_of(place * width, width), width)


def ffn_kernel(bits, tok, mine0, mine1, theirs0, theirs1, gains, g0, g1, g2, u0, u1, u2, n2, res, gate, up, act):
    width = g1.shape[0]

    @pl.when(pl.program_id(0) == 0)
    def _():
        for h, (mine, theirs) in enumerate(((mine0, theirs0), (mine1, theirs1))):
            res[h] = tok[h, : res.shape[1], :].astype(wide) + (
                mine[...].astype(wide) + theirs[...].astype(wide)
            )
        scale = row_scale([res[0], res[1]])
        for h in range(2):
            n2[h] = (res[h] * scale * gains[h]).astype(low)

    for which, (out, w0, w1, w2) in enumerate(((gate, g0, g1, g2), (up, u0, u1, u2))):
        total = dot_of(n2[0], w0[...], 1, 0)
        for piece, w in enumerate((w1, w2)):
            total += dot_of(n2[1, :, piece_at(bits, which, piece, width)], w[...], 1, 0)
        out[...] = total
    value = gate[...]
    act[...] = (value * jax.nn.sigmoid(value) * up[...]).astype(low)


def ffn_forward(bits, tok, mine, theirs, gains, weights):
    rows, width = mine[0].shape
    cols = weights[0].shape[1]
    tile = cols // 3
    both = (2, rows, width)
    full = whole_spec(both)
    wide_tile = pl.BlockSpec((rows, tile), lambda i, *_: (0, i))
    weight_specs = [pl.BlockSpec((w.shape[0], tile), lambda i, *_: (0, i)) for w in weights]
    return local_call(
        ffn_kernel,
        (3,),
        [whole_spec(tok.shape)]
        + [whole_spec((rows, width))] * 4
        + [whole_spec(gains.shape)]
        + weight_specs,
        [full, full, wide_tile, wide_tile, wide_tile],
        [
            shape_of(both, low),
            shape_of(both, wide),
            shape_of((rows, cols), wide),
            shape_of((rows, cols), wide),
            shape_of((rows, cols), low),
        ],
        [],
        (bits, tok, *mine, *theirs, gains, *weights),
        prefetch=1,
    )


def ffn_back_kernel(
    bits, cot, d_own, d_other, gate, up, g0, g1, g2, u0, u1, u2, g_gate, g_up, part0, part1, total
):
    width = g1.shape[0]

    @pl.when(pl.program_id(0) == 0)
    def _():
        total[...] = jnp.zeros_like(total)

    start = cot.shape[1] - gate.shape[0]
    g_act = dot_of(cot[0, start:, :], d_own[...], 1, 1) + dot_of(cot[1, start:, :], d_other[...], 1, 1)
    value = gate[...]
    sigma = jax.nn.sigmoid(value)
    g_gate[...] = (g_act * up[...] * sigma * (1.0 + value * (1.0 - sigma))).astype(low)
    g_up[...] = (g_act * (value * sigma)).astype(low)
    total[0] += dot_of(g_gate[...], g0[...], 1, 1) + dot_of(g_up[...], u0[...], 1, 1)
    for which, (grad, w1, w2) in enumerate(((g_gate, g1, g2), (g_up, u1, u2))):
        for piece, w in enumerate((w1, w2)):
            total[1, :, piece_at(bits, which, piece, width)] += dot_of(grad[...], w[...], 1, 1)

    @pl.when(pl.program_id(0) == pl.num_programs(0) - 1)
    def _():
        part0[...] = total[0].astype(low)
        part1[...] = total[1].astype(low)


def ffn_backward(bits, cot, downs, gate, up, weights):
    rows, cols = gate.shape
    tile = cols // 3
    part = (rows, cot.shape[2])
    wide_tile = pl.BlockSpec((rows, tile), lambda i, *_: (0, i))
    weight_specs = [pl.BlockSpec((w.shape[0], tile), lambda i, *_: (0, i)) for w in weights]
    down_spec = pl.BlockSpec((tile, downs[0].shape[1]), lambda i, *_: (i, 0))
    return local_call(
        ffn_back_kernel,
        (3,),
        [whole_spec(cot.shape), down_spec, down_spec, wide_tile, wide_tile] + weight_specs,
        [wide_tile, wide_tile, whole_spec(part), whole_spec(part)],
        [shape_of((rows, cols), low)] * 2 + [shape_of(part, low)] * 2,
        [pltpu.VMEM((2, *part), wide)],
        (bits, cot, *downs, gate, up, *weights),
        prefetch=1,
    )


def put(outs, half, rows, value):
    if len(outs) == 2:
        outs[half][rows, :] = value.astype(low)
    else:
        outs[0][half, rows, :] = value.astype(low)


def chunk_outs(split, rows, cols):
    if split:
        return [whole_spec((rows, cols))] * 2, [shape_of((rows, cols), low)] * 2
    return [whole_spec((2, rows, cols))], [shape_of((2, rows, cols), low)]


def pair_grad_kernel(items, n2, g_gate, g_up, *outs):
    rows = outs[0].shape[-2] // 2
    for at, split in items:
        count = 2 if split else 1
        mine, outs = outs[:count], outs[count:]
        for h in range(2):
            left = n2[h, :, at * rows : (at + 1) * rows]
            for side, grad in enumerate((g_gate, g_up)):
                put(mine, h, slice(side * rows, (side + 1) * rows), dot_of(left, grad[...], 0, 0))


def pair_grads(n2, g_gate, g_up, items, rows):
    specs, shapes = [], []
    for _, split in items:
        more = chunk_outs(split, 2 * rows, g_gate.shape[1])
        specs += more[0]
        shapes += more[1]
    outs = local_call(
        functools.partial(pair_grad_kernel, items),
        (1,),
        [whole_spec(n2.shape), whole_spec(g_gate.shape), whole_spec(g_up.shape)],
        specs,
        shapes,
        [],
        (n2, g_gate, g_up),
    )
    found = []
    for _, split in items:
        count = 2 if split else 1
        found.append(tuple(outs[:count]) if split else outs[0])
        outs = outs[count:]
    return found


def down_grad_kernel(act, cot, *outs):
    start = cot.shape[1] - act.shape[0]
    for h in range(2):
        put(outs, h, slice(None), dot_of(act[...], cot[h, start:, :], 0, 0))


def down_grads(act, cot, at, rows, split):
    specs, shapes = chunk_outs(split, rows, cot.shape[2])
    outs = local_call(
        down_grad_kernel,
        (1,),
        [pl.BlockSpec((act.shape[0], rows), lambda i: (0, at)), whole_spec(cot.shape)],
        specs,
        shapes,
        [],
        (act, cot),
    )
    return tuple(outs) if split else outs[0]


def branch_back_kernel(
    mine0, mine1, theirs0, theirs1, res, cot, gains, taps, own, other, gate_b, gate_c, gate_x, conv,
    g_res, g_low, g_proj, gain_grad, tap_grad, ext, ext_grad,
):
    _, rows, width = res.shape
    scale = row_scale([res[0], res[1]])
    grads = [
        mine[...].astype(wide) + theirs[...].astype(wide)
        for mine, theirs in ((mine0, theirs0), (mine1, theirs1))
    ]
    inner = sum(
        jnp.sum(grads[h] * gains[h] * res[h], axis=1, keepdims=True) for h in range(2)
    )
    factor = scale * scale * scale * inner / D
    for h in range(2):
        gain_grad[h] = jnp.sum(grads[h] * res[h] * scale, axis=0, keepdims=True)
        value = cot[h, cot.shape[1] - rows :, :].astype(wide) + (scale * (grads[h] * gains[h]) - res[h] * factor)
        g_res[h] = value
        g_low[h] = value.astype(low)
    g_hidden = dot_of(g_low[0], own[...], 1, 1) + dot_of(g_low[1], other[...], 1, 1)
    g_proj[1, :rows, :] = (g_hidden * conv[...]).astype(low)
    g_conv = g_hidden * gate_c[:rows, :]
    ext_grad[:rows, :] = g_conv
    ext_grad[rows:, :] = jnp.zeros((8, width), wide)
    ext[8 : 8 + rows, :] = gate_b[:rows, :] * gate_x[:rows, :]
    ext[6:8, :] = gate_b[rows : rows + 2, :] * gate_x[rows : rows + 2, :]
    for k in range(3):
        tap_grad[k : k + 1, :] = jnp.sum(
            g_conv * ext[6 + k : 6 + k + rows, :], axis=0, keepdims=True
        )
    g_mixed = sum(taps[2 - k] * ext_grad[k : k + rows, :] for k in range(3))
    g_proj[0, :rows, :] = (g_mixed * gate_x[:rows, :]).astype(low)
    g_proj[2, :rows, :] = (g_mixed * gate_b[:rows, :]).astype(low)
    tails = g_proj.shape[1] - rows
    row = lax.broadcasted_iota(jnp.int32, (tails, width), 0)
    first, second = ext_grad[0:1, :], ext_grad[1:2, :]
    g_before = jnp.where(
        row == 0,
        taps[0] * first,
        jnp.where(row == 1, taps[1] * first + taps[0] * second, 0.0),
    )
    g_proj[0, rows:, :] = (g_before * gate_x[rows:, :]).astype(low)
    g_proj[1, rows:, :] = jnp.zeros((tails, width), low)
    g_proj[2, rows:, :] = (g_before * gate_b[rows:, :]).astype(low)


def branch_backward(mine, theirs, res, cot, gains, taps, own, other, gates, conv):
    _, rows, width = res.shape
    long = gates[0].shape[0]
    out_weight = pl.BlockSpec((width, width), lambda i, *_: (3, 0))
    outs = [
        shape_of(res.shape, wide),
        shape_of(res.shape, low),
        shape_of((3, long, width), low),
        shape_of((2, 1, width), wide),
        shape_of((3, width), wide),
    ]
    full = whole_spec(res.shape)
    return local_call(
        branch_back_kernel,
        (1,),
        [whole_spec((rows, width))] * 4
        + [full, whole_spec(cot.shape), whole_spec(gains.shape), whole_spec(taps.shape)]
        + [out_weight, out_weight]
        + [whole_spec(g.shape) for g in gates]
        + [whole_spec(conv.shape)],
        [whole_spec(o.shape) for o in outs],
        outs,
        [pltpu.VMEM((rows + 8, width), wide), pltpu.VMEM((rows + 8, width), wide)],
        (*mine, *theirs, res, cot, gains, taps, own, other, *gates, conv),
    )


def branch_grad_kernel(left0, left1, right0, right1, own, other):
    rows = own.shape[0] // 2
    for h, out in enumerate((own, other)):
        for k, (left, right) in enumerate(((left0, right0), (left1, right1))):
            one = left[h] if len(left.shape) == 3 else left[...]
            two = right[h] if k == 1 and len(left.shape) == 2 else right[0]
            out[k * rows : (k + 1) * rows, :] = dot_of(one, two, 0, 0).astype(low)


def branch_grads(n1, g_proj, gate, second):
    width = n1.shape[2]
    gate_spec = pl.BlockSpec((1, *g_proj.shape[1:]), lambda i: (gate, 0, 0))
    if second is None:
        left, right = n1, g_proj
        right_spec = pl.BlockSpec((1, *g_proj.shape[1:]), lambda i: (gate + 1, 0, 0))
    else:
        left, right = second
        right_spec = whole_spec(right.shape)
    specs, shapes = chunk_outs(True, 2 * width, width)
    return local_call(
        branch_grad_kernel,
        (1,),
        [whole_spec(n1.shape), whole_spec(left.shape), gate_spec, right_spec],
        specs,
        shapes,
        [],
        (n1, left, g_proj, right),
    )


def shards(
    tokens,
    cotangent,
    input_projection_weight,
    conv_weight,
    output_projection_weight,
    norm_gains,
    gate_up_weight,
    down_projection_weight,
    in_first,
    in_second,
    conv_first,
    conv_second,
    out_first,
    out_second,
    gain_first,
    gain_second,
    gu_first,
    gu_second,
    down_first,
    down_second,
):
    feat_cols = tokens.shape[1]
    branch_cols = conv_weight.shape[1]
    hidden_cols = down_projection_weight.shape[0]
    block_rows = tokens.shape[0]
    seq_len = max(SEQ_LEAST, block_rows * lax.axis_size("dp") * lax.axis_size("col"))
    data_pos = lax.axis_index("dp")
    row_pos = lax.axis_index("row")
    col_pos = lax.axis_index("col")
    home = row_pos == col_pos
    tail_rows = 16

    in_low = jnp.transpose(input_projection_weight, (1, 0, 2)).astype(low).reshape(-1, branch_cols)
    io_low = jnp.concatenate([in_low, output_projection_weight.astype(low)])
    io_share = share_of(io_low, (1, 0))
    io_got = swap(io_share, "col")
    row_start = (data_pos * lax.axis_size("row") + row_pos) * block_rows
    tail = from_behind(tokens[-2:], ("dp", "row"), 1)
    tail = jnp.where(row_start % seq_len != 0, tail, jnp.zeros_like(tail))
    spare = jnp.zeros((tail_rows - 8, feat_cols), low)
    gain_parts = []
    left = norm_gains
    for _ in range(3):
        gain_parts.append(lax.reduce_precision(left, 8, 7))
        left = left - gain_parts[-1]
    gain_parts = jnp.concatenate(gain_parts).astype(low)
    extra = tie(jnp.concatenate([tail, gain_parts, spare]))
    block = jnp.concatenate([tie(tokens, io_got), extra, cotangent])
    away = to_home(block)
    gu_weight = to_linear(gate_up_weight)
    gate_low, up_low = split_pairs(gu_weight, feat_cols, hidden_cols)
    down_low = down_projection_weight.astype(low)
    both = jnp.stack([block, away])
    both = jnp.where(home, both, home_to_sibling(both))
    gains = both[:, block_rows + 2 : block_rows + 8].astype(wide)
    gains = gains[:, 0:2] + gains[:, 2:4] + gains[:, 4:6]
    gains = [gains[:, k : k + 1] for k in range(2)]
    gate_got = swap(tie(share_of(gate_low, (1, 0)), io_got), "col")
    up_got = swap(tie(share_of(up_low, (0, 1)), gate_got), "col")
    down_got = swap(tie(down_low, up_got), "col")
    io_pair = keep_or_join(0, io_got, flip(io_got, 0))
    io_other = keep_or_join(1, io_pair, flip(io_pair, 1))
    gate_pair = keep_or_join(0, gate_got, flip(tie(gate_got, io_pair), 0))
    up_pair = keep_or_join(1, up_got, flip(tie(up_got, io_pair), 1))
    gate_more = flip(gate_pair, 1)
    up_more = flip(up_pair, 0)
    weights = [gate_low, gate_pair, gate_more, up_low, up_pair, up_more]
    bits = jnp.stack([dp_bit(1), dp_bit(0)]).astype(jnp.int32)
    downs = [down_low, down_got]

    n1, gate_b, gate_c, gate_x, conv, hidden, *branch = branch_forward(
        both, block_rows, tail_rows, gains[0], conv_weight, io_low, io_other
    )
    n2, res, gate, upper, act = ffn_forward(
        bits, both, branch, swap_halves(branch), gains[1], weights
    )

    turns = Turns()
    orders = dict(D="xyl", d="ylx", a="xyl", b="lyx", c="xyl", e="lyx", I="xyl", i="xyl")
    down_half = hidden_cols // 2
    for k, name in enumerate("Dd"):
        split = orders[name][0] == "x"
        turns.add(name, down_grads(act, both, k, down_half, split), orders[name])
    turns.run("Dd")
    g_gate, g_up, *part_two = ffn_backward(
        bits, tie(both, *turns.after), downs, gate, upper, weights
    )
    quarter = feat_cols // 4
    for names in ("ab", "ce"):
        items = [("abce".index(name), orders[name][0] == "x") for name in names]
        for name, chunk in zip(names, pair_grads(n2, g_gate, g_up, items, quarter)):
            turns.add(name, chunk, orders[name])
    turns.run("abcDe")
    g_res, g_branch, g_proj, gain_two_grad, conv_grad = branch_backward(
        part_two,
        swap_halves(part_two),
        tie(res, *turns.after),
        both,
        gains[1],
        conv_weight,
        io_low,
        io_other,
        (gate_b, gate_c, gate_x),
        conv,
    )
    turns.add("I", branch_grads(n1, g_proj, 0, None), orders["I"])
    io_last = branch_grads(n1, g_proj, 2, (hidden, g_branch))
    turns.after += tuple(io_last)
    turns.run("IdabD")

    g_late = tie(g_proj, *turns.after)
    io_half = [half.reshape(4, feat_cols, branch_cols) for half in (io_low, io_other)]
    g_part = jnp.stack(
        [sum(mul_t(g_late[g], io_half[h][g]) for g in range(3)).astype(low) for h in range(2)]
    )
    g_long = g_part.astype(wide) + swap(g_part, "row").astype(wide)
    tok = both[:, : block_rows + 2].astype(wide)
    scale = lax.rsqrt(jnp.sum(tok * tok, axis=(0, 2)) / D + norm_eps)[None, :, None]
    gain_one_grad = jnp.sum(g_long[:, : block_rows + 2] * tok * scale, axis=1)
    small = [
        jnp.concatenate([conv_grad, gain_one_grad[h : h + 1], gain_two_grad[h]]) for h in range(2)
    ]
    spare = jnp.zeros((16, feat_cols), low)
    small = [jnp.pad(part, ((0, 11), (0, 0))).astype(low) for part in small]
    io_long = []
    for h in range(2):
        pieces = jnp.split(io_last[h], 4)
        io_long.append(
            jnp.concatenate(
                [pieces[0], small[h], pieces[1], spare, pieces[2], spare, pieces[3], spare]
            )
        )
    turns.add("i", io_long, orders["i"])
    turns.run("eiacbdDIcaeDciIabDdcieIDabd")

    def in_flat(values):
        return jnp.transpose(values, (1, 0, 2)).reshape(3 * feat_cols, branch_cols)

    def in_back(values):
        return jnp.transpose(values.reshape(3, feat_cols, branch_cols), (1, 0, 2))

    wheres = {name: where_of(orders[name]) for name in orders}
    down_state = (down_projection_weight, down_first, down_second)
    gu_state = (gu_weight, to_linear(gu_first), to_linear(gu_second))
    in_state = (in_flat(input_projection_weight), in_flat(in_first), in_flat(in_second))
    out_state = (output_projection_weight, out_first, out_second)
    pairs = 2 * hidden_cols // 128

    shares = turns.shares
    part_rows = feat_cols // 2
    turns.reach_shares("Dd")
    down_squares = sum(
        share_norms(wheres[n], shares[n], [(down_state, 4 * k)], down_half // 4)
        for k, n in enumerate("Dd")
    )
    turns.add_norms("p", down_squares)
    turns.run("pacpibpcep")
    turns.reach_shares("abce")
    gu_squares = sum(
        share_norms(wheres[n], shares[n], [(gu_state, 2 * k)], quarter // 2 * pairs, pairs=True)
        for k, n in enumerate("abce")
    )
    turns.add_norms("n", gu_squares, ("x", "row"))
    turns.run("nIdnbipn")
    turns.reach_shares("Ii")
    io_squares = share_norms(wheres["i"], shares["i"], [(in_state, 4), (out_state, 0)], part_rows)
    in_squares = share_norms(wheres["I"], shares["I"], [(in_state, 0)], part_rows)
    turns.add_norms(
        "m", io_squares + jnp.pad(in_squares, (0, 2)), others=lambda: turns.done["n"]
    )
    turns.run("medmIemimIim")
    turns.finish()
    sums, seen = turns.done, turns.seen

    back = tie(g_long[::-1, block_rows : block_rows + 2], seen["i"][4])
    back = from_behind(back, ("dp", "col"), -1)
    g_n1 = g_long[:, :block_rows].at[:, -2:].add(back)
    tok, scale = tok[:, :block_rows], scale[:, :block_rows]
    weighted = g_n1 * gains[0]
    inner = jnp.sum(weighted * tok, axis=(0, 2))[None, :, None]
    tok_half = (g_res + (scale * weighted - tok * (scale * scale * scale * inner / D))).astype(low)
    token_grad = jnp.where(home, tok_half[0], home_to_away(tok_half[1]))
    act = tie(act, seen["D"][1])
    ffn = jnp.stack([mul(act, downs[h]) for h in range(2)])
    out_half = (res + (ffn + sibling_to_home(ffn.astype(low)).astype(wide))).astype(low)
    output = jnp.where(home, out_half[0], home_to_away(out_half[1]))

    def gu_back(values):
        return from_linear(values, feat_cols, 2)

    def ratio_of(norms):
        norms = jnp.sqrt(norms)
        return norms, (learn_rate * (norms[0] / (norms[1] + adam_eps))).reshape(1)

    down_norms, down_ratio = ratio_of(sums["p"])
    (in_norms, in_ratio), (out_norms, out_ratio), (gu_norms, gu_ratio) = [
        ratio_of(sums["m"][k : k + 2]) for k in (0, 2, 4)
    ]

    def later_half(count):
        return functools.partial(lamb_plain, lambda i: (i >= count // 2).astype(jnp.int32))

    def fixed_half(half):
        return functools.partial(lamb_plain, lambda i: half)

    last = sums["i"]
    small = [part[part_rows : part_rows + 5] for part in last]
    small = jnp.where((wheres["i"][0] >> 1) == 0, small[0], small[1]).astype(wide)
    conv_grad, gains_grad = small[:3], small[3:]
    conv_m, conv_v, conv_u = lamb_moments(conv_weight, conv_grad, conv_first, conv_second, 0.0)
    gain_m, gain_v, gain_u = lamb_moments(norm_gains, gains_grad, gain_first, gain_second, 0.0)
    col_first = (col_pos == 0).astype(wide)
    row_first = (row_pos == 0).astype(wide)
    small_weight = jnp.concatenate([conv_weight, norm_gains])
    small_direction = jnp.concatenate([conv_u, gain_u])
    squares = jnp.stack(
        [
            jnp.sum(small_weight * small_weight, axis=1),
            jnp.sum(small_direction * small_direction, axis=1),
        ],
        axis=1,
    )
    small_norms = jnp.concatenate(
        [jnp.sum(squares[:3], axis=0, keepdims=True) * col_first, squares[3:] * row_first]
    )
    down_sums = [sums[name] for name in "Dd"]
    pair_sums = [sums[name] for name in "abce"]
    row_norms = small_norms + swap(small_norms, "row")
    pair_sums[2] = [tie(part, last[1]) for part in pair_sums[2]]
    pair_sums[1] = [tie(part, small_norms) for part in pair_sums[1]]
    pair_sums[3] = [tie(part, row_norms) for part in pair_sums[3]]
    down_sums[1] = [tie(part, row_norms) for part in down_sums[1]]
    down_new = None
    for k in (0, 1):
        name = "Dd"[k]
        block = down_half // 6
        down_new = lamb_call(
            later_half(6), wheres[name], down_ratio, down_sums[k], block, lambda i: i % 3,
            down_state, block, 6 * k, 6, down_new, [],
        )
    gu_new = None
    gu_rows = 32
    for k in (0, 2, 1, 3):
        name = "abce"[k]
        blocks = quarter // gu_rows
        gu_new = lamb_call(
            lamb_pairs, wheres[name], gu_ratio, pair_sums[k], gu_rows, lambda i: i,
            gu_state, gu_rows * pairs, k * blocks, blocks, gu_new,
            [pltpu.VMEM((gu_rows * pairs, 128), wide)],
        )
    small_norms = jnp.sqrt(row_norms + swap(row_norms, "col"))
    last = [tie(part, small_norms) for part in last]
    first_io = [tie(part, small_norms) for part in sums["I"]]
    in_new = lamb_call(
        later_half(4), wheres["I"], in_ratio, first_io, part_rows, lambda i: i % 2,
        in_state, part_rows, 0, 4, None, [],
    )
    in_new = lamb_call(
        fixed_half(0), wheres["i"], in_ratio, last, part_rows + 16, lambda i: i,
        in_state, part_rows, 4, 2, in_new, [],
    )
    out_new = lamb_call(
        fixed_half(1), wheres["i"], out_ratio, last, part_rows + 16, lambda i: i,
        out_state, part_rows, 0, 2, None, [],
    )

    trust_norms = jnp.stack(
        [
            in_norms,
            small_norms[0],
            out_norms,
            small_norms[1],
            small_norms[2],
            gu_norms,
            down_norms,
        ]
    )
    gains_new = jnp.stack(
        [
            apply_trust(norm_gains[0], gain_u[0], small_norms[1]),
            apply_trust(norm_gains[1], gain_u[1], small_norms[2]),
        ]
    )
    return (
        output,
        token_grad,
        *[in_back(values) for values in in_new],
        apply_trust(conv_weight, conv_u, small_norms[0]),
        conv_m,
        conv_v,
        *out_new,
        gains_new,
        gain_m,
        gain_v,
        *[gu_back(values) for values in gu_new],
        *down_new,
        trust_norms,
    )


def solution(mesh):
    in_specs = (
        P(("dp", "row"), "col"),
        P(("dp", "row"), "col"),
        P("col", None, "row"),
        P(None, "row"),
        P("row", "col"),
        P(None, "col"),
        P("col", None, "row"),
        P("row", "col"),
        P("col", None, "row"),
        P("col", None, "row"),
        P(None, "row"),
        P(None, "row"),
        P("row", "col"),
        P("row", "col"),
        P(None, "col"),
        P(None, "col"),
        P("col", None, "row"),
        P("col", None, "row"),
        P("row", "col"),
        P("row", "col"),
    )
    out_specs = (
        P(("dp", "row"), "col"),
        P(("dp", "row"), "col"),
        P("col", None, "row"),
        P("col", None, "row"),
        P("col", None, "row"),
        P(None, "row"),
        P(None, "row"),
        P(None, "row"),
        P("row", "col"),
        P("row", "col"),
        P("row", "col"),
        P(None, "col"),
        P(None, "col"),
        P(None, "col"),
        P("col", None, "row"),
        P("col", None, "row"),
        P("col", None, "row"),
        P("row", "col"),
        P("row", "col"),
        P("row", "col"),
        P(),
    )
    return jax.shard_map(shards, mesh=mesh, in_specs=in_specs, out_specs=out_specs, check_vma=False)
```
